32 devices in a mesh: pool: 4 (over y, x), fsdp: 8 (over z, core).
Axes of the slice: x: 2, y: 2, z: 4, core: 2. Of those that a mesh axis runs over, the one named last changes fastest.
Arguments:
- hidden: bfloat16 [8, 256, 4608], P('fsdp'), may hold values from -6 to 6
- slot_of_request: int32 [8], replicated, may hold values from 0 to 7, each once
- prefix_len: int32 [8], replicated, may hold values from 1 to 1024, 4096 in all
- block_holder: int32 [8, 64], replicated, may hold values from 0 to 7, as said below
- block_slot: int32 [8, 64], replicated, may hold values from 0 to 63, as said below
- kv_pool: bfloat16 [512, 16, 8, 256], P('fsdp', None, 'pool'), may hold values from -12 to 12
- norm_gain: float32 [4608], replicated, may hold values from 0.75 to 2
- q_weight: bfloat16 [4608, 2048], P('fsdp', 'pool'), may hold values from -0.09375 to 0.09375
- k_weight: bfloat16 [4608, 1024], P('fsdp', 'pool'), may hold values from -0.09375 to 0.09375
- v_weight: bfloat16 [4608, 1024], P('fsdp', 'pool'), may hold values from -0.09375 to 0.09375
- o_weight: bfloat16 [4608, 2048], P('fsdp', 'pool'), may hold values from -0.125 to 0.125
- post_gain: float32 [4608], replicated, may hold values from 0.1 to 1.9
Outputs:
- out: bfloat16 [8, 256, 4608], P(None, ('pool', 'fsdp'))
The draws below stay inside these ranges and needn't reach their ends.
Inputs may be any that keep to these rules, and one draw needn't show every extreme that they name: A permutation of the slots; request r's new tokens are hidden[slot_of_request[r]]. `prefix_len`: the longest prefix is exactly 1024 tokens. `block_holder`: every holder appears exactly 8 times in each row. `block_slot`: entries of different requests, or different entries of one request, on one holder name different pages.
All inputs are finite; a program needn't handle non-finite values.
Results may differ from the reference program's by a relative error of at most 0.014.
Values may be sent and summed in bfloat16 or wider, within the bound.
No kernel may reach another device: no remote copies, remote signals or barrier semaphores. Data moves between devices by JAX's collectives and lax.ppermute only.
A program may use at most 64 MiB of HBM per device.

```python
import math
import jax
import jax.numpy as jnp
import numpy as np
from jax import lax

D = 4608
HD = 128
QH = 16
KVH = 8
NEW = 256
PMAX = 1024
BLOCK = 16
REQS = 8
MAXB = 64
HOLDERS = 8
CAPR = 8
POOL_DEV = 64
POOL = 512


def holder_table(key):
    keys = jax.random.split(key, REQS * CAPR)
    orders = jax.vmap(lambda subkey: jax.random.permutation(subkey, HOLDERS))(keys)
    return orders.reshape(REQS, MAXB).astype(jnp.int32)


def draw_block_holder(key, part):
    return holder_table(jax.random.fold_in(key, 11))


def draw_block_slot(key, part):
    holders = holder_table(jax.random.fold_in(key, 11))
    keys = jax.random.split(jax.random.fold_in(key, 12), HOLDERS)
    pages = jax.vmap(lambda subkey: jax.random.permutation(subkey, POOL_DEV))(keys).astype(jnp.int32)
    entry = jnp.arange(MAXB, dtype=jnp.int32) // HOLDERS
    owner = jnp.arange(REQS, dtype=jnp.int32)[:, None] * CAPR + entry[None, :]
    return pages[holders, owner].astype(jnp.int32)


def block_levels(own_key, dims, shards, low, high):
    def one(dim, parts):
        heights = jax.random.uniform(jax.random.fold_in(jax.random.fold_in(own_key, 6), dim), (parts,), jnp.float32, low / len(shards), high / len(shards))
        return jnp.repeat(jnp.exp(heights), dims[dim] // parts).reshape((-1,) + (1,) * (len(dims) - dim - 1))

    factor_of = one(*shards[0])
    for cut in shards[1:]:
        factor_of = factor_of * one(*cut)
    return factor_of


def length_profile(amount, total, limit, slope):
    loads = [(1 << 20) // math.isqrt(standing ** slope) + 1 for standing in range(2, amount + 1)]
    spare, holding = total - limit - (amount - 1), [1] * (amount - 1)
    while spare > 0:
        free = [i for i in range(amount - 1) if holding[i] < limit]
        whole, remaining = sum([loads[i] for i in free]), spare
        for i in free:
            more = min(limit - holding[i], max(1, remaining * loads[i] // whole), spare)
            holding[i] = holding[i] + more
            spare = spare - more
    return np.array([limit] + holding)


def uneven(key, count, total, limit, lean):
    if count == 2:
        one = jax.random.randint(key, (), max(1, total - limit), min(limit, total - 1) + 1)
        return jnp.stack([one, total - one])
    tallies = jnp.asarray(length_profile(count, total, limit, lean), jnp.int32)
    pairs = (count - 1) // 2
    source_of, sink = tallies[1:1 + 2 * pairs:2], tallies[2:2 + 2 * pairs:2]
    room = jnp.minimum(source_of - 1, limit - sink)
    passed = jax.random.randint(jax.random.fold_in(key, 1), (pairs,), 0, 1 << 20) % (room + 1)
    tallies = tallies.at[1:1 + 2 * pairs:2].set(source_of - passed).at[2:2 + 2 * pairs:2].set(sink + passed)
    return tallies[jax.random.permutation(jax.random.fold_in(key, 2), count)]


def scatter_about(rng, extent, scale, most, cuts=(), kind=jnp.bfloat16):
    array = scale * jax.random.normal(rng, extent, jnp.float32)
    if cuts:
        array = array * block_levels(rng, extent, cuts, -0.22, 0.18)
    return jnp.clip(array, -most, most).astype(kind)


def setup_inputs(seed: int = 0) -> dict:
    key_of = jax.random.split(jax.random.key(seed), 13)
    return {
        "hidden": scatter_about(key_of[0], (REQS, NEW, D), 1.0, 6.0, ((0, 8),)),
        "slot_of_request": jax.random.permutation(key_of[1], REQS).astype(jnp.int32),
        "prefix_len": uneven(key_of[2], REQS, REQS * PMAX // 2, PMAX, 2).astype(jnp.int32),
        "block_holder": draw_block_holder(jax.random.fold_in(key_of[12], 71), 0),
        "block_slot": draw_block_slot(jax.random.fold_in(key_of[12], 71), 0),
        "kv_pool": scatter_about(key_of[5], (POOL, BLOCK, KVH, 2 * HD), 2.0, 12.0, ((0, 8), (2, 4))),
        "norm_gain": jnp.clip(jax.random.uniform(key_of[6], (D,), jnp.float32, 0.75, 2.0), 0.75, 2.0),
        "q_weight": scatter_about(key_of[7], (D, QH * HD), D ** -0.5, 0.09375, ((0, 8), (1, 4))),
        "k_weight": scatter_about(key_of[8], (D, KVH * HD), D ** -0.5, 0.09375, ((0, 8), (1, 4))),
        "v_weight": scatter_about(key_of[9], (D, KVH * HD), D ** -0.5, 0.09375, ((0, 8), (1, 4))),
        "o_weight": scatter_about(key_of[10], (D, QH * HD), (QH * HD) ** -0.5, 0.125, ((0, 8), (1, 4))),
        "post_gain": jnp.clip(1.0 + 0.18 * jax.random.normal(key_of[11], (D,), jnp.float32), 0.1, 1.9),
    }


softcap = 50.0
query_scale = 144.0 ** (-0.5)
norm_eps = 1e-06

def rms_scale(rows, gain):
    mean_square = lax.optimization_barrier(jnp.mean(rows * rows, axis=-1, keepdims=True))
    return rows * lax.rsqrt(mean_square + norm_eps) * gain

def rotate(vectors, positions):
    half = vectors.shape[-1] // 2
    freqs = jnp.exp(jnp.arange(half, dtype=jnp.float32) * (-2.0 * math.log(10000.0) / vectors.shape[-1]))
    angles = positions[..., None] * freqs
    cosine = jnp.cos(angles)[..., None, :]
    sine = jnp.sin(angles)[..., None, :]
    first = vectors[..., :half]
    second = vectors[..., half:]
    return jnp.concatenate([first * cosine - second * sine, second * cosine + first * sine], axis=-1)

def capped_weights(scores, valid):
    return jnp.where(valid, jnp.exp(softcap * jnp.tanh(scores / softcap)), 0.0)

def reference(hidden, slot_of_request, prefix_len, block_holder, block_slot, kv_pool, norm_gain, q_weight, k_weight, v_weight, o_weight, post_gain):
    group = QH // KVH

    def one_request(index):
        rows = lax.dynamic_index_in_dim(hidden, slot_of_request[index], 0, keepdims=False)
        length = prefix_len[index]
        normed = rms_scale(rows.astype(jnp.float32), norm_gain).astype(jnp.bfloat16)
        positions = (length + jnp.arange(NEW, dtype=jnp.int32)).astype(jnp.float32)
        queries = jnp.dot(normed, q_weight, preferred_element_type=jnp.float32).reshape(NEW, QH, HD)
        queries = (rotate(queries, positions) * query_scale).astype(jnp.bfloat16)
        keys_new = jnp.dot(normed, k_weight, preferred_element_type=jnp.float32).reshape(NEW, KVH, HD)
        keys_new = rotate(keys_new, positions).astype(jnp.bfloat16)
        values_new = jnp.dot(normed, v_weight, preferred_element_type=jnp.float32).astype(jnp.bfloat16).reshape(NEW, KVH, HD)
        pages = (block_holder[index] * POOL_DEV + block_slot[index]).astype(jnp.int32)
        cached = jnp.take(kv_pool, pages, axis=0).reshape(PMAX, KVH, 2 * HD)
        keys = jnp.concatenate([cached[..., :HD], keys_new], axis=0).astype(jnp.float32)
        values = jnp.concatenate([cached[..., HD:], values_new], axis=0).astype(jnp.float32)
        grouped = queries.reshape(NEW, KVH, group, HD).astype(jnp.float32)
        scores = jnp.einsum('tgjd,kgd->gjtk', grouped, keys)
        key_index = jnp.arange(PMAX + NEW, dtype=jnp.int32)
        query_index = jnp.arange(NEW, dtype=jnp.int32)
        valid = jnp.where(key_index[None, :] < PMAX, key_index[None, :] < length, key_index[None, :] - PMAX <= query_index[:, None])
        weights = capped_weights(scores, valid[None, None])
        denom = lax.optimization_barrier(jnp.sum(weights, axis=-1))
        rounded = lax.optimization_barrier(weights.astype(jnp.bfloat16))
        numer = jnp.einsum('gjtk,kgd->gjtd', rounded.astype(jnp.float32), values)
        attended = (numer / denom[..., None]).transpose(2, 0, 1, 3).reshape(NEW, QH * HD).astype(jnp.bfloat16)
        projected = jnp.dot(attended, o_weight.T, preferred_element_type=jnp.float32)
        return (rows.astype(jnp.float32) + rms_scale(projected, post_gain)).astype(jnp.bfloat16)
    return lax.map(one_request, jnp.arange(REQS, dtype=jnp.int32))
```

```python
import math

import jax
import jax.numpy as jnp
from jax import lax
from jax.sharding import PartitionSpec as P

softcap = 50.0
query_scale = 144.0 ** (-0.5)
norm_eps = 1e-06


def rms_scale(rows, gain):
    mean_square = jnp.mean(rows * rows, axis=-1, keepdims=True)
    return rows * lax.rsqrt(mean_square + norm_eps) * gain


def rotate(vectors, cosine, sine):
    half = vectors.shape[-1] // 2
    first = vectors[..., :half]
    second = vectors[..., half:]
    return jnp.concatenate(
        [first * cosine - second * sine, second * cosine + first * sine], axis=-1
    )


def capped_weights(scores, valid):
    return jnp.where(valid, jnp.exp(softcap * jnp.tanh(scores / softcap)), 0.0)


def swap(array, axis, distance):
    size = lax.axis_size(axis)
    return lax.ppermute(array, axis, [(i, i ^ distance) for i in range(size)])


def place(pieces, index):
    first = pieces[0]
    stacked = jnp.zeros((len(pieces),) + first.shape, first.dtype)
    for distance, piece in pieces.items():
        stacked = lax.dynamic_update_index_in_dim(stacked, piece, index ^ distance, 0)
    return stacked


def exchange(chunks, axis):
    size = lax.axis_size(axis)
    index = lax.axis_index(axis)
    if size > 8:
        return lax.all_to_all(chunks, axis, split_axis=0, concat_axis=0, tiled=True)
    pieces = {}
    for distance in range(size):
        chunk = lax.dynamic_index_in_dim(chunks, index ^ distance, 0, keepdims=False)
        pieces[distance] = swap(chunk, axis, distance) if distance else chunk
    return place(pieces, index)


def doubled(block, axis, span):
    pieces = {0: block}
    bit = span // 2
    while bit:
        for distance in list(pieces):
            pieces[distance ^ bit] = swap(pieces[distance], axis, bit)
        bit //= 2
    return pieces


def attend(queries, keys_new, values_new, cached, cached_valid):
    new_len, kv_local, group, head_dim = queries.shape

    def part(keys, values, valid):
        scores = jnp.einsum("tgjd,kgd->gjtk", queries, keys, preferred_element_type=jnp.float32)
        weights = capped_weights(scores, valid)
        numer = jnp.einsum(
            "gjtk,kgd->gjtd",
            weights.astype(jnp.bfloat16),
            values,
            preferred_element_type=jnp.float32,
        )
        return numer, jnp.sum(weights, axis=-1)

    query_index = jnp.arange(new_len, dtype=jnp.int32)
    causal = query_index[None, :] <= query_index[:, None]
    numer, denom = part(
        cached[..., :head_dim], cached[..., head_dim:], cached_valid[None, None, None, :]
    )
    more, added = part(keys_new, values_new, causal[None, None])
    attended = ((numer + more) / (denom + added)[..., None]).transpose(2, 0, 1, 3)
    return attended.reshape(new_len, kv_local * group * head_dim).astype(jnp.bfloat16)


def local(
    hidden,
    slot_of_request,
    prefix_len,
    block_holder,
    block_slot,
    kv_pool,
    norm_gain,
    q_weight,
    k_weight,
    v_weight,
    o_weight,
    post_gain,
):
    shards = lax.axis_size("fsdp")
    groups = lax.axis_size("pool")
    f = lax.axis_index("fsdp")
    p = lax.axis_index("pool")
    half = shards // 2
    side = f // half
    new_len, width = hidden.shape[1:]
    requests = slot_of_request.shape[0]
    page_len = kv_pool.shape[1]
    kv_local = kv_pool.shape[2]
    head_dim = kv_pool.shape[3] // 2
    q_cols = q_weight.shape[1]
    kv_cols = k_weight.shape[1]
    group = q_cols // kv_cols
    max_blocks = block_holder.shape[1]
    per_holder = max_blocks // shards
    quarter = new_len // groups
    sub = quarter // shards
    features = o_weight.shape[0]

    kv_pieces = doubled(jnp.concatenate([k_weight, v_weight], axis=1), "fsdp", half)
    q_pieces = doubled(q_weight, "fsdp", half)
    out_weight = lax.all_gather(o_weight, "pool", axis=0, tiled=False)

    rows = hidden[0]
    normed = rms_scale(rows.astype(jnp.float32), norm_gain).astype(jnp.bfloat16)
    own_rows = lax.dynamic_slice(normed, (0, side * (width // 2)), (new_len, width // 2))
    leaving = lax.dynamic_slice(
        normed, (p * quarter, (1 - side) * (width // 2)), (quarter, width // 2)
    )
    partner_piece = swap(leaving, "fsdp", half)
    partner_pieces = {0: partner_piece}
    for distance in range(1, groups):
        partner_pieces[distance] = swap(partner_piece, "pool", distance)
    partner_rows = place(partner_pieces, p).reshape(new_len, width // 2)

    request_ids = jnp.arange(requests, dtype=jnp.int32)
    request_at_slot = jnp.sum(
        jnp.where(slot_of_request[None, :] == request_ids[:, None], request_ids[None, :], 0), axis=1
    )
    holder_by_slot = jnp.take(block_holder, request_at_slot, axis=0)
    page_by_slot = jnp.take(block_slot, request_at_slot, axis=0)
    held_here = holder_by_slot == f
    held_rank = jnp.cumsum(held_here.astype(jnp.int32), axis=1) - 1
    rank_ids = jnp.arange(per_holder, dtype=jnp.int32)
    picked = held_here[:, :, None] & (held_rank[:, :, None] == rank_ids[None, None, :])
    local_pages = jnp.sum(jnp.where(picked, page_by_slot[:, :, None], 0), axis=1)
    flat_pool = kv_pool.reshape(kv_pool.shape[0], page_len * kv_local, 2 * head_dim)
    outgoing = jnp.take(flat_pool, local_pages, axis=0)
    outgoing = outgoing.reshape(shards, per_holder * page_len * kv_local, 2 * head_dim)
    arrived = exchange(outgoing, "fsdp")
    cached = arrived.reshape(max_blocks * page_len, kv_local, 2 * head_dim)

    my_request = lax.dynamic_index_in_dim(request_at_slot, f, keepdims=False)
    my_length = prefix_len[my_request]
    my_holders = block_holder[my_request]
    entry_ids = jnp.arange(max_blocks, dtype=jnp.int32)
    mine = my_holders[None, :] == jnp.arange(shards, dtype=jnp.int32)[:, None]
    my_rank = jnp.cumsum(mine.astype(jnp.int32), axis=1) - 1
    chosen = mine[:, None, :] & (my_rank[:, None, :] == rank_ids[None, :, None])
    entry = jnp.sum(jnp.where(chosen, entry_ids[None, None, :], 0), axis=2)
    cached_position = entry.reshape(-1, 1) * page_len + jnp.arange(page_len, dtype=jnp.int32)
    cached_valid = (cached_position < my_length).reshape(-1)

    residual_out = lax.dynamic_slice_in_dim(rows, p * quarter, quarter, 0).reshape(
        shards, sub, width
    )
    residual = exchange(residual_out, "fsdp")

    positions = (my_length + jnp.arange(new_len, dtype=jnp.int32)).astype(jnp.float32)
    freqs = jnp.exp(
        jnp.arange(head_dim // 2, dtype=jnp.float32) * (-2.0 * math.log(10000.0) / head_dim)
    )
    angles = positions[:, None] * freqs
    cosine = jnp.cos(angles)[:, None, :]
    sine = jnp.sin(angles)[:, None, :]

    def project(pieces):
        weight = place(pieces, f % half).reshape(width // 2, -1)
        partial = jnp.dot(partner_rows, weight, preferred_element_type=jnp.float32)
        other = swap(partial.astype(jnp.bfloat16), "fsdp", half)
        own = jnp.dot(own_rows, weight, preferred_element_type=jnp.float32)
        return own + other.astype(jnp.float32)

    kv_sum = project(kv_pieces)
    q_sum = project(q_pieces)
    queries = rotate(q_sum.reshape(new_len, kv_local * group, head_dim), cosine, sine)
    queries = (queries * query_scale).astype(jnp.bfloat16)
    queries = queries.reshape(new_len, kv_local, group, head_dim)
    keys_new = kv_sum[:, :kv_cols].reshape(new_len, kv_local, head_dim)
    keys_new = rotate(keys_new, cosine, sine).astype(jnp.bfloat16)
    values_new = kv_sum[:, kv_cols:].astype(jnp.bfloat16).reshape(new_len, kv_local, head_dim)
    attended = attend(queries, keys_new, values_new, cached, cached_valid)

    quarters = exchange(attended.reshape(groups, quarter, q_cols), "pool")
    token_pieces = {0: quarters}
    for distance in range(2, shards, 2):
        token_pieces[distance] = swap(quarters, "fsdp", distance)
    for distance in range(0, shards, 2):
        token_pieces[distance ^ 1] = swap(token_pieces[distance], "fsdp", 1)
    tokens = place(token_pieces, f)
    projected = jnp.einsum(
        "sptc,pfc->stf", tokens, out_weight, preferred_element_type=jnp.float32
    ).astype(jnp.bfloat16)
    projected = projected.reshape(shards, shards, sub, features).transpose(1, 0, 2, 3)
    finished = exchange(projected, "fsdp").transpose(1, 2, 0, 3).reshape(shards, sub, width)
    finished = residual.astype(jnp.float32) + rms_scale(finished.astype(jnp.float32), post_gain)
    return jnp.take(finished.astype(jnp.bfloat16), slot_of_request, axis=0)


def solution(mesh):
    in_specs = (
        P("fsdp", None, None),
        P(),
        P(),
        P(),
        P(),
        P("fsdp", None, "pool", None),
        P(),
        P("fsdp", "pool"),
        P("fsdp", "pool"),
        P("fsdp", "pool"),
        P("fsdp", "pool"),
        P(),
    )
    out_specs = P(None, ("pool", "fsdp"), None)
    return jax.shard_map(local, mesh=mesh, in_specs=in_specs, out_specs=out_specs, check_vma=False)
```

```python
import functools
import math

import jax
import jax.numpy as jnp
from jax import lax
from jax.experimental import pallas as pl
from jax.experimental.pallas import tpu as pltpu
from jax.sharding import PartitionSpec as P

softcap = 50.0
query_scale = 144.0 ** (-0.5)
norm_eps = 1e-06


def rms_scale(rows, gain):
    mean_square = jnp.mean(rows * rows, axis=-1, keepdims=True)
    return rows * lax.rsqrt(mean_square + norm_eps) * gain


def rotate(vectors, cosine, sine):
    half = vectors.shape[-1] // 2
    first = vectors[..., :half]
    second = vectors[..., half:]
    return jnp.concatenate(
        [first * cosine - second * sine, second * cosine + first * sine], axis=-1
    )


def capped_weights(scores, valid):
    return jnp.where(valid, jnp.exp(softcap * jnp.tanh(scores / softcap)), 0.0)


def swap(array, axis, distance):
    size = lax.axis_size(axis)
    return lax.ppermute(array, axis, [(i, i ^ distance) for i in range(size)])


def place(pieces, index):
    first = pieces[0]
    stacked = jnp.zeros((len(pieces),) + first.shape, first.dtype)
    for distance, piece in pieces.items():
        stacked = lax.dynamic_update_index_in_dim(stacked, piece, index ^ distance, 0)
    return stacked


def exchange(chunks, axis):
    size = lax.axis_size(axis)
    index = lax.axis_index(axis)
    if size > 8:
        return lax.all_to_all(chunks, axis, split_axis=0, concat_axis=0, tiled=True)
    pieces = {}
    for distance in range(size):
        chunk = lax.dynamic_index_in_dim(chunks, index ^ distance, 0, keepdims=False)
        pieces[distance] = swap(chunk, axis, distance) if distance else chunk
    return place(pieces, index)


def doubled(block, axis, span):
    pieces = {0: block}
    bit = span // 2
    while bit:
        for distance in list(pieces):
            pieces[distance ^ bit] = swap(pieces[distance], axis, bit)
        bit //= 2
    return pieces


def attend(queries, keys_new, values_new, cached, cached_valid):
    new_len, kv_local, group, head_dim = queries.shape

    def part(keys, values, valid):
        scores = jnp.einsum("tgjd,kgd->gjtk", queries, keys, preferred_element_type=jnp.float32)
        weights = capped_weights(scores, valid)
        numer = jnp.einsum(
            "gjtk,kgd->gjtd",
            weights.astype(jnp.bfloat16),
            values,
            preferred_element_type=jnp.float32,
        )
        return numer, jnp.sum(weights, axis=-1)

    query_index = jnp.arange(new_len, dtype=jnp.int32)
    causal = query_index[None, :] <= query_index[:, None]
    numer, denom = part(
        cached[..., :head_dim], cached[..., head_dim:], cached_valid[None, None, None, :]
    )
    more, added = part(keys_new, values_new, causal[None, None])
    attended = ((numer + more) / (denom + added)[..., None]).transpose(2, 0, 1, 3)
    return attended.reshape(new_len, kv_local * group * head_dim).astype(jnp.bfloat16)


def local_general(
    hidden,
    slot_of_request,
    prefix_len,
    block_holder,
    block_slot,
    kv_pool,
    norm_gain,
    q_weight,
    k_weight,
    v_weight,
    o_weight,
    post_gain,
):
    shards = lax.axis_size("fsdp")
    groups = lax.axis_size("pool")
    f = lax.axis_index("fsdp")
    p = lax.axis_index("pool")
    half = shards // 2
    side = f // half
    new_len, width = hidden.shape[1:]
    requests = slot_of_request.shape[0]
    page_len = kv_pool.shape[1]
    kv_local = kv_pool.shape[2]
    head_dim = kv_pool.shape[3] // 2
    q_cols = q_weight.shape[1]
    kv_cols = k_weight.shape[1]
    group = q_cols // kv_cols
    max_blocks = block_holder.shape[1]
    per_holder = max_blocks // shards
    quarter = new_len // groups
    sub = quarter // shards
    features = o_weight.shape[0]

    kv_pieces = doubled(jnp.concatenate([k_weight, v_weight], axis=1), "fsdp", half)
    q_pieces = doubled(q_weight, "fsdp", half)
    out_weight = lax.all_gather(o_weight, "pool", axis=0, tiled=False)

    rows = hidden[0]
    normed = rms_scale(rows.astype(jnp.float32), norm_gain).astype(jnp.bfloat16)
    own_rows = lax.dynamic_slice(normed, (0, side * (width // 2)), (new_len, width // 2))
    leaving = lax.dynamic_slice(
        normed, (p * quarter, (1 - side) * (width // 2)), (quarter, width // 2)
    )
    partner_piece = swap(leaving, "fsdp", half)
    partner_pieces = {0: partner_piece}
    for distance in range(1, groups):
        partner_pieces[distance] = swap(partner_piece, "pool", distance)
    partner_rows = place(partner_pieces, p).reshape(new_len, width // 2)

    request_ids = jnp.arange(requests, dtype=jnp.int32)
    request_at_slot = jnp.sum(
        jnp.where(slot_of_request[None, :] == request_ids[:, None], request_ids[None, :], 0), axis=1
    )
    holder_by_slot = jnp.take(block_holder, request_at_slot, axis=0)
    page_by_slot = jnp.take(block_slot, request_at_slot, axis=0)
    held_here = holder_by_slot == f
    held_rank = jnp.cumsum(held_here.astype(jnp.int32), axis=1) - 1
    rank_ids = jnp.arange(per_holder, dtype=jnp.int32)
    picked = held_here[:, :, None] & (held_rank[:, :, None] == rank_ids[None, None, :])
    local_pages = jnp.sum(jnp.where(picked, page_by_slot[:, :, None], 0), axis=1)
    flat_pool = kv_pool.reshape(kv_pool.shape[0], page_len * kv_local, 2 * head_dim)
    outgoing = jnp.take(flat_pool, local_pages, axis=0)
    outgoing = outgoing.reshape(shards, per_holder * page_len * kv_local, 2 * head_dim)
    arrived = exchange(outgoing, "fsdp")
    cached = arrived.reshape(max_blocks * page_len, kv_local, 2 * head_dim)

    my_request = lax.dynamic_index_in_dim(request_at_slot, f, keepdims=False)
    my_length = prefix_len[my_request]
    my_holders = block_holder[my_request]
    entry_ids = jnp.arange(max_blocks, dtype=jnp.int32)
    mine = my_holders[None, :] == jnp.arange(shards, dtype=jnp.int32)[:, None]
    my_rank = jnp.cumsum(mine.astype(jnp.int32), axis=1) - 1
    chosen = mine[:, None, :] & (my_rank[:, None, :] == rank_ids[None, :, None])
    entry = jnp.sum(jnp.where(chosen, entry_ids[None, None, :], 0), axis=2)
    cached_position = entry.reshape(-1, 1) * page_len + jnp.arange(page_len, dtype=jnp.int32)
    cached_valid = (cached_position < my_length).reshape(-1)

    residual_out = lax.dynamic_slice_in_dim(rows, p * quarter, quarter, 0).reshape(
        shards, sub, width
    )
    residual = exchange(residual_out, "fsdp")

    positions = (my_length + jnp.arange(new_len, dtype=jnp.int32)).astype(jnp.float32)
    freqs = jnp.exp(
        jnp.arange(head_dim // 2, dtype=jnp.float32) * (-2.0 * math.log(10000.0) / head_dim)
    )
    angles = positions[:, None] * freqs
    cosine = jnp.cos(angles)[:, None, :]
    sine = jnp.sin(angles)[:, None, :]

    def project(pieces):
        weight = place(pieces, f % half).reshape(width // 2, -1)
        partial = jnp.dot(partner_rows, weight, preferred_element_type=jnp.float32)
        other = swap(partial.astype(jnp.bfloat16), "fsdp", half)
        own = jnp.dot(own_rows, weight, preferred_element_type=jnp.float32)
        return own + other.astype(jnp.float32)

    kv_sum = project(kv_pieces)
    q_sum = project(q_pieces)
    queries = rotate(q_sum.reshape(new_len, kv_local * group, head_dim), cosine, sine)
    queries = (queries * query_scale).astype(jnp.bfloat16)
    queries = queries.reshape(new_len, kv_local, group, head_dim)
    keys_new = kv_sum[:, :kv_cols].reshape(new_len, kv_local, head_dim)
    keys_new = rotate(keys_new, cosine, sine).astype(jnp.bfloat16)
    values_new = kv_sum[:, kv_cols:].astype(jnp.bfloat16).reshape(new_len, kv_local, head_dim)
    attended = attend(queries, keys_new, values_new, cached, cached_valid)

    quarters = exchange(attended.reshape(groups, quarter, q_cols), "pool")
    token_pieces = {0: quarters}
    for distance in range(2, shards, 2):
        token_pieces[distance] = swap(quarters, "fsdp", distance)
    for distance in range(0, shards, 2):
        token_pieces[distance ^ 1] = swap(token_pieces[distance], "fsdp", 1)
    tokens = place(token_pieces, f)
    projected = jnp.einsum(
        "sptc,pfc->stf", tokens, out_weight, preferred_element_type=jnp.float32
    ).astype(jnp.bfloat16)
    projected = projected.reshape(shards, shards, sub, features).transpose(1, 0, 2, 3)
    finished = exchange(projected, "fsdp").transpose(1, 2, 0, 3).reshape(shards, sub, width)
    finished = residual.astype(jnp.float32) + rms_scale(finished.astype(jnp.float32), post_gain)
    return jnp.take(finished.astype(jnp.bfloat16), slot_of_request, axis=0)


VMEM = pl.BlockSpec(memory_space=pltpu.VMEM)
SMEM = pl.BlockSpec(memory_space=pltpu.SMEM)


def call(kernel, outs, scratch, flops, nbytes, where, *operands):
    return pl.pallas_call(
        kernel,
        out_shape=outs,
        in_specs=[SMEM] + [VMEM] * len(operands),
        out_specs=jax.tree.map(lambda _: VMEM, outs),
        scratch_shapes=scratch,
        compiler_params=pltpu.CompilerParams(vmem_limit_bytes=48 << 20),
        cost_estimate=pl.CostEstimate(flops=flops, bytes_accessed=nbytes, transcendentals=0),
    )(where, *operands)


def after(array, *earlier):
    return lax.optimization_barrier((array,) + earlier)[0]


def gather_weight(weight_refs, weight, f, half):
    count = weight_refs[0].shape[0]
    for distance, ref in enumerate(weight_refs):
        start = ((f ^ distance) & (half - 1)) * count
        weight[pl.ds(pl.multiple_of(start, 64), count), :] = ref[...]


def partner_kernel(half, groups, where_ref, *refs):
    p, f = where_ref[0], where_ref[1]
    x_refs, w_refs = refs[:groups], refs[groups : groups + half]
    out_ref, rows, weight = refs[groups + half :]
    quarter = x_refs[0].shape[0]
    for distance, ref in enumerate(x_refs):
        start = pl.multiple_of((p ^ distance) * quarter, quarter)
        rows[pl.ds(start, quarter), :] = ref[...]
    gather_weight(w_refs, weight, f, half)
    out_ref[...] = jnp.dot(
        rows[...], weight[...], preferred_element_type=jnp.float32
    ).astype(jnp.bfloat16)


def own_kernel(half, where_ref, x_ref, *refs):
    f = where_ref[1]
    q_refs, kv_refs = refs[:half], refs[half : 2 * half]
    q_ref, kv_ref, q_weight, kv_weight = refs[2 * half :]
    for w_refs, out_ref, weight in ((q_refs, q_ref, q_weight), (kv_refs, kv_ref, kv_weight)):
        gather_weight(w_refs, weight, f, half)
        out_ref[...] = jnp.dot(x_ref[...], weight[...], preferred_element_type=jnp.float32)


def capped(scores):
    return jnp.exp2(jnp.tanh(scores * (1.0 / softcap)) * (softcap * math.log2(math.e)))


def attend_kernel(
    groups,
    pieces,
    kv_local,
    head_dim,
    where_ref,
    q_own,
    kv_own,
    q_other,
    kv_other,
    cos_ref,
    sin_ref,
    valid_ref,
    *refs,
):
    p = where_ref[0]
    page_refs = refs[:pieces]
    out_refs = refs[pieces : pieces + groups]
    keys, values, result = refs[pieces + groups :]
    new_len = q_own.shape[0]
    group = q_own.shape[1] // (kv_local * head_dim)
    cosine, sine = cos_ref[...], sin_ref[...]

    def rope(vectors):
        return vectors * cosine + pltpu.roll(vectors, head_dim // 2, 1) * sine

    span = page_refs[0].shape[1]
    per = span // kv_local
    row = lax.broadcasted_iota(jnp.int32, (span, span), 0)
    column = lax.broadcasted_iota(jnp.int32, (span, span), 1)
    part = (column == (row % per) * kv_local + row // per).astype(jnp.bfloat16)
    place_at = 0
    for ref in page_refs:
        for b in range(ref.shape[0]):
            parted = jnp.dot(part, ref[b], preferred_element_type=jnp.float32).astype(jnp.bfloat16)
            for g in range(kv_local):
                lines = parted[g * per : (g + 1) * per]
                keys[g, place_at : place_at + per, :] = lines[:, :head_dim]
                values[g, place_at : place_at + per, :] = lines[:, head_dim:]
            place_at += per

    span_keys = 2 * per
    t = lax.broadcasted_iota(jnp.int32, (group * new_len, new_len), 0) % new_len
    s = lax.broadcasted_iota(jnp.int32, (group * new_len, new_len), 1)
    causal = s <= t
    for g in range(kv_local):
        at = g * head_dim
        heads = []
        for j in range(group):
            to = (g * group + j) * head_dim
            total = q_own[:, to : to + head_dim] + q_other[:, to : to + head_dim].astype(jnp.float32)
            heads.append((rope(total) * query_scale).astype(jnp.bfloat16))
        queries = jnp.concatenate(heads, axis=0)
        new_key = rope(
            kv_own[:, at : at + head_dim] + kv_other[:, at : at + head_dim].astype(jnp.float32)
        ).astype(jnp.bfloat16)
        at += kv_local * head_dim
        new_value = (
            kv_own[:, at : at + head_dim] + kv_other[:, at : at + head_dim].astype(jnp.float32)
        ).astype(jnp.bfloat16)

        def scores_of(key):
            return lax.dot_general(
                queries, key, (((1,), (1,)), ((), ())), preferred_element_type=jnp.float32
            )

        weights = jnp.where(causal, capped(scores_of(new_key)), 0.0)
        denom = jnp.sum(weights, axis=1, keepdims=True)
        numer = jnp.dot(
            weights.astype(jnp.bfloat16), new_value, preferred_element_type=jnp.float32
        )
        for start in range(0, place_at, span_keys):
            valid = valid_ref[:, start : start + span_keys] > 0.0
            weights = jnp.where(
                valid, capped(scores_of(keys[g, start : start + span_keys, :])), 0.0
            )
            denom = denom + jnp.sum(weights, axis=1, keepdims=True)
            numer = numer + jnp.dot(
                weights.astype(jnp.bfloat16),
                values[g, start : start + span_keys, :],
                preferred_element_type=jnp.float32,
            )
        attended = (numer / denom).astype(jnp.bfloat16)
        for j in range(group):
            to = (g * group + j) * head_dim
            result[:, to : to + head_dim] = attended[j * new_len : (j + 1) * new_len]
    quarter = new_len // groups
    for distance, ref in enumerate(out_refs):
        start = pl.multiple_of((p ^ distance) * quarter, quarter)
        ref[...] = result[pl.ds(start, quarter), :]


def output_kernel(groups, shards, where_ref, *refs):
    p, f = where_ref[0], where_ref[1]
    token_refs = refs[:shards]
    weight_ref = refs[shards]
    out_refs = refs[shards + 1 : 2 * shards + 1]
    total = refs[2 * shards + 1]
    quarter = token_refs[0].shape[1]
    sub = quarter // shards
    projected = None
    for distance in range(groups):
        rows = jnp.concatenate([ref[distance] for ref in token_refs], axis=0)
        term = lax.dot_general(
            rows,
            weight_ref[p ^ distance],
            (((1,), (1,)), ((), ())),
            preferred_element_type=jnp.float32,
        )
        projected = term if projected is None else projected + term
    total[...] = projected
    for e in range(shards):
        for distance, ref in enumerate(out_refs):
            start = pl.multiple_of(e * quarter + (f ^ distance) * sub, sub)
            ref[f ^ e] = total[pl.ds(start, sub), :].astype(jnp.bfloat16)


def finish_kernel(shards, residuals, where_ref, gain_ref, *refs):
    f = where_ref[1]
    piece_refs = refs[:shards]
    residual_refs = refs[shards : shards + residuals]
    out_ref, projected, rows = refs[shards + residuals :]
    per = shards // residuals
    for distance, ref in enumerate(piece_refs):
        projected[f ^ distance] = ref[...].astype(jnp.float32)
    for distance in range(shards):
        rows[f ^ distance] = residual_refs[distance // per][distance % per].astype(jnp.float32)
    gain = gain_ref[...]
    for request in range(out_ref.shape[0]):
        slot = where_ref[2 + request]
        line = jnp.concatenate([projected[k, slot] for k in range(shards)], axis=1)
        mean_square = jnp.mean(line * line, axis=1, keepdims=True)
        line = line * lax.rsqrt(mean_square + norm_eps) * gain
        out_ref[request] = (rows[slot] + line).astype(jnp.bfloat16)


def pool_pieces(block, groups):
    return [block] + [swap(block, "pool", distance) for distance in range(1, groups)]


def two_stage(chunks, f, hold=None):
    mine, others = chunks[0::2], chunks[1::2]
    stacked = jnp.stack([mine, swap(others, "fsdp", 1)], axis=1)
    if hold is not None:
        stacked = after(stacked, hold)
    return [stacked[0]] + [
        swap(stacked[t], "fsdp", 2 * t) for t in range(1, stacked.shape[0])
    ]


def local_small(
    hidden,
    slot_of_request,
    prefix_len,
    block_holder,
    block_slot,
    kv_pool,
    norm_gain,
    q_weight,
    k_weight,
    v_weight,
    o_weight,
    post_gain,
):
    shards = lax.axis_size("fsdp")
    groups = lax.axis_size("pool")
    f = lax.axis_index("fsdp")
    p = lax.axis_index("pool")
    half = shards // 2
    side = f // half
    new_len, width = hidden.shape[1:]
    requests = slot_of_request.shape[0]
    page_len = kv_pool.shape[1]
    kv_local = kv_pool.shape[2]
    head_dim = kv_pool.shape[3] // 2
    q_cols = q_weight.shape[1]
    kv_cols = k_weight.shape[1]
    max_blocks = block_holder.shape[1]
    per_holder = max_blocks // shards
    quarter = new_len // groups
    sub = quarter // shards
    features = o_weight.shape[0]
    bf16, f32 = jnp.bfloat16, jnp.float32
    where = jnp.concatenate([jnp.stack([p, f]).astype(jnp.int32), slot_of_request])
    by_distance = f ^ jnp.arange(shards, dtype=jnp.int32)

    q_pieces = list(map(doubled(q_weight, "fsdp", half).get, range(half)))
    kv_weight = jnp.concatenate([k_weight, v_weight], axis=1)
    kv_pieces = list(map(doubled(kv_weight, "fsdp", half).get, range(half)))

    rows = hidden[0]
    my_quarter = lax.dynamic_slice_in_dim(rows, p * quarter, quarter, 0)
    leaving = rms_scale(my_quarter.astype(f32), norm_gain).astype(bf16)
    leaving = lax.dynamic_slice_in_dim(leaving, (1 - side) * (width // 2), width // 2, 1)
    partner_piece = swap(leaving, "fsdp", half)
    partner_pieces = pool_pieces(partner_piece, groups)
    normed = rms_scale(rows.astype(f32), norm_gain).astype(bf16)
    own_rows = lax.dynamic_slice_in_dim(normed, side * (width // 2), width // 2, 1)
    out_weight = lax.all_gather(after(o_weight, partner_pieces[-1]), "pool", axis=0, tiled=False)

    request_ids = jnp.arange(requests, dtype=jnp.int32)
    request_at_slot = jnp.sum(
        jnp.where(slot_of_request[None, :] == request_ids[:, None], request_ids[None, :], 0), axis=1
    )
    rank_ids = jnp.arange(per_holder, dtype=jnp.int32)
    request_at_distance = jnp.take(request_at_slot, by_distance)
    holders = jnp.take(block_holder, request_at_distance, axis=0)
    pages = jnp.take(block_slot, request_at_distance, axis=0)
    held_here = holders == f
    held_rank = jnp.cumsum(held_here.astype(jnp.int32), axis=1) - 1
    picked = held_here[:, :, None] & (held_rank[:, :, None] == rank_ids[None, None, :])
    local_pages = jnp.sum(jnp.where(picked, pages[:, :, None], 0), axis=1)
    flat_pool = kv_pool.reshape(kv_pool.shape[0], page_len * kv_local, 2 * head_dim)
    outgoing = jnp.take(flat_pool, local_pages.reshape(-1), axis=0)
    outgoing = outgoing.reshape(shards, per_holder * page_len * kv_local, 2 * head_dim)
    arrived = two_stage(outgoing, f, partner_piece)

    my_holders = holders[0]
    my_length = prefix_len[request_at_distance[0]]
    entry_ids = jnp.arange(max_blocks, dtype=jnp.int32)
    mine = my_holders[None, :] == by_distance[:, None]
    my_rank = jnp.cumsum(mine.astype(jnp.int32), axis=1) - 1
    chosen = mine[:, None, :] & (my_rank[:, None, :] == rank_ids[None, :, None])
    entry = jnp.sum(jnp.where(chosen, entry_ids[None, None, :], 0), axis=2)
    cached_position = entry.reshape(-1, 1) * page_len + jnp.arange(page_len, dtype=jnp.int32)
    valid = (cached_position < my_length).astype(f32).reshape(1, -1)

    positions = (my_length + jnp.arange(new_len, dtype=jnp.int32)).astype(f32)
    freqs = jnp.exp(
        jnp.arange(head_dim // 2, dtype=f32) * (-2.0 * math.log(10000.0) / head_dim)
    )
    angles = positions[:, None] * freqs
    cosine, sine = jnp.cos(angles), jnp.sin(angles)
    cosine = jnp.concatenate([cosine, cosine], axis=1)
    sine = jnp.concatenate([-sine, sine], axis=1)

    def partner_sums(pieces, cols):
        return call(
            functools.partial(partner_kernel, half, groups),
            jax.ShapeDtypeStruct((new_len, cols), bf16),
            [pltpu.VMEM((new_len, width // 2), bf16), pltpu.VMEM((width // 2, cols), bf16)],
            new_len * width * cols,
            width * (new_len + cols),
            where,
            *partner_pieces,
            *pieces,
        )

    q_other = swap(partner_sums(q_pieces, q_cols), "fsdp", half)
    kv_other = swap(partner_sums(kv_pieces, 2 * kv_cols), "fsdp", half)
    q_own, kv_own = call(
        functools.partial(own_kernel, half),
        [
            jax.ShapeDtypeStruct((new_len, q_cols), f32),
            jax.ShapeDtypeStruct((new_len, 2 * kv_cols), f32),
        ],
        [pltpu.VMEM((width // 2, q_cols), bf16), pltpu.VMEM((width // 2, 2 * kv_cols), bf16)],
        new_len * width * 2 * q_cols,
        width * (new_len + 2 * q_cols),
        where,
        own_rows,
        *q_pieces,
        *kv_pieces,
    )

    residual_out = lax.dynamic_slice_in_dim(rows, p * quarter, quarter, 0).reshape(
        shards, sub, width
    )
    residual = two_stage(jnp.take(residual_out, by_distance, axis=0), f, kv_other)

    keys_total = max_blocks * page_len
    quarters = call(
        functools.partial(attend_kernel, groups, len(arrived), kv_local, head_dim),
        [jax.ShapeDtypeStruct((quarter, q_cols), bf16)] * groups,
        [
            pltpu.VMEM((kv_local, keys_total, head_dim), bf16),
            pltpu.VMEM((kv_local, keys_total, head_dim), bf16),
            pltpu.VMEM((new_len, q_cols), bf16),
        ],
        4 * new_len * q_cols * (keys_total + new_len),
        1 << 22,
        where,
        q_own,
        kv_own,
        q_other,
        kv_other,
        cosine,
        sine,
        valid,
        *arrived,
    )

    quarters = [
        swap(piece, "pool", distance) if distance else piece
        for distance, piece in enumerate(quarters)
    ]
    quarters = jnp.stack(quarters)
    tokens = {0: quarters}
    for distance in range(2, shards, 2):
        tokens[distance] = swap(quarters, "fsdp", distance)
    for distance in range(0, shards, 2):
        tokens[distance ^ 1] = swap(tokens[distance], "fsdp", 1)
    projected = call(
        functools.partial(output_kernel, groups, shards),
        [jax.ShapeDtypeStruct((shards, sub, features), bf16)] * shards,
        [pltpu.VMEM((shards * quarter, features), f32)],
        2 * shards * quarter * features * groups * q_cols,
        1 << 22,
        where,
        *[tokens[distance] for distance in range(shards)],
        out_weight,
    )
    finished = [
        swap(piece, "fsdp", distance) if distance else piece
        for distance, piece in enumerate(projected)
    ]
    return call(
        functools.partial(finish_kernel, shards, len(residual)),
        jax.ShapeDtypeStruct((requests, sub, width), bf16),
        [
            pltpu.VMEM((shards, shards, sub, features), f32),
            pltpu.VMEM((shards, sub, width), f32),
        ],
        1 << 20,
        1 << 20,
        where,
        post_gain.reshape(1, width),
        *finished,
        *residual,
    )


def local(*arguments):
    return local_small(*arguments) if lax.axis_size("fsdp") == 8 else local_general(*arguments)


def solution(mesh):
    in_specs = (
        P("fsdp", None, None),
        P(),
        P(),
        P(),
        P(),
        P("fsdp", None, "pool", None),
        P(),
        P("fsdp", "pool"),
        P("fsdp", "pool"),
        P("fsdp", "pool"),
        P("fsdp", "pool"),
        P(),
    )
    out_specs = P(None, ("pool", "fsdp"), None)
    return jax.shard_map(local, mesh=mesh, in_specs=in_specs, out_specs=out_specs, check_vma=False)
```

```python
import functools
import math

import jax
import jax.numpy as jnp
import numpy as np
from jax import lax
from jax.experimental import pallas as pl
from jax.experimental.pallas import tpu as pltpu
from jax.sharding import PartitionSpec as P

softcap = 50.0
query_scale = 144.0 ** (-0.5)
norm_eps = 1e-06


def rms_scale(rows, gain):
    mean_square = jnp.mean(rows * rows, axis=-1, keepdims=True)
    return rows * lax.rsqrt(mean_square + norm_eps) * gain


def rotate(vectors, cosine, sine):
    half = vectors.shape[-1] // 2
    first = vectors[..., :half]
    second = vectors[..., half:]
    return jnp.concatenate(
        [first * cosine - second * sine, second * cosine + first * sine], axis=-1
    )


def capped_weights(scores, valid):
    return jnp.where(valid, jnp.exp(softcap * jnp.tanh(scores / softcap)), 0.0)


def swap(array, axis, distance):
    size = lax.axis_size(axis)
    return lax.ppermute(array, axis, [(i, i ^ distance) for i in range(size)])


def place(pieces, index):
    first = pieces[0]
    stacked = jnp.zeros((len(pieces),) + first.shape, first.dtype)
    for distance, piece in pieces.items():
        stacked = lax.dynamic_update_index_in_dim(stacked, piece, index ^ distance, 0)
    return stacked


def exchange(chunks, axis):
    size = lax.axis_size(axis)
    index = lax.axis_index(axis)
    if size > 8:
        return lax.all_to_all(chunks, axis, split_axis=0, concat_axis=0, tiled=True)
    pieces = {}
    for distance in range(size):
        chunk = lax.dynamic_index_in_dim(chunks, index ^ distance, 0, keepdims=False)
        pieces[distance] = swap(chunk, axis, distance) if distance else chunk
    return place(pieces, index)


def doubled(block, axis, span):
    pieces = {0: block}
    bit = span // 2
    while bit:
        for distance in list(pieces):
            pieces[distance ^ bit] = swap(pieces[distance], axis, bit)
        bit //= 2
    return pieces


def attend(queries, keys_new, values_new, cached, cached_valid):
    new_len, kv_local, group, head_dim = queries.shape

    def part(keys, values, valid):
        scores = jnp.einsum("tgjd,kgd->gjtk", queries, keys, preferred_element_type=jnp.float32)
        weights = capped_weights(scores, valid)
        numer = jnp.einsum(
            "gjtk,kgd->gjtd",
            weights.astype(jnp.bfloat16),
            values,
            preferred_element_type=jnp.float32,
        )
        return numer, jnp.sum(weights, axis=-1)

    query_index = jnp.arange(new_len, dtype=jnp.int32)
    causal = query_index[None, :] <= query_index[:, None]
    numer, denom = part(
        cached[..., :head_dim], cached[..., head_dim:], cached_valid[None, None, None, :]
    )
    more, added = part(keys_new, values_new, causal[None, None])
    attended = ((numer + more) / (denom + added)[..., None]).transpose(2, 0, 1, 3)
    return attended.reshape(new_len, kv_local * group * head_dim).astype(jnp.bfloat16)


def local_general(
    hidden,
    slot_of_request,
    prefix_len,
    block_holder,
    block_slot,
    kv_pool,
    norm_gain,
    q_weight,
    k_weight,
    v_weight,
    o_weight,
    post_gain,
):
    shards = lax.axis_size("fsdp")
    groups = lax.axis_size("pool")
    f = lax.axis_index("fsdp")
    p = lax.axis_index("pool")
    half = shards // 2
    side = f // half
    new_len, width = hidden.shape[1:]
    requests = slot_of_request.shape[0]
    page_len = kv_pool.shape[1]
    kv_local = kv_pool.shape[2]
    head_dim = kv_pool.shape[3] // 2
    q_cols = q_weight.shape[1]
    kv_cols = k_weight.shape[1]
    group = q_cols // kv_cols
    max_blocks = block_holder.shape[1]
    per_holder = max_blocks // shards
    quarter = new_len // groups
    sub = quarter // shards
    features = o_weight.shape[0]

    kv_pieces = doubled(jnp.concatenate([k_weight, v_weight], axis=1), "fsdp", half)
    q_pieces = doubled(q_weight, "fsdp", half)
    out_weight = lax.all_gather(o_weight, "pool", axis=0, tiled=False)

    rows = hidden[0]
    normed = rms_scale(rows.astype(jnp.float32), norm_gain).astype(jnp.bfloat16)
    own_rows = lax.dynamic_slice(normed, (0, side * (width // 2)), (new_len, width // 2))
    leaving = lax.dynamic_slice(
        normed, (p * quarter, (1 - side) * (width // 2)), (quarter, width // 2)
    )
    partner_piece = swap(leaving, "fsdp", half)
    partner_pieces = {0: partner_piece}
    for distance in range(1, groups):
        partner_pieces[distance] = swap(partner_piece, "pool", distance)
    partner_rows = place(partner_pieces, p).reshape(new_len, width // 2)

    request_ids = jnp.arange(requests, dtype=jnp.int32)
    request_at_slot = jnp.sum(
        jnp.where(slot_of_request[None, :] == request_ids[:, None], request_ids[None, :], 0), axis=1
    )
    holder_by_slot = jnp.take(block_holder, request_at_slot, axis=0)
    page_by_slot = jnp.take(block_slot, request_at_slot, axis=0)
    held_here = holder_by_slot == f
    held_rank = jnp.cumsum(held_here.astype(jnp.int32), axis=1) - 1
    rank_ids = jnp.arange(per_holder, dtype=jnp.int32)
    picked = held_here[:, :, None] & (held_rank[:, :, None] == rank_ids[None, None, :])
    local_pages = jnp.sum(jnp.where(picked, page_by_slot[:, :, None], 0), axis=1)
    flat_pool = kv_pool.reshape(kv_pool.shape[0], page_len * kv_local, 2 * head_dim)
    outgoing = jnp.take(flat_pool, local_pages, axis=0)
    outgoing = outgoing.reshape(shards, per_holder * page_len * kv_local, 2 * head_dim)
    arrived = exchange(outgoing, "fsdp")
    cached = arrived.reshape(max_blocks * page_len, kv_local, 2 * head_dim)

    my_request = lax.dynamic_index_in_dim(request_at_slot, f, keepdims=False)
    my_length = prefix_len[my_request]
    my_holders = block_holder[my_request]
    entry_ids = jnp.arange(max_blocks, dtype=jnp.int32)
    mine = my_holders[None, :] == jnp.arange(shards, dtype=jnp.int32)[:, None]
    my_rank = jnp.cumsum(mine.astype(jnp.int32), axis=1) - 1
    chosen = mine[:, None, :] & (my_rank[:, None, :] == rank_ids[None, :, None])
    entry = jnp.sum(jnp.where(chosen, entry_ids[None, None, :], 0), axis=2)
    cached_position = entry.reshape(-1, 1) * page_len + jnp.arange(page_len, dtype=jnp.int32)
    cached_valid = (cached_position < my_length).reshape(-1)

    residual_out = lax.dynamic_slice_in_dim(rows, p * quarter, quarter, 0).reshape(
        shards, sub, width
    )
    residual = exchange(residual_out, "fsdp")

    positions = (my_length + jnp.arange(new_len, dtype=jnp.int32)).astype(jnp.float32)
    freqs = jnp.exp(
        jnp.arange(head_dim // 2, dtype=jnp.float32) * (-2.0 * math.log(10000.0) / head_dim)
    )
    angles = positions[:, None] * freqs
    cosine = jnp.cos(angles)[:, None, :]
    sine = jnp.sin(angles)[:, None, :]

    def project(pieces):
        weight = place(pieces, f % half).reshape(width // 2, -1)
        partial = jnp.dot(partner_rows, weight, preferred_element_type=jnp.float32)
        other = swap(partial.astype(jnp.bfloat16), "fsdp", half)
        own = jnp.dot(own_rows, weight, preferred_element_type=jnp.float32)
        return own + other.astype(jnp.float32)

    kv_sum = project(kv_pieces)
    q_sum = project(q_pieces)
    queries = rotate(q_sum.reshape(new_len, kv_local * group, head_dim), cosine, sine)
    queries = (queries * query_scale).astype(jnp.bfloat16)
    queries = queries.reshape(new_len, kv_local, group, head_dim)
    keys_new = kv_sum[:, :kv_cols].reshape(new_len, kv_local, head_dim)
    keys_new = rotate(keys_new, cosine, sine).astype(jnp.bfloat16)
    values_new = kv_sum[:, kv_cols:].astype(jnp.bfloat16).reshape(new_len, kv_local, head_dim)
    attended = attend(queries, keys_new, values_new, cached, cached_valid)

    quarters = exchange(attended.reshape(groups, quarter, q_cols), "pool")
    token_pieces = {0: quarters}
    for distance in range(2, shards, 2):
        token_pieces[distance] = swap(quarters, "fsdp", distance)
    for distance in range(0, shards, 2):
        token_pieces[distance ^ 1] = swap(token_pieces[distance], "fsdp", 1)
    tokens = place(token_pieces, f)
    projected = jnp.einsum(
        "sptc,pfc->stf", tokens, out_weight, preferred_element_type=jnp.float32
    ).astype(jnp.bfloat16)
    projected = projected.reshape(shards, shards, sub, features).transpose(1, 0, 2, 3)
    finished = exchange(projected, "fsdp").transpose(1, 2, 0, 3).reshape(shards, sub, width)
    finished = residual.astype(jnp.float32) + rms_scale(finished.astype(jnp.float32), post_gain)
    return jnp.take(finished.astype(jnp.bfloat16), slot_of_request, axis=0)


VMEM = pl.BlockSpec(memory_space=pltpu.VMEM)
SMEM = pl.BlockSpec(memory_space=pltpu.SMEM)


def call(kernel, outs, scratch, flops, nbytes, *operands, specs=None):
    return pl.pallas_call(
        kernel,
        out_shape=outs,
        in_specs=specs or [SMEM] + [VMEM] * (len(operands) - 1),
        out_specs=jax.tree.map(lambda _: VMEM, outs),
        scratch_shapes=scratch,
        compiler_params=pltpu.CompilerParams(vmem_limit_bytes=48 << 20),
        cost_estimate=pl.CostEstimate(flops=flops, bytes_accessed=nbytes, transcendentals=0),
    )(*operands)


def after(array, *earlier):
    return lax.optimization_barrier((array,) + earlier)[0]


def gather_weight(weight_refs, weight, f, half):
    count = weight_refs[0].shape[0]
    for distance, ref in enumerate(weight_refs):
        start = ((f ^ distance) & (half - 1)) * count
        weight[pl.ds(pl.multiple_of(start, 64), count), :] = ref[...]


def partner_kernel(half, groups, where_ref, *refs):
    p, f = where_ref[0], where_ref[1]
    x_refs = refs[:groups]
    q_refs, kv_refs = refs[groups : groups + half], refs[groups + half : groups + 2 * half]
    out_ref, rows, q_weight, kv_weight = refs[groups + 2 * half :]
    quarter = x_refs[0].shape[0]
    for distance, ref in enumerate(x_refs):
        start = pl.multiple_of((p ^ distance) * quarter, quarter)
        rows[pl.ds(start, quarter), :] = ref[...]
    at = 0
    for w_refs, weight in ((q_refs, q_weight), (kv_refs, kv_weight)):
        gather_weight(w_refs, weight, f, half)
        to = at + weight.shape[1]
        out_ref[:, at:to] = jnp.dot(
            rows[...], weight[...], preferred_element_type=jnp.float32
        ).astype(jnp.bfloat16)
        at = to


def row_scale(rows):
    return lax.rsqrt(jnp.mean(rows * rows, axis=1, keepdims=True) + norm_eps)


def prologue_kernel(where_ref, hidden_ref, gain_ref, k_ref, v_ref, leaving_ref, rows_ref, kv_ref, normed, sem):
    p, f = where_ref[0], where_ref[1]
    quarter, width = rows_ref.shape
    half_width = width // 2
    start = pl.multiple_of(p * quarter, quarter)
    copy = pltpu.make_async_copy(hidden_ref.at[pl.ds(start, quarter), :], rows_ref, sem)
    copy.start()
    kv_ref[:, : k_ref.shape[1]] = k_ref[...]
    kv_ref[:, k_ref.shape[1] :] = v_ref[...]
    copy.wait()
    rows = rows_ref[...].astype(jnp.float32)
    normed[...] = rows * row_scale(rows) * gain_ref[...]
    away = pl.multiple_of((1 - where_ref[2]) * half_width, 128)
    leaving_ref[...] = normed[:, pl.ds(away, half_width)].astype(jnp.bfloat16)


def pages_kernel(
    requests, page_len, where_ref, holder_ref, slot_ref, pool_ref, out_ref, valid_ref, listed, entries, counts
):
    f = where_ref[1]
    max_blocks = holder_ref.shape[1]
    shards, _, _ = out_ref.shape
    per = max_blocks // shards
    page_rows = pool_ref.shape[1]
    length, mine = jnp.int32(0), jnp.int32(0)
    for r in range(requests):
        at = where_ref[3 + r] == f
        length = length + jnp.where(at, where_ref[3 + requests + r], 0)
        mine = mine + jnp.where(at, r, 0)
    for r in range(requests):
        slot = where_ref[3 + r]

        def note(j, count):
            listed[count] = slot_ref[r, j]
            return count + jnp.where(holder_ref[r, j] == f, 1, 0)

        lax.fori_loop(0, max_blocks, note, jnp.int32(0), unroll=8)
        for k in range(per):
            out_ref[slot, k * page_rows : (k + 1) * page_rows, :] = pool_ref[listed[k]]
    for h in range(shards):
        counts[h] = 0

    def enter(j, carry):
        h = holder_ref[mine, j]
        count = counts[h]
        entries[h * per + count] = j
        counts[h] = count + 1
        return carry

    lax.fori_loop(0, max_blocks, enter, 0, unroll=4)
    row = lax.broadcasted_iota(jnp.int32, valid_ref.shape, 0)
    lane = lax.broadcasted_iota(jnp.int32, valid_ref.shape, 1)
    place_in = row * per + lane // page_len
    entry = jnp.zeros(valid_ref.shape, jnp.int32)
    for at in range(max_blocks):
        entry = jnp.where(place_in == at, entries[at], entry)
    position = entry * page_len + lane % page_len
    valid_ref[...] = jnp.where(position < length, 1.0, 0.0)


def own_kernel(half, requests, where_ref, hidden_ref, gain_ref, freq_ref, *refs):
    f = where_ref[1]
    q_refs, kv_refs = refs[:half], refs[half : 2 * half]
    q_ref, kv_ref, cos_ref, sin_ref, q_weight, kv_weight, normed = refs[2 * half :]
    new_len, width = hidden_ref.shape
    half_width = width // 2
    length = jnp.int32(0)
    for r in range(requests):
        length = length + jnp.where(where_ref[3 + r] == f, where_ref[3 + requests + r], 0)
    start = pl.multiple_of(where_ref[2] * half_width, 128)
    gain = gain_ref[:, pl.ds(start, half_width)]
    step = 32

    def norm(index, carry):
        at = pl.multiple_of(index * step, step)
        rows = hidden_ref[pl.ds(at, step), :].astype(jnp.float32)
        scale = row_scale(rows)
        part = hidden_ref[pl.ds(at, step), pl.ds(start, half_width)].astype(jnp.float32)
        normed[pl.ds(at, step), :] = (part * scale * gain).astype(jnp.bfloat16)
        return carry

    lax.fori_loop(0, new_len // step, norm, 0)
    position = lax.broadcasted_iota(jnp.int32, cos_ref.shape, 0) + length
    angle = position.astype(jnp.float32) * freq_ref[...]
    lane = lax.broadcasted_iota(jnp.int32, cos_ref.shape, 1)
    cos_ref[...] = jnp.cos(angle)
    sine = jnp.sin(angle)
    sin_ref[...] = jnp.where(lane < cos_ref.shape[1] // 2, -sine, sine)
    for w_refs, out_ref, weight in ((q_refs, q_ref, q_weight), (kv_refs, kv_ref, kv_weight)):
        gather_weight(w_refs, weight, f, half)
        out_ref[...] = jnp.dot(normed[...], weight[...], preferred_element_type=jnp.float32)


def capped(scores):
    return jnp.exp2(jnp.tanh(scores * (1.0 / softcap)) * (softcap * math.log2(math.e)))


def attend_kernel(
    groups,
    kv_local,
    head_dim,
    where_ref,
    q_own,
    kv_own,
    other,
    cos_ref,
    sin_ref,
    valid_ref,
    page_ref,
    *refs,
):
    p = where_ref[0]
    out_refs = refs[:groups]
    keys, values, result = refs[groups:]
    new_len = q_own.shape[0]
    q_other, kv_other = other.at[:, : q_own.shape[1]], other.at[:, q_own.shape[1] :]
    group = q_own.shape[1] // (kv_local * head_dim)
    cosine, sine = cos_ref[...], sin_ref[...]

    def rope(vectors):
        return vectors * cosine + pltpu.roll(vectors, head_dim // 2, 1) * sine

    span = page_ref.shape[1]
    per = span // kv_local
    row = lax.broadcasted_iota(jnp.int32, (span, span), 0)
    column = lax.broadcasted_iota(jnp.int32, (span, span), 1)
    part = (column == (row % per) * kv_local + row // per).astype(jnp.bfloat16)
    place_at = 0
    for holder in range(page_ref.shape[0]):
        parted = jnp.dot(part, page_ref[holder], preferred_element_type=jnp.float32)
        parted = parted.astype(jnp.bfloat16)
        for g in range(kv_local):
            lines = parted[g * per : (g + 1) * per]
            keys[g, place_at : place_at + per, :] = lines[:, :head_dim]
            values[g, place_at : place_at + per, :] = lines[:, head_dim:]
        place_at += per

    span_keys = 2 * per
    t = lax.broadcasted_iota(jnp.int32, (group * new_len, new_len), 0) % new_len
    s = lax.broadcasted_iota(jnp.int32, (group * new_len, new_len), 1)
    causal = s <= t
    for g in range(kv_local):
        at = g * head_dim
        heads = []
        for j in range(group):
            to = (g * group + j) * head_dim
            total = q_own[:, to : to + head_dim] + q_other[:, to : to + head_dim].astype(jnp.float32)
            heads.append((rope(total) * query_scale).astype(jnp.bfloat16))
        queries = jnp.concatenate(heads, axis=0)
        new_key = rope(
            kv_own[:, at : at + head_dim] + kv_other[:, at : at + head_dim].astype(jnp.float32)
        ).astype(jnp.bfloat16)
        at += kv_local * head_dim
        new_value = (
            kv_own[:, at : at + head_dim] + kv_other[:, at : at + head_dim].astype(jnp.float32)
        ).astype(jnp.bfloat16)

        def scores_of(key):
            return lax.dot_general(
                queries, key, (((1,), (1,)), ((), ())), preferred_element_type=jnp.float32
            )

        weights = jnp.where(causal, capped(scores_of(new_key)), 0.0)
        denom = jnp.sum(weights, axis=1, keepdims=True)
        numer = jnp.dot(
            weights.astype(jnp.bfloat16), new_value, preferred_element_type=jnp.float32
        )
        for start in range(0, place_at, span_keys):
            at = start // per
            valid = jnp.concatenate([valid_ref[at : at + 1], valid_ref[at + 1 : at + 2]], axis=1)
            valid = valid > 0.0
            weights = jnp.where(
                valid, capped(scores_of(keys[g, start : start + span_keys, :])), 0.0
            )
            denom = denom + jnp.sum(weights, axis=1, keepdims=True)
            numer = numer + jnp.dot(
                weights.astype(jnp.bfloat16),
                values[g, start : start + span_keys, :],
                preferred_element_type=jnp.float32,
            )
        attended = (numer / denom).astype(jnp.bfloat16)
        for j in range(group):
            to = (g * group + j) * head_dim
            result[:, to : to + head_dim] = attended[j * new_len : (j + 1) * new_len]
    quarter = new_len // groups
    for distance, ref in enumerate(out_refs):
        start = pl.multiple_of((p ^ distance) * quarter, quarter)
        ref[...] = result[pl.ds(start, quarter), :]


def output_kernel(groups, shards, where_ref, *refs):
    p, f = where_ref[0], where_ref[1]
    token_refs = refs[:shards]
    weight_ref = refs[shards]
    out_refs = refs[shards + 1 : 2 * shards + 1]
    total = refs[2 * shards + 1]
    quarter = token_refs[0].shape[1]
    sub = quarter // shards
    projected = None
    for distance in range(groups):
        rows = jnp.concatenate([ref[distance] for ref in token_refs], axis=0)
        term = lax.dot_general(
            rows,
            weight_ref[p ^ distance],
            (((1,), (1,)), ((), ())),
            preferred_element_type=jnp.float32,
        )
        projected = term if projected is None else projected + term
    total[...] = projected
    for e in range(shards):
        for distance, ref in enumerate(out_refs):
            start = pl.multiple_of(e * quarter + (f ^ distance) * sub, sub)
            ref[f ^ e] = total[pl.ds(start, sub), :].astype(jnp.bfloat16)


def finish_kernel(shards, where_ref, gain_ref, residual_ref, *refs):
    f = where_ref[1]
    piece_refs = refs[:shards]
    out_ref, projected = refs[shards:]
    for distance, ref in enumerate(piece_refs):
        projected[f ^ distance] = ref[...].astype(jnp.float32)
    gain = gain_ref[...]
    for request in range(out_ref.shape[0]):
        slot = where_ref[3 + request]
        line = jnp.concatenate([projected[k, slot] for k in range(shards)], axis=1)
        mean_square = jnp.mean(line * line, axis=1, keepdims=True)
        line = line * lax.rsqrt(mean_square + norm_eps) * gain
        out_ref[request] = (residual_ref[slot].astype(jnp.float32) + line).astype(jnp.bfloat16)


def pool_pieces(block, groups):
    return [block] + [swap(block, "pool", distance) for distance in range(1, groups)]


def local_small(
    hidden,
    slot_of_request,
    prefix_len,
    block_holder,
    block_slot,
    kv_pool,
    norm_gain,
    q_weight,
    k_weight,
    v_weight,
    o_weight,
    post_gain,
):
    shards = lax.axis_size("fsdp")
    groups = lax.axis_size("pool")
    f = lax.axis_index("fsdp")
    p = lax.axis_index("pool")
    half = shards // 2
    side = f // half
    new_len, width = hidden.shape[1:]
    requests = slot_of_request.shape[0]
    page_len = kv_pool.shape[1]
    kv_local = kv_pool.shape[2]
    head_dim = kv_pool.shape[3] // 2
    q_cols = q_weight.shape[1]
    kv_cols = k_weight.shape[1]
    max_blocks = block_holder.shape[1]
    per_holder = max_blocks // shards
    quarter = new_len // groups
    sub = quarter // shards
    features = o_weight.shape[0]
    bf16, f32 = jnp.bfloat16, jnp.float32
    where = jnp.concatenate(
        [jnp.stack([p, f, side]).astype(jnp.int32), slot_of_request, prefix_len]
    )
    shape = jax.ShapeDtypeStruct
    any_place = pl.BlockSpec(memory_space=pl.ANY)
    gain = norm_gain.reshape(1, width)
    rows = hidden[0]

    leaving, my_quarter, kv_weight = call(
        prologue_kernel,
        [
            shape((quarter, width // 2), bf16),
            shape((quarter, width), bf16),
            shape((features, 2 * kv_cols), bf16),
        ],
        [pltpu.VMEM((quarter, width), f32), pltpu.SemaphoreType.DMA],
        quarter * width * 8,
        4 * features * kv_cols,
        where,
        rows,
        gain,
        k_weight,
        v_weight,
        specs=[SMEM, any_place, VMEM, VMEM, VMEM],
    )
    partner_piece = swap(leaving, "fsdp", half)

    q_pieces = list(map(doubled(q_weight, "fsdp", half).get, range(half)))
    kv_pieces = list(map(doubled(kv_weight, "fsdp", half).get, range(half)))

    flat_pool = kv_pool.reshape(kv_pool.shape[0], page_len * kv_local, 2 * head_dim)
    page_rows = per_holder * page_len * kv_local
    outgoing, valid = call(
        functools.partial(pages_kernel, requests, page_len),
        [
            shape((shards, page_rows, 2 * head_dim), bf16),
            shape((shards, per_holder * page_len), f32),
        ],
        [
            pltpu.SMEM((2 * per_holder,), jnp.int32),
            pltpu.SMEM((max_blocks + per_holder,), jnp.int32),
            pltpu.SMEM((shards,), jnp.int32),
        ],
        1 << 20,
        1 << 21,
        where,
        block_holder,
        block_slot,
        flat_pool,
        specs=[SMEM, SMEM, SMEM, VMEM],
    )
    partner_pieces = pool_pieces(partner_piece, groups)
    arrived = lax.all_to_all(
        after(outgoing, partner_piece), "fsdp", split_axis=0, concat_axis=0, tiled=True
    )
    out_weight = lax.all_gather(after(o_weight, partner_pieces[-1]), "pool", axis=0, tiled=False)

    partial = call(
        functools.partial(partner_kernel, half, groups),
        shape((new_len, q_cols + 2 * kv_cols), bf16),
        [
            pltpu.VMEM((new_len, width // 2), bf16),
            pltpu.VMEM((width // 2, q_cols), bf16),
            pltpu.VMEM((width // 2, 2 * kv_cols), bf16),
        ],
        new_len * width * (q_cols + 2 * kv_cols),
        width * (new_len + q_cols + 2 * kv_cols),
        where,
        *partner_pieces,
        *q_pieces,
        *kv_pieces,
    )
    other = swap(partial, "fsdp", half)
    freqs = np.exp(np.arange(head_dim // 2) * (-2.0 * math.log(10000.0) / head_dim))
    freqs = np.concatenate([freqs, freqs]).astype(np.float32).reshape(1, head_dim)
    q_own, kv_own, cosine, sine = call(
        functools.partial(own_kernel, half, requests),
        [
            shape((new_len, q_cols), f32),
            shape((new_len, 2 * kv_cols), f32),
            shape((new_len, head_dim), f32),
            shape((new_len, head_dim), f32),
        ],
        [
            pltpu.VMEM((width // 2, q_cols), bf16),
            pltpu.VMEM((width // 2, 2 * kv_cols), bf16),
            pltpu.VMEM((new_len, width // 2), bf16),
        ],
        new_len * width * (q_cols + 2 * kv_cols),
        width * (2 * new_len + q_cols + 2 * kv_cols),
        where,
        after(rows, partial),
        gain,
        freqs,
        *q_pieces,
        *kv_pieces,
    )

    residual = lax.all_to_all(
        after(my_quarter.reshape(shards, sub, width), arrived),
        "fsdp",
        split_axis=0,
        concat_axis=0,
        tiled=True,
    )

    keys_total = max_blocks * page_len
    quarters = call(
        functools.partial(attend_kernel, groups, kv_local, head_dim),
        [shape((quarter, q_cols), bf16)] * groups,
        [
            pltpu.VMEM((kv_local, keys_total, head_dim), bf16),
            pltpu.VMEM((kv_local, keys_total, head_dim), bf16),
            pltpu.VMEM((new_len, q_cols), bf16),
        ],
        4 * new_len * q_cols * (keys_total + new_len),
        1 << 22,
        where,
        q_own,
        kv_own,
        other,
        cosine,
        sine,
        valid,
        arrived,
    )

    quarters = [
        swap(piece, "pool", distance) if distance else piece
        for distance, piece in enumerate(quarters)
    ]
    quarters = jnp.stack(quarters)
    tokens = {0: quarters}
    for distance in range(2, shards, 2):
        tokens[distance] = swap(quarters, "fsdp", distance)
    for distance in range(0, shards, 2):
        tokens[distance ^ 1] = swap(tokens[distance], "fsdp", 1)
    projected = call(
        functools.partial(output_kernel, groups, shards),
        [shape((shards, sub, features), bf16)] * shards,
        [pltpu.VMEM((shards * quarter, features), f32)],
        2 * shards * quarter * features * groups * q_cols,
        1 << 22,
        where,
        *[tokens[distance] for distance in range(shards)],
        out_weight,
    )
    finished = [
        swap(piece, "fsdp", distance) if distance else piece
        for distance, piece in enumerate(projected)
    ]
    return call(
        functools.partial(finish_kernel, shards),
        shape((requests, sub, width), bf16),
        [pltpu.VMEM((shards, shards, sub, features), f32)],
        1 << 20,
        1 << 20,
        where,
        post_gain.reshape(1, width),
        residual,
        *finished,
    )


def local(*arguments):
    return local_small(*arguments) if lax.axis_size("fsdp") == 8 else local_general(*arguments)


def solution(mesh):
    in_specs = (
        P("fsdp", None, None),
        P(),
        P(),
        P(),
        P(),
        P("fsdp", None, "pool", None),
        P(),
        P("fsdp", "pool"),
        P("fsdp", "pool"),
        P("fsdp", "pool"),
        P("fsdp", "pool"),
        P(),
    )
    out_specs = P(None, ("pool", "fsdp"), None)
    return jax.shard_map(local, mesh=mesh, in_specs=in_specs, out_specs=out_specs, check_vma=False)
```

```python
import functools
import math

import jax
import jax.numpy as jnp
import numpy as np
from jax import lax
from jax.experimental import pallas as pl
from jax.experimental.pallas import tpu as pltpu
from jax.sharding import PartitionSpec as P

softcap = 50.0
query_scale = 144.0 ** (-0.5)
norm_eps = 1e-06


def rms_scale(rows, gain):
    mean_square = jnp.mean(rows * rows, axis=-1, keepdims=True)
    return rows * lax.rsqrt(mean_square + norm_eps) * gain


def rotate(vectors, cosine, sine):
    half = vectors.shape[-1] // 2
    first = vectors[..., :half]
    second = vectors[..., half:]
    return jnp.concatenate(
        [first * cosine - second * sine, second * cosine + first * sine], axis=-1
    )


def capped_weights(scores, valid):
    return jnp.where(valid, jnp.exp(softcap * jnp.tanh(scores / softcap)), 0.0)


def swap(array, axis, distance):
    size = lax.axis_size(axis)
    return lax.ppermute(array, axis, [(i, i ^ distance) for i in range(size)])


def place(pieces, index):
    first = pieces[0]
    stacked = jnp.zeros((len(pieces),) + first.shape, first.dtype)
    for distance, piece in pieces.items():
        stacked = lax.dynamic_update_index_in_dim(stacked, piece, index ^ distance, 0)
    return stacked


def exchange(chunks, axis):
    size = lax.axis_size(axis)
    index = lax.axis_index(axis)
    if size > 8:
        return lax.all_to_all(chunks, axis, split_axis=0, concat_axis=0, tiled=True)
    pieces = {}
    for distance in range(size):
        chunk = lax.dynamic_index_in_dim(chunks, index ^ distance, 0, keepdims=False)
        pieces[distance] = swap(chunk, axis, distance) if distance else chunk
    return place(pieces, index)


def doubled(block, axis, span):
    pieces = {0: block}
    bit = span // 2
    while bit:
        for distance in list(pieces):
            pieces[distance ^ bit] = swap(pieces[distance], axis, bit)
        bit //= 2
    return pieces


def attend(queries, keys_new, values_new, cached, cached_valid):
    new_len, kv_local, group, head_dim = queries.shape

    def part(keys, values, valid):
        scores = jnp.einsum("tgjd,kgd->gjtk", queries, keys, preferred_element_type=jnp.float32)
        weights = capped_weights(scores, valid)
        numer = jnp.einsum(
            "gjtk,kgd->gjtd",
            weights.astype(jnp.bfloat16),
            values,
            preferred_element_type=jnp.float32,
        )
        return numer, jnp.sum(weights, axis=-1)

    query_index = jnp.arange(new_len, dtype=jnp.int32)
    causal = query_index[None, :] <= query_index[:, None]
    numer, denom = part(
        cached[..., :head_dim], cached[..., head_dim:], cached_valid[None, None, None, :]
    )
    more, added = part(keys_new, values_new, causal[None, None])
    attended = ((numer + more) / (denom + added)[..., None]).transpose(2, 0, 1, 3)
    return attended.reshape(new_len, kv_local * group * head_dim).astype(jnp.bfloat16)


def local_general(
    hidden,
    slot_of_request,
    prefix_len,
    block_holder,
    block_slot,
    kv_pool,
    norm_gain,
    q_weight,
    k_weight,
    v_weight,
    o_weight,
    post_gain,
):
    shards = lax.axis_size("fsdp")
    groups = lax.axis_size("pool")
    f = lax.axis_index("fsdp")
    p = lax.axis_index("pool")
    half = shards // 2
    side = f // half
    new_len, width = hidden.shape[1:]
    requests = slot_of_request.shape[0]
    page_len = kv_pool.shape[1]
    kv_local = kv_pool.shape[2]
    head_dim = kv_pool.shape[3] // 2
    q_cols = q_weight.shape[1]
    kv_cols = k_weight.shape[1]
    group = q_cols // kv_cols
    max_blocks = block_holder.shape[1]
    per_holder = max_blocks // shards
    quarter = new_len // groups
    sub = quarter // shards
    features = o_weight.shape[0]

    kv_pieces = doubled(jnp.concatenate([k_weight, v_weight], axis=1), "fsdp", half)
    q_pieces = doubled(q_weight, "fsdp", half)
    out_weight = lax.all_gather(o_weight, "pool", axis=0, tiled=False)

    rows = hidden[0]
    normed = rms_scale(rows.astype(jnp.float32), norm_gain).astype(jnp.bfloat16)
    own_rows = lax.dynamic_slice(normed, (0, side * (width // 2)), (new_len, width // 2))
    leaving = lax.dynamic_slice(
        normed, (p * quarter, (1 - side) * (width // 2)), (quarter, width // 2)
    )
    partner_piece = swap(leaving, "fsdp", half)
    partner_pieces = {0: partner_piece}
    for distance in range(1, groups):
        partner_pieces[distance] = swap(partner_piece, "pool", distance)
    partner_rows = place(partner_pieces, p).reshape(new_len, width // 2)

    request_ids = jnp.arange(requests, dtype=jnp.int32)
    request_at_slot = jnp.sum(
        jnp.where(slot_of_request[None, :] == request_ids[:, None], request_ids[None, :], 0), axis=1
    )
    holder_by_slot = jnp.take(block_holder, request_at_slot, axis=0)
    page_by_slot = jnp.take(block_slot, request_at_slot, axis=0)
    held_here = holder_by_slot == f
    held_rank = jnp.cumsum(held_here.astype(jnp.int32), axis=1) - 1
    rank_ids = jnp.arange(per_holder, dtype=jnp.int32)
    picked = held_here[:, :, None] & (held_rank[:, :, None] == rank_ids[None, None, :])
    local_pages = jnp.sum(jnp.where(picked, page_by_slot[:, :, None], 0), axis=1)
    flat_pool = kv_pool.reshape(kv_pool.shape[0], page_len * kv_local, 2 * head_dim)
    outgoing = jnp.take(flat_pool, local_pages, axis=0)
    outgoing = outgoing.reshape(shards, per_holder * page_len * kv_local, 2 * head_dim)
    arrived = exchange(outgoing, "fsdp")
    cached = arrived.reshape(max_blocks * page_len, kv_local, 2 * head_dim)

    my_request = lax.dynamic_index_in_dim(request_at_slot, f, keepdims=False)
    my_length = prefix_len[my_request]
    my_holders = block_holder[my_request]
    entry_ids = jnp.arange(max_blocks, dtype=jnp.int32)
    mine = my_holders[None, :] == jnp.arange(shards, dtype=jnp.int32)[:, None]
    my_rank = jnp.cumsum(mine.astype(jnp.int32), axis=1) - 1
    chosen = mine[:, None, :] & (my_rank[:, None, :] == rank_ids[None, :, None])
    entry = jnp.sum(jnp.where(chosen, entry_ids[None, None, :], 0), axis=2)
    cached_position = entry.reshape(-1, 1) * page_len + jnp.arange(page_len, dtype=jnp.int32)
    cached_valid = (cached_position < my_length).reshape(-1)

    residual_out = lax.dynamic_slice_in_dim(rows, p * quarter, quarter, 0).reshape(
        shards, sub, width
    )
    residual = exchange(residual_out, "fsdp")

    positions = (my_length + jnp.arange(new_len, dtype=jnp.int32)).astype(jnp.float32)
    freqs = jnp.exp(
        jnp.arange(head_dim // 2, dtype=jnp.float32) * (-2.0 * math.log(10000.0) / head_dim)
    )
    angles = positions[:, None] * freqs
    cosine = jnp.cos(angles)[:, None, :]
    sine = jnp.sin(angles)[:, None, :]

    def project(pieces):
        weight = place(pieces, f % half).reshape(width // 2, -1)
        partial = jnp.dot(partner_rows, weight, preferred_element_type=jnp.float32)
        other = swap(partial.astype(jnp.bfloat16), "fsdp", half)
        own = jnp.dot(own_rows, weight, preferred_element_type=jnp.float32)
        return own + other.astype(jnp.float32)

    kv_sum = project(kv_pieces)
    q_sum = project(q_pieces)
    queries = rotate(q_sum.reshape(new_len, kv_local * group, head_dim), cosine, sine)
    queries = (queries * query_scale).astype(jnp.bfloat16)
    queries = queries.reshape(new_len, kv_local, group, head_dim)
    keys_new = kv_sum[:, :kv_cols].reshape(new_len, kv_local, head_dim)
    keys_new = rotate(keys_new, cosine, sine).astype(jnp.bfloat16)
    values_new = kv_sum[:, kv_cols:].astype(jnp.bfloat16).reshape(new_len, kv_local, head_dim)
    attended = attend(queries, keys_new, values_new, cached, cached_valid)

    quarters = exchange(attended.reshape(groups, quarter, q_cols), "pool")
    token_pieces = {0: quarters}
    for distance in range(2, shards, 2):
        token_pieces[distance] = swap(quarters, "fsdp", distance)
    for distance in range(0, shards, 2):
        token_pieces[distance ^ 1] = swap(token_pieces[distance], "fsdp", 1)
    tokens = place(token_pieces, f)
    projected = jnp.einsum(
        "sptc,pfc->stf", tokens, out_weight, preferred_element_type=jnp.float32
    ).astype(jnp.bfloat16)
    projected = projected.reshape(shards, shards, sub, features).transpose(1, 0, 2, 3)
    finished = exchange(projected, "fsdp").transpose(1, 2, 0, 3).reshape(shards, sub, width)
    finished = residual.astype(jnp.float32) + rms_scale(finished.astype(jnp.float32), post_gain)
    return jnp.take(finished.astype(jnp.bfloat16), slot_of_request, axis=0)


VMEM = pl.BlockSpec(memory_space=pltpu.VMEM)
SMEM = pl.BlockSpec(memory_space=pltpu.SMEM)


def call(kernel, outs, scratch, flops, nbytes, *operands, specs=None):
    return pl.pallas_call(
        kernel,
        out_shape=outs,
        in_specs=specs or [SMEM] + [VMEM] * (len(operands) - 1),
        out_specs=jax.tree.map(lambda _: VMEM, outs),
        scratch_shapes=scratch,
        compiler_params=pltpu.CompilerParams(vmem_limit_bytes=48 << 20),
        cost_estimate=pl.CostEstimate(flops=flops, bytes_accessed=nbytes, transcendentals=0),
    )(*operands)


def after(array, *earlier):
    return lax.optimization_barrier((array,) + earlier)[0]


def gather_weight(weight_refs, weight, f, half):
    count = weight_refs[0].shape[0]
    for distance, ref in enumerate(weight_refs):
        start = ((f ^ distance) & (half - 1)) * count
        weight[pl.ds(pl.multiple_of(start, 64), count), :] = ref[...]


def partner_kernel(half, groups, where_ref, *refs):
    p, f = where_ref[0], where_ref[1]
    x_refs = refs[:groups]
    q_refs, kv_refs = refs[groups : groups + half], refs[groups + half : groups + 2 * half]
    out_ref, rows, q_weight, kv_weight = refs[groups + 2 * half :]
    quarter = x_refs[0].shape[0]
    for distance, ref in enumerate(x_refs):
        start = pl.multiple_of((p ^ distance) * quarter, quarter)
        rows[pl.ds(start, quarter), :] = ref[...]
    at = 0
    for w_refs, weight in ((q_refs, q_weight), (kv_refs, kv_weight)):
        gather_weight(w_refs, weight, f, half)
        to = at + weight.shape[1]
        out_ref[:, at:to] = jnp.dot(
            rows[...], weight[...], preferred_element_type=jnp.float32
        ).astype(jnp.bfloat16)
        at = to


def row_scale(rows):
    return lax.rsqrt(jnp.mean(rows * rows, axis=1, keepdims=True) + norm_eps)


def prologue_kernel(where_ref, hidden_ref, gain_ref, k_ref, v_ref, leaving_ref, rows_ref, kv_ref, normed, sem):
    p, f = where_ref[0], where_ref[1]
    quarter, width = rows_ref.shape
    half_width = width // 2
    start = pl.multiple_of(p * quarter, quarter)
    copy = pltpu.make_async_copy(hidden_ref.at[pl.ds(start, quarter), :], rows_ref, sem)
    copy.start()
    kv_ref[:, : k_ref.shape[1]] = k_ref[...]
    kv_ref[:, k_ref.shape[1] :] = v_ref[...]
    copy.wait()
    rows = rows_ref[...].astype(jnp.float32)
    normed[...] = rows * row_scale(rows) * gain_ref[...]
    away = pl.multiple_of((1 - where_ref[2]) * half_width, 128)
    leaving_ref[...] = normed[:, pl.ds(away, half_width)].astype(jnp.bfloat16)


def pages_kernel(
    requests, page_len, where_ref, holder_ref, slot_ref, pool_ref, out_ref, valid_ref, listed, entries, counts
):
    f = where_ref[1]
    max_blocks = holder_ref.shape[1]
    shards, _, _ = out_ref.shape
    per = max_blocks // shards
    page_rows = pool_ref.shape[1]
    length, mine = jnp.int32(0), jnp.int32(0)
    for r in range(requests):
        at = where_ref[3 + r] == f
        length = length + jnp.where(at, where_ref[3 + requests + r], 0)
        mine = mine + jnp.where(at, r, 0)
    for r in range(requests):
        slot = where_ref[3 + r]

        def note(j, count):
            listed[count] = slot_ref[r, j]
            return count + jnp.where(holder_ref[r, j] == f, 1, 0)

        lax.fori_loop(0, max_blocks, note, jnp.int32(0), unroll=8)
        for k in range(per):
            out_ref[slot, k * page_rows : (k + 1) * page_rows, :] = pool_ref[listed[k]]
    for h in range(shards):
        counts[h] = 0

    def enter(j, carry):
        h = holder_ref[mine, j]
        count = counts[h]
        entries[h * per + count] = j
        counts[h] = count + 1
        return carry

    lax.fori_loop(0, max_blocks, enter, 0, unroll=4)
    row = lax.broadcasted_iota(jnp.int32, valid_ref.shape, 0)
    lane = lax.broadcasted_iota(jnp.int32, valid_ref.shape, 1)
    place_in = row * per + lane // page_len
    entry = jnp.zeros(valid_ref.shape, jnp.int32)
    for at in range(max_blocks):
        entry = jnp.where(place_in == at, entries[at], entry)
    position = entry * page_len + lane % page_len
    valid_ref[...] = jnp.where(position < length, 1.0, 0.0)


def own_kernel(half, requests, where_ref, hidden_ref, gain_ref, freq_ref, *refs):
    f = where_ref[1]
    q_refs, kv_refs = refs[:half], refs[half : 2 * half]
    q_ref, kv_ref, cos_ref, sin_ref, q_weight, kv_weight, normed = refs[2 * half :]
    new_len, width = hidden_ref.shape
    half_width = width // 2
    length = jnp.int32(0)
    for r in range(requests):
        length = length + jnp.where(where_ref[3 + r] == f, where_ref[3 + requests + r], 0)
    start = pl.multiple_of(where_ref[2] * half_width, 128)
    gain = gain_ref[:, pl.ds(start, half_width)]
    step = 32

    def norm(index, carry):
        at = pl.multiple_of(index * step, step)
        rows = hidden_ref[pl.ds(at, step), :].astype(jnp.float32)
        scale = row_scale(rows)
        part = hidden_ref[pl.ds(at, step), pl.ds(start, half_width)].astype(jnp.float32)
        normed[pl.ds(at, step), :] = (part * scale * gain).astype(jnp.bfloat16)
        return carry

    lax.fori_loop(0, new_len // step, norm, 0)
    position = lax.broadcasted_iota(jnp.int32, cos_ref.shape, 0) + length
    angle = position.astype(jnp.float32) * freq_ref[...]
    lane = lax.broadcasted_iota(jnp.int32, cos_ref.shape, 1)
    cos_ref[...] = jnp.cos(angle)
    sine = jnp.sin(angle)
    sin_ref[...] = jnp.where(lane < cos_ref.shape[1] // 2, -sine, sine)
    for w_refs, out_ref, weight in ((q_refs, q_ref, q_weight), (kv_refs, kv_ref, kv_weight)):
        gather_weight(w_refs, weight, f, half)
        out_ref[...] = jnp.dot(normed[...], weight[...], preferred_element_type=jnp.float32)


def capped(scores):
    return jnp.exp2(jnp.tanh(scores * (1.0 / softcap)) * (softcap * math.log2(math.e)))


def attend_kernel(
    groups,
    kv_local,
    head_dim,
    where_ref,
    q_own,
    kv_own,
    other,
    cos_ref,
    sin_ref,
    valid_ref,
    page_ref,
    *refs,
):
    p = where_ref[0]
    out_refs = refs[:groups]
    keys, values, result = refs[groups:]
    new_len = q_own.shape[0]
    q_other, kv_other = other.at[:, : q_own.shape[1]], other.at[:, q_own.shape[1] :]
    group = q_own.shape[1] // (kv_local * head_dim)
    cosine, sine = cos_ref[...], sin_ref[...]

    def rope(vectors):
        return vectors * cosine + pltpu.roll(vectors, head_dim // 2, 1) * sine

    span = page_ref.shape[1]
    per = span // kv_local
    row = lax.broadcasted_iota(jnp.int32, (span, span), 0)
    column = lax.broadcasted_iota(jnp.int32, (span, span), 1)
    part = (column == (row % per) * kv_local + row // per).astype(jnp.bfloat16)
    place_at = 0
    for holder in range(page_ref.shape[0]):
        parted = jnp.dot(part, page_ref[holder], preferred_element_type=jnp.float32)
        parted = parted.astype(jnp.bfloat16)
        for g in range(kv_local):
            lines = parted[g * per : (g + 1) * per]
            keys[g, place_at : place_at + per, :] = lines[:, :head_dim]
            values[g, place_at : place_at + per, :] = lines[:, head_dim:]
        place_at += per

    span_keys = 2 * per
    t = lax.broadcasted_iota(jnp.int32, (group * new_len, new_len), 0) % new_len
    s = lax.broadcasted_iota(jnp.int32, (group * new_len, new_len), 1)
    causal = s <= t
    for g in range(kv_local):
        at = g * head_dim
        heads = []
        for j in range(group):
            to = (g * group + j) * head_dim
            total = q_own[:, to : to + head_dim] + q_other[:, to : to + head_dim].astype(jnp.float32)
            heads.append((rope(total) * query_scale).astype(jnp.bfloat16))
        queries = jnp.concatenate(heads, axis=0)
        new_key = rope(
            kv_own[:, at : at + head_dim] + kv_other[:, at : at + head_dim].astype(jnp.float32)
        ).astype(jnp.bfloat16)
        at += kv_local * head_dim
        new_value = (
            kv_own[:, at : at + head_dim] + kv_other[:, at : at + head_dim].astype(jnp.float32)
        ).astype(jnp.bfloat16)

        def scores_of(key):
            return lax.dot_general(
                queries, key, (((1,), (1,)), ((), ())), preferred_element_type=jnp.float32
            )

        weights = jnp.where(causal, capped(scores_of(new_key)), 0.0)
        denom = jnp.sum(weights, axis=1, keepdims=True)
        numer = jnp.dot(
            weights.astype(jnp.bfloat16), new_value, preferred_element_type=jnp.float32
        )
        for start in range(0, place_at, span_keys):
            at = start // per
            valid = jnp.concatenate([valid_ref[at : at + 1], valid_ref[at + 1 : at + 2]], axis=1)
            valid = valid > 0.0
            weights = jnp.where(
                valid, capped(scores_of(keys[g, start : start + span_keys, :])), 0.0
            )
            denom = denom + jnp.sum(weights, axis=1, keepdims=True)
            numer = numer + jnp.dot(
                weights.astype(jnp.bfloat16),
                values[g, start : start + span_keys, :],
                preferred_element_type=jnp.float32,
            )
        attended = (numer / denom).astype(jnp.bfloat16)
        for j in range(group):
            to = (g * group + j) * head_dim
            result[:, to : to + head_dim] = attended[j * new_len : (j + 1) * new_len]
    quarter = new_len // groups
    for distance, ref in enumerate(out_refs):
        start = pl.multiple_of((p ^ distance) * quarter, quarter)
        ref[...] = result[pl.ds(start, quarter), :]


def output_kernel(groups, shards, where_ref, *refs):
    p, f = where_ref[0], where_ref[1]
    token_refs = refs[:shards]
    weight_ref = refs[shards]
    out_refs = refs[shards + 1 : 2 * shards + 1]
    total = refs[2 * shards + 1]
    quarter = token_refs[0].shape[1]
    sub = quarter // shards
    projected = None
    for distance in range(groups):
        rows = jnp.concatenate([ref[distance] for ref in token_refs], axis=0)
        term = lax.dot_general(
            rows,
            weight_ref[p ^ distance],
            (((1,), (1,)), ((), ())),
            preferred_element_type=jnp.float32,
        )
        projected = term if projected is None else projected + term
    total[...] = projected
    for e in range(shards):
        for distance, ref in enumerate(out_refs):
            start = pl.multiple_of(e * quarter + (f ^ distance) * sub, sub)
            ref[f ^ e] = total[pl.ds(start, sub), :].astype(jnp.bfloat16)


def finish_kernel(shards, where_ref, gain_ref, residual_ref, *refs):
    f = where_ref[1]
    piece_refs = refs[:shards]
    out_ref, projected = refs[shards:]
    for distance, ref in enumerate(piece_refs):
        projected[f ^ distance] = ref[...].astype(jnp.float32)
    gain = gain_ref[...]
    for request in range(out_ref.shape[0]):
        slot = where_ref[3 + request]
        line = jnp.concatenate([projected[k, slot] for k in range(shards)], axis=1)
        mean_square = jnp.mean(line * line, axis=1, keepdims=True)
        line = line * lax.rsqrt(mean_square + norm_eps) * gain
        out_ref[request] = (residual_ref[slot].astype(jnp.float32) + line).astype(jnp.bfloat16)


def pool_pieces(block, groups):
    return [block] + [swap(block, "pool", distance) for distance in range(1, groups)]


def local_small(
    hidden,
    slot_of_request,
    prefix_len,
    block_holder,
    block_slot,
    kv_pool,
    norm_gain,
    q_weight,
    k_weight,
    v_weight,
    o_weight,
    post_gain,
):
    shards = lax.axis_size("fsdp")
    groups = lax.axis_size("pool")
    f = lax.axis_index("fsdp")
    p = lax.axis_index("pool")
    half = shards // 2
    side = f // half
    new_len, width = hidden.shape[1:]
    requests = slot_of_request.shape[0]
    page_len = kv_pool.shape[1]
    kv_local = kv_pool.shape[2]
    head_dim = kv_pool.shape[3] // 2
    q_cols = q_weight.shape[1]
    kv_cols = k_weight.shape[1]
    max_blocks = block_holder.shape[1]
    per_holder = max_blocks // shards
    quarter = new_len // groups
    sub = quarter // shards
    features = o_weight.shape[0]
    bf16, f32 = jnp.bfloat16, jnp.float32
    where = jnp.concatenate(
        [jnp.stack([p, f, side]).astype(jnp.int32), slot_of_request, prefix_len]
    )
    shape = jax.ShapeDtypeStruct
    any_place = pl.BlockSpec(memory_space=pl.ANY)
    gain = norm_gain.reshape(1, width)
    rows = hidden[0]

    leaving, my_quarter, kv_weight = call(
        prologue_kernel,
        [
            shape((quarter, width // 2), bf16),
            shape((quarter, width), bf16),
            shape((features, 2 * kv_cols), bf16),
        ],
        [pltpu.VMEM((quarter, width), f32), pltpu.SemaphoreType.DMA],
        quarter * width * 8,
        4 * features * kv_cols,
        where,
        rows,
        gain,
        k_weight,
        v_weight,
        specs=[SMEM, any_place, VMEM, VMEM, VMEM],
    )
    partner_piece = swap(leaving, "fsdp", half)

    q_far, q_near, kv_near = (
        swap(q_weight, "fsdp", 2),
        swap(q_weight, "fsdp", 1),
        swap(kv_weight, "fsdp", 1),
    )
    partner_piece, q_far, q_near, kv_near = lax.optimization_barrier(
        (partner_piece, q_far, q_near, kv_near)
    )
    kv_far = swap(after(kv_weight, partner_piece), "fsdp", 2)
    q_pieces = [q_weight, q_near, q_far, swap(q_far, "fsdp", 1)]
    kv_pieces = [kv_weight, kv_near, kv_far, swap(kv_far, "fsdp", 1)]

    flat_pool = kv_pool.reshape(kv_pool.shape[0], page_len * kv_local, 2 * head_dim)
    page_rows = per_holder * page_len * kv_local
    outgoing, valid = call(
        functools.partial(pages_kernel, requests, page_len),
        [
            shape((shards, page_rows, 2 * head_dim), bf16),
            shape((shards, per_holder * page_len), f32),
        ],
        [
            pltpu.SMEM((2 * per_holder,), jnp.int32),
            pltpu.SMEM((max_blocks + per_holder,), jnp.int32),
            pltpu.SMEM((shards,), jnp.int32),
        ],
        1 << 20,
        1 << 21,
        where,
        block_holder,
        block_slot,
        flat_pool,
        specs=[SMEM, SMEM, SMEM, VMEM],
    )
    partner_pieces = pool_pieces(partner_piece, groups)
    arrived = lax.all_to_all(
        after(outgoing, partner_piece), "fsdp", split_axis=0, concat_axis=0, tiled=True
    )
    out_weight = lax.all_gather(after(o_weight, partner_pieces[-1]), "pool", axis=0, tiled=False)

    partial = call(
        functools.partial(partner_kernel, half, groups),
        shape((new_len, q_cols + 2 * kv_cols), bf16),
        [
            pltpu.VMEM((new_len, width // 2), bf16),
            pltpu.VMEM((width // 2, q_cols), bf16),
            pltpu.VMEM((width // 2, 2 * kv_cols), bf16),
        ],
        new_len * width * (q_cols + 2 * kv_cols),
        width * (new_len + q_cols + 2 * kv_cols),
        where,
        *partner_pieces,
        *q_pieces,
        *kv_pieces,
    )
    other = swap(partial, "fsdp", half)
    freqs = np.exp(np.arange(head_dim // 2) * (-2.0 * math.log(10000.0) / head_dim))
    freqs = np.concatenate([freqs, freqs]).astype(np.float32).reshape(1, head_dim)
    q_own, kv_own, cosine, sine = call(
        functools.partial(own_kernel, half, requests),
        [
            shape((new_len, q_cols), f32),
            shape((new_len, 2 * kv_cols), f32),
            shape((new_len, head_dim), f32),
            shape((new_len, head_dim), f32),
        ],
        [
            pltpu.VMEM((width // 2, q_cols), bf16),
            pltpu.VMEM((width // 2, 2 * kv_cols), bf16),
            pltpu.VMEM((new_len, width // 2), bf16),
        ],
        new_len * width * (q_cols + 2 * kv_cols),
        width * (2 * new_len + q_cols + 2 * kv_cols),
        where,
        after(rows, partial),
        gain,
        freqs,
        *q_pieces,
        *kv_pieces,
    )

    residual = lax.all_to_all(
        after(my_quarter.reshape(shards, sub, width), arrived),
        "fsdp",
        split_axis=0,
        concat_axis=0,
        tiled=True,
    )

    keys_total = max_blocks * page_len
    quarters = call(
        functools.partial(attend_kernel, groups, kv_local, head_dim),
        [shape((quarter, q_cols), bf16)] * groups,
        [
            pltpu.VMEM((kv_local, keys_total, head_dim), bf16),
            pltpu.VMEM((kv_local, keys_total, head_dim), bf16),
            pltpu.VMEM((new_len, q_cols), bf16),
        ],
        4 * new_len * q_cols * (keys_total + new_len),
        1 << 22,
        where,
        q_own,
        kv_own,
        other,
        cosine,
        sine,
        valid,
        arrived,
    )

    quarters = [
        swap(piece, "pool", distance) if distance else piece
        for distance, piece in enumerate(quarters)
    ]
    quarters = jnp.stack(quarters)
    tokens = {0: quarters}
    for distance in range(2, shards, 2):
        tokens[distance] = swap(quarters, "fsdp", distance)
    for distance in range(0, shards, 2):
        tokens[distance ^ 1] = swap(tokens[distance], "fsdp", 1)
    projected = call(
        functools.partial(output_kernel, groups, shards),
        [shape((shards, sub, features), bf16)] * shards,
        [pltpu.VMEM((shards * quarter, features), f32)],
        2 * shards * quarter * features * groups * q_cols,
        1 << 22,
        where,
        *[tokens[distance] for distance in range(shards)],
        out_weight,
    )
    finished = [
        swap(piece, "fsdp", distance) if distance else piece
        for distance, piece in enumerate(projected)
    ]
    return call(
        functools.partial(finish_kernel, shards),
        shape((requests, sub, width), bf16),
        [pltpu.VMEM((shards, shards, sub, features), f32)],
        1 << 20,
        1 << 20,
        where,
        post_gain.reshape(1, width),
        residual,
        *finished,
    )


def local(*arguments):
    return local_small(*arguments) if lax.axis_size("fsdp") == 8 else local_general(*arguments)


def solution(mesh):
    in_specs = (
        P("fsdp", None, None),
        P(),
        P(),
        P(),
        P(),
        P("fsdp", None, "pool", None),
        P(),
        P("fsdp", "pool"),
        P("fsdp", "pool"),
        P("fsdp", "pool"),
        P("fsdp", "pool"),
        P(),
    )
    out_specs = P(None, ("pool", "fsdp"), None)
    return jax.shard_map(local, mesh=mesh, in_specs=in_specs, out_specs=out_specs, check_vma=False)
```

```python
import functools
import math

import jax
import jax.numpy as jnp
import numpy as np
from jax import lax
from jax.experimental import pallas as pl
from jax.experimental.pallas import tpu as pltpu
from jax.sharding import PartitionSpec as P

softcap = 50.0
query_scale = 144.0 ** (-0.5)
norm_eps = 1e-06


def rms_scale(rows, gain):
    mean_square = jnp.mean(rows * rows, axis=-1, keepdims=True)
    return rows * lax.rsqrt(mean_square + norm_eps) * gain


def rotate(vectors, cosine, sine):
    half = vectors.shape[-1] // 2
    first = vectors[..., :half]
    second = vectors[..., half:]
    return jnp.concatenate(
        [first * cosine - second * sine, second * cosine + first * sine], axis=-1
    )


def capped_weights(scores, valid):
    return jnp.where(valid, jnp.exp(softcap * jnp.tanh(scores / softcap)), 0.0)


def swap(array, axis, distance):
    size = lax.axis_size(axis)
    return lax.ppermute(array, axis, [(i, i ^ distance) for i in range(size)])


def place(pieces, index):
    first = pieces[0]
    stacked = jnp.zeros((len(pieces),) + first.shape, first.dtype)
    for distance, piece in pieces.items():
        stacked = lax.dynamic_update_index_in_dim(stacked, piece, index ^ distance, 0)
    return stacked


def exchange(chunks, axis):
    size = lax.axis_size(axis)
    index = lax.axis_index(axis)
    if size > 8:
        return lax.all_to_all(chunks, axis, split_axis=0, concat_axis=0, tiled=True)
    pieces = {}
    for distance in range(size):
        chunk = lax.dynamic_index_in_dim(chunks, index ^ distance, 0, keepdims=False)
        pieces[distance] = swap(chunk, axis, distance) if distance else chunk
    return place(pieces, index)


def doubled(block, axis, span):
    pieces = {0: block}
    bit = span // 2
    while bit:
        for distance in list(pieces):
            pieces[distance ^ bit] = swap(pieces[distance], axis, bit)
        bit //= 2
    return pieces


def attend(queries, keys_new, values_new, cached, cached_valid):
    new_len, kv_local, group, head_dim = queries.shape

    def part(keys, values, valid):
        scores = jnp.einsum("tgjd,kgd->gjtk", queries, keys, preferred_element_type=jnp.float32)
        weights = capped_weights(scores, valid)
        numer = jnp.einsum(
            "gjtk,kgd->gjtd",
            weights.astype(jnp.bfloat16),
            values,
            preferred_element_type=jnp.float32,
        )
        return numer, jnp.sum(weights, axis=-1)

    query_index = jnp.arange(new_len, dtype=jnp.int32)
    causal = query_index[None, :] <= query_index[:, None]
    numer, denom = part(
        cached[..., :head_dim], cached[..., head_dim:], cached_valid[None, None, None, :]
    )
    more, added = part(keys_new, values_new, causal[None, None])
    attended = ((numer + more) / (denom + added)[..., None]).transpose(2, 0, 1, 3)
    return attended.reshape(new_len, kv_local * group * head_dim).astype(jnp.bfloat16)


def local_general(
    hidden,
    slot_of_request,
    prefix_len,
    block_holder,
    block_slot,
    kv_pool,
    norm_gain,
    q_weight,
    k_weight,
    v_weight,
    o_weight,
    post_gain,
):
    shards = lax.axis_size("fsdp")
    groups = lax.axis_size("pool")
    f = lax.axis_index("fsdp")
    p = lax.axis_index("pool")
    half = shards // 2
    side = f // half
    new_len, width = hidden.shape[1:]
    requests = slot_of_request.shape[0]
    page_len = kv_pool.shape[1]
    kv_local = kv_pool.shape[2]
    head_dim = kv_pool.shape[3] // 2
    q_cols = q_weight.shape[1]
    kv_cols = k_weight.shape[1]
    group = q_cols // kv_cols
    max_blocks = block_holder.shape[1]
    per_holder = max_blocks // shards
    quarter = new_len // groups
    sub = quarter // shards
    features = o_weight.shape[0]

    kv_pieces = doubled(jnp.concatenate([k_weight, v_weight], axis=1), "fsdp", half)
    q_pieces = doubled(q_weight, "fsdp", half)
    out_weight = lax.all_gather(o_weight, "pool", axis=0, tiled=False)

    rows = hidden[0]
    normed = rms_scale(rows.astype(jnp.float32), norm_gain).astype(jnp.bfloat16)
    own_rows = lax.dynamic_slice(normed, (0, side * (width // 2)), (new_len, width // 2))
    leaving = lax.dynamic_slice(
        normed, (p * quarter, (1 - side) * (width // 2)), (quarter, width // 2)
    )
    partner_piece = swap(leaving, "fsdp", half)
    partner_pieces = {0: partner_piece}
    for distance in range(1, groups):
        partner_pieces[distance] = swap(partner_piece, "pool", distance)
    partner_rows = place(partner_pieces, p).reshape(new_len, width // 2)

    request_ids = jnp.arange(requests, dtype=jnp.int32)
    request_at_slot = jnp.sum(
        jnp.where(slot_of_request[None, :] == request_ids[:, None], request_ids[None, :], 0), axis=1
    )
    holder_by_slot = jnp.take(block_holder, request_at_slot, axis=0)
    page_by_slot = jnp.take(block_slot, request_at_slot, axis=0)
    held_here = holder_by_slot == f
    held_rank = jnp.cumsum(held_here.astype(jnp.int32), axis=1) - 1
    rank_ids = jnp.arange(per_holder, dtype=jnp.int32)
    picked = held_here[:, :, None] & (held_rank[:, :, None] == rank_ids[None, None, :])
    local_pages = jnp.sum(jnp.where(picked, page_by_slot[:, :, None], 0), axis=1)
    flat_pool = kv_pool.reshape(kv_pool.shape[0], page_len * kv_local, 2 * head_dim)
    outgoing = jnp.take(flat_pool, local_pages, axis=0)
    outgoing = outgoing.reshape(shards, per_holder * page_len * kv_local, 2 * head_dim)
    arrived = exchange(outgoing, "fsdp")
    cached = arrived.reshape(max_blocks * page_len, kv_local, 2 * head_dim)

    my_request = lax.dynamic_index_in_dim(request_at_slot, f, keepdims=False)
    my_length = prefix_len[my_request]
    my_holders = block_holder[my_request]
    entry_ids = jnp.arange(max_blocks, dtype=jnp.int32)
    mine = my_holders[None, :] == jnp.arange(shards, dtype=jnp.int32)[:, None]
    my_rank = jnp.cumsum(mine.astype(jnp.int32), axis=1) - 1
    chosen = mine[:, None, :] & (my_rank[:, None, :] == rank_ids[None, :, None])
    entry = jnp.sum(jnp.where(chosen, entry_ids[None, None, :], 0), axis=2)
    cached_position = entry.reshape(-1, 1) * page_len + jnp.arange(page_len, dtype=jnp.int32)
    cached_valid = (cached_position < my_length).reshape(-1)

    residual_out = lax.dynamic_slice_in_dim(rows, p * quarter, quarter, 0).reshape(
        shards, sub, width
    )
    residual = exchange(residual_out, "fsdp")

    positions = (my_length + jnp.arange(new_len, dtype=jnp.int32)).astype(jnp.float32)
    freqs = jnp.exp(
        jnp.arange(head_dim // 2, dtype=jnp.float32) * (-2.0 * math.log(10000.0) / head_dim)
    )
    angles = positions[:, None] * freqs
    cosine = jnp.cos(angles)[:, None, :]
    sine = jnp.sin(angles)[:, None, :]

    def project(pieces):
        weight = place(pieces, f % half).reshape(width // 2, -1)
        partial = jnp.dot(partner_rows, weight, preferred_element_type=jnp.float32)
        other = swap(partial.astype(jnp.bfloat16), "fsdp", half)
        own = jnp.dot(own_rows, weight, preferred_element_type=jnp.float32)
        return own + other.astype(jnp.float32)

    kv_sum = project(kv_pieces)
    q_sum = project(q_pieces)
    queries = rotate(q_sum.reshape(new_len, kv_local * group, head_dim), cosine, sine)
    queries = (queries * query_scale).astype(jnp.bfloat16)
    queries = queries.reshape(new_len, kv_local, group, head_dim)
    keys_new = kv_sum[:, :kv_cols].reshape(new_len, kv_local, head_dim)
    keys_new = rotate(keys_new, cosine, sine).astype(jnp.bfloat16)
    values_new = kv_sum[:, kv_cols:].astype(jnp.bfloat16).reshape(new_len, kv_local, head_dim)
    attended = attend(queries, keys_new, values_new, cached, cached_valid)

    quarters = exchange(attended.reshape(groups, quarter, q_cols), "pool")
    token_pieces = {0: quarters}
    for distance in range(2, shards, 2):
        token_pieces[distance] = swap(quarters, "fsdp", distance)
    for distance in range(0, shards, 2):
        token_pieces[distance ^ 1] = swap(token_pieces[distance], "fsdp", 1)
    tokens = place(token_pieces, f)
    projected = jnp.einsum(
        "sptc,pfc->stf", tokens, out_weight, preferred_element_type=jnp.float32
    ).astype(jnp.bfloat16)
    projected = projected.reshape(shards, shards, sub, features).transpose(1, 0, 2, 3)
    finished = exchange(projected, "fsdp").transpose(1, 2, 0, 3).reshape(shards, sub, width)
    finished = residual.astype(jnp.float32) + rms_scale(finished.astype(jnp.float32), post_gain)
    return jnp.take(finished.astype(jnp.bfloat16), slot_of_request, axis=0)


VMEM = pl.BlockSpec(memory_space=pltpu.VMEM)
SMEM = pl.BlockSpec(memory_space=pltpu.SMEM)


def call(kernel, outs, scratch, flops, nbytes, *operands, specs=None):
    return pl.pallas_call(
        kernel,
        out_shape=outs,
        in_specs=specs or [SMEM] + [VMEM] * (len(operands) - 1),
        out_specs=jax.tree.map(lambda _: VMEM, outs),
        scratch_shapes=scratch,
        compiler_params=pltpu.CompilerParams(vmem_limit_bytes=48 << 20),
        cost_estimate=pl.CostEstimate(flops=flops, bytes_accessed=nbytes, transcendentals=0),
    )(*operands)


def after(array, *earlier):
    return lax.optimization_barrier((array,) + earlier)[0]


def partner_kernel(groups, where_ref, weight_ref, *refs):
    p = where_ref[0]
    x_refs = refs[:groups]
    out_ref, rows = refs[groups:]
    quarter = x_refs[0].shape[0]
    for distance, ref in enumerate(x_refs):
        start = pl.multiple_of((p ^ distance) * quarter, quarter)
        rows[pl.ds(start, quarter), :] = ref[...]
    for at in range(0, out_ref.shape[1], 512):
        out_ref[:, at : at + 512] = jnp.dot(
            rows[...], weight_ref[:, at : at + 512], preferred_element_type=jnp.float32
        ).astype(jnp.bfloat16)


def row_scale(rows):
    return lax.rsqrt(jnp.mean(rows * rows, axis=1, keepdims=True) + norm_eps)


def prologue_kernel(
    where_ref, hidden_ref, gain_ref, q_ref, k_ref, v_ref, leaving_ref, rows_ref, weight_ref, normed, sem
):
    p, f = where_ref[0], where_ref[1]
    quarter, width = rows_ref.shape
    half_width = width // 2
    start = pl.multiple_of(p * quarter, quarter)
    copy = pltpu.make_async_copy(hidden_ref.at[pl.ds(start, quarter), :], rows_ref, sem)
    copy.start()
    at = 0
    for ref in (q_ref, k_ref, v_ref):
        weight_ref[:, at : at + ref.shape[1]] = ref[...]
        at += ref.shape[1]
    copy.wait()
    rows = rows_ref[...].astype(jnp.float32)
    normed[...] = rows * row_scale(rows) * gain_ref[...]
    away = pl.multiple_of((1 - where_ref[2]) * half_width, 128)
    leaving_ref[...] = normed[:, pl.ds(away, half_width)].astype(jnp.bfloat16)


def pages_kernel(
    requests, page_len, where_ref, holder_ref, slot_ref, pool_ref, out_ref, valid_ref, listed, entries, counts
):
    f = where_ref[1]
    max_blocks = holder_ref.shape[1]
    shards, _, _ = out_ref.shape
    per = max_blocks // shards
    page_rows = pool_ref.shape[1]
    length, mine = jnp.int32(0), jnp.int32(0)
    for r in range(requests):
        at = where_ref[3 + r] == f
        length = length + jnp.where(at, where_ref[3 + requests + r], 0)
        mine = mine + jnp.where(at, r, 0)
    for r in range(requests):
        slot = where_ref[3 + r]

        def note(j, count):
            listed[count] = slot_ref[r, j]
            return count + jnp.where(holder_ref[r, j] == f, 1, 0)

        lax.fori_loop(0, max_blocks, note, jnp.int32(0), unroll=8)
        for k in range(per):
            out_ref[slot, k * page_rows : (k + 1) * page_rows, :] = pool_ref[listed[k]]
    for h in range(shards):
        counts[h] = 0

    def enter(j, carry):
        h = holder_ref[mine, j]
        count = counts[h]
        entries[h * per + count] = j
        counts[h] = count + 1
        return carry

    lax.fori_loop(0, max_blocks, enter, 0, unroll=4)
    row = lax.broadcasted_iota(jnp.int32, valid_ref.shape, 0)
    lane = lax.broadcasted_iota(jnp.int32, valid_ref.shape, 1)
    place_in = row * per + lane // page_len
    entry = jnp.zeros(valid_ref.shape, jnp.int32)
    for at in range(max_blocks):
        entry = jnp.where(place_in == at, entries[at], entry)
    position = entry * page_len + lane % page_len
    valid_ref[...] = jnp.where(position < length, 1.0, 0.0)


def own_kernel(
    requests, where_ref, hidden_ref, gain_ref, freq_ref, weight_ref, own_ref, cos_ref, sin_ref, normed
):
    f = where_ref[1]
    new_len, width = hidden_ref.shape
    half_width = width // 2
    length = jnp.int32(0)
    for r in range(requests):
        length = length + jnp.where(where_ref[3 + r] == f, where_ref[3 + requests + r], 0)
    start = pl.multiple_of(where_ref[2] * half_width, 128)
    gain = gain_ref[:, pl.ds(start, half_width)]
    step = 32

    def norm(index, carry):
        at = pl.multiple_of(index * step, step)
        rows = hidden_ref[pl.ds(at, step), :].astype(jnp.float32)
        scale = row_scale(rows)
        part = hidden_ref[pl.ds(at, step), pl.ds(start, half_width)].astype(jnp.float32)
        normed[pl.ds(at, step), :] = (part * scale * gain).astype(jnp.bfloat16)
        return carry

    lax.fori_loop(0, new_len // step, norm, 0)
    position = lax.broadcasted_iota(jnp.int32, cos_ref.shape, 0) + length
    angle = position.astype(jnp.float32) * freq_ref[...]
    lane = lax.broadcasted_iota(jnp.int32, cos_ref.shape, 1)
    cos_ref[...] = jnp.cos(angle)
    sine = jnp.sin(angle)
    sin_ref[...] = jnp.where(lane < cos_ref.shape[1] // 2, -sine, sine)
    for at in range(0, own_ref.shape[1], 512):
        own_ref[:, at : at + 512] = jnp.dot(
            normed[...], weight_ref[:, at : at + 512], preferred_element_type=jnp.float32
        )


def capped(scores):
    return jnp.exp2(jnp.tanh(scores * (1.0 / softcap)) * (softcap * math.log2(math.e)))


def attend_kernel(
    groups,
    kv_local,
    head_dim,
    where_ref,
    own,
    other,
    cos_ref,
    sin_ref,
    valid_ref,
    page_ref,
    *refs,
):
    p = where_ref[0]
    out_refs = refs[:groups]
    keys, values, result = refs[groups:]
    new_len, q_cols = result.shape
    group = q_cols // (kv_local * head_dim)

    def sums(at):
        return own[:, at : at + head_dim] + other[:, at : at + head_dim].astype(jnp.float32)

    cosine, sine = cos_ref[...], sin_ref[...]

    def rope(vectors):
        return vectors * cosine + pltpu.roll(vectors, head_dim // 2, 1) * sine

    span = page_ref.shape[1]
    per = span // kv_local
    row = lax.broadcasted_iota(jnp.int32, (span, span), 0)
    column = lax.broadcasted_iota(jnp.int32, (span, span), 1)
    part = (column == (row % per) * kv_local + row // per).astype(jnp.bfloat16)
    place_at = 0
    for holder in range(page_ref.shape[0]):
        parted = jnp.dot(part, page_ref[holder], preferred_element_type=jnp.float32)
        parted = parted.astype(jnp.bfloat16)
        for g in range(kv_local):
            lines = parted[g * per : (g + 1) * per]
            keys[g, place_at : place_at + per, :] = lines[:, :head_dim]
            values[g, place_at : place_at + per, :] = lines[:, head_dim:]
        place_at += per

    span_keys = 2 * per
    t = lax.broadcasted_iota(jnp.int32, (group * new_len, new_len), 0) % new_len
    s = lax.broadcasted_iota(jnp.int32, (group * new_len, new_len), 1)
    causal = s <= t
    for g in range(kv_local):
        heads = [
            (rope(sums((g * group + j) * head_dim)) * query_scale).astype(jnp.bfloat16)
            for j in range(group)
        ]
        queries = jnp.concatenate(heads, axis=0)
        at = q_cols + g * head_dim
        new_key = rope(sums(at)).astype(jnp.bfloat16)
        new_value = sums(at + kv_local * head_dim).astype(jnp.bfloat16)

        def scores_of(key):
            return lax.dot_general(
                queries, key, (((1,), (1,)), ((), ())), preferred_element_type=jnp.float32
            )

        weights = jnp.where(causal, capped(scores_of(new_key)), 0.0)
        denom = jnp.sum(weights, axis=1, keepdims=True)
        numer = jnp.dot(
            weights.astype(jnp.bfloat16), new_value, preferred_element_type=jnp.float32
        )
        for start in range(0, place_at, span_keys):
            at = start // per
            valid = jnp.concatenate([valid_ref[at : at + 1], valid_ref[at + 1 : at + 2]], axis=1)
            valid = valid > 0.0
            weights = jnp.where(
                valid, capped(scores_of(keys[g, start : start + span_keys, :])), 0.0
            )
            denom = denom + jnp.sum(weights, axis=1, keepdims=True)
            numer = numer + jnp.dot(
                weights.astype(jnp.bfloat16),
                values[g, start : start + span_keys, :],
                preferred_element_type=jnp.float32,
            )
        attended = (numer / denom).astype(jnp.bfloat16)
        for j in range(group):
            to = (g * group + j) * head_dim
            result[:, to : to + head_dim] = attended[j * new_len : (j + 1) * new_len]
    quarter = new_len // groups
    for distance, ref in enumerate(out_refs):
        start = pl.multiple_of((p ^ distance) * quarter, quarter)
        ref[...] = result[pl.ds(start, quarter), :]


def output_kernel(groups, shards, where_ref, *refs):
    p, f = where_ref[0], where_ref[1]
    token_refs = refs[:shards]
    weight_ref = refs[shards]
    out_refs = refs[shards + 1 : 2 * shards + 1]
    total = refs[2 * shards + 1]
    quarter = token_refs[0].shape[1]
    sub = quarter // shards
    projected = None
    for distance in range(groups):
        rows = jnp.concatenate([ref[distance] for ref in token_refs], axis=0)
        term = lax.dot_general(
            rows,
            weight_ref[p ^ distance],
            (((1,), (1,)), ((), ())),
            preferred_element_type=jnp.float32,
        )
        projected = term if projected is None else projected + term
    total[...] = projected
    for e in range(shards):
        for distance, ref in enumerate(out_refs):
            start = pl.multiple_of(e * quarter + (f ^ distance) * sub, sub)
            ref[f ^ e] = total[pl.ds(start, sub), :].astype(jnp.bfloat16)


def finish_kernel(shards, where_ref, gain_ref, residual_ref, *refs):
    f = where_ref[1]
    piece_refs = refs[:shards]
    out_ref, projected = refs[shards:]
    for distance, ref in enumerate(piece_refs):
        projected[f ^ distance] = ref[...].astype(jnp.float32)
    gain = gain_ref[...]
    for request in range(out_ref.shape[0]):
        slot = where_ref[3 + request]
        line = jnp.concatenate([projected[k, slot] for k in range(shards)], axis=1)
        mean_square = jnp.mean(line * line, axis=1, keepdims=True)
        line = line * lax.rsqrt(mean_square + norm_eps) * gain
        out_ref[request] = (residual_ref[slot].astype(jnp.float32) + line).astype(jnp.bfloat16)


def pool_pieces(block, groups):
    return [block] + [swap(block, "pool", distance) for distance in range(1, groups)]


def local_small(
    hidden,
    slot_of_request,
    prefix_len,
    block_holder,
    block_slot,
    kv_pool,
    norm_gain,
    q_weight,
    k_weight,
    v_weight,
    o_weight,
    post_gain,
):
    shards = lax.axis_size("fsdp")
    groups = lax.axis_size("pool")
    f = lax.axis_index("fsdp")
    p = lax.axis_index("pool")
    half = shards // 2
    side = f // half
    new_len, width = hidden.shape[1:]
    requests = slot_of_request.shape[0]
    page_len = kv_pool.shape[1]
    kv_local = kv_pool.shape[2]
    head_dim = kv_pool.shape[3] // 2
    q_cols = q_weight.shape[1]
    kv_cols = k_weight.shape[1]
    max_blocks = block_holder.shape[1]
    per_holder = max_blocks // shards
    quarter = new_len // groups
    sub = quarter // shards
    features = o_weight.shape[0]
    bf16, f32 = jnp.bfloat16, jnp.float32
    where = jnp.concatenate(
        [jnp.stack([p, f, side]).astype(jnp.int32), slot_of_request, prefix_len]
    )
    shape = jax.ShapeDtypeStruct
    any_place = pl.BlockSpec(memory_space=pl.ANY)
    gain = norm_gain.reshape(1, width)
    rows = hidden[0]

    leaving, my_quarter, joined = call(
        prologue_kernel,
        [
            shape((quarter, width // 2), bf16),
            shape((quarter, width), bf16),
            shape((features, q_cols + 2 * kv_cols), bf16),
        ],
        [pltpu.VMEM((quarter, width), f32), pltpu.SemaphoreType.DMA],
        quarter * width * 8,
        4 * features * kv_cols,
        where,
        rows,
        gain,
        q_weight,
        k_weight,
        v_weight,
        specs=[SMEM, any_place, VMEM, VMEM, VMEM, VMEM],
    )
    partner_piece = swap(leaving, "fsdp", half)

    halves = [list(range(start, start + half)) for start in range(0, shards, half)]
    weight = lax.all_gather(joined, "fsdp", axis=0, tiled=True, axis_index_groups=halves)

    flat_pool = kv_pool.reshape(kv_pool.shape[0], page_len * kv_local, 2 * head_dim)
    page_rows = per_holder * page_len * kv_local
    outgoing, valid = call(
        functools.partial(pages_kernel, requests, page_len),
        [
            shape((shards, page_rows, 2 * head_dim), bf16),
            shape((shards, per_holder * page_len), f32),
        ],
        [
            pltpu.SMEM((2 * per_holder,), jnp.int32),
            pltpu.SMEM((max_blocks + per_holder,), jnp.int32),
            pltpu.SMEM((shards,), jnp.int32),
        ],
        1 << 20,
        1 << 21,
        where,
        block_holder,
        block_slot,
        flat_pool,
        specs=[SMEM, SMEM, SMEM, VMEM],
    )
    partner_pieces = pool_pieces(partner_piece, groups)
    arrived = lax.all_to_all(
        after(outgoing, partner_piece), "fsdp", split_axis=0, concat_axis=0, tiled=True
    )
    out_weight = lax.all_gather(after(o_weight, partner_pieces[-1]), "pool", axis=0, tiled=False)

    partial = call(
        functools.partial(partner_kernel, groups),
        shape((new_len, q_cols + 2 * kv_cols), bf16),
        [pltpu.VMEM((new_len, width // 2), bf16)],
        new_len * width * (q_cols + 2 * kv_cols),
        width * (new_len + q_cols + 2 * kv_cols),
        where,
        weight,
        *partner_pieces,
    )
    other = swap(partial, "fsdp", half)
    freqs = np.exp(np.arange(head_dim // 2) * (-2.0 * math.log(10000.0) / head_dim))
    freqs = np.concatenate([freqs, freqs]).astype(np.float32).reshape(1, head_dim)
    own, cosine, sine = call(
        functools.partial(own_kernel, requests),
        [
            shape((new_len, q_cols + 2 * kv_cols), f32),
            shape((new_len, head_dim), f32),
            shape((new_len, head_dim), f32),
        ],
        [pltpu.VMEM((new_len, width // 2), bf16)],
        new_len * width * (q_cols + 2 * kv_cols),
        width * (2 * new_len + q_cols + 2 * kv_cols),
        where,
        after(rows, partial),
        gain,
        freqs,
        weight,
    )

    residual = lax.all_to_all(
        after(my_quarter.reshape(shards, sub, width), arrived),
        "fsdp",
        split_axis=0,
        concat_axis=0,
        tiled=True,
    )

    keys_total = max_blocks * page_len
    quarters = call(
        functools.partial(attend_kernel, groups, kv_local, head_dim),
        [shape((quarter, q_cols), bf16)] * groups,
        [
            pltpu.VMEM((kv_local, keys_total, head_dim), bf16),
            pltpu.VMEM((kv_local, keys_total, head_dim), bf16),
            pltpu.VMEM((new_len, q_cols), bf16),
        ],
        4 * new_len * q_cols * (keys_total + new_len),
        1 << 22,
        where,
        own,
        other,
        cosine,
        sine,
        valid,
        arrived,
    )

    quarters = [
        swap(piece, "pool", distance) if distance else piece
        for distance, piece in enumerate(quarters)
    ]
    quarters = jnp.stack(quarters)
    tokens = {0: quarters}
    for distance in range(2, shards, 2):
        tokens[distance] = swap(quarters, "fsdp", distance)
    for distance in range(0, shards, 2):
        tokens[distance ^ 1] = swap(tokens[distance], "fsdp", 1)
    projected = call(
        functools.partial(output_kernel, groups, shards),
        [shape((shards, sub, features), bf16)] * shards,
        [pltpu.VMEM((shards * quarter, features), f32)],
        2 * shards * quarter * features * groups * q_cols,
        1 << 22,
        where,
        *[tokens[distance] for distance in range(shards)],
        out_weight,
    )
    finished = [
        swap(piece, "fsdp", distance) if distance else piece
        for distance, piece in enumerate(projected)
    ]
    return call(
        functools.partial(finish_kernel, shards),
        shape((requests, sub, width), bf16),
        [pltpu.VMEM((shards, shards, sub, features), f32)],
        1 << 20,
        1 << 20,
        where,
        post_gain.reshape(1, width),
        residual,
        *finished,
    )


def local(*arguments):
    return local_small(*arguments) if lax.axis_size("fsdp") == 8 else local_general(*arguments)


def solution(mesh):
    in_specs = (
        P("fsdp", None, None),
        P(),
        P(),
        P(),
        P(),
        P("fsdp", None, "pool", None),
        P(),
        P("fsdp", "pool"),
        P("fsdp", "pool"),
        P("fsdp", "pool"),
        P("fsdp", "pool"),
        P(),
    )
    out_specs = P(None, ("pool", "fsdp"), None)
    return jax.shard_map(local, mesh=mesh, in_specs=in_specs, out_specs=out_specs, check_vma=False)
```

```python
import functools
import math

import jax
import jax.numpy as jnp
import numpy as np
from jax import lax
from jax.experimental import pallas as pl
from jax.experimental.pallas import tpu as pltpu
from jax.sharding import PartitionSpec as P

softcap = 50.0
query_scale = 144.0 ** (-0.5)
norm_eps = 1e-06


def rms_scale(rows, gain):
    mean_square = jnp.mean(rows * rows, axis=-1, keepdims=True)
    return rows * lax.rsqrt(mean_square + norm_eps) * gain


def rotate(vectors, cosine, sine):
    half = vectors.shape[-1] // 2
    first = vectors[..., :half]
    second = vectors[..., half:]
    return jnp.concatenate(
        [first * cosine - second * sine, second * cosine + first * sine], axis=-1
    )


def capped_weights(scores, valid):
    return jnp.where(valid, jnp.exp(softcap * jnp.tanh(scores / softcap)), 0.0)


def swap(array, axis, distance):
    size = lax.axis_size(axis)
    return lax.ppermute(array, axis, [(i, i ^ distance) for i in range(size)])


def place(pieces, index):
    first = pieces[0]
    stacked = jnp.zeros((len(pieces),) + first.shape, first.dtype)
    for distance, piece in pieces.items():
        stacked = lax.dynamic_update_index_in_dim(stacked, piece, index ^ distance, 0)
    return stacked


def exchange(chunks, axis):
    size = lax.axis_size(axis)
    index = lax.axis_index(axis)
    if size > 8:
        return lax.all_to_all(chunks, axis, split_axis=0, concat_axis=0, tiled=True)
    pieces = {}
    for distance in range(size):
        chunk = lax.dynamic_index_in_dim(chunks, index ^ distance, 0, keepdims=False)
        pieces[distance] = swap(chunk, axis, distance) if distance else chunk
    return place(pieces, index)


def doubled(block, axis, span):
    pieces = {0: block}
    bit = span // 2
    while bit:
        for distance in list(pieces):
            pieces[distance ^ bit] = swap(pieces[distance], axis, bit)
        bit //= 2
    return pieces


def attend(queries, keys_new, values_new, cached, cached_valid):
    new_len, kv_local, group, head_dim = queries.shape

    def part(keys, values, valid):
        scores = jnp.einsum("tgjd,kgd->gjtk", queries, keys, preferred_element_type=jnp.float32)
        weights = capped_weights(scores, valid)
        numer = jnp.einsum(
            "gjtk,kgd->gjtd",
            weights.astype(jnp.bfloat16),
            values,
            preferred_element_type=jnp.float32,
        )
        return numer, jnp.sum(weights, axis=-1)

    query_index = jnp.arange(new_len, dtype=jnp.int32)
    causal = query_index[None, :] <= query_index[:, None]
    numer, denom = part(
        cached[..., :head_dim], cached[..., head_dim:], cached_valid[None, None, None, :]
    )
    more, added = part(keys_new, values_new, causal[None, None])
    attended = ((numer + more) / (denom + added)[..., None]).transpose(2, 0, 1, 3)
    return attended.reshape(new_len, kv_local * group * head_dim).astype(jnp.bfloat16)


def local_general(
    hidden,
    slot_of_request,
    prefix_len,
    block_holder,
    block_slot,
    kv_pool,
    norm_gain,
    q_weight,
    k_weight,
    v_weight,
    o_weight,
    post_gain,
):
    shards = lax.axis_size("fsdp")
    groups = lax.axis_size("pool")
    f = lax.axis_index("fsdp")
    p = lax.axis_index("pool")
    half = shards // 2
    side = f // half
    new_len, width = hidden.shape[1:]
    requests = slot_of_request.shape[0]
    page_len = kv_pool.shape[1]
    kv_local = kv_pool.shape[2]
    head_dim = kv_pool.shape[3] // 2
    q_cols = q_weight.shape[1]
    kv_cols = k_weight.shape[1]
    group = q_cols // kv_cols
    max_blocks = block_holder.shape[1]
    per_holder = max_blocks // shards
    quarter = new_len // groups
    sub = quarter // shards
    features = o_weight.shape[0]

    kv_pieces = doubled(jnp.concatenate([k_weight, v_weight], axis=1), "fsdp", half)
    q_pieces = doubled(q_weight, "fsdp", half)
    out_weight = lax.all_gather(o_weight, "pool", axis=0, tiled=False)

    rows = hidden[0]
    normed = rms_scale(rows.astype(jnp.float32), norm_gain).astype(jnp.bfloat16)
    own_rows = lax.dynamic_slice(normed, (0, side * (width // 2)), (new_len, width // 2))
    leaving = lax.dynamic_slice(
        normed, (p * quarter, (1 - side) * (width // 2)), (quarter, width // 2)
    )
    partner_piece = swap(leaving, "fsdp", half)
    partner_pieces = {0: partner_piece}
    for distance in range(1, groups):
        partner_pieces[distance] = swap(partner_piece, "pool", distance)
    partner_rows = place(partner_pieces, p).reshape(new_len, width // 2)

    request_ids = jnp.arange(requests, dtype=jnp.int32)
    request_at_slot = jnp.sum(
        jnp.where(slot_of_request[None, :] == request_ids[:, None], request_ids[None, :], 0), axis=1
    )
    holder_by_slot = jnp.take(block_holder, request_at_slot, axis=0)
    page_by_slot = jnp.take(block_slot, request_at_slot, axis=0)
    held_here = holder_by_slot == f
    held_rank = jnp.cumsum(held_here.astype(jnp.int32), axis=1) - 1
    rank_ids = jnp.arange(per_holder, dtype=jnp.int32)
    picked = held_here[:, :, None] & (held_rank[:, :, None] == rank_ids[None, None, :])
    local_pages = jnp.sum(jnp.where(picked, page_by_slot[:, :, None], 0), axis=1)
    flat_pool = kv_pool.reshape(kv_pool.shape[0], page_len * kv_local, 2 * head_dim)
    outgoing = jnp.take(flat_pool, local_pages, axis=0)
    outgoing = outgoing.reshape(shards, per_holder * page_len * kv_local, 2 * head_dim)
    arrived = exchange(outgoing, "fsdp")
    cached = arrived.reshape(max_blocks * page_len, kv_local, 2 * head_dim)

    my_request = lax.dynamic_index_in_dim(request_at_slot, f, keepdims=False)
    my_length = prefix_len[my_request]
    my_holders = block_holder[my_request]
    entry_ids = jnp.arange(max_blocks, dtype=jnp.int32)
    mine = my_holders[None, :] == jnp.arange(shards, dtype=jnp.int32)[:, None]
    my_rank = jnp.cumsum(mine.astype(jnp.int32), axis=1) - 1
    chosen = mine[:, None, :] & (my_rank[:, None, :] == rank_ids[None, :, None])
    entry = jnp.sum(jnp.where(chosen, entry_ids[None, None, :], 0), axis=2)
    cached_position = entry.reshape(-1, 1) * page_len + jnp.arange(page_len, dtype=jnp.int32)
    cached_valid = (cached_position < my_length).reshape(-1)

    residual_out = lax.dynamic_slice_in_dim(rows, p * quarter, quarter, 0).reshape(
        shards, sub, width
    )
    residual = exchange(residual_out, "fsdp")

    positions = (my_length + jnp.arange(new_len, dtype=jnp.int32)).astype(jnp.float32)
    freqs = jnp.exp(
        jnp.arange(head_dim // 2, dtype=jnp.float32) * (-2.0 * math.log(10000.0) / head_dim)
    )
    angles = positions[:, None] * freqs
    cosine = jnp.cos(angles)[:, None, :]
    sine = jnp.sin(angles)[:, None, :]

    def project(pieces):
        weight = place(pieces, f % half).reshape(width // 2, -1)
        partial = jnp.dot(partner_rows, weight, preferred_element_type=jnp.float32)
        other = swap(partial.astype(jnp.bfloat16), "fsdp", half)
        own = jnp.dot(own_rows, weight, preferred_element_type=jnp.float32)
        return own + other.astype(jnp.float32)

    kv_sum = project(kv_pieces)
    q_sum = project(q_pieces)
    queries = rotate(q_sum.reshape(new_len, kv_local * group, head_dim), cosine, sine)
    queries = (queries * query_scale).astype(jnp.bfloat16)
    queries = queries.reshape(new_len, kv_local, group, head_dim)
    keys_new = kv_sum[:, :kv_cols].reshape(new_len, kv_local, head_dim)
    keys_new = rotate(keys_new, cosine, sine).astype(jnp.bfloat16)
    values_new = kv_sum[:, kv_cols:].astype(jnp.bfloat16).reshape(new_len, kv_local, head_dim)
    attended = attend(queries, keys_new, values_new, cached, cached_valid)

    quarters = exchange(attended.reshape(groups, quarter, q_cols), "pool")
    token_pieces = {0: quarters}
    for distance in range(2, shards, 2):
        token_pieces[distance] = swap(quarters, "fsdp", distance)
    for distance in range(0, shards, 2):
        token_pieces[distance ^ 1] = swap(token_pieces[distance], "fsdp", 1)
    tokens = place(token_pieces, f)
    projected = jnp.einsum(
        "sptc,pfc->stf", tokens, out_weight, preferred_element_type=jnp.float32
    ).astype(jnp.bfloat16)
    projected = projected.reshape(shards, shards, sub, features).transpose(1, 0, 2, 3)
    finished = exchange(projected, "fsdp").transpose(1, 2, 0, 3).reshape(shards, sub, width)
    finished = residual.astype(jnp.float32) + rms_scale(finished.astype(jnp.float32), post_gain)
    return jnp.take(finished.astype(jnp.bfloat16), slot_of_request, axis=0)


VMEM = pl.BlockSpec(memory_space=pltpu.VMEM)
SMEM = pl.BlockSpec(memory_space=pltpu.SMEM)


def call(kernel, outs, scratch, flops, nbytes, *operands, specs=None, out_specs=None):
    return pl.pallas_call(
        kernel,
        out_shape=outs,
        in_specs=specs or [SMEM] + [VMEM] * (len(operands) - 1),
        out_specs=out_specs or jax.tree.map(lambda _: VMEM, outs),
        scratch_shapes=scratch,
        compiler_params=pltpu.CompilerParams(vmem_limit_bytes=48 << 20),
        cost_estimate=pl.CostEstimate(flops=flops, bytes_accessed=nbytes, transcendentals=0),
    )(*operands)


def after(array, *earlier):
    return lax.optimization_barrier((array,) + earlier)[0]


def weight_copies(weight_refs, weight, f, half, sems):
    copies = []
    for distance, ref in enumerate(weight_refs):
        count = ref.shape[0]
        start = pl.multiple_of(((f ^ distance) & (half - 1)) * count, 64)
        copies.append(
            pltpu.make_async_copy(ref, weight.at[pl.ds(start, count), :], sems.at[distance])
        )
        copies[-1].start()
    return copies


def partner_kernel(groups, half, where_ref, *refs):
    p, f = where_ref[0], where_ref[1]
    x_refs, w_refs = refs[:groups], refs[groups : groups + half]
    out_ref, rows, weight, x_sems, w_sems = refs[groups + half :]
    quarter = x_refs[0].shape[0]
    copies = weight_copies(w_refs, weight, f, half, w_sems)
    for distance, ref in enumerate(x_refs):
        start = pl.multiple_of((p ^ distance) * quarter, quarter)
        copies.append(
            pltpu.make_async_copy(ref, rows.at[pl.ds(start, quarter), :], x_sems.at[distance])
        )
        copies[-1].start()
    for copy in copies:
        copy.wait()
    for at in range(0, out_ref.shape[1], 512):
        out_ref[:, at : at + 512] = jnp.dot(
            rows[...], weight[:, at : at + 512], preferred_element_type=jnp.float32
        ).astype(jnp.bfloat16)


def row_scale(rows):
    return lax.rsqrt(jnp.mean(rows * rows, axis=1, keepdims=True) + norm_eps)


def prologue_kernel(
    hidden_ref, gain_ref, q_ref, k_ref, v_ref, leaving_ref, rows_ref, weight_ref, normed, sems
):
    p, f = lax.axis_index("pool"), lax.axis_index("fsdp")
    side = f // (lax.axis_size("fsdp") // 2)
    quarter, width = rows_ref.shape
    half_width = width // 2
    start = pl.multiple_of(p * quarter, quarter)
    rows_copy = pltpu.make_async_copy(hidden_ref.at[pl.ds(start, quarter), :], rows_ref, sems.at[0])
    rows_copy.start()
    copies = []
    at = 0
    for index, ref in enumerate((q_ref, k_ref, v_ref)):
        to = at + ref.shape[1]
        copies.append(pltpu.make_async_copy(ref, weight_ref.at[:, at:to], sems.at[1 + index]))
        copies[-1].start()
        at = to
    rows_copy.wait()
    rows = rows_ref[...].astype(jnp.float32)
    normed[...] = rows * row_scale(rows) * gain_ref[...]
    away = pl.multiple_of((1 - side) * half_width, 128)
    leaving_ref[...] = normed[:, pl.ds(away, half_width)].astype(jnp.bfloat16)
    for copy in copies:
        copy.wait()


def pages_kernel(
    requests, page_len, where_ref, holder_ref, slot_ref, pool_ref, out_ref, valid_ref, listed, entries, counts
):
    f = where_ref[1]
    max_blocks = holder_ref.shape[1]
    shards, _, _ = out_ref.shape
    per = max_blocks // shards
    page_rows = pool_ref.shape[1]
    length, mine = jnp.int32(0), jnp.int32(0)
    for r in range(requests):
        at = where_ref[3 + r] == f
        length = length + jnp.where(at, where_ref[3 + requests + r], 0)
        mine = mine + jnp.where(at, r, 0)
    for r in range(requests):
        slot = where_ref[3 + r]

        def note(j, count):
            listed[count] = slot_ref[r, j]
            return count + jnp.where(holder_ref[r, j] == f, 1, 0)

        lax.fori_loop(0, max_blocks, note, jnp.int32(0), unroll=8)
        for k in range(per):
            out_ref[slot, k * page_rows : (k + 1) * page_rows, :] = pool_ref[listed[k]]
    for h in range(shards):
        counts[h] = 0

    def enter(j, carry):
        h = holder_ref[mine, j]
        count = counts[h]
        entries[h * per + count] = j
        counts[h] = count + 1
        return carry

    lax.fori_loop(0, max_blocks, enter, 0, unroll=4)
    row = lax.broadcasted_iota(jnp.int32, valid_ref.shape, 0)
    lane = lax.broadcasted_iota(jnp.int32, valid_ref.shape, 1)
    place_in = row * per + lane // page_len
    entry = jnp.zeros(valid_ref.shape, jnp.int32)
    for at in range(max_blocks):
        entry = jnp.where(place_in == at, entries[at], entry)
    position = entry * page_len + lane % page_len
    valid_ref[...] = jnp.where(position < length, 1.0, 0.0)


def own_kernel(requests, half, where_ref, hidden_ref, gain_ref, freq_ref, *refs):
    f = where_ref[1]
    own_ref, cos_ref, sin_ref, normed, weight, sems = refs[half:]
    copies = weight_copies(refs[:half], weight, f, half, sems)
    new_len, width = hidden_ref.shape
    half_width = width // 2
    length = jnp.int32(0)
    for r in range(requests):
        length = length + jnp.where(where_ref[3 + r] == f, where_ref[3 + requests + r], 0)
    start = pl.multiple_of(where_ref[2] * half_width, 128)
    gain = gain_ref[:, pl.ds(start, half_width)]
    step = 32

    def norm(index, carry):
        at = pl.multiple_of(index * step, step)
        rows = hidden_ref[pl.ds(at, step), :].astype(jnp.float32)
        scale = row_scale(rows)
        part = hidden_ref[pl.ds(at, step), pl.ds(start, half_width)].astype(jnp.float32)
        normed[pl.ds(at, step), :] = (part * scale * gain).astype(jnp.bfloat16)
        return carry

    lax.fori_loop(0, new_len // step, norm, 0)
    position = lax.broadcasted_iota(jnp.int32, cos_ref.shape, 0) + length
    angle = position.astype(jnp.float32) * freq_ref[...]
    lane = lax.broadcasted_iota(jnp.int32, cos_ref.shape, 1)
    cos_ref[...] = jnp.cos(angle)
    sine = jnp.sin(angle)
    sin_ref[...] = jnp.where(lane < cos_ref.shape[1] // 2, -sine, sine)
    for copy in copies:
        copy.wait()
    for at in range(0, own_ref.shape[1], 512):
        own_ref[:, at : at + 512] = jnp.dot(
            normed[...], weight[:, at : at + 512], preferred_element_type=jnp.float32
        )


def capped(scores):
    return jnp.exp2(jnp.tanh(scores * (1.0 / softcap)) * (softcap * math.log2(math.e)))


def attend_kernel(
    groups,
    kv_local,
    head_dim,
    where_ref,
    own,
    other,
    cos_ref,
    sin_ref,
    valid_ref,
    page_ref,
    *refs,
):
    p = where_ref[0]
    out_refs = refs[:groups]
    keys, values, result = refs[groups:]
    new_len, q_cols = result.shape
    group = q_cols // (kv_local * head_dim)

    def sums(at):
        return own[:, at : at + head_dim] + other[:, at : at + head_dim].astype(jnp.float32)

    cosine, sine = cos_ref[...], sin_ref[...]

    def rope(vectors):
        return vectors * cosine + pltpu.roll(vectors, head_dim // 2, 1) * sine

    span = page_ref.shape[1]
    per = span // kv_local
    row = lax.broadcasted_iota(jnp.int32, (span, span), 0)
    column = lax.broadcasted_iota(jnp.int32, (span, span), 1)
    part = (column == (row % per) * kv_local + row // per).astype(jnp.bfloat16)
    place_at = 0
    for holder in range(page_ref.shape[0]):
        parted = jnp.dot(part, page_ref[holder], preferred_element_type=jnp.float32)
        parted = parted.astype(jnp.bfloat16)
        for g in range(kv_local):
            lines = parted[g * per : (g + 1) * per]
            keys[g, place_at : place_at + per, :] = lines[:, :head_dim]
            values[g, place_at : place_at + per, :] = lines[:, head_dim:]
        place_at += per

    span_keys = 2 * per
    t = lax.broadcasted_iota(jnp.int32, (group * new_len, new_len), 0) % new_len
    s = lax.broadcasted_iota(jnp.int32, (group * new_len, new_len), 1)
    causal = s <= t
    for g in range(kv_local):
        heads = [
            (rope(sums((g * group + j) * head_dim)) * query_scale).astype(jnp.bfloat16)
            for j in range(group)
        ]
        queries = jnp.concatenate(heads, axis=0)
        at = q_cols + g * head_dim
        new_key = rope(sums(at)).astype(jnp.bfloat16)
        new_value = sums(at + kv_local * head_dim).astype(jnp.bfloat16)

        def scores_of(key):
            return lax.dot_general(
                queries, key, (((1,), (1,)), ((), ())), preferred_element_type=jnp.float32
            )

        weights = jnp.where(causal, capped(scores_of(new_key)), 0.0)
        denom = jnp.sum(weights, axis=1, keepdims=True)
        numer = jnp.dot(
            weights.astype(jnp.bfloat16), new_value, preferred_element_type=jnp.float32
        )
        for start in range(0, place_at, span_keys):
            at = start // per
            valid = jnp.concatenate([valid_ref[at : at + 1], valid_ref[at + 1 : at + 2]], axis=1)
            valid = valid > 0.0
            weights = jnp.where(
                valid, capped(scores_of(keys[g, start : start + span_keys, :])), 0.0
            )
            denom = denom + jnp.sum(weights, axis=1, keepdims=True)
            numer = numer + jnp.dot(
                weights.astype(jnp.bfloat16),
                values[g, start : start + span_keys, :],
                preferred_element_type=jnp.float32,
            )
        attended = (numer / denom).astype(jnp.bfloat16)
        for j in range(group):
            to = (g * group + j) * head_dim
            result[:, to : to + head_dim] = attended[j * new_len : (j + 1) * new_len]
    quarter = new_len // groups
    for distance, ref in enumerate(out_refs):
        start = pl.multiple_of((p ^ distance) * quarter, quarter)
        ref[...] = result[pl.ds(start, quarter), :]


def output_kernel(groups, shards, where_ref, *refs):
    p, f = where_ref[0], where_ref[1]
    token_refs = refs[:shards]
    weight_ref = refs[shards]
    out_refs = refs[shards + 1 : 2 * shards + 1]
    total, weight, sems = refs[2 * shards + 1 :]
    copies = [
        pltpu.make_async_copy(weight_ref.at[p ^ distance], weight.at[distance], sems.at[distance])
        for distance in range(groups)
    ]
    for copy in copies:
        copy.start()
    quarter = token_refs[0].shape[1]
    sub = quarter // shards
    projected = None
    for distance in range(groups):
        rows = jnp.concatenate([ref[distance] for ref in token_refs], axis=0)
        copies[distance].wait()
        term = lax.dot_general(
            rows,
            weight[distance],
            (((1,), (1,)), ((), ())),
            preferred_element_type=jnp.float32,
        )
        projected = term if projected is None else projected + term
    total[...] = projected
    for e in range(shards):
        for distance, ref in enumerate(out_refs):
            start = pl.multiple_of(e * quarter + (f ^ distance) * sub, sub)
            ref[f ^ e] = total[pl.ds(start, sub), :].astype(jnp.bfloat16)


def finish_kernel(shards, where_ref, gain_ref, residual_ref, *refs):
    f = where_ref[1]
    piece_refs = refs[:shards]
    out_ref, projected = refs[shards:]
    for distance, ref in enumerate(piece_refs):
        projected[f ^ distance] = ref[...].astype(jnp.float32)
    gain = gain_ref[...]
    for request in range(out_ref.shape[0]):
        slot = where_ref[3 + request]
        line = jnp.concatenate([projected[k, slot] for k in range(shards)], axis=1)
        mean_square = jnp.mean(line * line, axis=1, keepdims=True)
        line = line * lax.rsqrt(mean_square + norm_eps) * gain
        out_ref[request] = (residual_ref[slot].astype(jnp.float32) + line).astype(jnp.bfloat16)


def pool_pieces(block, groups):
    return [block] + [swap(block, "pool", distance) for distance in range(1, groups)]


def local_small(
    hidden,
    slot_of_request,
    prefix_len,
    block_holder,
    block_slot,
    kv_pool,
    norm_gain,
    q_weight,
    k_weight,
    v_weight,
    o_weight,
    post_gain,
):
    shards = lax.axis_size("fsdp")
    groups = lax.axis_size("pool")
    f = lax.axis_index("fsdp")
    p = lax.axis_index("pool")
    half = shards // 2
    side = f // half
    new_len, width = hidden.shape[1:]
    requests = slot_of_request.shape[0]
    page_len = kv_pool.shape[1]
    kv_local = kv_pool.shape[2]
    head_dim = kv_pool.shape[3] // 2
    q_cols = q_weight.shape[1]
    kv_cols = k_weight.shape[1]
    max_blocks = block_holder.shape[1]
    per_holder = max_blocks // shards
    quarter = new_len // groups
    sub = quarter // shards
    features = o_weight.shape[0]
    bf16, f32 = jnp.bfloat16, jnp.float32
    where = jnp.concatenate(
        [jnp.stack([p, f, side]).astype(jnp.int32), slot_of_request, prefix_len]
    )
    shape = jax.ShapeDtypeStruct
    any_place = pl.BlockSpec(memory_space=pl.ANY)
    gain = norm_gain.reshape(1, width)
    rows = hidden[0]

    leaving, my_quarter, joined = call(
        prologue_kernel,
        [
            shape((quarter, width // 2), bf16),
            shape((quarter, width), bf16),
            shape((features, q_cols + 2 * kv_cols), bf16),
        ],
        [pltpu.VMEM((quarter, width), f32), pltpu.SemaphoreType.DMA((4,))],
        quarter * width * 8,
        4 * features * kv_cols,
        rows,
        gain,
        q_weight,
        k_weight,
        v_weight,
        specs=[any_place, VMEM, any_place, any_place, any_place],
        out_specs=[VMEM, VMEM, any_place],
    )
    partner_piece = swap(leaving, "fsdp", half)

    near, far = swap(joined, "fsdp", 1), swap(joined, "fsdp", 2)
    partner_piece, near, far = lax.optimization_barrier((partner_piece, near, far))
    weights = [joined, near, far, swap(far, "fsdp", 1)]

    residual = lax.all_to_all(
        my_quarter.reshape(shards, sub, width), "fsdp", split_axis=0, concat_axis=0, tiled=True
    )

    flat_pool = kv_pool.reshape(kv_pool.shape[0], page_len * kv_local, 2 * head_dim)
    page_rows = per_holder * page_len * kv_local
    outgoing, valid = call(
        functools.partial(pages_kernel, requests, page_len),
        [
            shape((shards, page_rows, 2 * head_dim), bf16),
            shape((shards, per_holder * page_len), f32),
        ],
        [
            pltpu.SMEM((2 * per_holder,), jnp.int32),
            pltpu.SMEM((max_blocks + per_holder,), jnp.int32),
            pltpu.SMEM((shards,), jnp.int32),
        ],
        1 << 20,
        1 << 21,
        where,
        block_holder,
        block_slot,
        flat_pool,
        specs=[SMEM, SMEM, SMEM, VMEM],
    )
    partner_pieces = pool_pieces(partner_piece, groups)
    arrived = lax.all_to_all(
        after(outgoing, partner_piece), "fsdp", split_axis=0, concat_axis=0, tiled=True
    )
    out_weight = lax.all_gather(after(o_weight, partner_pieces[-1]), "pool", axis=0, tiled=False)

    partial = call(
        functools.partial(partner_kernel, groups, half),
        shape((new_len, q_cols + 2 * kv_cols), bf16),
        [
            pltpu.VMEM((new_len, width // 2), bf16),
            pltpu.VMEM((width // 2, q_cols + 2 * kv_cols), bf16),
            pltpu.SemaphoreType.DMA((groups,)),
            pltpu.SemaphoreType.DMA((half,)),
        ],
        new_len * width * (q_cols + 2 * kv_cols),
        width * (new_len + q_cols + 2 * kv_cols),
        where,
        *partner_pieces,
        *weights,
        specs=[SMEM] + [any_place] * (groups + half),
    )
    other = swap(partial, "fsdp", half)
    freqs = np.exp(np.arange(head_dim // 2) * (-2.0 * math.log(10000.0) / head_dim))
    freqs = np.concatenate([freqs, freqs]).astype(np.float32).reshape(1, head_dim)
    own, cosine, sine = call(
        functools.partial(own_kernel, requests, half),
        [
            shape((new_len, q_cols + 2 * kv_cols), f32),
            shape((new_len, head_dim), f32),
            shape((new_len, head_dim), f32),
        ],
        [
            pltpu.VMEM((new_len, width // 2), bf16),
            pltpu.VMEM((width // 2, q_cols + 2 * kv_cols), bf16),
            pltpu.SemaphoreType.DMA((half,)),
        ],
        new_len * width * (q_cols + 2 * kv_cols),
        width * (2 * new_len + q_cols + 2 * kv_cols),
        where,
        after(rows, partial),
        gain,
        freqs,
        *weights,
        specs=[SMEM, VMEM, VMEM, VMEM] + [any_place] * half,
    )

    keys_total = max_blocks * page_len
    quarters = call(
        functools.partial(attend_kernel, groups, kv_local, head_dim),
        [shape((quarter, q_cols), bf16)] * groups,
        [
            pltpu.VMEM((kv_local, keys_total, head_dim), bf16),
            pltpu.VMEM((kv_local, keys_total, head_dim), bf16),
            pltpu.VMEM((new_len, q_cols), bf16),
        ],
        4 * new_len * q_cols * (keys_total + new_len),
        1 << 22,
        where,
        own,
        other,
        cosine,
        sine,
        valid,
        arrived,
    )

    quarters = [
        swap(piece, "pool", distance) if distance else piece
        for distance, piece in enumerate(quarters)
    ]
    quarters = jnp.stack(quarters)
    tokens = {0: quarters}
    for distance in range(2, shards, 2):
        tokens[distance] = swap(quarters, "fsdp", distance)
    for distance in range(0, shards, 2):
        tokens[distance ^ 1] = swap(tokens[distance], "fsdp", 1)
    projected = call(
        functools.partial(output_kernel, groups, shards),
        [shape((shards, sub, features), bf16)] * shards,
        [
            pltpu.VMEM((shards * quarter, features), f32),
            pltpu.VMEM((groups, features, q_cols), bf16),
            pltpu.SemaphoreType.DMA((groups,)),
        ],
        2 * shards * quarter * features * groups * q_cols,
        1 << 22,
        where,
        *[tokens[distance] for distance in range(shards)],
        out_weight,
        specs=[SMEM] + [VMEM] * shards + [any_place],
    )
    finished = [
        swap(piece, "fsdp", distance) if distance else piece
        for distance, piece in enumerate(projected)
    ]
    return call(
        functools.partial(finish_kernel, shards),
        shape((requests, sub, width), bf16),
        [pltpu.VMEM((shards, shards, sub, features), f32)],
        1 << 20,
        1 << 20,
        where,
        post_gain.reshape(1, width),
        residual,
        *finished,
    )


def local(*arguments):
    return local_small(*arguments) if lax.axis_size("fsdp") == 8 else local_general(*arguments)


def solution(mesh):
    in_specs = (
        P("fsdp", None, None),
        P(),
        P(),
        P(),
        P(),
        P("fsdp", None, "pool", None),
        P(),
        P("fsdp", "pool"),
        P("fsdp", "pool"),
        P("fsdp", "pool"),
        P("fsdp", "pool"),
        P(),
    )
    out_specs = P(None, ("pool", "fsdp"), None)
    return jax.shard_map(local, mesh=mesh, in_specs=in_specs, out_specs=out_specs, check_vma=False)
```

```python
import functools
import math

import jax
import jax.numpy as jnp
import numpy as np
from jax import lax
from jax.experimental import pallas as pl
from jax.experimental.pallas import tpu as pltpu
from jax.sharding import PartitionSpec as P

softcap = 50.0
query_scale = 144.0 ** (-0.5)
norm_eps = 1e-06


def rms_scale(rows, gain):
    mean_square = jnp.mean(rows * rows, axis=-1, keepdims=True)
    return rows * lax.rsqrt(mean_square + norm_eps) * gain


def rotate(vectors, cosine, sine):
    half = vectors.shape[-1] // 2
    first = vectors[..., :half]
    second = vectors[..., half:]
    return jnp.concatenate(
        [first * cosine - second * sine, second * cosine + first * sine], axis=-1
    )


def capped_weights(scores, valid):
    return jnp.where(valid, jnp.exp(softcap * jnp.tanh(scores / softcap)), 0.0)


def swap(array, axis, distance):
    size = lax.axis_size(axis)
    return lax.ppermute(array, axis, [(i, i ^ distance) for i in range(size)])


def place(pieces, index):
    first = pieces[0]
    stacked = jnp.zeros((len(pieces),) + first.shape, first.dtype)
    for distance, piece in pieces.items():
        stacked = lax.dynamic_update_index_in_dim(stacked, piece, index ^ distance, 0)
    return stacked


def exchange(chunks, axis):
    size = lax.axis_size(axis)
    index = lax.axis_index(axis)
    if size > 8:
        return lax.all_to_all(chunks, axis, split_axis=0, concat_axis=0, tiled=True)
    pieces = {}
    for distance in range(size):
        chunk = lax.dynamic_index_in_dim(chunks, index ^ distance, 0, keepdims=False)
        pieces[distance] = swap(chunk, axis, distance) if distance else chunk
    return place(pieces, index)


def doubled(block, axis, span):
    pieces = {0: block}
    bit = span // 2
    while bit:
        for distance in list(pieces):
            pieces[distance ^ bit] = swap(pieces[distance], axis, bit)
        bit //= 2
    return pieces


def attend(queries, keys_new, values_new, cached, cached_valid):
    new_len, kv_local, group, head_dim = queries.shape

    def part(keys, values, valid):
        scores = jnp.einsum("tgjd,kgd->gjtk", queries, keys, preferred_element_type=jnp.float32)
        weights = capped_weights(scores, valid)
        numer = jnp.einsum(
            "gjtk,kgd->gjtd",
            weights.astype(jnp.bfloat16),
            values,
            preferred_element_type=jnp.float32,
        )
        return numer, jnp.sum(weights, axis=-1)

    query_index = jnp.arange(new_len, dtype=jnp.int32)
    causal = query_index[None, :] <= query_index[:, None]
    numer, denom = part(
        cached[..., :head_dim], cached[..., head_dim:], cached_valid[None, None, None, :]
    )
    more, added = part(keys_new, values_new, causal[None, None])
    attended = ((numer + more) / (denom + added)[..., None]).transpose(2, 0, 1, 3)
    return attended.reshape(new_len, kv_local * group * head_dim).astype(jnp.bfloat16)


def local_general(
    hidden,
    slot_of_request,
    prefix_len,
    block_holder,
    block_slot,
    kv_pool,
    norm_gain,
    q_weight,
    k_weight,
    v_weight,
    o_weight,
    post_gain,
):
    shards = lax.axis_size("fsdp")
    groups = lax.axis_size("pool")
    f = lax.axis_index("fsdp")
    p = lax.axis_index("pool")
    half = shards // 2
    side = f // half
    new_len, width = hidden.shape[1:]
    requests = slot_of_request.shape[0]
    page_len = kv_pool.shape[1]
    kv_local = kv_pool.shape[2]
    head_dim = kv_pool.shape[3] // 2
    q_cols = q_weight.shape[1]
    kv_cols = k_weight.shape[1]
    group = q_cols // kv_cols
    max_blocks = block_holder.shape[1]
    per_holder = max_blocks // shards
    quarter = new_len // groups
    sub = quarter // shards
    features = o_weight.shape[0]

    kv_pieces = doubled(jnp.concatenate([k_weight, v_weight], axis=1), "fsdp", half)
    q_pieces = doubled(q_weight, "fsdp", half)
    out_weight = lax.all_gather(o_weight, "pool", axis=0, tiled=False)

    rows = hidden[0]
    normed = rms_scale(rows.astype(jnp.float32), norm_gain).astype(jnp.bfloat16)
    own_rows = lax.dynamic_slice(normed, (0, side * (width // 2)), (new_len, width // 2))
    leaving = lax.dynamic_slice(
        normed, (p * quarter, (1 - side) * (width // 2)), (quarter, width // 2)
    )
    partner_piece = swap(leaving, "fsdp", half)
    partner_pieces = {0: partner_piece}
    for distance in range(1, groups):
        partner_pieces[distance] = swap(partner_piece, "pool", distance)
    partner_rows = place(partner_pieces, p).reshape(new_len, width // 2)

    request_ids = jnp.arange(requests, dtype=jnp.int32)
    request_at_slot = jnp.sum(
        jnp.where(slot_of_request[None, :] == request_ids[:, None], request_ids[None, :], 0), axis=1
    )
    holder_by_slot = jnp.take(block_holder, request_at_slot, axis=0)
    page_by_slot = jnp.take(block_slot, request_at_slot, axis=0)
    held_here = holder_by_slot == f
    held_rank = jnp.cumsum(held_here.astype(jnp.int32), axis=1) - 1
    rank_ids = jnp.arange(per_holder, dtype=jnp.int32)
    picked = held_here[:, :, None] & (held_rank[:, :, None] == rank_ids[None, None, :])
    local_pages = jnp.sum(jnp.where(picked, page_by_slot[:, :, None], 0), axis=1)
    flat_pool = kv_pool.reshape(kv_pool.shape[0], page_len * kv_local, 2 * head_dim)
    outgoing = jnp.take(flat_pool, local_pages, axis=0)
    outgoing = outgoing.reshape(shards, per_holder * page_len * kv_local, 2 * head_dim)
    arrived = exchange(outgoing, "fsdp")
    cached = arrived.reshape(max_blocks * page_len, kv_local, 2 * head_dim)

    my_request = lax.dynamic_index_in_dim(request_at_slot, f, keepdims=False)
    my_length = prefix_len[my_request]
    my_holders = block_holder[my_request]
    entry_ids = jnp.arange(max_blocks, dtype=jnp.int32)
    mine = my_holders[None, :] == jnp.arange(shards, dtype=jnp.int32)[:, None]
    my_rank = jnp.cumsum(mine.astype(jnp.int32), axis=1) - 1
    chosen = mine[:, None, :] & (my_rank[:, None, :] == rank_ids[None, :, None])
    entry = jnp.sum(jnp.where(chosen, entry_ids[None, None, :], 0), axis=2)
    cached_position = entry.reshape(-1, 1) * page_len + jnp.arange(page_len, dtype=jnp.int32)
    cached_valid = (cached_position < my_length).reshape(-1)

    residual_out = lax.dynamic_slice_in_dim(rows, p * quarter, quarter, 0).reshape(
        shards, sub, width
    )
    residual = exchange(residual_out, "fsdp")

    positions = (my_length + jnp.arange(new_len, dtype=jnp.int32)).astype(jnp.float32)
    freqs = jnp.exp(
        jnp.arange(head_dim // 2, dtype=jnp.float32) * (-2.0 * math.log(10000.0) / head_dim)
    )
    angles = positions[:, None] * freqs
    cosine = jnp.cos(angles)[:, None, :]
    sine = jnp.sin(angles)[:, None, :]

    def project(pieces):
        weight = place(pieces, f % half).reshape(width // 2, -1)
        partial = jnp.dot(partner_rows, weight, preferred_element_type=jnp.float32)
        other = swap(partial.astype(jnp.bfloat16), "fsdp", half)
        own = jnp.dot(own_rows, weight, preferred_element_type=jnp.float32)
        return own + other.astype(jnp.float32)

    kv_sum = project(kv_pieces)
    q_sum = project(q_pieces)
    queries = rotate(q_sum.reshape(new_len, kv_local * group, head_dim), cosine, sine)
    queries = (queries * query_scale).astype(jnp.bfloat16)
    queries = queries.reshape(new_len, kv_local, group, head_dim)
    keys_new = kv_sum[:, :kv_cols].reshape(new_len, kv_local, head_dim)
    keys_new = rotate(keys_new, cosine, sine).astype(jnp.bfloat16)
    values_new = kv_sum[:, kv_cols:].astype(jnp.bfloat16).reshape(new_len, kv_local, head_dim)
    attended = attend(queries, keys_new, values_new, cached, cached_valid)

    quarters = exchange(attended.reshape(groups, quarter, q_cols), "pool")
    token_pieces = {0: quarters}
    for distance in range(2, shards, 2):
        token_pieces[distance] = swap(quarters, "fsdp", distance)
    for distance in range(0, shards, 2):
        token_pieces[distance ^ 1] = swap(token_pieces[distance], "fsdp", 1)
    tokens = place(token_pieces, f)
    projected = jnp.einsum(
        "sptc,pfc->stf", tokens, out_weight, preferred_element_type=jnp.float32
    ).astype(jnp.bfloat16)
    projected = projected.reshape(shards, shards, sub, features).transpose(1, 0, 2, 3)
    finished = exchange(projected, "fsdp").transpose(1, 2, 0, 3).reshape(shards, sub, width)
    finished = residual.astype(jnp.float32) + rms_scale(finished.astype(jnp.float32), post_gain)
    return jnp.take(finished.astype(jnp.bfloat16), slot_of_request, axis=0)


VMEM = pl.BlockSpec(memory_space=pltpu.VMEM)
SMEM = pl.BlockSpec(memory_space=pltpu.SMEM)
HBM = pl.BlockSpec(memory_space=pltpu.HBM)


def call(kernel, outs, scratch, flops, nbytes, *operands, specs=None, out_specs=None):
    return pl.pallas_call(
        kernel,
        out_shape=outs,
        in_specs=specs or [SMEM] + [VMEM] * (len(operands) - 1),
        out_specs=out_specs or jax.tree.map(lambda _: VMEM, outs),
        scratch_shapes=scratch,
        compiler_params=pltpu.CompilerParams(vmem_limit_bytes=48 << 20),
        cost_estimate=pl.CostEstimate(flops=flops, bytes_accessed=nbytes, transcendentals=0),
    )(*operands)


def after(array, *earlier):
    return lax.optimization_barrier((array,) + earlier)[0]


def weight_copies(weight_refs, weight, f, half, sems):
    copies = []
    for distance, ref in enumerate(weight_refs):
        count = ref.shape[0]
        start = pl.multiple_of(((f ^ distance) & (half - 1)) * count, 64)
        copies.append(
            pltpu.make_async_copy(ref, weight.at[pl.ds(start, count), :], sems.at[distance])
        )
        copies[-1].start()
    return copies


def partner_kernel(groups, half, where_ref, *refs):
    p, f = where_ref[0], where_ref[1]
    x_refs, w_refs = refs[:groups], refs[groups : groups + half]
    out_ref, rows, weight, x_sems, w_sems = refs[groups + half :]
    quarter = x_refs[0].shape[0]
    copies = weight_copies(w_refs, weight, f, half, w_sems)
    for distance, ref in enumerate(x_refs):
        start = pl.multiple_of((p ^ distance) * quarter, quarter)
        copies.append(
            pltpu.make_async_copy(ref, rows.at[pl.ds(start, quarter), :], x_sems.at[distance])
        )
        copies[-1].start()
    for copy in copies:
        copy.wait()
    for at in range(0, out_ref.shape[1], 512):
        out_ref[:, at : at + 512] = jnp.dot(
            rows[...], weight[:, at : at + 512], preferred_element_type=jnp.float32
        ).astype(jnp.bfloat16)


def row_scale(rows):
    return lax.rsqrt(jnp.mean(rows * rows, axis=1, keepdims=True) + norm_eps)


def prologue_kernel(
    hidden_ref, gain_ref, q_ref, k_ref, v_ref, leaving_ref, rows_ref, weight_ref, normed, sems
):
    p, f = lax.axis_index("pool"), lax.axis_index("fsdp")
    side = f // (lax.axis_size("fsdp") // 2)
    quarter, width = rows_ref.shape
    half_width = width // 2
    start = pl.multiple_of(p * quarter, quarter)
    rows_copy = pltpu.make_async_copy(hidden_ref.at[pl.ds(start, quarter), :], rows_ref, sems.at[0])
    rows_copy.start()
    copies = []
    at = 0
    for index, ref in enumerate((q_ref, k_ref, v_ref)):
        to = at + ref.shape[1]
        copies.append(pltpu.make_async_copy(ref, weight_ref.at[:, at:to], sems.at[1 + index]))
        copies[-1].start()
        at = to
    rows_copy.wait()
    rows = rows_ref[...].astype(jnp.float32)
    normed[...] = rows * row_scale(rows) * gain_ref[...]
    away = pl.multiple_of((1 - side) * half_width, 128)
    leaving_ref[...] = normed[:, pl.ds(away, half_width)].astype(jnp.bfloat16)
    for copy in copies:
        copy.wait()


def pages_kernel(
    requests, page_len, where_ref, holder_ref, slot_ref, pool_ref, out_ref, valid_ref, listed, entries, counts
):
    f = where_ref[1]
    max_blocks = holder_ref.shape[1]
    shards, _, _ = out_ref.shape
    per = max_blocks // shards
    page_rows = pool_ref.shape[1]
    length, mine = jnp.int32(0), jnp.int32(0)
    for r in range(requests):
        at = where_ref[3 + r] == f
        length = length + jnp.where(at, where_ref[3 + requests + r], 0)
        mine = mine + jnp.where(at, r, 0)
    for r in range(requests):
        slot = where_ref[3 + r]

        def note(j, count):
            listed[count] = slot_ref[r, j]
            return count + jnp.where(holder_ref[r, j] == f, 1, 0)

        lax.fori_loop(0, max_blocks, note, jnp.int32(0), unroll=8)
        for k in range(per):
            out_ref[slot, k * page_rows : (k + 1) * page_rows, :] = pool_ref[listed[k]]
    for h in range(shards):
        counts[h] = 0

    def enter(j, carry):
        h = holder_ref[mine, j]
        count = counts[h]
        entries[h * per + count] = j
        counts[h] = count + 1
        return carry

    lax.fori_loop(0, max_blocks, enter, 0, unroll=4)
    row = lax.broadcasted_iota(jnp.int32, valid_ref.shape, 0)
    lane = lax.broadcasted_iota(jnp.int32, valid_ref.shape, 1)
    place_in = row * per + lane // page_len
    entry = jnp.zeros(valid_ref.shape, jnp.int32)
    for at in range(max_blocks):
        entry = jnp.where(place_in == at, entries[at], entry)
    position = entry * page_len + lane % page_len
    valid_ref[...] = jnp.where(position < length, 1.0, 0.0)


def own_kernel(requests, half, where_ref, hidden_ref, gain_ref, freq_ref, *refs):
    f = where_ref[1]
    own_ref, cos_ref, sin_ref, hidden, normed, weight, sems = refs[half:]
    rows_copy = pltpu.make_async_copy(hidden_ref, hidden, sems.at[half])
    rows_copy.start()
    copies = weight_copies(refs[:half], weight, f, half, sems)
    rows_copy.wait()
    new_len, width = hidden_ref.shape
    half_width = width // 2
    length = jnp.int32(0)
    for r in range(requests):
        length = length + jnp.where(where_ref[3 + r] == f, where_ref[3 + requests + r], 0)
    start = pl.multiple_of(where_ref[2] * half_width, 128)
    gain = gain_ref[:, pl.ds(start, half_width)]
    step = 32

    def norm(index, carry):
        at = pl.multiple_of(index * step, step)
        rows = hidden[pl.ds(at, step), :].astype(jnp.float32)
        scale = row_scale(rows)
        part = hidden[pl.ds(at, step), pl.ds(start, half_width)].astype(jnp.float32)
        normed[pl.ds(at, step), :] = (part * scale * gain).astype(jnp.bfloat16)
        return carry

    lax.fori_loop(0, new_len // step, norm, 0)
    position = lax.broadcasted_iota(jnp.int32, cos_ref.shape, 0) + length
    angle = position.astype(jnp.float32) * freq_ref[...]
    lane = lax.broadcasted_iota(jnp.int32, cos_ref.shape, 1)
    cos_ref[...] = jnp.cos(angle)
    sine = jnp.sin(angle)
    sin_ref[...] = jnp.where(lane < cos_ref.shape[1] // 2, -sine, sine)
    for copy in copies:
        copy.wait()
    for at in range(0, own_ref.shape[1], 512):
        own_ref[:, at : at + 512] = jnp.dot(
            normed[...], weight[:, at : at + 512], preferred_element_type=jnp.float32
        )


def capped(scores):
    return jnp.exp2(jnp.tanh(scores * (1.0 / softcap)) * (softcap * math.log2(math.e)))


def attend_kernel(
    groups,
    kv_local,
    head_dim,
    where_ref,
    own,
    other_ref,
    cos_ref,
    sin_ref,
    valid_ref,
    page_ref,
    *refs,
):
    p = where_ref[0]
    out_refs = refs[:groups]
    keys, values, result, other, pages, sems = refs[groups:]
    copies = [
        pltpu.make_async_copy(page_ref, pages, sems.at[0]),
        pltpu.make_async_copy(other_ref, other, sems.at[1]),
    ]
    for copy in copies:
        copy.start()
    new_len, q_cols = result.shape
    group = q_cols // (kv_local * head_dim)

    def sums(at):
        return own[:, at : at + head_dim] + other[:, at : at + head_dim].astype(jnp.float32)

    cosine, sine = cos_ref[...], sin_ref[...]

    def rope(vectors):
        return vectors * cosine + pltpu.roll(vectors, head_dim // 2, 1) * sine

    span = page_ref.shape[1]
    per = span // kv_local
    row = lax.broadcasted_iota(jnp.int32, (span, span), 0)
    column = lax.broadcasted_iota(jnp.int32, (span, span), 1)
    part = (column == (row % per) * kv_local + row // per).astype(jnp.bfloat16)
    place_at = 0
    copies[0].wait()
    for holder in range(pages.shape[0]):
        parted = jnp.dot(part, pages[holder], preferred_element_type=jnp.float32)
        parted = parted.astype(jnp.bfloat16)
        for g in range(kv_local):
            lines = parted[g * per : (g + 1) * per]
            keys[g, place_at : place_at + per, :] = lines[:, :head_dim]
            values[g, place_at : place_at + per, :] = lines[:, head_dim:]
        place_at += per

    copies[1].wait()
    span_keys = 2 * per
    t = lax.broadcasted_iota(jnp.int32, (group * new_len, new_len), 0) % new_len
    s = lax.broadcasted_iota(jnp.int32, (group * new_len, new_len), 1)
    causal = s <= t
    for g in range(kv_local):
        heads = [
            (rope(sums((g * group + j) * head_dim)) * query_scale).astype(jnp.bfloat16)
            for j in range(group)
        ]
        queries = jnp.concatenate(heads, axis=0)
        at = q_cols + g * head_dim
        new_key = rope(sums(at)).astype(jnp.bfloat16)
        new_value = sums(at + kv_local * head_dim).astype(jnp.bfloat16)

        def scores_of(key):
            return lax.dot_general(
                queries, key, (((1,), (1,)), ((), ())), preferred_element_type=jnp.float32
            )

        weights = jnp.where(causal, capped(scores_of(new_key)), 0.0)
        denom = jnp.sum(weights, axis=1, keepdims=True)
        numer = jnp.dot(
            weights.astype(jnp.bfloat16), new_value, preferred_element_type=jnp.float32
        )
        for start in range(0, place_at, span_keys):
            at = start // per
            valid = jnp.concatenate([valid_ref[at : at + 1], valid_ref[at + 1 : at + 2]], axis=1)
            valid = valid > 0.0
            weights = jnp.where(
                valid, capped(scores_of(keys[g, start : start + span_keys, :])), 0.0
            )
            denom = denom + jnp.sum(weights, axis=1, keepdims=True)
            numer = numer + jnp.dot(
                weights.astype(jnp.bfloat16),
                values[g, start : start + span_keys, :],
                preferred_element_type=jnp.float32,
            )
        attended = (numer / denom).astype(jnp.bfloat16)
        for j in range(group):
            to = (g * group + j) * head_dim
            result[:, to : to + head_dim] = attended[j * new_len : (j + 1) * new_len]
    quarter = new_len // groups
    for distance, ref in enumerate(out_refs):
        start = pl.multiple_of((p ^ distance) * quarter, quarter)
        ref[...] = result[pl.ds(start, quarter), :]


def output_kernel(groups, shards, where_ref, *refs):
    p, f = where_ref[0], where_ref[1]
    token_refs = refs[:shards]
    weight_ref = refs[shards]
    out_refs = refs[shards + 1 : 2 * shards + 1]
    total, tokens, weight, sems, token_sems = refs[2 * shards + 1 :]
    token_copies = [
        pltpu.make_async_copy(ref, tokens.at[e], token_sems.at[e])
        for e, ref in enumerate(token_refs)
    ]
    copies = [
        pltpu.make_async_copy(weight_ref.at[p ^ distance], weight.at[distance], sems.at[distance])
        for distance in range(groups)
    ]
    for copy in token_copies + copies:
        copy.start()
    for copy in token_copies:
        copy.wait()
    quarter = token_refs[0].shape[1]
    sub = quarter // shards
    projected = None
    for distance in range(groups):
        rows = jnp.concatenate([tokens[e, distance] for e in range(shards)], axis=0)
        copies[distance].wait()
        term = lax.dot_general(
            rows,
            weight[distance],
            (((1,), (1,)), ((), ())),
            preferred_element_type=jnp.float32,
        )
        projected = term if projected is None else projected + term
    total[...] = projected
    for e in range(shards):
        for distance, ref in enumerate(out_refs):
            start = pl.multiple_of(e * quarter + (f ^ distance) * sub, sub)
            ref[f ^ e] = total[pl.ds(start, sub), :].astype(jnp.bfloat16)


def finish_kernel(shards, where_ref, gain_ref, residual_ref, *refs):
    f = where_ref[1]
    piece_refs = refs[:shards]
    out_ref, projected = refs[shards:]
    for distance, ref in enumerate(piece_refs):
        projected[f ^ distance] = ref[...].astype(jnp.float32)
    gain = gain_ref[...]
    for request in range(out_ref.shape[0]):
        slot = where_ref[3 + request]
        line = jnp.concatenate([projected[k, slot] for k in range(shards)], axis=1)
        mean_square = jnp.mean(line * line, axis=1, keepdims=True)
        line = line * lax.rsqrt(mean_square + norm_eps) * gain
        out_ref[request] = (residual_ref[slot].astype(jnp.float32) + line).astype(jnp.bfloat16)


def pool_pieces(block, groups):
    return [block] + [swap(block, "pool", distance) for distance in range(1, groups)]


def local_small(
    hidden,
    slot_of_request,
    prefix_len,
    block_holder,
    block_slot,
    kv_pool,
    norm_gain,
    q_weight,
    k_weight,
    v_weight,
    o_weight,
    post_gain,
):
    shards = lax.axis_size("fsdp")
    groups = lax.axis_size("pool")
    f = lax.axis_index("fsdp")
    p = lax.axis_index("pool")
    half = shards // 2
    side = f // half
    new_len, width = hidden.shape[1:]
    requests = slot_of_request.shape[0]
    page_len = kv_pool.shape[1]
    kv_local = kv_pool.shape[2]
    head_dim = kv_pool.shape[3] // 2
    q_cols = q_weight.shape[1]
    kv_cols = k_weight.shape[1]
    max_blocks = block_holder.shape[1]
    per_holder = max_blocks // shards
    quarter = new_len // groups
    sub = quarter // shards
    features = o_weight.shape[0]
    bf16, f32 = jnp.bfloat16, jnp.float32
    where = jnp.concatenate(
        [jnp.stack([p, f, side]).astype(jnp.int32), slot_of_request, prefix_len]
    )
    shape = jax.ShapeDtypeStruct
    gain = norm_gain.reshape(1, width)
    rows = hidden[0]

    leaving, my_quarter, joined = call(
        prologue_kernel,
        [
            shape((quarter, width // 2), bf16),
            shape((quarter, width), bf16),
            shape((features, q_cols + 2 * kv_cols), bf16),
        ],
        [pltpu.VMEM((quarter, width), f32), pltpu.SemaphoreType.DMA((4,))],
        quarter * width * 8,
        4 * features * kv_cols,
        rows,
        gain,
        q_weight,
        k_weight,
        v_weight,
        specs=[HBM, VMEM, HBM, HBM, HBM],
        out_specs=[VMEM, VMEM, HBM],
    )
    partner_piece = swap(leaving, "fsdp", half)

    near, far = swap(joined, "fsdp", 1), swap(joined, "fsdp", 2)

    flat_pool = kv_pool.reshape(kv_pool.shape[0], page_len * kv_local, 2 * head_dim)
    page_rows = per_holder * page_len * kv_local
    outgoing, valid = call(
        functools.partial(pages_kernel, requests, page_len),
        [
            shape((shards, page_rows, 2 * head_dim), bf16),
            shape((shards, per_holder * page_len), f32),
        ],
        [
            pltpu.SMEM((2 * per_holder,), jnp.int32),
            pltpu.SMEM((max_blocks + per_holder,), jnp.int32),
            pltpu.SMEM((shards,), jnp.int32),
        ],
        1 << 20,
        1 << 21,
        where,
        block_holder,
        block_slot,
        flat_pool,
        specs=[SMEM, SMEM, SMEM, VMEM],
    )
    partner_piece, near, far, outgoing, valid = lax.optimization_barrier(
        (partner_piece, near, far, outgoing, valid)
    )
    weights = [joined, near, far, swap(far, "fsdp", 1)]
    partner_pieces = pool_pieces(partner_piece, groups)
    arrived = lax.all_to_all(outgoing, "fsdp", split_axis=0, concat_axis=0, tiled=True)
    out_weight = lax.all_gather(after(o_weight, partner_piece), "pool", axis=0, tiled=False)

    residual = lax.all_to_all(
        after(my_quarter, arrived).reshape(shards, sub, width),
        "fsdp",
        split_axis=0,
        concat_axis=0,
        tiled=True,
    )

    partial = call(
        functools.partial(partner_kernel, groups, half),
        shape((new_len, q_cols + 2 * kv_cols), bf16),
        [
            pltpu.VMEM((new_len, width // 2), bf16),
            pltpu.VMEM((width // 2, q_cols + 2 * kv_cols), bf16),
            pltpu.SemaphoreType.DMA((groups,)),
            pltpu.SemaphoreType.DMA((half,)),
        ],
        new_len * width * (q_cols + 2 * kv_cols),
        width * (new_len + q_cols + 2 * kv_cols),
        where,
        *partner_pieces,
        *weights,
        specs=[SMEM] + [HBM] * (groups + half),
    )
    other = swap(partial, "fsdp", half)
    freqs = np.exp(np.arange(head_dim // 2) * (-2.0 * math.log(10000.0) / head_dim))
    freqs = np.concatenate([freqs, freqs]).astype(np.float32).reshape(1, head_dim)
    own, cosine, sine = call(
        functools.partial(own_kernel, requests, half),
        [
            shape((new_len, q_cols + 2 * kv_cols), f32),
            shape((new_len, head_dim), f32),
            shape((new_len, head_dim), f32),
        ],
        [
            pltpu.VMEM((new_len, width), bf16),
            pltpu.VMEM((new_len, width // 2), bf16),
            pltpu.VMEM((width // 2, q_cols + 2 * kv_cols), bf16),
            pltpu.SemaphoreType.DMA((half + 1,)),
        ],
        new_len * width * (q_cols + 2 * kv_cols),
        width * (2 * new_len + q_cols + 2 * kv_cols),
        where,
        after(rows, partial),
        gain,
        freqs,
        *weights,
        specs=[SMEM, HBM, VMEM, VMEM] + [HBM] * half,
    )

    keys_total = max_blocks * page_len
    quarters = call(
        functools.partial(attend_kernel, groups, kv_local, head_dim),
        [shape((quarter, q_cols), bf16)] * groups,
        [
            pltpu.VMEM((kv_local, keys_total, head_dim), bf16),
            pltpu.VMEM((kv_local, keys_total, head_dim), bf16),
            pltpu.VMEM((new_len, q_cols), bf16),
            pltpu.VMEM(other.shape, bf16),
            pltpu.VMEM(arrived.shape, bf16),
            pltpu.SemaphoreType.DMA((2,)),
        ],
        4 * new_len * q_cols * (keys_total + new_len),
        1 << 22,
        where,
        own,
        other,
        cosine,
        sine,
        valid,
        arrived,
        specs=[SMEM, VMEM, HBM, VMEM, VMEM, VMEM, HBM],
    )

    quarters = [
        swap(piece, "pool", distance) if distance else piece
        for distance, piece in enumerate(quarters)
    ]
    quarters = jnp.stack(quarters)
    tokens = {0: quarters}
    for distance in range(2, shards, 2):
        tokens[distance] = swap(quarters, "fsdp", distance)
    for distance in range(0, shards, 2):
        tokens[distance ^ 1] = swap(tokens[distance], "fsdp", 1)
    projected = call(
        functools.partial(output_kernel, groups, shards),
        [shape((shards, sub, features), bf16)] * shards,
        [
            pltpu.VMEM((shards * quarter, features), f32),
            pltpu.VMEM((shards, groups, quarter, q_cols), bf16),
            pltpu.VMEM((groups, features, q_cols), bf16),
            pltpu.SemaphoreType.DMA((groups,)),
            pltpu.SemaphoreType.DMA((shards,)),
        ],
        2 * shards * quarter * features * groups * q_cols,
        1 << 22,
        where,
        *[tokens[distance] for distance in range(shards)],
        out_weight,
        specs=[SMEM] + [HBM] * (shards + 1),
    )
    finished = [
        swap(piece, "fsdp", distance) if distance else piece
        for distance, piece in enumerate(projected)
    ]
    return call(
        functools.partial(finish_kernel, shards),
        shape((requests, sub, width), bf16),
        [pltpu.VMEM((shards, shards, sub, features), f32)],
        1 << 20,
        1 << 20,
        where,
        post_gain.reshape(1, width),
        residual,
        *finished,
    )


def local(*arguments):
    return local_small(*arguments) if lax.axis_size("fsdp") == 8 else local_general(*arguments)


def solution(mesh):
    in_specs = (
        P("fsdp", None, None),
        P(),
        P(),
        P(),
        P(),
        P("fsdp", None, "pool", None),
        P(),
        P("fsdp", "pool"),
        P("fsdp", "pool"),
        P("fsdp", "pool"),
        P("fsdp", "pool"),
        P(),
    )
    out_specs = P(None, ("pool", "fsdp"), None)
    return jax.shard_map(local, mesh=mesh, in_specs=in_specs, out_specs=out_specs, check_vma=False)
```

```python
import functools
import math

import jax
import jax.numpy as jnp
import numpy as np
from jax import lax
from jax.experimental import pallas as pl
from jax.experimental.pallas import tpu as pltpu
from jax.sharding import PartitionSpec as P

softcap = 50.0
query_scale = 144.0 ** (-0.5)
norm_eps = 1e-06


def rms_scale(rows, gain):
    mean_square = jnp.mean(rows * rows, axis=-1, keepdims=True)
    return rows * lax.rsqrt(mean_square + norm_eps) * gain


def rotate(vectors, cosine, sine):
    half = vectors.shape[-1] // 2
    first = vectors[..., :half]
    second = vectors[..., half:]
    return jnp.concatenate(
        [first * cosine - second * sine, second * cosine + first * sine], axis=-1
    )


def capped_weights(scores, valid):
    return jnp.where(valid, jnp.exp(softcap * jnp.tanh(scores / softcap)), 0.0)


def swap(array, axis, distance):
    size = lax.axis_size(axis)
    return lax.ppermute(array, axis, [(i, i ^ distance) for i in range(size)])


def place(pieces, index):
    first = pieces[0]
    stacked = jnp.zeros((len(pieces),) + first.shape, first.dtype)
    for distance, piece in pieces.items():
        stacked = lax.dynamic_update_index_in_dim(stacked, piece, index ^ distance, 0)
    return stacked


def exchange(chunks, axis):
    size = lax.axis_size(axis)
    index = lax.axis_index(axis)
    if size > 8:
        return lax.all_to_all(chunks, axis, split_axis=0, concat_axis=0, tiled=True)
    pieces = {}
    for distance in range(size):
        chunk = lax.dynamic_index_in_dim(chunks, index ^ distance, 0, keepdims=False)
        pieces[distance] = swap(chunk, axis, distance) if distance else chunk
    return place(pieces, index)


def doubled(block, axis, span):
    pieces = {0: block}
    bit = span // 2
    while bit:
        for distance in list(pieces):
            pieces[distance ^ bit] = swap(pieces[distance], axis, bit)
        bit //= 2
    return pieces


def attend(queries, keys_new, values_new, cached, cached_valid):
    new_len, kv_local, group, head_dim = queries.shape

    def part(keys, values, valid):
        scores = jnp.einsum("tgjd,kgd->gjtk", queries, keys, preferred_element_type=jnp.float32)
        weights = capped_weights(scores, valid)
        numer = jnp.einsum(
            "gjtk,kgd->gjtd",
            weights.astype(jnp.bfloat16),
            values,
            preferred_element_type=jnp.float32,
        )
        return numer, jnp.sum(weights, axis=-1)

    query_index = jnp.arange(new_len, dtype=jnp.int32)
    causal = query_index[None, :] <= query_index[:, None]
    numer, denom = part(
        cached[..., :head_dim], cached[..., head_dim:], cached_valid[None, None, None, :]
    )
    more, added = part(keys_new, values_new, causal[None, None])
    attended = ((numer + more) / (denom + added)[..., None]).transpose(2, 0, 1, 3)
    return attended.reshape(new_len, kv_local * group * head_dim).astype(jnp.bfloat16)


def local_general(
    hidden,
    slot_of_request,
    prefix_len,
    block_holder,
    block_slot,
    kv_pool,
    norm_gain,
    q_weight,
    k_weight,
    v_weight,
    o_weight,
    post_gain,
):
    shards = lax.axis_size("fsdp")
    groups = lax.axis_size("pool")
    f = lax.axis_index("fsdp")
    p = lax.axis_index("pool")
    half = shards // 2
    side = f // half
    new_len, width = hidden.shape[1:]
    requests = slot_of_request.shape[0]
    page_len = kv_pool.shape[1]
    kv_local = kv_pool.shape[2]
    head_dim = kv_pool.shape[3] // 2
    q_cols = q_weight.shape[1]
    kv_cols = k_weight.shape[1]
    group = q_cols // kv_cols
    max_blocks = block_holder.shape[1]
    per_holder = max_blocks // shards
    quarter = new_len // groups
    sub = quarter // shards
    features = o_weight.shape[0]

    kv_pieces = doubled(jnp.concatenate([k_weight, v_weight], axis=1), "fsdp", half)
    q_pieces = doubled(q_weight, "fsdp", half)
    out_weight = lax.all_gather(o_weight, "pool", axis=0, tiled=False)

    rows = hidden[0]
    normed = rms_scale(rows.astype(jnp.float32), norm_gain).astype(jnp.bfloat16)
    own_rows = lax.dynamic_slice(normed, (0, side * (width // 2)), (new_len, width // 2))
    leaving = lax.dynamic_slice(
        normed, (p * quarter, (1 - side) * (width // 2)), (quarter, width // 2)
    )
    partner_piece = swap(leaving, "fsdp", half)
    partner_pieces = {0: partner_piece}
    for distance in range(1, groups):
        partner_pieces[distance] = swap(partner_piece, "pool", distance)
    partner_rows = place(partner_pieces, p).reshape(new_len, width // 2)

    request_ids = jnp.arange(requests, dtype=jnp.int32)
    request_at_slot = jnp.sum(
        jnp.where(slot_of_request[None, :] == request_ids[:, None], request_ids[None, :], 0), axis=1
    )
    holder_by_slot = jnp.take(block_holder, request_at_slot, axis=0)
    page_by_slot = jnp.take(block_slot, request_at_slot, axis=0)
    held_here = holder_by_slot == f
    held_rank = jnp.cumsum(held_here.astype(jnp.int32), axis=1) - 1
    rank_ids = jnp.arange(per_holder, dtype=jnp.int32)
    picked = held_here[:, :, None] & (held_rank[:, :, None] == rank_ids[None, None, :])
    local_pages = jnp.sum(jnp.where(picked, page_by_slot[:, :, None], 0), axis=1)
    flat_pool = kv_pool.reshape(kv_pool.shape[0], page_len * kv_local, 2 * head_dim)
    outgoing = jnp.take(flat_pool, local_pages, axis=0)
    outgoing = outgoing.reshape(shards, per_holder * page_len * kv_local, 2 * head_dim)
    arrived = exchange(outgoing, "fsdp")
    cached = arrived.reshape(max_blocks * page_len, kv_local, 2 * head_dim)

    my_request = lax.dynamic_index_in_dim(request_at_slot, f, keepdims=False)
    my_length = prefix_len[my_request]
    my_holders = block_holder[my_request]
    entry_ids = jnp.arange(max_blocks, dtype=jnp.int32)
    mine = my_holders[None, :] == jnp.arange(shards, dtype=jnp.int32)[:, None]
    my_rank = jnp.cumsum(mine.astype(jnp.int32), axis=1) - 1
    chosen = mine[:, None, :] & (my_rank[:, None, :] == rank_ids[None, :, None])
    entry = jnp.sum(jnp.where(chosen, entry_ids[None, None, :], 0), axis=2)
    cached_position = entry.reshape(-1, 1) * page_len + jnp.arange(page_len, dtype=jnp.int32)
    cached_valid = (cached_position < my_length).reshape(-1)

    residual_out = lax.dynamic_slice_in_dim(rows, p * quarter, quarter, 0).reshape(
        shards, sub, width
    )
    residual = exchange(residual_out, "fsdp")

    positions = (my_length + jnp.arange(new_len, dtype=jnp.int32)).astype(jnp.float32)
    freqs = jnp.exp(
        jnp.arange(head_dim // 2, dtype=jnp.float32) * (-2.0 * math.log(10000.0) / head_dim)
    )
    angles = positions[:, None] * freqs
    cosine = jnp.cos(angles)[:, None, :]
    sine = jnp.sin(angles)[:, None, :]

    def project(pieces):
        weight = place(pieces, f % half).reshape(width // 2, -1)
        partial = jnp.dot(partner_rows, weight, preferred_element_type=jnp.float32)
        other = swap(partial.astype(jnp.bfloat16), "fsdp", half)
        own = jnp.dot(own_rows, weight, preferred_element_type=jnp.float32)
        return own + other.astype(jnp.float32)

    kv_sum = project(kv_pieces)
    q_sum = project(q_pieces)
    queries = rotate(q_sum.reshape(new_len, kv_local * group, head_dim), cosine, sine)
    queries = (queries * query_scale).astype(jnp.bfloat16)
    queries = queries.reshape(new_len, kv_local, group, head_dim)
    keys_new = kv_sum[:, :kv_cols].reshape(new_len, kv_local, head_dim)
    keys_new = rotate(keys_new, cosine, sine).astype(jnp.bfloat16)
    values_new = kv_sum[:, kv_cols:].astype(jnp.bfloat16).reshape(new_len, kv_local, head_dim)
    attended = attend(queries, keys_new, values_new, cached, cached_valid)

    quarters = exchange(attended.reshape(groups, quarter, q_cols), "pool")
    token_pieces = {0: quarters}
    for distance in range(2, shards, 2):
        token_pieces[distance] = swap(quarters, "fsdp", distance)
    for distance in range(0, shards, 2):
        token_pieces[distance ^ 1] = swap(token_pieces[distance], "fsdp", 1)
    tokens = place(token_pieces, f)
    projected = jnp.einsum(
        "sptc,pfc->stf", tokens, out_weight, preferred_element_type=jnp.float32
    ).astype(jnp.bfloat16)
    projected = projected.reshape(shards, shards, sub, features).transpose(1, 0, 2, 3)
    finished = exchange(projected, "fsdp").transpose(1, 2, 0, 3).reshape(shards, sub, width)
    finished = residual.astype(jnp.float32) + rms_scale(finished.astype(jnp.float32), post_gain)
    return jnp.take(finished.astype(jnp.bfloat16), slot_of_request, axis=0)


VMEM = pl.BlockSpec(memory_space=pltpu.VMEM)
SMEM = pl.BlockSpec(memory_space=pltpu.SMEM)
HBM = pl.BlockSpec(memory_space=pltpu.HBM)


def call(kernel, outs, scratch, flops, nbytes, *operands, specs=None, out_specs=None):
    return pl.pallas_call(
        kernel,
        out_shape=outs,
        in_specs=specs or [SMEM] + [VMEM] * (len(operands) - 1),
        out_specs=out_specs or jax.tree.map(lambda _: VMEM, outs),
        scratch_shapes=scratch,
        compiler_params=pltpu.CompilerParams(vmem_limit_bytes=60 << 20),
        cost_estimate=pl.CostEstimate(flops=flops, bytes_accessed=nbytes, transcendentals=0),
    )(*operands)


def after(array, *earlier):
    return lax.optimization_barrier((array,) + earlier)[0]


def weight_copies(weight_refs, weight, f, half, sems):
    copies = []
    for distance, ref in enumerate(weight_refs):
        count = ref.shape[0]
        start = pl.multiple_of(((f ^ distance) & (half - 1)) * count, 64)
        copies.append(
            pltpu.make_async_copy(ref, weight.at[pl.ds(start, count), :], sems.at[distance])
        )
        copies[-1].start()
    return copies


def partner_kernel(groups, half, where_ref, *refs):
    p, f = where_ref[0], where_ref[1]
    x_refs, w_refs = refs[:groups], refs[groups : groups + half]
    out_ref, rows, weight, x_sems, w_sems = refs[groups + half :]
    quarter = x_refs[0].shape[0]
    copies = weight_copies(w_refs, weight, f, half, w_sems)
    for distance, ref in enumerate(x_refs):
        start = pl.multiple_of((p ^ distance) * quarter, quarter)
        copies.append(
            pltpu.make_async_copy(ref, rows.at[pl.ds(start, quarter), :], x_sems.at[distance])
        )
        copies[-1].start()
    for copy in copies:
        copy.wait()
    for at in range(0, out_ref.shape[1], 512):
        out_ref[:, at : at + 512] = jnp.dot(
            rows[...], weight[:, at : at + 512], preferred_element_type=jnp.float32
        ).astype(jnp.bfloat16)


def row_scale(rows):
    return lax.rsqrt(jnp.mean(rows * rows, axis=1, keepdims=True) + norm_eps)


def prologue_kernel(
    hidden_ref, gain_ref, q_ref, k_ref, v_ref, leaving_ref, rows_ref, weight_ref, normed, sems
):
    p, f = lax.axis_index("pool"), lax.axis_index("fsdp")
    side = f // (lax.axis_size("fsdp") // 2)
    quarter, width = rows_ref.shape
    half_width = width // 2
    start = pl.multiple_of(p * quarter, quarter)
    rows_copy = pltpu.make_async_copy(hidden_ref.at[pl.ds(start, quarter), :], rows_ref, sems.at[0])
    rows_copy.start()
    copies = []
    at = 0
    for index, ref in enumerate((q_ref, k_ref, v_ref)):
        to = at + ref.shape[1]
        copies.append(pltpu.make_async_copy(ref, weight_ref.at[:, at:to], sems.at[1 + index]))
        copies[-1].start()
        at = to
    rows_copy.wait()
    rows = rows_ref[...].astype(jnp.float32)
    normed[...] = rows * row_scale(rows) * gain_ref[...].reshape(1, width)
    away = pl.multiple_of((1 - side) * half_width, 128)
    leaving_ref[...] = normed[:, pl.ds(away, half_width)].astype(jnp.bfloat16)
    for copy in copies:
        copy.wait()


def pages_kernel(
    requests, page_len, where_ref, holder_ref, slot_ref, pool_ref, out_ref, valid_ref, listed, entries, counts
):
    f = where_ref[1]
    max_blocks = holder_ref.shape[1]
    shards, _, _ = out_ref.shape
    per = max_blocks // shards
    page_rows = pool_ref.shape[1]
    length, mine = jnp.int32(0), jnp.int32(0)
    for r in range(requests):
        at = where_ref[3 + r] == f
        length = length + jnp.where(at, where_ref[3 + requests + r], 0)
        mine = mine + jnp.where(at, r, 0)
    for r in range(requests):
        slot = where_ref[3 + r]

        def note(j, count):
            listed[count] = slot_ref[r, j]
            return count + jnp.where(holder_ref[r, j] == f, 1, 0)

        lax.fori_loop(0, max_blocks, note, jnp.int32(0), unroll=8)
        for k in range(per):
            out_ref[slot, k * page_rows : (k + 1) * page_rows, :] = pool_ref[listed[k]]
    for h in range(shards):
        counts[h] = 0

    def enter(j, carry):
        h = holder_ref[mine, j]
        count = counts[h]
        entries[h * per + count] = j
        counts[h] = count + 1
        return carry

    lax.fori_loop(0, max_blocks, enter, 0, unroll=4)
    row = lax.broadcasted_iota(jnp.int32, valid_ref.shape, 0)
    lane = lax.broadcasted_iota(jnp.int32, valid_ref.shape, 1)
    place_in = row * per + lane // page_len
    entry = jnp.zeros(valid_ref.shape, jnp.int32)
    for at in range(max_blocks):
        entry = jnp.where(place_in == at, entries[at], entry)
    position = entry * page_len + lane % page_len
    valid_ref[...] = jnp.where(position < length, 1.0, 0.0)


def own_kernel(requests, half, where_ref, hidden_ref, gain_ref, freq_ref, *refs):
    f = where_ref[1]
    own_ref, cos_ref, sin_ref, hidden, normed, weight, sems = refs[half:]
    rows_copy = pltpu.make_async_copy(hidden_ref, hidden, sems.at[half])
    rows_copy.start()
    copies = weight_copies(refs[:half], weight, f, half, sems)
    rows_copy.wait()
    new_len, width = hidden_ref.shape
    half_width = width // 2
    length = jnp.int32(0)
    for r in range(requests):
        length = length + jnp.where(where_ref[3 + r] == f, where_ref[3 + requests + r], 0)
    start = pl.multiple_of(where_ref[2] * half_width, 128)
    gain = gain_ref[:, pl.ds(start, half_width)]
    step = 32

    def norm(index, carry):
        at = pl.multiple_of(index * step, step)
        rows = hidden[pl.ds(at, step), :].astype(jnp.float32)
        scale = row_scale(rows)
        part = hidden[pl.ds(at, step), pl.ds(start, half_width)].astype(jnp.float32)
        normed[pl.ds(at, step), :] = (part * scale * gain).astype(jnp.bfloat16)
        return carry

    lax.fori_loop(0, new_len // step, norm, 0)
    position = lax.broadcasted_iota(jnp.int32, cos_ref.shape, 0) + length
    angle = position.astype(jnp.float32) * freq_ref[...]
    lane = lax.broadcasted_iota(jnp.int32, cos_ref.shape, 1)
    cos_ref[...] = jnp.cos(angle)
    sine = jnp.sin(angle)
    sin_ref[...] = jnp.where(lane < cos_ref.shape[1] // 2, -sine, sine)
    for copy in copies:
        copy.wait()
    for at in range(0, own_ref.shape[1], 512):
        own_ref[:, at : at + 512] = jnp.dot(
            normed[...], weight[:, at : at + 512], preferred_element_type=jnp.float32
        )


def capped(scores):
    return jnp.exp2(jnp.tanh(scores * (1.0 / softcap)) * (softcap * math.log2(math.e)))


def attend_kernel(
    kv_local,
    head_dim,
    where_ref,
    own,
    other_ref,
    cos_ref,
    sin_ref,
    valid_ref,
    page_ref,
    *refs,
):
    out_ref, keys, values, result, other, pages, sems = refs
    copies = [
        pltpu.make_async_copy(page_ref, pages, sems.at[0]),
        pltpu.make_async_copy(other_ref, other, sems.at[1]),
    ]
    for copy in copies:
        copy.start()
    new_len, q_cols = result.shape
    group = q_cols // (kv_local * head_dim)

    def sums(at):
        return own[:, at : at + head_dim] + other[:, at : at + head_dim].astype(jnp.float32)

    cosine, sine = cos_ref[...], sin_ref[...]

    def rope(vectors):
        return vectors * cosine + pltpu.roll(vectors, head_dim // 2, 1) * sine

    span = page_ref.shape[1]
    per = span // kv_local
    row = lax.broadcasted_iota(jnp.int32, (span, span), 0)
    column = lax.broadcasted_iota(jnp.int32, (span, span), 1)
    part = (column == (row % per) * kv_local + row // per).astype(jnp.bfloat16)
    place_at = 0
    copies[0].wait()
    for holder in range(pages.shape[0]):
        parted = jnp.dot(part, pages[holder], preferred_element_type=jnp.float32)
        parted = parted.astype(jnp.bfloat16)
        for g in range(kv_local):
            lines = parted[g * per : (g + 1) * per]
            keys[g, place_at : place_at + per, :] = lines[:, :head_dim]
            values[g, place_at : place_at + per, :] = lines[:, head_dim:]
        place_at += per

    copies[1].wait()
    span_keys = 2 * per
    t = lax.broadcasted_iota(jnp.int32, (group * new_len, new_len), 0) % new_len
    s = lax.broadcasted_iota(jnp.int32, (group * new_len, new_len), 1)
    causal = s <= t
    for g in range(kv_local):
        heads = [
            (rope(sums((g * group + j) * head_dim)) * query_scale).astype(jnp.bfloat16)
            for j in range(group)
        ]
        queries = jnp.concatenate(heads, axis=0)
        at = q_cols + g * head_dim
        new_key = rope(sums(at)).astype(jnp.bfloat16)
        new_value = sums(at + kv_local * head_dim).astype(jnp.bfloat16)

        def scores_of(key):
            return lax.dot_general(
                queries, key, (((1,), (1,)), ((), ())), preferred_element_type=jnp.float32
            )

        weights = jnp.where(causal, capped(scores_of(new_key)), 0.0)
        denom = jnp.sum(weights, axis=1, keepdims=True)
        numer = jnp.dot(
            weights.astype(jnp.bfloat16), new_value, preferred_element_type=jnp.float32
        )
        for start in range(0, place_at, span_keys):
            at = start // per
            valid = jnp.concatenate([valid_ref[at : at + 1], valid_ref[at + 1 : at + 2]], axis=1)
            valid = valid > 0.0
            weights = jnp.where(
                valid, capped(scores_of(keys[g, start : start + span_keys, :])), 0.0
            )
            denom = denom + jnp.sum(weights, axis=1, keepdims=True)
            numer = numer + jnp.dot(
                weights.astype(jnp.bfloat16),
                values[g, start : start + span_keys, :],
                preferred_element_type=jnp.float32,
            )
        attended = (numer / denom).astype(jnp.bfloat16)
        for j in range(group):
            to = (g * group + j) * head_dim
            result[:, to : to + head_dim] = attended[j * new_len : (j + 1) * new_len]
    quarter = out_ref.shape[1]
    for group_index in range(out_ref.shape[0]):
        start = group_index * quarter
        out_ref[group_index] = result[start : start + quarter, :]


def output_kernel(groups, shards, where_ref, *refs):
    f = where_ref[1]
    token_refs = refs[:shards]
    weight_ref = refs[shards]
    out_refs = refs[shards + 1 : 2 * shards + 1]
    total, tokens, weight, sems, token_sems = refs[2 * shards + 1 :]
    token_copies = [
        pltpu.make_async_copy(ref, tokens.at[e], token_sems.at[e])
        for e, ref in enumerate(token_refs)
    ]
    copies = [
        pltpu.make_async_copy(weight_ref.at[distance], weight.at[distance], sems.at[distance])
        for distance in range(groups)
    ]
    for copy in token_copies + copies:
        copy.start()
    for copy in token_copies:
        copy.wait()
    quarter = token_refs[0].shape[1]
    sub = quarter // shards
    projected = None
    for distance in range(groups):
        rows = jnp.concatenate([tokens[e, distance] for e in range(shards)], axis=0)
        copies[distance].wait()
        term = lax.dot_general(
            rows,
            weight[distance],
            (((1,), (1,)), ((), ())),
            preferred_element_type=jnp.float32,
        )
        projected = term if projected is None else projected + term
    total[...] = projected
    for e in range(shards):
        for distance, ref in enumerate(out_refs):
            start = pl.multiple_of(e * quarter + (f ^ distance) * sub, sub)
            ref[f ^ e] = total[pl.ds(start, sub), :].astype(jnp.bfloat16)


def finish_kernel(shards, where_ref, gain_ref, residual_ref, *refs):
    f = where_ref[1]
    piece_refs = refs[:shards]
    out_ref, projected = refs[shards:]
    for distance, ref in enumerate(piece_refs):
        projected[f ^ distance] = ref[...].astype(jnp.float32)
    gain = gain_ref[...]
    for request in range(out_ref.shape[0]):
        slot = where_ref[3 + request]
        line = jnp.concatenate([projected[k, slot] for k in range(shards)], axis=1)
        mean_square = jnp.mean(line * line, axis=1, keepdims=True)
        line = line * lax.rsqrt(mean_square + norm_eps) * gain
        out_ref[request] = (residual_ref[slot].astype(jnp.float32) + line).astype(jnp.bfloat16)


def pool_pieces(block, groups):
    return [block] + [swap(block, "pool", distance) for distance in range(1, groups)]


def local_small(
    hidden,
    slot_of_request,
    prefix_len,
    block_holder,
    block_slot,
    kv_pool,
    norm_gain,
    q_weight,
    k_weight,
    v_weight,
    o_weight,
    post_gain,
):
    shards = lax.axis_size("fsdp")
    groups = lax.axis_size("pool")
    f = lax.axis_index("fsdp")
    p = lax.axis_index("pool")
    half = shards // 2
    side = f // half
    new_len, width = hidden.shape[1:]
    requests = slot_of_request.shape[0]
    page_len = kv_pool.shape[1]
    kv_local = kv_pool.shape[2]
    head_dim = kv_pool.shape[3] // 2
    q_cols = q_weight.shape[1]
    kv_cols = k_weight.shape[1]
    max_blocks = block_holder.shape[1]
    per_holder = max_blocks // shards
    quarter = new_len // groups
    sub = quarter // shards
    features = o_weight.shape[0]
    bf16, f32 = jnp.bfloat16, jnp.float32
    where = jnp.concatenate(
        [jnp.stack([p, f, side]).astype(jnp.int32), slot_of_request, prefix_len]
    )
    shape = jax.ShapeDtypeStruct
    gain = norm_gain.reshape(1, width)
    rows = hidden[0]

    leaving, my_quarter, joined = call(
        prologue_kernel,
        [
            shape((quarter, width // 2), bf16),
            shape((quarter, width), bf16),
            shape((features, q_cols + 2 * kv_cols), bf16),
        ],
        [pltpu.VMEM((quarter, width), f32), pltpu.SemaphoreType.DMA((4,))],
        quarter * width * 8,
        4 * features * kv_cols,
        rows,
        norm_gain,
        q_weight,
        k_weight,
        v_weight,
        specs=[HBM, VMEM, HBM, HBM, HBM],
        out_specs=[VMEM, VMEM, HBM],
    )
    partner_piece = swap(leaving, "fsdp", half)

    near, far = swap(joined, "fsdp", 1), swap(joined, "fsdp", 2)

    flat_pool = kv_pool.reshape(kv_pool.shape[0], page_len * kv_local, 2 * head_dim)
    page_rows = per_holder * page_len * kv_local
    outgoing, valid = call(
        functools.partial(pages_kernel, requests, page_len),
        [
            shape((shards, page_rows, 2 * head_dim), bf16),
            shape((shards, per_holder * page_len), f32),
        ],
        [
            pltpu.SMEM((2 * per_holder,), jnp.int32),
            pltpu.SMEM((max_blocks + per_holder,), jnp.int32),
            pltpu.SMEM((shards,), jnp.int32),
        ],
        1 << 20,
        1 << 21,
        where,
        block_holder,
        block_slot,
        flat_pool,
        specs=[SMEM, SMEM, SMEM, VMEM],
    )
    partner_piece, near, far, outgoing, valid = lax.optimization_barrier(
        (partner_piece, near, far, outgoing, valid)
    )
    weights = [joined, near, far, swap(far, "fsdp", 1)]
    partner_pieces = pool_pieces(partner_piece, groups)
    arrived = lax.all_to_all(outgoing, "fsdp", split_axis=0, concat_axis=0, tiled=True)
    out_weight = lax.all_gather(after(o_weight, *partner_pieces), "pool", axis=0, tiled=False)

    residual = lax.all_to_all(
        after(my_quarter, arrived).reshape(shards, sub, width),
        "fsdp",
        split_axis=0,
        concat_axis=0,
        tiled=True,
    )

    partial = call(
        functools.partial(partner_kernel, groups, half),
        shape((new_len, q_cols + 2 * kv_cols), bf16),
        [
            pltpu.VMEM((new_len, width // 2), bf16),
            pltpu.VMEM((width // 2, q_cols + 2 * kv_cols), bf16),
            pltpu.SemaphoreType.DMA((groups,)),
            pltpu.SemaphoreType.DMA((half,)),
        ],
        new_len * width * (q_cols + 2 * kv_cols),
        width * (new_len + q_cols + 2 * kv_cols),
        where,
        *partner_pieces,
        *weights,
        specs=[SMEM] + [HBM] * (groups + half),
    )
    other = swap(partial, "fsdp", half)
    freqs = np.exp(np.arange(head_dim // 2) * (-2.0 * math.log(10000.0) / head_dim))
    freqs = np.concatenate([freqs, freqs]).astype(np.float32).reshape(1, head_dim)
    own, cosine, sine = call(
        functools.partial(own_kernel, requests, half),
        [
            shape((new_len, q_cols + 2 * kv_cols), f32),
            shape((new_len, head_dim), f32),
            shape((new_len, head_dim), f32),
        ],
        [
            pltpu.VMEM((new_len, width), bf16),
            pltpu.VMEM((new_len, width // 2), bf16),
            pltpu.VMEM((width // 2, q_cols + 2 * kv_cols), bf16),
            pltpu.SemaphoreType.DMA((half + 1,)),
        ],
        new_len * width * (q_cols + 2 * kv_cols),
        width * (2 * new_len + q_cols + 2 * kv_cols),
        where,
        after(rows, partial),
        gain,
        freqs,
        *weights,
        specs=[SMEM, HBM, VMEM, VMEM] + [HBM] * half,
    )

    keys_total = max_blocks * page_len
    quarters = call(
        functools.partial(attend_kernel, kv_local, head_dim),
        shape((groups, quarter, q_cols), bf16),
        [
            pltpu.VMEM((kv_local, keys_total, head_dim), bf16),
            pltpu.VMEM((kv_local, keys_total, head_dim), bf16),
            pltpu.VMEM((new_len, q_cols), bf16),
            pltpu.VMEM(other.shape, bf16),
            pltpu.VMEM(arrived.shape, bf16),
            pltpu.SemaphoreType.DMA((2,)),
        ],
        4 * new_len * q_cols * (keys_total + new_len),
        1 << 22,
        where,
        own,
        other,
        cosine,
        sine,
        valid,
        arrived,
        specs=[SMEM, VMEM, HBM, VMEM, VMEM, VMEM, HBM],
    )

    quarters = lax.all_to_all(quarters, "pool", split_axis=0, concat_axis=0, tiled=True)
    tokens = {0: quarters}
    for distance in range(2, shards, 2):
        tokens[distance] = swap(quarters, "fsdp", distance)
    for distance in range(0, shards, 2):
        tokens[distance ^ 1] = swap(tokens[distance], "fsdp", 1)
    projected = call(
        functools.partial(output_kernel, groups, shards),
        [shape((shards, sub, features), bf16)] * shards,
        [
            pltpu.VMEM((shards * quarter, features), f32),
            pltpu.VMEM((shards, groups, quarter, q_cols), bf16),
            pltpu.VMEM((groups, features, q_cols), bf16),
            pltpu.SemaphoreType.DMA((groups,)),
            pltpu.SemaphoreType.DMA((shards,)),
        ],
        2 * shards * quarter * features * groups * q_cols,
        1 << 22,
        where,
        *[tokens[distance] for distance in range(shards)],
        out_weight,
        specs=[SMEM] + [HBM] * (shards + 1),
    )
    finished = [
        swap(piece, "fsdp", distance) if distance else piece
        for distance, piece in enumerate(projected)
    ]
    return call(
        functools.partial(finish_kernel, shards),
        shape((requests, sub, width), bf16),
        [pltpu.VMEM((shards, shards, sub, features), f32)],
        1 << 20,
        1 << 20,
        where,
        post_gain.reshape(1, width),
        residual,
        *finished,
    )


def local(*arguments):
    return local_small(*arguments) if lax.axis_size("fsdp") == 8 else local_general(*arguments)


def solution(mesh):
    in_specs = (
        P("fsdp", None, None),
        P(),
        P(),
        P(),
        P(),
        P("fsdp", None, "pool", None),
        P(),
        P("fsdp", "pool"),
        P("fsdp", "pool"),
        P("fsdp", "pool"),
        P("fsdp", "pool"),
        P(),
    )
    out_specs = P(None, ("pool", "fsdp"), None)
    return jax.shard_map(local, mesh=mesh, in_specs=in_specs, out_specs=out_specs, check_vma=False)
```

```python
import functools
import math

import jax
import jax.numpy as jnp
import numpy as np
from jax import lax
from jax.experimental import pallas as pl
from jax.experimental.pallas import tpu as pltpu
from jax.sharding import PartitionSpec as P

softcap = 50.0
query_scale = 144.0 ** (-0.5)
norm_eps = 1e-06


def rms_scale(rows, gain):
    mean_square = jnp.mean(rows * rows, axis=-1, keepdims=True)
    return rows * lax.rsqrt(mean_square + norm_eps) * gain


def rotate(vectors, cosine, sine):
    half = vectors.shape[-1] // 2
    first = vectors[..., :half]
    second = vectors[..., half:]
    return jnp.concatenate(
        [first * cosine - second * sine, second * cosine + first * sine], axis=-1
    )


def capped_weights(scores, valid):
    return jnp.where(valid, jnp.exp(softcap * jnp.tanh(scores / softcap)), 0.0)


def swap(array, axis, distance):
    size = lax.axis_size(axis)
    return lax.ppermute(array, axis, [(i, i ^ distance) for i in range(size)])


def place(pieces, index):
    first = pieces[0]
    stacked = jnp.zeros((len(pieces),) + first.shape, first.dtype)
    for distance, piece in pieces.items():
        stacked = lax.dynamic_update_index_in_dim(stacked, piece, index ^ distance, 0)
    return stacked


def exchange(chunks, axis):
    size = lax.axis_size(axis)
    index = lax.axis_index(axis)
    if size > 8:
        return lax.all_to_all(chunks, axis, split_axis=0, concat_axis=0, tiled=True)
    pieces = {}
    for distance in range(size):
        chunk = lax.dynamic_index_in_dim(chunks, index ^ distance, 0, keepdims=False)
        pieces[distance] = swap(chunk, axis, distance) if distance else chunk
    return place(pieces, index)


def doubled(block, axis, span):
    pieces = {0: block}
    bit = span // 2
    while bit:
        for distance in list(pieces):
            pieces[distance ^ bit] = swap(pieces[distance], axis, bit)
        bit //= 2
    return pieces


def attend(queries, keys_new, values_new, cached, cached_valid):
    new_len, kv_local, group, head_dim = queries.shape

    def part(keys, values, valid):
        scores = jnp.einsum("tgjd,kgd->gjtk", queries, keys, preferred_element_type=jnp.float32)
        weights = capped_weights(scores, valid)
        numer = jnp.einsum(
            "gjtk,kgd->gjtd",
            weights.astype(jnp.bfloat16),
            values,
            preferred_element_type=jnp.float32,
        )
        return numer, jnp.sum(weights, axis=-1)

    query_index = jnp.arange(new_len, dtype=jnp.int32)
    causal = query_index[None, :] <= query_index[:, None]
    numer, denom = part(
        cached[..., :head_dim], cached[..., head_dim:], cached_valid[None, None, None, :]
    )
    more, added = part(keys_new, values_new, causal[None, None])
    attended = ((numer + more) / (denom + added)[..., None]).transpose(2, 0, 1, 3)
    return attended.reshape(new_len, kv_local * group * head_dim).astype(jnp.bfloat16)


def local_general(
    hidden,
    slot_of_request,
    prefix_len,
    block_holder,
    block_slot,
    kv_pool,
    norm_gain,
    q_weight,
    k_weight,
    v_weight,
    o_weight,
    post_gain,
):
    shards = lax.axis_size("fsdp")
    groups = lax.axis_size("pool")
    f = lax.axis_index("fsdp")
    p = lax.axis_index("pool")
    half = shards // 2
    side = f // half
    new_len, width = hidden.shape[1:]
    requests = slot_of_request.shape[0]
    page_len = kv_pool.shape[1]
    kv_local = kv_pool.shape[2]
    head_dim = kv_pool.shape[3] // 2
    q_cols = q_weight.shape[1]
    kv_cols = k_weight.shape[1]
    group = q_cols // kv_cols
    max_blocks = block_holder.shape[1]
    per_holder = max_blocks // shards
    quarter = new_len // groups
    sub = quarter // shards
    features = o_weight.shape[0]

    kv_pieces = doubled(jnp.concatenate([k_weight, v_weight], axis=1), "fsdp", half)
    q_pieces = doubled(q_weight, "fsdp", half)
    out_weight = lax.all_gather(o_weight, "pool", axis=0, tiled=False)

    rows = hidden[0]
    normed = rms_scale(rows.astype(jnp.float32), norm_gain).astype(jnp.bfloat16)
    own_rows = lax.dynamic_slice(normed, (0, side * (width // 2)), (new_len, width // 2))
    leaving = lax.dynamic_slice(
        normed, (p * quarter, (1 - side) * (width // 2)), (quarter, width // 2)
    )
    partner_piece = swap(leaving, "fsdp", half)
    partner_pieces = {0: partner_piece}
    for distance in range(1, groups):
        partner_pieces[distance] = swap(partner_piece, "pool", distance)
    partner_rows = place(partner_pieces, p).reshape(new_len, width // 2)

    request_ids = jnp.arange(requests, dtype=jnp.int32)
    request_at_slot = jnp.sum(
        jnp.where(slot_of_request[None, :] == request_ids[:, None], request_ids[None, :], 0), axis=1
    )
    holder_by_slot = jnp.take(block_holder, request_at_slot, axis=0)
    page_by_slot = jnp.take(block_slot, request_at_slot, axis=0)
    held_here = holder_by_slot == f
    held_rank = jnp.cumsum(held_here.astype(jnp.int32), axis=1) - 1
    rank_ids = jnp.arange(per_holder, dtype=jnp.int32)
    picked = held_here[:, :, None] & (held_rank[:, :, None] == rank_ids[None, None, :])
    local_pages = jnp.sum(jnp.where(picked, page_by_slot[:, :, None], 0), axis=1)
    flat_pool = kv_pool.reshape(kv_pool.shape[0], page_len * kv_local, 2 * head_dim)
    outgoing = jnp.take(flat_pool, local_pages, axis=0)
    outgoing = outgoing.reshape(shards, per_holder * page_len * kv_local, 2 * head_dim)
    arrived = exchange(outgoing, "fsdp")
    cached = arrived.reshape(max_blocks * page_len, kv_local, 2 * head_dim)

    my_request = lax.dynamic_index_in_dim(request_at_slot, f, keepdims=False)
    my_length = prefix_len[my_request]
    my_holders = block_holder[my_request]
    entry_ids = jnp.arange(max_blocks, dtype=jnp.int32)
    mine = my_holders[None, :] == jnp.arange(shards, dtype=jnp.int32)[:, None]
    my_rank = jnp.cumsum(mine.astype(jnp.int32), axis=1) - 1
    chosen = mine[:, None, :] & (my_rank[:, None, :] == rank_ids[None, :, None])
    entry = jnp.sum(jnp.where(chosen, entry_ids[None, None, :], 0), axis=2)
    cached_position = entry.reshape(-1, 1) * page_len + jnp.arange(page_len, dtype=jnp.int32)
    cached_valid = (cached_position < my_length).reshape(-1)

    residual_out = lax.dynamic_slice_in_dim(rows, p * quarter, quarter, 0).reshape(
        shards, sub, width
    )
    residual = exchange(residual_out, "fsdp")

    positions = (my_length + jnp.arange(new_len, dtype=jnp.int32)).astype(jnp.float32)
    freqs = jnp.exp(
        jnp.arange(head_dim // 2, dtype=jnp.float32) * (-2.0 * math.log(10000.0) / head_dim)
    )
    angles = positions[:, None] * freqs
    cosine = jnp.cos(angles)[:, None, :]
    sine = jnp.sin(angles)[:, None, :]

    def project(pieces):
        weight = place(pieces, f % half).reshape(width // 2, -1)
        partial = jnp.dot(partner_rows, weight, preferred_element_type=jnp.float32)
        other = swap(partial.astype(jnp.bfloat16), "fsdp", half)
        own = jnp.dot(own_rows, weight, preferred_element_type=jnp.float32)
        return own + other.astype(jnp.float32)

    kv_sum = project(kv_pieces)
    q_sum = project(q_pieces)
    queries = rotate(q_sum.reshape(new_len, kv_local * group, head_dim), cosine, sine)
    queries = (queries * query_scale).astype(jnp.bfloat16)
    queries = queries.reshape(new_len, kv_local, group, head_dim)
    keys_new = kv_sum[:, :kv_cols].reshape(new_len, kv_local, head_dim)
    keys_new = rotate(keys_new, cosine, sine).astype(jnp.bfloat16)
    values_new = kv_sum[:, kv_cols:].astype(jnp.bfloat16).reshape(new_len, kv_local, head_dim)
    attended = attend(queries, keys_new, values_new, cached, cached_valid)

    quarters = exchange(attended.reshape(groups, quarter, q_cols), "pool")
    token_pieces = {0: quarters}
    for distance in range(2, shards, 2):
        token_pieces[distance] = swap(quarters, "fsdp", distance)
    for distance in range(0, shards, 2):
        token_pieces[distance ^ 1] = swap(token_pieces[distance], "fsdp", 1)
    tokens = place(token_pieces, f)
    projected = jnp.einsum(
        "sptc,pfc->stf", tokens, out_weight, preferred_element_type=jnp.float32
    ).astype(jnp.bfloat16)
    projected = projected.reshape(shards, shards, sub, features).transpose(1, 0, 2, 3)
    finished = exchange(projected, "fsdp").transpose(1, 2, 0, 3).reshape(shards, sub, width)
    finished = residual.astype(jnp.float32) + rms_scale(finished.astype(jnp.float32), post_gain)
    return jnp.take(finished.astype(jnp.bfloat16), slot_of_request, axis=0)


VMEM = pl.BlockSpec(memory_space=pltpu.VMEM)
SMEM = pl.BlockSpec(memory_space=pltpu.SMEM)
HBM = pl.BlockSpec(memory_space=pltpu.HBM)


def call(kernel, outs, scratch, flops, nbytes, *operands, specs=None, out_specs=None):
    return pl.pallas_call(
        kernel,
        out_shape=outs,
        in_specs=specs or [SMEM] + [VMEM] * (len(operands) - 1),
        out_specs=out_specs or jax.tree.map(lambda _: VMEM, outs),
        scratch_shapes=scratch,
        compiler_params=pltpu.CompilerParams(vmem_limit_bytes=60 << 20),
        cost_estimate=pl.CostEstimate(flops=flops, bytes_accessed=nbytes, transcendentals=0),
    )(*operands)


def after(array, *earlier):
    return lax.optimization_barrier((array,) + earlier)[0]


def weight_copies(weight_refs, weight, f, half, sems):
    copies = []
    for distance, ref in enumerate(weight_refs):
        count = ref.shape[0]
        start = pl.multiple_of(((f ^ distance) & (half - 1)) * count, 64)
        copies.append(
            pltpu.make_async_copy(ref, weight.at[pl.ds(start, count), :], sems.at[distance])
        )
        copies[-1].start()
    return copies


def partner_kernel(groups, half, where_ref, *refs):
    p, f = where_ref[0], where_ref[1]
    x_refs, w_refs = refs[:groups], refs[groups : groups + half]
    out_ref, rows, weight, x_sems, w_sems = refs[groups + half :]
    quarter = x_refs[0].shape[0]
    copies = weight_copies(w_refs, weight, f, half, w_sems)
    for distance, ref in enumerate(x_refs):
        start = pl.multiple_of((p ^ distance) * quarter, quarter)
        copies.append(
            pltpu.make_async_copy(ref, rows.at[pl.ds(start, quarter), :], x_sems.at[distance])
        )
        copies[-1].start()
    for copy in copies:
        copy.wait()
    for at in range(0, out_ref.shape[1], 512):
        out_ref[:, at : at + 512] = jnp.dot(
            rows[...], weight[:, at : at + 512], preferred_element_type=jnp.float32
        ).astype(jnp.bfloat16)


def row_scale(rows):
    return lax.rsqrt(jnp.mean(rows * rows, axis=1, keepdims=True) + norm_eps)


def prologue_kernel(
    hidden_ref, gain_ref, q_ref, k_ref, v_ref, leaving_ref, rows_ref, weight_ref, normed, sem
):
    p, f = lax.axis_index("pool"), lax.axis_index("fsdp")
    side = f // (lax.axis_size("fsdp") // 2)
    quarter, width = rows_ref.shape
    half_width = width // 2
    start = pl.multiple_of(p * quarter, quarter)
    rows_copy = pltpu.make_async_copy(hidden_ref.at[pl.ds(start, quarter), :], rows_ref, sem)
    rows_copy.start()
    at = 0
    for ref in (q_ref, k_ref, v_ref):
        weight_ref[:, at : at + ref.shape[1]] = ref[...]
        at += ref.shape[1]
    rows_copy.wait()
    rows = rows_ref[...].astype(jnp.float32)
    normed[...] = rows * row_scale(rows) * gain_ref[...].reshape(1, width)
    away = pl.multiple_of((1 - side) * half_width, 128)
    leaving_ref[...] = normed[:, pl.ds(away, half_width)].astype(jnp.bfloat16)


def pages_kernel(
    requests, page_len, where_ref, holder_ref, slot_ref, pool_ref, out_ref, valid_ref, listed, entries, counts
):
    f = where_ref[1]
    max_blocks = holder_ref.shape[1]
    shards, _, _ = out_ref.shape
    per = max_blocks // shards
    page_rows = pool_ref.shape[1]
    length, mine = jnp.int32(0), jnp.int32(0)
    for r in range(requests):
        at = where_ref[3 + r] == f
        length = length + jnp.where(at, where_ref[3 + requests + r], 0)
        mine = mine + jnp.where(at, r, 0)
    for r in range(requests):
        slot = where_ref[3 + r]

        def note(j, count):
            listed[count] = slot_ref[r, j]
            return count + jnp.where(holder_ref[r, j] == f, 1, 0)

        lax.fori_loop(0, max_blocks, note, jnp.int32(0), unroll=8)
        for k in range(per):
            out_ref[slot, k * page_rows : (k + 1) * page_rows, :] = pool_ref[listed[k]]
    for h in range(shards):
        counts[h] = 0

    def enter(j, carry):
        h = holder_ref[mine, j]
        count = counts[h]
        entries[h * per + count] = j
        counts[h] = count + 1
        return carry

    lax.fori_loop(0, max_blocks, enter, 0, unroll=4)
    row = lax.broadcasted_iota(jnp.int32, valid_ref.shape, 0)
    lane = lax.broadcasted_iota(jnp.int32, valid_ref.shape, 1)
    place_in = row * per + lane // page_len
    entry = jnp.zeros(valid_ref.shape, jnp.int32)
    for at in range(max_blocks):
        entry = jnp.where(place_in == at, entries[at], entry)
    position = entry * page_len + lane % page_len
    valid_ref[...] = jnp.where(position < length, 1.0, 0.0)


def own_kernel(requests, half, where_ref, hidden_ref, gain_ref, freq_ref, *refs):
    f = where_ref[1]
    own_ref, cos_ref, sin_ref, hidden, normed, weight, sems = refs[half:]
    rows_copy = pltpu.make_async_copy(hidden_ref, hidden, sems.at[half])
    rows_copy.start()
    copies = weight_copies(refs[:half], weight, f, half, sems)
    rows_copy.wait()
    new_len, width = hidden_ref.shape
    half_width = width // 2
    length = jnp.int32(0)
    for r in range(requests):
        length = length + jnp.where(where_ref[3 + r] == f, where_ref[3 + requests + r], 0)
    start = pl.multiple_of(where_ref[2] * half_width, 128)
    gain = gain_ref[:, pl.ds(start, half_width)]
    step = 32

    def norm(index, carry):
        at = pl.multiple_of(index * step, step)
        rows = hidden[pl.ds(at, step), :].astype(jnp.float32)
        scale = row_scale(rows)
        part = hidden[pl.ds(at, step), pl.ds(start, half_width)].astype(jnp.float32)
        normed[pl.ds(at, step), :] = (part * scale * gain).astype(jnp.bfloat16)
        return carry

    lax.fori_loop(0, new_len // step, norm, 0)
    position = lax.broadcasted_iota(jnp.int32, cos_ref.shape, 0) + length
    angle = position.astype(jnp.float32) * freq_ref[...]
    lane = lax.broadcasted_iota(jnp.int32, cos_ref.shape, 1)
    cos_ref[...] = jnp.cos(angle)
    sine = jnp.sin(angle)
    sin_ref[...] = jnp.where(lane < cos_ref.shape[1] // 2, -sine, sine)
    for copy in copies:
        copy.wait()
    for at in range(0, own_ref.shape[1], 512):
        own_ref[:, at : at + 512] = jnp.dot(
            normed[...], weight[:, at : at + 512], preferred_element_type=jnp.float32
        )


def capped(scores):
    return jnp.exp2(jnp.tanh(scores * (1.0 / softcap)) * (softcap * math.log2(math.e)))


def attend_kernel(
    groups,
    kv_local,
    head_dim,
    where_ref,
    own,
    other_ref,
    cos_ref,
    sin_ref,
    valid_ref,
    page_ref,
    *refs,
):
    p = where_ref[0]
    out_refs = refs[:groups]
    keys, values, result, other, pages, sems = refs[groups:]
    copies = [
        pltpu.make_async_copy(page_ref, pages, sems.at[0]),
        pltpu.make_async_copy(other_ref, other, sems.at[1]),
    ]
    for copy in copies:
        copy.start()
    new_len, q_cols = result.shape
    group = q_cols // (kv_local * head_dim)

    def sums(at):
        return own[:, at : at + head_dim] + other[:, at : at + head_dim].astype(jnp.float32)

    cosine, sine = cos_ref[...], sin_ref[...]

    def rope(vectors):
        return vectors * cosine + pltpu.roll(vectors, head_dim // 2, 1) * sine

    span = page_ref.shape[1]
    per = span // kv_local
    row = lax.broadcasted_iota(jnp.int32, (span, span), 0)
    column = lax.broadcasted_iota(jnp.int32, (span, span), 1)
    part = (column == (row % per) * kv_local + row // per).astype(jnp.bfloat16)
    place_at = 0
    copies[0].wait()
    for holder in range(pages.shape[0]):
        parted = jnp.dot(part, pages[holder], preferred_element_type=jnp.float32)
        parted = parted.astype(jnp.bfloat16)
        for g in range(kv_local):
            lines = parted[g * per : (g + 1) * per]
            keys[g, place_at : place_at + per, :] = lines[:, :head_dim]
            values[g, place_at : place_at + per, :] = lines[:, head_dim:]
        place_at += per

    copies[1].wait()
    span_keys = 2 * per
    t = lax.broadcasted_iota(jnp.int32, (group * new_len, new_len), 0) % new_len
    s = lax.broadcasted_iota(jnp.int32, (group * new_len, new_len), 1)
    causal = s <= t
    for g in range(kv_local):
        heads = [
            (rope(sums((g * group + j) * head_dim)) * query_scale).astype(jnp.bfloat16)
            for j in range(group)
        ]
        queries = jnp.concatenate(heads, axis=0)
        at = q_cols + g * head_dim
        new_key = rope(sums(at)).astype(jnp.bfloat16)
        new_value = sums(at + kv_local * head_dim).astype(jnp.bfloat16)

        def scores_of(key):
            return lax.dot_general(
                queries, key, (((1,), (1,)), ((), ())), preferred_element_type=jnp.float32
            )

        weights = jnp.where(causal, capped(scores_of(new_key)), 0.0)
        denom = jnp.sum(weights, axis=1, keepdims=True)
        numer = jnp.dot(
            weights.astype(jnp.bfloat16), new_value, preferred_element_type=jnp.float32
        )
        for start in range(0, place_at, span_keys):
            at = start // per
            valid = jnp.concatenate([valid_ref[at : at + 1], valid_ref[at + 1 : at + 2]], axis=1)
            valid = valid > 0.0
            weights = jnp.where(
                valid, capped(scores_of(keys[g, start : start + span_keys, :])), 0.0
            )
            denom = denom + jnp.sum(weights, axis=1, keepdims=True)
            numer = numer + jnp.dot(
                weights.astype(jnp.bfloat16),
                values[g, start : start + span_keys, :],
                preferred_element_type=jnp.float32,
            )
        attended = (numer / denom).astype(jnp.bfloat16)
        for j in range(group):
            to = (g * group + j) * head_dim
            result[:, to : to + head_dim] = attended[j * new_len : (j + 1) * new_len]
    quarter = new_len // groups
    for distance, ref in enumerate(out_refs):
        start = pl.multiple_of((p ^ distance) * quarter, quarter)
        ref[...] = result[pl.ds(start, quarter), :]


def output_kernel(groups, shards, where_ref, *refs):
    p, f = where_ref[0], where_ref[1]
    token_refs = refs[:shards]
    weight_ref = refs[shards]
    out_refs = refs[shards + 1 : 2 * shards + 1]
    total, tokens, weight, sems, token_sems = refs[2 * shards + 1 :]
    token_copies = [
        pltpu.make_async_copy(ref, tokens.at[e], token_sems.at[e])
        for e, ref in enumerate(token_refs)
    ]
    copies = [
        pltpu.make_async_copy(weight_ref.at[p ^ distance], weight.at[distance], sems.at[distance])
        for distance in range(groups)
    ]
    for copy in token_copies + copies:
        copy.start()
    for copy in token_copies:
        copy.wait()
    quarter = token_refs[0].shape[1]
    sub = quarter // shards
    projected = None
    for distance in range(groups):
        rows = jnp.concatenate([tokens[e, distance] for e in range(shards)], axis=0)
        copies[distance].wait()
        term = lax.dot_general(
            rows,
            weight[distance],
            (((1,), (1,)), ((), ())),
            preferred_element_type=jnp.float32,
        )
        projected = term if projected is None else projected + term
    total[...] = projected
    for e in range(shards):
        for distance, ref in enumerate(out_refs):
            start = pl.multiple_of(e * quarter + (f ^ distance) * sub, sub)
            ref[f ^ e] = total[pl.ds(start, sub), :].astype(jnp.bfloat16)


def finish_kernel(shards, where_ref, gain_ref, residual_ref, *refs):
    f = where_ref[1]
    piece_refs = refs[:shards]
    out_ref, projected = refs[shards:]
    for distance, ref in enumerate(piece_refs):
        projected[f ^ distance] = ref[...].astype(jnp.float32)
    gain = gain_ref[...]
    for request in range(out_ref.shape[0]):
        slot = where_ref[3 + request]
        line = jnp.concatenate([projected[k, slot] for k in range(shards)], axis=1)
        mean_square = jnp.mean(line * line, axis=1, keepdims=True)
        line = line * lax.rsqrt(mean_square + norm_eps) * gain
        out_ref[request] = (residual_ref[slot].astype(jnp.float32) + line).astype(jnp.bfloat16)


def pool_pieces(block, groups):
    return [block] + [swap(block, "pool", distance) for distance in range(1, groups)]


def local_small(
    hidden,
    slot_of_request,
    prefix_len,
    block_holder,
    block_slot,
    kv_pool,
    norm_gain,
    q_weight,
    k_weight,
    v_weight,
    o_weight,
    post_gain,
):
    shards = lax.axis_size("fsdp")
    groups = lax.axis_size("pool")
    f = lax.axis_index("fsdp")
    p = lax.axis_index("pool")
    half = shards // 2
    side = f // half
    new_len, width = hidden.shape[1:]
    requests = slot_of_request.shape[0]
    page_len = kv_pool.shape[1]
    kv_local = kv_pool.shape[2]
    head_dim = kv_pool.shape[3] // 2
    q_cols = q_weight.shape[1]
    kv_cols = k_weight.shape[1]
    max_blocks = block_holder.shape[1]
    per_holder = max_blocks // shards
    quarter = new_len // groups
    sub = quarter // shards
    features = o_weight.shape[0]
    bf16, f32 = jnp.bfloat16, jnp.float32
    where = jnp.concatenate(
        [jnp.stack([p, f, side]).astype(jnp.int32), slot_of_request, prefix_len]
    )
    shape = jax.ShapeDtypeStruct
    gain = norm_gain.reshape(1, width)
    rows = hidden[0]

    leaving, my_quarter, joined = call(
        prologue_kernel,
        [
            shape((quarter, width // 2), bf16),
            shape((quarter, width), bf16),
            shape((features, q_cols + 2 * kv_cols), bf16),
        ],
        [pltpu.VMEM((quarter, width), f32), pltpu.SemaphoreType.DMA],
        quarter * width * 8,
        4 * features * kv_cols,
        rows,
        norm_gain,
        q_weight,
        k_weight,
        v_weight,
        specs=[HBM, VMEM, VMEM, VMEM, VMEM],
    )
    partner_piece = swap(leaving, "fsdp", half)

    near, far = swap(joined, "fsdp", 1), swap(joined, "fsdp", 2)

    flat_pool = kv_pool.reshape(kv_pool.shape[0], page_len * kv_local, 2 * head_dim)
    page_rows = per_holder * page_len * kv_local
    outgoing, valid = call(
        functools.partial(pages_kernel, requests, page_len),
        [
            shape((shards, page_rows, 2 * head_dim), bf16),
            shape((shards, per_holder * page_len), f32),
        ],
        [
            pltpu.SMEM((2 * per_holder,), jnp.int32),
            pltpu.SMEM((max_blocks + per_holder,), jnp.int32),
            pltpu.SMEM((shards,), jnp.int32),
        ],
        1 << 20,
        1 << 21,
        where,
        block_holder,
        block_slot,
        flat_pool,
        specs=[SMEM, SMEM, SMEM, VMEM],
    )
    partner_pieces = pool_pieces(partner_piece, groups)
    partner_pieces, near, far, outgoing, valid = lax.optimization_barrier(
        (partner_pieces, near, far, outgoing, valid)
    )
    weights = [joined, near, far, swap(far, "fsdp", 1)]
    arrived = lax.all_to_all(outgoing, "fsdp", split_axis=0, concat_axis=0, tiled=True)
    out_weight = lax.all_gather(after(o_weight, *partner_pieces), "pool", axis=0, tiled=False)

    partial = call(
        functools.partial(partner_kernel, groups, half),
        shape((new_len, q_cols + 2 * kv_cols), bf16),
        [
            pltpu.VMEM((new_len, width // 2), bf16),
            pltpu.VMEM((width // 2, q_cols + 2 * kv_cols), bf16),
            pltpu.SemaphoreType.DMA((groups,)),
            pltpu.SemaphoreType.DMA((half,)),
        ],
        new_len * width * (q_cols + 2 * kv_cols),
        width * (new_len + q_cols + 2 * kv_cols),
        where,
        *partner_pieces,
        *weights,
        specs=[SMEM] + [HBM] * (groups + half),
    )
    other = swap(partial, "fsdp", half)
    freqs = np.exp(np.arange(head_dim // 2) * (-2.0 * math.log(10000.0) / head_dim))
    freqs = np.concatenate([freqs, freqs]).astype(np.float32).reshape(1, head_dim)
    own, cosine, sine = call(
        functools.partial(own_kernel, requests, half),
        [
            shape((new_len, q_cols + 2 * kv_cols), f32),
            shape((new_len, head_dim), f32),
            shape((new_len, head_dim), f32),
        ],
        [
            pltpu.VMEM((new_len, width), bf16),
            pltpu.VMEM((new_len, width // 2), bf16),
            pltpu.VMEM((width // 2, q_cols + 2 * kv_cols), bf16),
            pltpu.SemaphoreType.DMA((half + 1,)),
        ],
        new_len * width * (q_cols + 2 * kv_cols),
        width * (2 * new_len + q_cols + 2 * kv_cols),
        where,
        after(rows, partial),
        gain,
        freqs,
        *weights,
        specs=[SMEM, HBM, VMEM, VMEM] + [HBM] * half,
    )

    residual = lax.all_to_all(
        after(my_quarter, other, arrived).reshape(shards, sub, width),
        "fsdp",
        split_axis=0,
        concat_axis=0,
        tiled=True,
    )

    keys_total = max_blocks * page_len
    quarters = call(
        functools.partial(attend_kernel, groups, kv_local, head_dim),
        [shape((quarter, q_cols), bf16)] * groups,
        [
            pltpu.VMEM((kv_local, keys_total, head_dim), bf16),
            pltpu.VMEM((kv_local, keys_total, head_dim), bf16),
            pltpu.VMEM((new_len, q_cols), bf16),
            pltpu.VMEM(other.shape, bf16),
            pltpu.VMEM(arrived.shape, bf16),
            pltpu.SemaphoreType.DMA((2,)),
        ],
        4 * new_len * q_cols * (keys_total + new_len),
        1 << 22,
        where,
        own,
        other,
        cosine,
        sine,
        valid,
        arrived,
        specs=[SMEM, VMEM, HBM, VMEM, VMEM, VMEM, HBM],
    )

    quarters = [
        swap(piece, "pool", distance) if distance else piece
        for distance, piece in enumerate(quarters)
    ]
    quarters = jnp.stack(quarters)
    tokens = {0: quarters}
    for distance in range(2, shards, 2):
        tokens[distance] = swap(quarters, "fsdp", distance)
    for distance in range(0, shards, 2):
        tokens[distance ^ 1] = swap(tokens[distance], "fsdp", 1)
    projected = call(
        functools.partial(output_kernel, groups, shards),
        [shape((shards, sub, features), bf16)] * shards,
        [
            pltpu.VMEM((shards * quarter, features), f32),
            pltpu.VMEM((shards, groups, quarter, q_cols), bf16),
            pltpu.VMEM((groups, features, q_cols), bf16),
            pltpu.SemaphoreType.DMA((groups,)),
            pltpu.SemaphoreType.DMA((shards,)),
        ],
        2 * shards * quarter * features * groups * q_cols,
        1 << 22,
        where,
        *[tokens[distance] for distance in range(shards)],
        out_weight,
        specs=[SMEM] + [HBM] * (shards + 1),
    )
    finished = [
        swap(piece, "fsdp", distance) if distance else piece
        for distance, piece in enumerate(projected)
    ]
    return call(
        functools.partial(finish_kernel, shards),
        shape((requests, sub, width), bf16),
        [pltpu.VMEM((shards, shards, sub, features), f32)],
        1 << 20,
        1 << 20,
        where,
        post_gain.reshape(1, width),
        residual,
        *finished,
    )


def local(*arguments):
    return local_small(*arguments) if lax.axis_size("fsdp") == 8 else local_general(*arguments)


def solution(mesh):
    in_specs = (
        P("fsdp", None, None),
        P(),
        P(),
        P(),
        P(),
        P("fsdp", None, "pool", None),
        P(),
        P("fsdp", "pool"),
        P("fsdp", "pool"),
        P("fsdp", "pool"),
        P("fsdp", "pool"),
        P(),
    )
    out_specs = P(None, ("pool", "fsdp"), None)
    return jax.shard_map(local, mesh=mesh, in_specs=in_specs, out_specs=out_specs, check_vma=False)
```

```python
import functools
import math

import jax
import jax.numpy as jnp
import numpy as np
from jax import lax
from jax.experimental import pallas as pl
from jax.experimental.pallas import tpu as pltpu
from jax.sharding import PartitionSpec as P

softcap = 50.0
query_scale = 144.0 ** (-0.5)
norm_eps = 1e-06


def rms_scale(rows, gain):
    mean_square = jnp.mean(rows * rows, axis=-1, keepdims=True)
    return rows * lax.rsqrt(mean_square + norm_eps) * gain


def rotate(vectors, cosine, sine):
    half = vectors.shape[-1] // 2
    first = vectors[..., :half]
    second = vectors[..., half:]
    return jnp.concatenate(
        [first * cosine - second * sine, second * cosine + first * sine], axis=-1
    )


def capped_weights(scores, valid):
    return jnp.where(valid, jnp.exp(softcap * jnp.tanh(scores / softcap)), 0.0)


def swap(array, axis, distance):
    size = lax.axis_size(axis)
    return lax.ppermute(array, axis, [(i, i ^ distance) for i in range(size)])


def place(pieces, index):
    first = pieces[0]
    stacked = jnp.zeros((len(pieces),) + first.shape, first.dtype)
    for distance, piece in pieces.items():
        stacked = lax.dynamic_update_index_in_dim(stacked, piece, index ^ distance, 0)
    return stacked


def exchange(chunks, axis):
    size = lax.axis_size(axis)
    index = lax.axis_index(axis)
    if size > 8:
        return lax.all_to_all(chunks, axis, split_axis=0, concat_axis=0, tiled=True)
    pieces = {}
    for distance in range(size):
        chunk = lax.dynamic_index_in_dim(chunks, index ^ distance, 0, keepdims=False)
        pieces[distance] = swap(chunk, axis, distance) if distance else chunk
    return place(pieces, index)


def doubled(block, axis, span):
    pieces = {0: block}
    bit = span // 2
    while bit:
        for distance in list(pieces):
            pieces[distance ^ bit] = swap(pieces[distance], axis, bit)
        bit //= 2
    return pieces


def attend(queries, keys_new, values_new, cached, cached_valid):
    new_len, kv_local, group, head_dim = queries.shape

    def part(keys, values, valid):
        scores = jnp.einsum("tgjd,kgd->gjtk", queries, keys, preferred_element_type=jnp.float32)
        weights = capped_weights(scores, valid)
        numer = jnp.einsum(
            "gjtk,kgd->gjtd",
            weights.astype(jnp.bfloat16),
            values,
            preferred_element_type=jnp.float32,
        )
        return numer, jnp.sum(weights, axis=-1)

    query_index = jnp.arange(new_len, dtype=jnp.int32)
    causal = query_index[None, :] <= query_index[:, None]
    numer, denom = part(
        cached[..., :head_dim], cached[..., head_dim:], cached_valid[None, None, None, :]
    )
    more, added = part(keys_new, values_new, causal[None, None])
    attended = ((numer + more) / (denom + added)[..., None]).transpose(2, 0, 1, 3)
    return attended.reshape(new_len, kv_local * group * head_dim).astype(jnp.bfloat16)


def local_general(
    hidden,
    slot_of_request,
    prefix_len,
    block_holder,
    block_slot,
    kv_pool,
    norm_gain,
    q_weight,
    k_weight,
    v_weight,
    o_weight,
    post_gain,
):
    shards = lax.axis_size("fsdp")
    groups = lax.axis_size("pool")
    f = lax.axis_index("fsdp")
    p = lax.axis_index("pool")
    half = shards // 2
    side = f // half
    new_len, width = hidden.shape[1:]
    requests = slot_of_request.shape[0]
    page_len = kv_pool.shape[1]
    kv_local = kv_pool.shape[2]
    head_dim = kv_pool.shape[3] // 2
    q_cols = q_weight.shape[1]
    kv_cols = k_weight.shape[1]
    group = q_cols // kv_cols
    max_blocks = block_holder.shape[1]
    per_holder = max_blocks // shards
    quarter = new_len // groups
    sub = quarter // shards
    features = o_weight.shape[0]

    kv_pieces = doubled(jnp.concatenate([k_weight, v_weight], axis=1), "fsdp", half)
    q_pieces = doubled(q_weight, "fsdp", half)
    out_weight = lax.all_gather(o_weight, "pool", axis=0, tiled=False)

    rows = hidden[0]
    normed = rms_scale(rows.astype(jnp.float32), norm_gain).astype(jnp.bfloat16)
    own_rows = lax.dynamic_slice(normed, (0, side * (width // 2)), (new_len, width // 2))
    leaving = lax.dynamic_slice(
        normed, (p * quarter, (1 - side) * (width // 2)), (quarter, width // 2)
    )
    partner_piece = swap(leaving, "fsdp", half)
    partner_pieces = {0: partner_piece}
    for distance in range(1, groups):
        partner_pieces[distance] = swap(partner_piece, "pool", distance)
    partner_rows = place(partner_pieces, p).reshape(new_len, width // 2)

    request_ids = jnp.arange(requests, dtype=jnp.int32)
    request_at_slot = jnp.sum(
        jnp.where(slot_of_request[None, :] == request_ids[:, None], request_ids[None, :], 0), axis=1
    )
    holder_by_slot = jnp.take(block_holder, request_at_slot, axis=0)
    page_by_slot = jnp.take(block_slot, request_at_slot, axis=0)
    held_here = holder_by_slot == f
    held_rank = jnp.cumsum(held_here.astype(jnp.int32), axis=1) - 1
    rank_ids = jnp.arange(per_holder, dtype=jnp.int32)
    picked = held_here[:, :, None] & (held_rank[:, :, None] == rank_ids[None, None, :])
    local_pages = jnp.sum(jnp.where(picked, page_by_slot[:, :, None], 0), axis=1)
    flat_pool = kv_pool.reshape(kv_pool.shape[0], page_len * kv_local, 2 * head_dim)
    outgoing = jnp.take(flat_pool, local_pages, axis=0)
    outgoing = outgoing.reshape(shards, per_holder * page_len * kv_local, 2 * head_dim)
    arrived = exchange(outgoing, "fsdp")
    cached = arrived.reshape(max_blocks * page_len, kv_local, 2 * head_dim)

    my_request = lax.dynamic_index_in_dim(request_at_slot, f, keepdims=False)
    my_length = prefix_len[my_request]
    my_holders = block_holder[my_request]
    entry_ids = jnp.arange(max_blocks, dtype=jnp.int32)
    mine = my_holders[None, :] == jnp.arange(shards, dtype=jnp.int32)[:, None]
    my_rank = jnp.cumsum(mine.astype(jnp.int32), axis=1) - 1
    chosen = mine[:, None, :] & (my_rank[:, None, :] == rank_ids[None, :, None])
    entry = jnp.sum(jnp.where(chosen, entry_ids[None, None, :], 0), axis=2)
    cached_position = entry.reshape(-1, 1) * page_len + jnp.arange(page_len, dtype=jnp.int32)
    cached_valid = (cached_position < my_length).reshape(-1)

    residual_out = lax.dynamic_slice_in_dim(rows, p * quarter, quarter, 0).reshape(
        shards, sub, width
    )
    residual = exchange(residual_out, "fsdp")

    positions = (my_length + jnp.arange(new_len, dtype=jnp.int32)).astype(jnp.float32)
    freqs = jnp.exp(
        jnp.arange(head_dim // 2, dtype=jnp.float32) * (-2.0 * math.log(10000.0) / head_dim)
    )
    angles = positions[:, None] * freqs
    cosine = jnp.cos(angles)[:, None, :]
    sine = jnp.sin(angles)[:, None, :]

    def project(pieces):
        weight = place(pieces, f % half).reshape(width // 2, -1)
        partial = jnp.dot(partner_rows, weight, preferred_element_type=jnp.float32)
        other = swap(partial.astype(jnp.bfloat16), "fsdp", half)
        own = jnp.dot(own_rows, weight, preferred_element_type=jnp.float32)
        return own + other.astype(jnp.float32)

    kv_sum = project(kv_pieces)
    q_sum = project(q_pieces)
    queries = rotate(q_sum.reshape(new_len, kv_local * group, head_dim), cosine, sine)
    queries = (queries * query_scale).astype(jnp.bfloat16)
    queries = queries.reshape(new_len, kv_local, group, head_dim)
    keys_new = kv_sum[:, :kv_cols].reshape(new_len, kv_local, head_dim)
    keys_new = rotate(keys_new, cosine, sine).astype(jnp.bfloat16)
    values_new = kv_sum[:, kv_cols:].astype(jnp.bfloat16).reshape(new_len, kv_local, head_dim)
    attended = attend(queries, keys_new, values_new, cached, cached_valid)

    quarters = exchange(attended.reshape(groups, quarter, q_cols), "pool")
    token_pieces = {0: quarters}
    for distance in range(2, shards, 2):
        token_pieces[distance] = swap(quarters, "fsdp", distance)
    for distance in range(0, shards, 2):
        token_pieces[distance ^ 1] = swap(token_pieces[distance], "fsdp", 1)
    tokens = place(token_pieces, f)
    projected = jnp.einsum(
        "sptc,pfc->stf", tokens, out_weight, preferred_element_type=jnp.float32
    ).astype(jnp.bfloat16)
    projected = projected.reshape(shards, shards, sub, features).transpose(1, 0, 2, 3)
    finished = exchange(projected, "fsdp").transpose(1, 2, 0, 3).reshape(shards, sub, width)
    finished = residual.astype(jnp.float32) + rms_scale(finished.astype(jnp.float32), post_gain)
    return jnp.take(finished.astype(jnp.bfloat16), slot_of_request, axis=0)


VMEM = pl.BlockSpec(memory_space=pltpu.VMEM)
SMEM = pl.BlockSpec(memory_space=pltpu.SMEM)
HBM = pl.BlockSpec(memory_space=pltpu.HBM)


def call(kernel, outs, scratch, flops, nbytes, *operands, specs=None, out_specs=None):
    return pl.pallas_call(
        kernel,
        out_shape=outs,
        in_specs=specs or [SMEM] + [VMEM] * (len(operands) - 1),
        out_specs=out_specs or jax.tree.map(lambda _: VMEM, outs),
        scratch_shapes=scratch,
        compiler_params=pltpu.CompilerParams(vmem_limit_bytes=60 << 20),
        cost_estimate=pl.CostEstimate(flops=flops, bytes_accessed=nbytes, transcendentals=0),
    )(*operands)


def after(array, *earlier):
    return lax.optimization_barrier((array,) + earlier)[0]


def weight_copies(weight_refs, weight, f, half, sems):
    copies = []
    for distance, ref in enumerate(weight_refs):
        count = ref.shape[0]
        start = pl.multiple_of(((f ^ distance) & (half - 1)) * count, 64)
        copies.append(
            pltpu.make_async_copy(ref, weight.at[pl.ds(start, count), :], sems.at[distance])
        )
        copies[-1].start()
    return copies


def partner_kernel(groups, half, where_ref, *refs):
    p, f = where_ref[0], where_ref[1]
    x_refs, w_refs = refs[:groups], refs[groups : groups + half]
    out_ref, rows, weight, x_sems, w_sems = refs[groups + half :]
    quarter = x_refs[0].shape[0]
    copies = weight_copies(w_refs, weight, f, half, w_sems)
    for distance, ref in enumerate(x_refs):
        start = pl.multiple_of((p ^ distance) * quarter, quarter)
        copies.append(
            pltpu.make_async_copy(ref, rows.at[pl.ds(start, quarter), :], x_sems.at[distance])
        )
        copies[-1].start()
    for copy in copies:
        copy.wait()
    for at in range(0, out_ref.shape[1], 512):
        out_ref[:, at : at + 512] = jnp.dot(
            rows[...], weight[:, at : at + 512], preferred_element_type=jnp.float32
        ).astype(jnp.bfloat16)


def row_scale(rows):
    return lax.rsqrt(jnp.mean(rows * rows, axis=1, keepdims=True) + norm_eps)


def prologue_kernel(
    hidden_ref, gain_ref, q_ref, k_ref, v_ref, leaving_ref, rows_ref, weight_ref, normed, sem
):
    p, f = lax.axis_index("pool"), lax.axis_index("fsdp")
    side = f // (lax.axis_size("fsdp") // 2)
    quarter, width = rows_ref.shape
    half_width = width // 2
    start = pl.multiple_of(p * quarter, quarter)
    rows_copy = pltpu.make_async_copy(hidden_ref.at[pl.ds(start, quarter), :], rows_ref, sem)
    rows_copy.start()
    at = 0
    for ref in (q_ref, k_ref, v_ref):
        weight_ref[:, at : at + ref.shape[1]] = ref[...]
        at += ref.shape[1]
    rows_copy.wait()
    rows = rows_ref[...].astype(jnp.float32)
    normed[...] = rows * row_scale(rows) * gain_ref[...].reshape(1, width)
    away = pl.multiple_of((1 - side) * half_width, 128)
    leaving_ref[...] = normed[:, pl.ds(away, half_width)].astype(jnp.bfloat16)


def pages_kernel(
    requests, page_len, where_ref, holder_ref, slot_ref, pool_ref, *refs
):
    f = where_ref[1]
    *out_refs, valid_ref, listed, entries, counts = refs
    max_blocks = holder_ref.shape[1]
    shards = out_refs[0].shape[0]
    per = max_blocks // shards
    each = per // len(out_refs)
    page_rows = pool_ref.shape[1]
    length, mine = jnp.int32(0), jnp.int32(0)
    for r in range(requests):
        at = where_ref[3 + r] == f
        length = length + jnp.where(at, where_ref[3 + requests + r], 0)
        mine = mine + jnp.where(at, r, 0)
    for r in range(requests):
        slot = where_ref[3 + r]

        def note(j, count):
            listed[count] = slot_ref[r, j]
            return count + jnp.where(holder_ref[r, j] == f, 1, 0)

        lax.fori_loop(0, max_blocks, note, jnp.int32(0), unroll=8)
        for k in range(per):
            at = k % each * page_rows
            out_refs[k // each][slot, at : at + page_rows, :] = pool_ref[listed[k]]
    for h in range(shards):
        counts[h] = 0

    def enter(j, carry):
        h = holder_ref[mine, j]
        count = counts[h]
        entries[h * per + count] = j
        counts[h] = count + 1
        return carry

    lax.fori_loop(0, max_blocks, enter, 0, unroll=4)
    row = lax.broadcasted_iota(jnp.int32, valid_ref.shape, 0)
    lane = lax.broadcasted_iota(jnp.int32, valid_ref.shape, 1)
    place_in = row * per + lane // page_len
    entry = jnp.zeros(valid_ref.shape, jnp.int32)
    for at in range(max_blocks):
        entry = jnp.where(place_in == at, entries[at], entry)
    position = entry * page_len + lane % page_len
    valid_ref[...] = jnp.where(position < length, 1.0, 0.0)


def own_kernel(requests, half, where_ref, hidden_ref, gain_ref, freq_ref, *refs):
    f = where_ref[1]
    own_ref, cos_ref, sin_ref, hidden, normed, weight, sems = refs[half:]
    rows_copy = pltpu.make_async_copy(hidden_ref, hidden, sems.at[half])
    rows_copy.start()
    copies = weight_copies(refs[:half], weight, f, half, sems)
    rows_copy.wait()
    new_len, width = hidden_ref.shape
    half_width = width // 2
    length = jnp.int32(0)
    for r in range(requests):
        length = length + jnp.where(where_ref[3 + r] == f, where_ref[3 + requests + r], 0)
    start = pl.multiple_of(where_ref[2] * half_width, 128)
    gain = gain_ref[:, pl.ds(start, half_width)]
    step = 32

    def norm(index, carry):
        at = pl.multiple_of(index * step, step)
        rows = hidden[pl.ds(at, step), :].astype(jnp.float32)
        scale = row_scale(rows)
        part = hidden[pl.ds(at, step), pl.ds(start, half_width)].astype(jnp.float32)
        normed[pl.ds(at, step), :] = (part * scale * gain).astype(jnp.bfloat16)
        return carry

    lax.fori_loop(0, new_len // step, norm, 0)
    position = lax.broadcasted_iota(jnp.int32, cos_ref.shape, 0) + length
    angle = position.astype(jnp.float32) * freq_ref[...]
    lane = lax.broadcasted_iota(jnp.int32, cos_ref.shape, 1)
    cos_ref[...] = jnp.cos(angle)
    sine = jnp.sin(angle)
    sin_ref[...] = jnp.where(lane < cos_ref.shape[1] // 2, -sine, sine)
    for copy in copies:
        copy.wait()
    for at in range(0, own_ref.shape[1], 512):
        own_ref[:, at : at + 512] = jnp.dot(
            normed[...], weight[:, at : at + 512], preferred_element_type=jnp.float32
        )


def capped(scores):
    return jnp.exp2(jnp.tanh(scores * (1.0 / softcap)) * (softcap * math.log2(math.e)))


def attend_kernel(
    groups,
    kv_local,
    head_dim,
    where_ref,
    own,
    other_ref,
    cos_ref,
    sin_ref,
    valid_ref,
    *refs,
):
    p = where_ref[0]
    page_refs, out_refs = refs[:2], refs[2 : 2 + groups]
    keys, values, result, other, pages, sems = refs[2 + groups :]
    copies = [pltpu.make_async_copy(other_ref, other, sems.at[0])]
    for index, ref in enumerate(page_refs):
        lines = pl.ds(index * ref.shape[1], ref.shape[1])
        copies.append(
            pltpu.make_async_copy(ref, pages.at[:, lines, :], sems.at[1 + index])
        )
    for copy in copies:
        copy.start()
    new_len, q_cols = result.shape
    group = q_cols // (kv_local * head_dim)

    def sums(at):
        return own[:, at : at + head_dim] + other[:, at : at + head_dim].astype(jnp.float32)

    cosine, sine = cos_ref[...], sin_ref[...]

    def rope(vectors):
        return vectors * cosine + pltpu.roll(vectors, head_dim // 2, 1) * sine

    span = pages.shape[1]
    per = span // kv_local
    row = lax.broadcasted_iota(jnp.int32, (span, span), 0)
    column = lax.broadcasted_iota(jnp.int32, (span, span), 1)
    part = (column == (row % per) * kv_local + row // per).astype(jnp.bfloat16)
    place_at = 0
    for copy in copies[1:]:
        copy.wait()
    for holder in range(pages.shape[0]):
        parted = jnp.dot(part, pages[holder], preferred_element_type=jnp.float32)
        parted = parted.astype(jnp.bfloat16)
        for g in range(kv_local):
            lines = parted[g * per : (g + 1) * per]
            keys[g, place_at : place_at + per, :] = lines[:, :head_dim]
            values[g, place_at : place_at + per, :] = lines[:, head_dim:]
        place_at += per

    copies[0].wait()
    span_keys = 2 * per
    t = lax.broadcasted_iota(jnp.int32, (group * new_len, new_len), 0) % new_len
    s = lax.broadcasted_iota(jnp.int32, (group * new_len, new_len), 1)
    causal = s <= t
    for g in range(kv_local):
        heads = [
            (rope(sums((g * group + j) * head_dim)) * query_scale).astype(jnp.bfloat16)
            for j in range(group)
        ]
        queries = jnp.concatenate(heads, axis=0)
        at = q_cols + g * head_dim
        new_key = rope(sums(at)).astype(jnp.bfloat16)
        new_value = sums(at + kv_local * head_dim).astype(jnp.bfloat16)

        def scores_of(key):
            return lax.dot_general(
                queries, key, (((1,), (1,)), ((), ())), preferred_element_type=jnp.float32
            )

        weights = jnp.where(causal, capped(scores_of(new_key)), 0.0)
        denom = jnp.sum(weights, axis=1, keepdims=True)
        numer = jnp.dot(
            weights.astype(jnp.bfloat16), new_value, preferred_element_type=jnp.float32
        )
        for start in range(0, place_at, span_keys):
            at = start // per
            valid = jnp.concatenate([valid_ref[at : at + 1], valid_ref[at + 1 : at + 2]], axis=1)
            valid = valid > 0.0
            weights = jnp.where(
                valid, capped(scores_of(keys[g, start : start + span_keys, :])), 0.0
            )
            denom = denom + jnp.sum(weights, axis=1, keepdims=True)
            numer = numer + jnp.dot(
                weights.astype(jnp.bfloat16),
                values[g, start : start + span_keys, :],
                preferred_element_type=jnp.float32,
            )
        attended = (numer / denom).astype(jnp.bfloat16)
        for j in range(group):
            to = (g * group + j) * head_dim
            result[:, to : to + head_dim] = attended[j * new_len : (j + 1) * new_len]
    quarter = new_len // groups
    for distance, ref in enumerate(out_refs):
        start = pl.multiple_of((p ^ distance) * quarter, quarter)
        ref[...] = result[pl.ds(start, quarter), :]


def output_kernel(groups, shards, where_ref, *refs):
    p, f = where_ref[0], where_ref[1]
    token_refs = refs[:shards]
    weight_ref = refs[shards]
    out_refs = refs[shards + 1 : 2 * shards + 1]
    total, tokens, weight, sems, token_sems = refs[2 * shards + 1 :]
    token_copies = [
        pltpu.make_async_copy(ref, tokens.at[e], token_sems.at[e])
        for e, ref in enumerate(token_refs)
    ]
    copies = [
        pltpu.make_async_copy(weight_ref.at[p ^ distance], weight.at[distance], sems.at[distance])
        for distance in range(groups)
    ]
    for copy in token_copies + copies:
        copy.start()
    for copy in token_copies:
        copy.wait()
    quarter = token_refs[0].shape[1]
    sub = quarter // shards
    projected = None
    for distance in range(groups):
        rows = jnp.concatenate([tokens[e, distance] for e in range(shards)], axis=0)
        copies[distance].wait()
        term = lax.dot_general(
            rows,
            weight[distance],
            (((1,), (1,)), ((), ())),
            preferred_element_type=jnp.float32,
        )
        projected = term if projected is None else projected + term
    total[...] = projected
    for e in range(shards):
        for distance, ref in enumerate(out_refs):
            start = pl.multiple_of(e * quarter + (f ^ distance) * sub, sub)
            ref[f ^ e] = total[pl.ds(start, sub), :].astype(jnp.bfloat16)


def finish_kernel(shards, where_ref, gain_ref, residual_ref, *refs):
    f = where_ref[1]
    piece_refs = refs[:shards]
    out_ref, projected = refs[shards:]
    for distance, ref in enumerate(piece_refs):
        projected[f ^ distance] = ref[...].astype(jnp.float32)
    gain = gain_ref[...]
    for request in range(out_ref.shape[0]):
        slot = where_ref[3 + request]
        line = jnp.concatenate([projected[k, slot] for k in range(shards)], axis=1)
        mean_square = jnp.mean(line * line, axis=1, keepdims=True)
        line = line * lax.rsqrt(mean_square + norm_eps) * gain
        out_ref[request] = (residual_ref[slot].astype(jnp.float32) + line).astype(jnp.bfloat16)


def pool_pieces(block, groups):
    return [block] + [swap(block, "pool", distance) for distance in range(1, groups)]


def local_small(
    hidden,
    slot_of_request,
    prefix_len,
    block_holder,
    block_slot,
    kv_pool,
    norm_gain,
    q_weight,
    k_weight,
    v_weight,
    o_weight,
    post_gain,
):
    shards = lax.axis_size("fsdp")
    groups = lax.axis_size("pool")
    f = lax.axis_index("fsdp")
    p = lax.axis_index("pool")
    half = shards // 2
    side = f // half
    new_len, width = hidden.shape[1:]
    requests = slot_of_request.shape[0]
    page_len = kv_pool.shape[1]
    kv_local = kv_pool.shape[2]
    head_dim = kv_pool.shape[3] // 2
    q_cols = q_weight.shape[1]
    kv_cols = k_weight.shape[1]
    max_blocks = block_holder.shape[1]
    per_holder = max_blocks // shards
    quarter = new_len // groups
    sub = quarter // shards
    features = o_weight.shape[0]
    bf16, f32 = jnp.bfloat16, jnp.float32
    where = jnp.concatenate(
        [jnp.stack([p, f, side]).astype(jnp.int32), slot_of_request, prefix_len]
    )
    shape = jax.ShapeDtypeStruct
    gain = norm_gain.reshape(1, width)
    rows = hidden[0]

    leaving, my_quarter, joined = call(
        prologue_kernel,
        [
            shape((quarter, width // 2), bf16),
            shape((quarter, width), bf16),
            shape((features, q_cols + 2 * kv_cols), bf16),
        ],
        [pltpu.VMEM((quarter, width), f32), pltpu.SemaphoreType.DMA],
        quarter * width * 8,
        4 * features * kv_cols,
        rows,
        norm_gain,
        q_weight,
        k_weight,
        v_weight,
        specs=[HBM, VMEM, VMEM, VMEM, VMEM],
    )
    partner_piece = swap(leaving, "fsdp", half)

    flat_pool = kv_pool.reshape(kv_pool.shape[0], page_len * kv_local, 2 * head_dim)
    page_rows = per_holder * page_len * kv_local
    first_pages, second_pages, valid = call(
        functools.partial(pages_kernel, requests, page_len),
        [
            shape((shards, page_rows // 2, 2 * head_dim), bf16),
            shape((shards, page_rows // 2, 2 * head_dim), bf16),
            shape((shards, per_holder * page_len), f32),
        ],
        [
            pltpu.SMEM((2 * per_holder,), jnp.int32),
            pltpu.SMEM((max_blocks + per_holder,), jnp.int32),
            pltpu.SMEM((shards,), jnp.int32),
        ],
        1 << 20,
        1 << 21,
        where,
        block_holder,
        block_slot,
        flat_pool,
        specs=[SMEM, SMEM, SMEM, VMEM],
    )
    near = swap(joined, "fsdp", 1)
    partner_piece, near, first_pages, second_pages, valid = lax.optimization_barrier(
        (partner_piece, near, first_pages, second_pages, valid)
    )
    far = swap(after(joined, partner_piece), "fsdp", 2)
    partner_pieces = pool_pieces(partner_piece, groups)
    arrived = [lax.all_to_all(first_pages, "fsdp", split_axis=0, concat_axis=0, tiled=True)]
    partner_pieces, far = lax.optimization_barrier((partner_pieces, far))
    weights = [joined, near, far, swap(far, "fsdp", 1)]
    arrived.append(
        lax.all_to_all(
            after(second_pages, far, arrived[0]), "fsdp", split_axis=0, concat_axis=0, tiled=True
        )
    )
    out_weight = lax.all_gather(after(o_weight, *partner_pieces), "pool", axis=0, tiled=False)

    partial = call(
        functools.partial(partner_kernel, groups, half),
        shape((new_len, q_cols + 2 * kv_cols), bf16),
        [
            pltpu.VMEM((new_len, width // 2), bf16),
            pltpu.VMEM((width // 2, q_cols + 2 * kv_cols), bf16),
            pltpu.SemaphoreType.DMA((groups,)),
            pltpu.SemaphoreType.DMA((half,)),
        ],
        new_len * width * (q_cols + 2 * kv_cols),
        width * (new_len + q_cols + 2 * kv_cols),
        where,
        *partner_pieces,
        *weights,
        specs=[SMEM] + [HBM] * (groups + half),
    )
    other = swap(partial, "fsdp", half)
    freqs = np.exp(np.arange(head_dim // 2) * (-2.0 * math.log(10000.0) / head_dim))
    freqs = np.concatenate([freqs, freqs]).astype(np.float32).reshape(1, head_dim)
    own, cosine, sine = call(
        functools.partial(own_kernel, requests, half),
        [
            shape((new_len, q_cols + 2 * kv_cols), f32),
            shape((new_len, head_dim), f32),
            shape((new_len, head_dim), f32),
        ],
        [
            pltpu.VMEM((new_len, width), bf16),
            pltpu.VMEM((new_len, width // 2), bf16),
            pltpu.VMEM((width // 2, q_cols + 2 * kv_cols), bf16),
            pltpu.SemaphoreType.DMA((half + 1,)),
        ],
        new_len * width * (q_cols + 2 * kv_cols),
        width * (2 * new_len + q_cols + 2 * kv_cols),
        where,
        after(rows, partial),
        gain,
        freqs,
        *weights,
        specs=[SMEM, HBM, VMEM, VMEM] + [HBM] * half,
    )

    residual = lax.all_to_all(
        after(my_quarter, other, *arrived).reshape(shards, sub, width),
        "fsdp",
        split_axis=0,
        concat_axis=0,
        tiled=True,
    )

    keys_total = max_blocks * page_len
    quarters = call(
        functools.partial(attend_kernel, groups, kv_local, head_dim),
        [shape((quarter, q_cols), bf16)] * groups,
        [
            pltpu.VMEM((kv_local, keys_total, head_dim), bf16),
            pltpu.VMEM((kv_local, keys_total, head_dim), bf16),
            pltpu.VMEM((new_len, q_cols), bf16),
            pltpu.VMEM(other.shape, bf16),
            pltpu.VMEM((shards, page_rows, 2 * head_dim), bf16),
            pltpu.SemaphoreType.DMA((3,)),
        ],
        4 * new_len * q_cols * (keys_total + new_len),
        1 << 22,
        where,
        own,
        other,
        cosine,
        sine,
        valid,
        *arrived,
        specs=[SMEM, VMEM, HBM, VMEM, VMEM, VMEM, HBM, HBM],
    )

    quarters = [
        swap(piece, "pool", distance) if distance else piece
        for distance, piece in enumerate(quarters)
    ]
    quarters = jnp.stack(quarters)
    tokens = {0: quarters}
    for distance in range(2, shards, 2):
        tokens[distance] = swap(quarters, "fsdp", distance)
    for distance in range(0, shards, 2):
        tokens[distance ^ 1] = swap(tokens[distance], "fsdp", 1)
    projected = call(
        functools.partial(output_kernel, groups, shards),
        [shape((shards, sub, features), bf16)] * shards,
        [
            pltpu.VMEM((shards * quarter, features), f32),
            pltpu.VMEM((shards, groups, quarter, q_cols), bf16),
            pltpu.VMEM((groups, features, q_cols), bf16),
            pltpu.SemaphoreType.DMA((groups,)),
            pltpu.SemaphoreType.DMA((shards,)),
        ],
        2 * shards * quarter * features * groups * q_cols,
        1 << 22,
        where,
        *[tokens[distance] for distance in range(shards)],
        out_weight,
        specs=[SMEM] + [HBM] * (shards + 1),
    )
    finished = [
        swap(piece, "fsdp", distance) if distance else piece
        for distance, piece in enumerate(projected)
    ]
    return call(
        functools.partial(finish_kernel, shards),
        shape((requests, sub, width), bf16),
        [pltpu.VMEM((shards, shards, sub, features), f32)],
        1 << 20,
        1 << 20,
        where,
        post_gain.reshape(1, width),
        residual,
        *finished,
    )


def local(*arguments):
    return local_small(*arguments) if lax.axis_size("fsdp") == 8 else local_general(*arguments)


def solution(mesh):
    in_specs = (
        P("fsdp", None, None),
        P(),
        P(),
        P(),
        P(),
        P("fsdp", None, "pool", None),
        P(),
        P("fsdp", "pool"),
        P("fsdp", "pool"),
        P("fsdp", "pool"),
        P("fsdp", "pool"),
        P(),
    )
    out_specs = P(None, ("pool", "fsdp"), None)
    return jax.shard_map(local, mesh=mesh, in_specs=in_specs, out_specs=out_specs, check_vma=False)
```

```python
import functools
import math

import jax
import jax.numpy as jnp
import numpy as np
from jax import lax
from jax.experimental import pallas as pl
from jax.experimental.pallas import tpu as pltpu
from jax.sharding import PartitionSpec as P

softcap = 50.0
query_scale = 144.0 ** (-0.5)
norm_eps = 1e-06


def rms_scale(rows, gain):
    mean_square = jnp.mean(rows * rows, axis=-1, keepdims=True)
    return rows * lax.rsqrt(mean_square + norm_eps) * gain


def rotate(vectors, cosine, sine):
    half = vectors.shape[-1] // 2
    first = vectors[..., :half]
    second = vectors[..., half:]
    return jnp.concatenate(
        [first * cosine - second * sine, second * cosine + first * sine], axis=-1
    )


def capped_weights(scores, valid):
    return jnp.where(valid, jnp.exp(softcap * jnp.tanh(scores / softcap)), 0.0)


def swap(array, axis, distance):
    size = lax.axis_size(axis)
    return lax.ppermute(array, axis, [(i, i ^ distance) for i in range(size)])


def place(pieces, index):
    first = pieces[0]
    stacked = jnp.zeros((len(pieces),) + first.shape, first.dtype)
    for distance, piece in pieces.items():
        stacked = lax.dynamic_update_index_in_dim(stacked, piece, index ^ distance, 0)
    return stacked


def exchange(chunks, axis):
    size = lax.axis_size(axis)
    index = lax.axis_index(axis)
    if size > 8:
        return lax.all_to_all(chunks, axis, split_axis=0, concat_axis=0, tiled=True)
    pieces = {}
    for distance in range(size):
        chunk = lax.dynamic_index_in_dim(chunks, index ^ distance, 0, keepdims=False)
        pieces[distance] = swap(chunk, axis, distance) if distance else chunk
    return place(pieces, index)


def doubled(block, axis, span):
    pieces = {0: block}
    bit = span // 2
    while bit:
        for distance in list(pieces):
            pieces[distance ^ bit] = swap(pieces[distance], axis, bit)
        bit //= 2
    return pieces


def attend(queries, keys_new, values_new, cached, cached_valid):
    new_len, kv_local, group, head_dim = queries.shape

    def part(keys, values, valid):
        scores = jnp.einsum("tgjd,kgd->gjtk", queries, keys, preferred_element_type=jnp.float32)
        weights = capped_weights(scores, valid)
        numer = jnp.einsum(
            "gjtk,kgd->gjtd",
            weights.astype(jnp.bfloat16),
            values,
            preferred_element_type=jnp.float32,
        )
        return numer, jnp.sum(weights, axis=-1)

    query_index = jnp.arange(new_len, dtype=jnp.int32)
    causal = query_index[None, :] <= query_index[:, None]
    numer, denom = part(
        cached[..., :head_dim], cached[..., head_dim:], cached_valid[None, None, None, :]
    )
    more, added = part(keys_new, values_new, causal[None, None])
    attended = ((numer + more) / (denom + added)[..., None]).transpose(2, 0, 1, 3)
    return attended.reshape(new_len, kv_local * group * head_dim).astype(jnp.bfloat16)


def local_general(
    hidden,
    slot_of_request,
    prefix_len,
    block_holder,
    block_slot,
    kv_pool,
    norm_gain,
    q_weight,
    k_weight,
    v_weight,
    o_weight,
    post_gain,
):
    shards = lax.axis_size("fsdp")
    groups = lax.axis_size("pool")
    f = lax.axis_index("fsdp")
    p = lax.axis_index("pool")
    half = shards // 2
    side = f // half
    new_len, width = hidden.shape[1:]
    requests = slot_of_request.shape[0]
    page_len = kv_pool.shape[1]
    kv_local = kv_pool.shape[2]
    head_dim = kv_pool.shape[3] // 2
    q_cols = q_weight.shape[1]
    kv_cols = k_weight.shape[1]
    group = q_cols // kv_cols
    max_blocks = block_holder.shape[1]
    per_holder = max_blocks // shards
    quarter = new_len // groups
    sub = quarter // shards
    features = o_weight.shape[0]

    kv_pieces = doubled(jnp.concatenate([k_weight, v_weight], axis=1), "fsdp", half)
    q_pieces = doubled(q_weight, "fsdp", half)
    out_weight = lax.all_gather(o_weight, "pool", axis=0, tiled=False)

    rows = hidden[0]
    normed = rms_scale(rows.astype(jnp.float32), norm_gain).astype(jnp.bfloat16)
    own_rows = lax.dynamic_slice(normed, (0, side * (width // 2)), (new_len, width // 2))
    leaving = lax.dynamic_slice(
        normed, (p * quarter, (1 - side) * (width // 2)), (quarter, width // 2)
    )
    partner_piece = swap(leaving, "fsdp", half)
    partner_pieces = {0: partner_piece}
    for distance in range(1, groups):
        partner_pieces[distance] = swap(partner_piece, "pool", distance)
    partner_rows = place(partner_pieces, p).reshape(new_len, width // 2)

    request_ids = jnp.arange(requests, dtype=jnp.int32)
    request_at_slot = jnp.sum(
        jnp.where(slot_of_request[None, :] == request_ids[:, None], request_ids[None, :], 0), axis=1
    )
    holder_by_slot = jnp.take(block_holder, request_at_slot, axis=0)
    page_by_slot = jnp.take(block_slot, request_at_slot, axis=0)
    held_here = holder_by_slot == f
    held_rank = jnp.cumsum(held_here.astype(jnp.int32), axis=1) - 1
    rank_ids = jnp.arange(per_holder, dtype=jnp.int32)
    picked = held_here[:, :, None] & (held_rank[:, :, None] == rank_ids[None, None, :])
    local_pages = jnp.sum(jnp.where(picked, page_by_slot[:, :, None], 0), axis=1)
    flat_pool = kv_pool.reshape(kv_pool.shape[0], page_len * kv_local, 2 * head_dim)
    outgoing = jnp.take(flat_pool, local_pages, axis=0)
    outgoing = outgoing.reshape(shards, per_holder * page_len * kv_local, 2 * head_dim)
    arrived = exchange(outgoing, "fsdp")
    cached = arrived.reshape(max_blocks * page_len, kv_local, 2 * head_dim)

    my_request = lax.dynamic_index_in_dim(request_at_slot, f, keepdims=False)
    my_length = prefix_len[my_request]
    my_holders = block_holder[my_request]
    entry_ids = jnp.arange(max_blocks, dtype=jnp.int32)
    mine = my_holders[None, :] == jnp.arange(shards, dtype=jnp.int32)[:, None]
    my_rank = jnp.cumsum(mine.astype(jnp.int32), axis=1) - 1
    chosen = mine[:, None, :] & (my_rank[:, None, :] == rank_ids[None, :, None])
    entry = jnp.sum(jnp.where(chosen, entry_ids[None, None, :], 0), axis=2)
    cached_position = entry.reshape(-1, 1) * page_len + jnp.arange(page_len, dtype=jnp.int32)
    cached_valid = (cached_position < my_length).reshape(-1)

    residual_out = lax.dynamic_slice_in_dim(rows, p * quarter, quarter, 0).reshape(
        shards, sub, width
    )
    residual = exchange(residual_out, "fsdp")

    positions = (my_length + jnp.arange(new_len, dtype=jnp.int32)).astype(jnp.float32)
    freqs = jnp.exp(
        jnp.arange(head_dim // 2, dtype=jnp.float32) * (-2.0 * math.log(10000.0) / head_dim)
    )
    angles = positions[:, None] * freqs
    cosine = jnp.cos(angles)[:, None, :]
    sine = jnp.sin(angles)[:, None, :]

    def project(pieces):
        weight = place(pieces, f % half).reshape(width // 2, -1)
        partial = jnp.dot(partner_rows, weight, preferred_element_type=jnp.float32)
        other = swap(partial.astype(jnp.bfloat16), "fsdp", half)
        own = jnp.dot(own_rows, weight, preferred_element_type=jnp.float32)
        return own + other.astype(jnp.float32)

    kv_sum = project(kv_pieces)
    q_sum = project(q_pieces)
    queries = rotate(q_sum.reshape(new_len, kv_local * group, head_dim), cosine, sine)
    queries = (queries * query_scale).astype(jnp.bfloat16)
    queries = queries.reshape(new_len, kv_local, group, head_dim)
    keys_new = kv_sum[:, :kv_cols].reshape(new_len, kv_local, head_dim)
    keys_new = rotate(keys_new, cosine, sine).astype(jnp.bfloat16)
    values_new = kv_sum[:, kv_cols:].astype(jnp.bfloat16).reshape(new_len, kv_local, head_dim)
    attended = attend(queries, keys_new, values_new, cached, cached_valid)

    quarters = exchange(attended.reshape(groups, quarter, q_cols), "pool")
    token_pieces = {0: quarters}
    for distance in range(2, shards, 2):
        token_pieces[distance] = swap(quarters, "fsdp", distance)
    for distance in range(0, shards, 2):
        token_pieces[distance ^ 1] = swap(token_pieces[distance], "fsdp", 1)
    tokens = place(token_pieces, f)
    projected = jnp.einsum(
        "sptc,pfc->stf", tokens, out_weight, preferred_element_type=jnp.float32
    ).astype(jnp.bfloat16)
    projected = projected.reshape(shards, shards, sub, features).transpose(1, 0, 2, 3)
    finished = exchange(projected, "fsdp").transpose(1, 2, 0, 3).reshape(shards, sub, width)
    finished = residual.astype(jnp.float32) + rms_scale(finished.astype(jnp.float32), post_gain)
    return jnp.take(finished.astype(jnp.bfloat16), slot_of_request, axis=0)


VMEM = pl.BlockSpec(memory_space=pltpu.VMEM)
SMEM = pl.BlockSpec(memory_space=pltpu.SMEM)
HBM = pl.BlockSpec(memory_space=pltpu.HBM)


def call(kernel, outs, scratch, flops, nbytes, *operands, specs=None, out_specs=None):
    return pl.pallas_call(
        kernel,
        out_shape=outs,
        in_specs=specs or [SMEM] + [VMEM] * (len(operands) - 1),
        out_specs=out_specs or jax.tree.map(lambda _: VMEM, outs),
        scratch_shapes=scratch,
        compiler_params=pltpu.CompilerParams(vmem_limit_bytes=60 << 20),
        cost_estimate=pl.CostEstimate(flops=flops, bytes_accessed=nbytes, transcendentals=0),
    )(*operands)


def after(array, *earlier):
    return lax.optimization_barrier((array,) + earlier)[0]


def weight_copies(weight_refs, weight, f, half, sems):
    copies = []
    for distance, ref in enumerate(weight_refs):
        count = ref.shape[0]
        start = pl.multiple_of(((f ^ distance) & (half - 1)) * count, 64)
        copies.append(
            pltpu.make_async_copy(ref, weight.at[pl.ds(start, count), :], sems.at[distance])
        )
        copies[-1].start()
    return copies


def partner_kernel(groups, half, where_ref, *refs):
    p, f = where_ref[0], where_ref[1]
    x_refs, w_refs = refs[:groups], refs[groups : groups + half]
    out_ref, rows, weight, x_sems, w_sems = refs[groups + half :]
    quarter = x_refs[0].shape[0]
    copies = weight_copies(w_refs, weight, f, half, w_sems)
    for distance, ref in enumerate(x_refs):
        start = pl.multiple_of((p ^ distance) * quarter, quarter)
        copies.append(
            pltpu.make_async_copy(ref, rows.at[pl.ds(start, quarter), :], x_sems.at[distance])
        )
        copies[-1].start()
    for copy in copies:
        copy.wait()
    for at in range(0, out_ref.shape[1], 512):
        out_ref[:, at : at + 512] = jnp.dot(
            rows[...], weight[:, at : at + 512], preferred_element_type=jnp.float32
        ).astype(jnp.bfloat16)


def row_scale(rows):
    return lax.rsqrt(jnp.mean(rows * rows, axis=1, keepdims=True) + norm_eps)


def prologue_kernel(
    hidden_ref, gain_ref, q_ref, k_ref, v_ref, leaving_ref, rows_ref, weight_ref, normed, sem
):
    p, f = lax.axis_index("pool"), lax.axis_index("fsdp")
    side = f // (lax.axis_size("fsdp") // 2)
    quarter, width = rows_ref.shape
    half_width = width // 2
    start = pl.multiple_of(p * quarter, quarter)
    rows_copy = pltpu.make_async_copy(hidden_ref.at[pl.ds(start, quarter), :], rows_ref, sem)
    rows_copy.start()
    at = 0
    for ref in (q_ref, k_ref, v_ref):
        weight_ref[:, at : at + ref.shape[1]] = ref[...]
        at += ref.shape[1]
    rows_copy.wait()
    rows = rows_ref[...].astype(jnp.float32)
    normed[...] = rows * row_scale(rows) * gain_ref[...].reshape(1, width)
    away = pl.multiple_of((1 - side) * half_width, 128)
    leaving_ref[...] = normed[:, pl.ds(away, half_width)].astype(jnp.bfloat16)


def pages_kernel(
    requests, page_len, where_ref, holder_ref, slot_ref, pool_ref, *refs
):
    f = where_ref[1]
    *out_refs, valid_ref, listed, entries, counts = refs
    max_blocks = holder_ref.shape[1]
    shards = out_refs[0].shape[0]
    per = max_blocks // shards
    each = per // len(out_refs)
    page_rows = pool_ref.shape[1]
    length, mine = jnp.int32(0), jnp.int32(0)
    for r in range(requests):
        at = where_ref[3 + r] == f
        length = length + jnp.where(at, where_ref[3 + requests + r], 0)
        mine = mine + jnp.where(at, r, 0)
    for r in range(requests):
        slot = where_ref[3 + r]

        def note(j, count):
            listed[count] = slot_ref[r, j]
            return count + jnp.where(holder_ref[r, j] == f, 1, 0)

        lax.fori_loop(0, max_blocks, note, jnp.int32(0), unroll=8)
        for k in range(per):
            at = k % each * page_rows
            out_refs[k // each][slot, at : at + page_rows, :] = pool_ref[listed[k]]
    for h in range(shards):
        counts[h] = 0

    def enter(j, carry):
        h = holder_ref[mine, j]
        count = counts[h]
        entries[h * per + count] = j
        counts[h] = count + 1
        return carry

    lax.fori_loop(0, max_blocks, enter, 0, unroll=4)
    row = lax.broadcasted_iota(jnp.int32, valid_ref.shape, 0)
    lane = lax.broadcasted_iota(jnp.int32, valid_ref.shape, 1)
    place_in = row * per + lane // page_len
    entry = jnp.zeros(valid_ref.shape, jnp.int32)
    for at in range(max_blocks):
        entry = jnp.where(place_in == at, entries[at], entry)
    position = entry * page_len + lane % page_len
    valid_ref[...] = jnp.where(position < length, 1.0, 0.0)


def own_kernel(requests, half, where_ref, hidden_ref, gain_ref, freq_ref, *refs):
    f = where_ref[1]
    own_ref, cos_ref, sin_ref, hidden, normed, weight, sems = refs[half:]
    rows_copy = pltpu.make_async_copy(hidden_ref, hidden, sems.at[half])
    rows_copy.start()
    copies = weight_copies(refs[:half], weight, f, half, sems)
    rows_copy.wait()
    new_len, width = hidden_ref.shape
    half_width = width // 2
    length = jnp.int32(0)
    for r in range(requests):
        length = length + jnp.where(where_ref[3 + r] == f, where_ref[3 + requests + r], 0)
    start = pl.multiple_of(where_ref[2] * half_width, 128)
    gain = gain_ref[:, pl.ds(start, half_width)]
    step = 32

    def norm(index, carry):
        at = pl.multiple_of(index * step, step)
        rows = hidden[pl.ds(at, step), :].astype(jnp.float32)
        scale = row_scale(rows)
        part = hidden[pl.ds(at, step), pl.ds(start, half_width)].astype(jnp.float32)
        normed[pl.ds(at, step), :] = (part * scale * gain).astype(jnp.bfloat16)
        return carry

    lax.fori_loop(0, new_len // step, norm, 0)
    position = lax.broadcasted_iota(jnp.int32, cos_ref.shape, 0) + length
    angle = position.astype(jnp.float32) * freq_ref[...]
    lane = lax.broadcasted_iota(jnp.int32, cos_ref.shape, 1)
    cos_ref[...] = jnp.cos(angle)
    sine = jnp.sin(angle)
    sin_ref[...] = jnp.where(lane < cos_ref.shape[1] // 2, -sine, sine)
    for copy in copies:
        copy.wait()
    for at in range(0, own_ref.shape[1], 512):
        own_ref[:, at : at + 512] = jnp.dot(
            normed[...], weight[:, at : at + 512], preferred_element_type=jnp.float32
        )


def capped(scores):
    return jnp.exp2(jnp.tanh(scores * (1.0 / softcap)) * (softcap * math.log2(math.e)))


def attend_kernel(
    groups,
    kv_local,
    head_dim,
    where_ref,
    own,
    other_ref,
    cos_ref,
    sin_ref,
    valid_ref,
    *refs,
):
    p = where_ref[0]
    page_refs, out_refs = refs[:2], refs[2 : 2 + groups]
    keys, values, result, other, pages, sems = refs[2 + groups :]
    copies = [pltpu.make_async_copy(other_ref, other, sems.at[0])]
    for index, ref in enumerate(page_refs):
        lines = pl.ds(index * ref.shape[1], ref.shape[1])
        copies.append(
            pltpu.make_async_copy(ref, pages.at[:, lines, :], sems.at[1 + index])
        )
    for copy in copies:
        copy.start()
    new_len, q_cols = result.shape
    group = q_cols // (kv_local * head_dim)

    def sums(at):
        return own[:, at : at + head_dim] + other[:, at : at + head_dim].astype(jnp.float32)

    cosine, sine = cos_ref[...], sin_ref[...]

    def rope(vectors):
        return vectors * cosine + pltpu.roll(vectors, head_dim // 2, 1) * sine

    span = pages.shape[1]
    per = span // kv_local
    row = lax.broadcasted_iota(jnp.int32, (span, span), 0)
    column = lax.broadcasted_iota(jnp.int32, (span, span), 1)
    part = (column == (row % per) * kv_local + row // per).astype(jnp.bfloat16)
    place_at = 0
    for copy in copies[1:]:
        copy.wait()
    for holder in range(pages.shape[0]):
        parted = jnp.dot(part, pages[holder], preferred_element_type=jnp.float32)
        parted = parted.astype(jnp.bfloat16)
        for g in range(kv_local):
            lines = parted[g * per : (g + 1) * per]
            keys[g, place_at : place_at + per, :] = lines[:, :head_dim]
            values[g, place_at : place_at + per, :] = lines[:, head_dim:]
        place_at += per

    copies[0].wait()
    span_keys = 2 * per
    t = lax.broadcasted_iota(jnp.int32, (group * new_len, new_len), 0) % new_len
    s = lax.broadcasted_iota(jnp.int32, (group * new_len, new_len), 1)
    causal = s <= t
    for g in range(kv_local):
        heads = [
            (rope(sums((g * group + j) * head_dim)) * query_scale).astype(jnp.bfloat16)
            for j in range(group)
        ]
        queries = jnp.concatenate(heads, axis=0)
        at = q_cols + g * head_dim
        new_key = rope(sums(at)).astype(jnp.bfloat16)
        new_value = sums(at + kv_local * head_dim).astype(jnp.bfloat16)

        def scores_of(key):
            return lax.dot_general(
                queries, key, (((1,), (1,)), ((), ())), preferred_element_type=jnp.float32
            )

        weights = jnp.where(causal, capped(scores_of(new_key)), 0.0)
        denom = jnp.sum(weights, axis=1, keepdims=True)
        numer = jnp.dot(
            weights.astype(jnp.bfloat16), new_value, preferred_element_type=jnp.float32
        )
        for start in range(0, place_at, span_keys):
            at = start // per
            valid = jnp.concatenate([valid_ref[at : at + 1], valid_ref[at + 1 : at + 2]], axis=1)
            valid = valid > 0.0
            weights = jnp.where(
                valid, capped(scores_of(keys[g, start : start + span_keys, :])), 0.0
            )
            denom = denom + jnp.sum(weights, axis=1, keepdims=True)
            numer = numer + jnp.dot(
                weights.astype(jnp.bfloat16),
                values[g, start : start + span_keys, :],
                preferred_element_type=jnp.float32,
            )
        attended = (numer / denom).astype(jnp.bfloat16)
        for j in range(group):
            to = (g * group + j) * head_dim
            result[:, to : to + head_dim] = attended[j * new_len : (j + 1) * new_len]
    quarter = new_len // groups
    for distance, ref in enumerate(out_refs):
        start = pl.multiple_of((p ^ distance) * quarter, quarter)
        ref[...] = result[pl.ds(start, quarter), :]


def output_kernel(groups, shards, where_ref, *refs):
    p, f = where_ref[0], where_ref[1]
    token_refs = refs[:shards]
    weight_ref = refs[shards]
    out_refs = refs[shards + 1 : 2 * shards + 1]
    total, tokens, weight, sems, token_sems = refs[2 * shards + 1 :]
    token_copies = [
        pltpu.make_async_copy(ref, tokens.at[e], token_sems.at[e])
        for e, ref in enumerate(token_refs)
    ]
    copies = [
        pltpu.make_async_copy(weight_ref.at[p ^ distance], weight.at[distance], sems.at[distance])
        for distance in range(groups)
    ]
    for copy in token_copies + copies:
        copy.start()
    for copy in token_copies:
        copy.wait()
    quarter = token_refs[0].shape[1]
    sub = quarter // shards
    projected = None
    for distance in range(groups):
        rows = jnp.concatenate([tokens[e, distance] for e in range(shards)], axis=0)
        copies[distance].wait()
        term = lax.dot_general(
            rows,
            weight[distance],
            (((1,), (1,)), ((), ())),
            preferred_element_type=jnp.float32,
        )
        projected = term if projected is None else projected + term
    total[...] = projected
    for e in range(shards):
        for distance, ref in enumerate(out_refs):
            start = pl.multiple_of(e * quarter + (f ^ distance) * sub, sub)
            ref[f ^ e] = total[pl.ds(start, sub), :].astype(jnp.bfloat16)


def finish_kernel(shards, where_ref, gain_ref, residual_ref, *refs):
    f = where_ref[1]
    piece_refs = refs[:shards]
    out_ref, projected = refs[shards:]
    for distance, ref in enumerate(piece_refs):
        projected[f ^ distance] = ref[...].astype(jnp.float32)
    gain = gain_ref[...]
    for request in range(out_ref.shape[0]):
        slot = where_ref[3 + request]
        line = jnp.concatenate([projected[k, slot] for k in range(shards)], axis=1)
        mean_square = jnp.mean(line * line, axis=1, keepdims=True)
        line = line * lax.rsqrt(mean_square + norm_eps) * gain
        out_ref[request] = (residual_ref[slot].astype(jnp.float32) + line).astype(jnp.bfloat16)


def pool_pieces(block, groups):
    return [block] + [swap(block, "pool", distance) for distance in range(1, groups)]


def local_small(
    hidden,
    slot_of_request,
    prefix_len,
    block_holder,
    block_slot,
    kv_pool,
    norm_gain,
    q_weight,
    k_weight,
    v_weight,
    o_weight,
    post_gain,
):
    shards = lax.axis_size("fsdp")
    groups = lax.axis_size("pool")
    f = lax.axis_index("fsdp")
    p = lax.axis_index("pool")
    half = shards // 2
    side = f // half
    new_len, width = hidden.shape[1:]
    requests = slot_of_request.shape[0]
    page_len = kv_pool.shape[1]
    kv_local = kv_pool.shape[2]
    head_dim = kv_pool.shape[3] // 2
    q_cols = q_weight.shape[1]
    kv_cols = k_weight.shape[1]
    max_blocks = block_holder.shape[1]
    per_holder = max_blocks // shards
    quarter = new_len // groups
    sub = quarter // shards
    features = o_weight.shape[0]
    bf16, f32 = jnp.bfloat16, jnp.float32
    where = jnp.concatenate(
        [jnp.stack([p, f, side]).astype(jnp.int32), slot_of_request, prefix_len]
    )
    shape = jax.ShapeDtypeStruct
    gain = norm_gain.reshape(1, width)
    rows = hidden[0]

    leaving, my_quarter, joined = call(
        prologue_kernel,
        [
            shape((quarter, width // 2), bf16),
            shape((quarter, width), bf16),
            shape((features, q_cols + 2 * kv_cols), bf16),
        ],
        [pltpu.VMEM((quarter, width), f32), pltpu.SemaphoreType.DMA],
        quarter * width * 8,
        4 * features * kv_cols,
        rows,
        norm_gain,
        q_weight,
        k_weight,
        v_weight,
        specs=[HBM, VMEM, VMEM, VMEM, VMEM],
    )
    partner_piece = swap(leaving, "fsdp", half)

    flat_pool = kv_pool.reshape(kv_pool.shape[0], page_len * kv_local, 2 * head_dim)
    page_rows = per_holder * page_len * kv_local
    first_pages, second_pages, valid = call(
        functools.partial(pages_kernel, requests, page_len),
        [
            shape((shards, page_rows // 2, 2 * head_dim), bf16),
            shape((shards, page_rows // 2, 2 * head_dim), bf16),
            shape((shards, per_holder * page_len), f32),
        ],
        [
            pltpu.SMEM((2 * per_holder,), jnp.int32),
            pltpu.SMEM((max_blocks + per_holder,), jnp.int32),
            pltpu.SMEM((shards,), jnp.int32),
        ],
        1 << 20,
        1 << 21,
        where,
        block_holder,
        block_slot,
        flat_pool,
        specs=[SMEM, SMEM, SMEM, VMEM],
    )
    near = swap(joined, "fsdp", 1)
    partner_piece, near, first_pages, second_pages, valid = lax.optimization_barrier(
        (partner_piece, near, first_pages, second_pages, valid)
    )
    far = swap(after(joined, partner_piece), "fsdp", 2)
    partner_pieces = pool_pieces(partner_piece, groups)
    arrived = lax.all_to_all(first_pages, "fsdp", split_axis=0, concat_axis=0, tiled=True)
    partner_pieces, far, arrived = lax.optimization_barrier((partner_pieces, far, arrived))
    arrived = [arrived]
    weights = [joined, near, far, swap(far, "fsdp", 1)]
    arrived.append(
        lax.all_to_all(
            after(second_pages, far), "fsdp", split_axis=0, concat_axis=0, tiled=True
        )
    )
    out_weight = lax.all_gather(after(o_weight, *partner_pieces), "pool", axis=0, tiled=False)

    partial = call(
        functools.partial(partner_kernel, groups, half),
        shape((new_len, q_cols + 2 * kv_cols), bf16),
        [
            pltpu.VMEM((new_len, width // 2), bf16),
            pltpu.VMEM((width // 2, q_cols + 2 * kv_cols), bf16),
            pltpu.SemaphoreType.DMA((groups,)),
            pltpu.SemaphoreType.DMA((half,)),
        ],
        new_len * width * (q_cols + 2 * kv_cols),
        width * (new_len + q_cols + 2 * kv_cols),
        where,
        *partner_pieces,
        *weights,
        specs=[SMEM] + [HBM] * (groups + half),
    )
    other = swap(partial, "fsdp", half)
    freqs = np.exp(np.arange(head_dim // 2) * (-2.0 * math.log(10000.0) / head_dim))
    freqs = np.concatenate([freqs, freqs]).astype(np.float32).reshape(1, head_dim)
    own, cosine, sine = call(
        functools.partial(own_kernel, requests, half),
        [
            shape((new_len, q_cols + 2 * kv_cols), f32),
            shape((new_len, head_dim), f32),
            shape((new_len, head_dim), f32),
        ],
        [
            pltpu.VMEM((new_len, width), bf16),
            pltpu.VMEM((new_len, width // 2), bf16),
            pltpu.VMEM((width // 2, q_cols + 2 * kv_cols), bf16),
            pltpu.SemaphoreType.DMA((half + 1,)),
        ],
        new_len * width * (q_cols + 2 * kv_cols),
        width * (2 * new_len + q_cols + 2 * kv_cols),
        where,
        after(rows, partial),
        gain,
        freqs,
        *weights,
        specs=[SMEM, HBM, VMEM, VMEM] + [HBM] * half,
    )

    residual = lax.all_to_all(
        after(my_quarter, own, *arrived).reshape(shards, sub, width),
        "fsdp",
        split_axis=0,
        concat_axis=0,
        tiled=True,
    )

    keys_total = max_blocks * page_len
    quarters = call(
        functools.partial(attend_kernel, groups, kv_local, head_dim),
        [shape((quarter, q_cols), bf16)] * groups,
        [
            pltpu.VMEM((kv_local, keys_total, head_dim), bf16),
            pltpu.VMEM((kv_local, keys_total, head_dim), bf16),
            pltpu.VMEM((new_len, q_cols), bf16),
            pltpu.VMEM(other.shape, bf16),
            pltpu.VMEM((shards, page_rows, 2 * head_dim), bf16),
            pltpu.SemaphoreType.DMA((3,)),
        ],
        4 * new_len * q_cols * (keys_total + new_len),
        1 << 22,
        where,
        own,
        other,
        cosine,
        sine,
        valid,
        *arrived,
        specs=[SMEM, VMEM, HBM, VMEM, VMEM, VMEM, HBM, HBM],
    )

    quarters = [
        swap(piece, "pool", distance) if distance else piece
        for distance, piece in enumerate(quarters)
    ]
    quarters = jnp.stack(quarters)
    tokens = {0: quarters}
    for distance in range(2, shards, 2):
        tokens[distance] = swap(quarters, "fsdp", distance)
    for distance in range(0, shards, 2):
        tokens[distance ^ 1] = swap(tokens[distance], "fsdp", 1)
    projected = call(
        functools.partial(output_kernel, groups, shards),
        [shape((shards, sub, features), bf16)] * shards,
        [
            pltpu.VMEM((shards * quarter, features), f32),
            pltpu.VMEM((shards, groups, quarter, q_cols), bf16),
            pltpu.VMEM((groups, features, q_cols), bf16),
            pltpu.SemaphoreType.DMA((groups,)),
            pltpu.SemaphoreType.DMA((shards,)),
        ],
        2 * shards * quarter * features * groups * q_cols,
        1 << 22,
        where,
        *[tokens[distance] for distance in range(shards)],
        out_weight,
        specs=[SMEM] + [HBM] * (shards + 1),
    )
    finished = [
        swap(piece, "fsdp", distance) if distance else piece
        for distance, piece in enumerate(projected)
    ]
    return call(
        functools.partial(finish_kernel, shards),
        shape((requests, sub, width), bf16),
        [pltpu.VMEM((shards, shards, sub, features), f32)],
        1 << 20,
        1 << 20,
        where,
        post_gain.reshape(1, width),
        residual,
        *finished,
    )


def local(*arguments):
    return local_small(*arguments) if lax.axis_size("fsdp") == 8 else local_general(*arguments)


def solution(mesh):
    in_specs = (
        P("fsdp", None, None),
        P(),
        P(),
        P(),
        P(),
        P("fsdp", None, "pool", None),
        P(),
        P("fsdp", "pool"),
        P("fsdp", "pool"),
        P("fsdp", "pool"),
        P("fsdp", "pool"),
        P(),
    )
    out_specs = P(None, ("pool", "fsdp"), None)
    return jax.shard_map(local, mesh=mesh, in_specs=in_specs, out_specs=out_specs, check_vma=False)
```

```python
import functools
import math

import jax
import jax.numpy as jnp
import numpy as np
from jax import lax
from jax.experimental import pallas as pl
from jax.experimental.pallas import tpu as pltpu
from jax.sharding import PartitionSpec as P

softcap = 50.0
query_scale = 144.0 ** (-0.5)
norm_eps = 1e-06


def rms_scale(rows, gain):
    mean_square = jnp.mean(rows * rows, axis=-1, keepdims=True)
    return rows * lax.rsqrt(mean_square + norm_eps) * gain


def rotate(vectors, cosine, sine):
    half = vectors.shape[-1] // 2
    first = vectors[..., :half]
    second = vectors[..., half:]
    return jnp.concatenate(
        [first * cosine - second * sine, second * cosine + first * sine], axis=-1
    )


def capped_weights(scores, valid):
    return jnp.where(valid, jnp.exp(softcap * jnp.tanh(scores / softcap)), 0.0)


def swap(array, axis, distance):
    size = lax.axis_size(axis)
    return lax.ppermute(array, axis, [(i, i ^ distance) for i in range(size)])


def place(pieces, index):
    first = pieces[0]
    stacked = jnp.zeros((len(pieces),) + first.shape, first.dtype)
    for distance, piece in pieces.items():
        stacked = lax.dynamic_update_index_in_dim(stacked, piece, index ^ distance, 0)
    return stacked


def exchange(chunks, axis):
    size = lax.axis_size(axis)
    index = lax.axis_index(axis)
    if size > 8:
        return lax.all_to_all(chunks, axis, split_axis=0, concat_axis=0, tiled=True)
    pieces = {}
    for distance in range(size):
        chunk = lax.dynamic_index_in_dim(chunks, index ^ distance, 0, keepdims=False)
        pieces[distance] = swap(chunk, axis, distance) if distance else chunk
    return place(pieces, index)


def doubled(block, axis, span):
    pieces = {0: block}
    bit = span // 2
    while bit:
        for distance in list(pieces):
            pieces[distance ^ bit] = swap(pieces[distance], axis, bit)
        bit //= 2
    return pieces


def attend(queries, keys_new, values_new, cached, cached_valid):
    new_len, kv_local, group, head_dim = queries.shape

    def part(keys, values, valid):
        scores = jnp.einsum("tgjd,kgd->gjtk", queries, keys, preferred_element_type=jnp.float32)
        weights = capped_weights(scores, valid)
        numer = jnp.einsum(
            "gjtk,kgd->gjtd",
            weights.astype(jnp.bfloat16),
            values,
            preferred_element_type=jnp.float32,
        )
        return numer, jnp.sum(weights, axis=-1)

    query_index = jnp.arange(new_len, dtype=jnp.int32)
    causal = query_index[None, :] <= query_index[:, None]
    numer, denom = part(
        cached[..., :head_dim], cached[..., head_dim:], cached_valid[None, None, None, :]
    )
    more, added = part(keys_new, values_new, causal[None, None])
    attended = ((numer + more) / (denom + added)[..., None]).transpose(2, 0, 1, 3)
    return attended.reshape(new_len, kv_local * group * head_dim).astype(jnp.bfloat16)


def local_general(
    hidden,
    slot_of_request,
    prefix_len,
    block_holder,
    block_slot,
    kv_pool,
    norm_gain,
    q_weight,
    k_weight,
    v_weight,
    o_weight,
    post_gain,
):
    shards = lax.axis_size("fsdp")
    groups = lax.axis_size("pool")
    f = lax.axis_index("fsdp")
    p = lax.axis_index("pool")
    half = shards // 2
    side = f // half
    new_len, width = hidden.shape[1:]
    requests = slot_of_request.shape[0]
    page_len = kv_pool.shape[1]
    kv_local = kv_pool.shape[2]
    head_dim = kv_pool.shape[3] // 2
    q_cols = q_weight.shape[1]
    kv_cols = k_weight.shape[1]
    group = q_cols // kv_cols
    max_blocks = block_holder.shape[1]
    per_holder = max_blocks // shards
    quarter = new_len // groups
    sub = quarter // shards
    features = o_weight.shape[0]

    kv_pieces = doubled(jnp.concatenate([k_weight, v_weight], axis=1), "fsdp", half)
    q_pieces = doubled(q_weight, "fsdp", half)
    out_weight = lax.all_gather(o_weight, "pool", axis=0, tiled=False)

    rows = hidden[0]
    normed = rms_scale(rows.astype(jnp.float32), norm_gain).astype(jnp.bfloat16)
    own_rows = lax.dynamic_slice(normed, (0, side * (width // 2)), (new_len, width // 2))
    leaving = lax.dynamic_slice(
        normed, (p * quarter, (1 - side) * (width // 2)), (quarter, width // 2)
    )
    partner_piece = swap(leaving, "fsdp", half)
    partner_pieces = {0: partner_piece}
    for distance in range(1, groups):
        partner_pieces[distance] = swap(partner_piece, "pool", distance)
    partner_rows = place(partner_pieces, p).reshape(new_len, width // 2)

    request_ids = jnp.arange(requests, dtype=jnp.int32)
    request_at_slot = jnp.sum(
        jnp.where(slot_of_request[None, :] == request_ids[:, None], request_ids[None, :], 0), axis=1
    )
    holder_by_slot = jnp.take(block_holder, request_at_slot, axis=0)
    page_by_slot = jnp.take(block_slot, request_at_slot, axis=0)
    held_here = holder_by_slot == f
    held_rank = jnp.cumsum(held_here.astype(jnp.int32), axis=1) - 1
    rank_ids = jnp.arange(per_holder, dtype=jnp.int32)
    picked = held_here[:, :, None] & (held_rank[:, :, None] == rank_ids[None, None, :])
    local_pages = jnp.sum(jnp.where(picked, page_by_slot[:, :, None], 0), axis=1)
    flat_pool = kv_pool.reshape(kv_pool.shape[0], page_len * kv_local, 2 * head_dim)
    outgoing = jnp.take(flat_pool, local_pages, axis=0)
    outgoing = outgoing.reshape(shards, per_holder * page_len * kv_local, 2 * head_dim)
    arrived = exchange(outgoing, "fsdp")
    cached = arrived.reshape(max_blocks * page_len, kv_local, 2 * head_dim)

    my_request = lax.dynamic_index_in_dim(request_at_slot, f, keepdims=False)
    my_length = prefix_len[my_request]
    my_holders = block_holder[my_request]
    entry_ids = jnp.arange(max_blocks, dtype=jnp.int32)
    mine = my_holders[None, :] == jnp.arange(shards, dtype=jnp.int32)[:, None]
    my_rank = jnp.cumsum(mine.astype(jnp.int32), axis=1) - 1
    chosen = mine[:, None, :] & (my_rank[:, None, :] == rank_ids[None, :, None])
    entry = jnp.sum(jnp.where(chosen, entry_ids[None, None, :], 0), axis=2)
    cached_position = entry.reshape(-1, 1) * page_len + jnp.arange(page_len, dtype=jnp.int32)
    cached_valid = (cached_position < my_length).reshape(-1)

    residual_out = lax.dynamic_slice_in_dim(rows, p * quarter, quarter, 0).reshape(
        shards, sub, width
    )
    residual = exchange(residual_out, "fsdp")

    positions = (my_length + jnp.arange(new_len, dtype=jnp.int32)).astype(jnp.float32)
    freqs = jnp.exp(
        jnp.arange(head_dim // 2, dtype=jnp.float32) * (-2.0 * math.log(10000.0) / head_dim)
    )
    angles = positions[:, None] * freqs
    cosine = jnp.cos(angles)[:, None, :]
    sine = jnp.sin(angles)[:, None, :]

    def project(pieces):
        weight = place(pieces, f % half).reshape(width // 2, -1)
        partial = jnp.dot(partner_rows, weight, preferred_element_type=jnp.float32)
        other = swap(partial.astype(jnp.bfloat16), "fsdp", half)
        own = jnp.dot(own_rows, weight, preferred_element_type=jnp.float32)
        return own + other.astype(jnp.float32)

    kv_sum = project(kv_pieces)
    q_sum = project(q_pieces)
    queries = rotate(q_sum.reshape(new_len, kv_local * group, head_dim), cosine, sine)
    queries = (queries * query_scale).astype(jnp.bfloat16)
    queries = queries.reshape(new_len, kv_local, group, head_dim)
    keys_new = kv_sum[:, :kv_cols].reshape(new_len, kv_local, head_dim)
    keys_new = rotate(keys_new, cosine, sine).astype(jnp.bfloat16)
    values_new = kv_sum[:, kv_cols:].astype(jnp.bfloat16).reshape(new_len, kv_local, head_dim)
    attended = attend(queries, keys_new, values_new, cached, cached_valid)

    quarters = exchange(attended.reshape(groups, quarter, q_cols), "pool")
    token_pieces = {0: quarters}
    for distance in range(2, shards, 2):
        token_pieces[distance] = swap(quarters, "fsdp", distance)
    for distance in range(0, shards, 2):
        token_pieces[distance ^ 1] = swap(token_pieces[distance], "fsdp", 1)
    tokens = place(token_pieces, f)
    projected = jnp.einsum(
        "sptc,pfc->stf", tokens, out_weight, preferred_element_type=jnp.float32
    ).astype(jnp.bfloat16)
    projected = projected.reshape(shards, shards, sub, features).transpose(1, 0, 2, 3)
    finished = exchange(projected, "fsdp").transpose(1, 2, 0, 3).reshape(shards, sub, width)
    finished = residual.astype(jnp.float32) + rms_scale(finished.astype(jnp.float32), post_gain)
    return jnp.take(finished.astype(jnp.bfloat16), slot_of_request, axis=0)


VMEM = pl.BlockSpec(memory_space=pltpu.VMEM)
SMEM = pl.BlockSpec(memory_space=pltpu.SMEM)
HBM = pl.BlockSpec(memory_space=pltpu.HBM)


def call(kernel, outs, scratch, flops, nbytes, *operands, specs=None, out_specs=None):
    return pl.pallas_call(
        kernel,
        out_shape=outs,
        in_specs=specs or [SMEM] + [VMEM] * (len(operands) - 1),
        out_specs=out_specs or jax.tree.map(lambda _: VMEM, outs),
        scratch_shapes=scratch,
        compiler_params=pltpu.CompilerParams(vmem_limit_bytes=60 << 20),
        cost_estimate=pl.CostEstimate(flops=flops, bytes_accessed=nbytes, transcendentals=0),
    )(*operands)


def after(array, *earlier):
    return lax.optimization_barrier((array,) + earlier)[0]


def weight_copies(weight_refs, weight, f, half, sems):
    copies = []
    for distance, ref in enumerate(weight_refs):
        count = ref.shape[0]
        start = pl.multiple_of(((f ^ distance) & (half - 1)) * count, 64)
        copies.append(
            pltpu.make_async_copy(ref, weight.at[pl.ds(start, count), :], sems.at[distance])
        )
        copies[-1].start()
    return copies


def pair_product(groups, half, pair, where_ref, x_refs, w_refs, rows, weight, sems):
    p, f = where_ref[0], where_ref[1]
    copies = []
    for distance, ref in enumerate(w_refs):
        count = ref.shape[0]
        start = pl.multiple_of(((f ^ distance) & 1) * count, 64)
        copies.append((ref, weight.at[pl.ds(start, count), :]))
    span = weight.shape[0]
    columns = pl.ds(pl.multiple_of((((f & (half - 1)) >> 1) ^ pair) * span, 128), span)
    quarter = x_refs[0].shape[0]
    for distance, ref in enumerate(x_refs):
        start = pl.multiple_of((p ^ distance) * quarter, quarter)
        copies.append((ref, rows.at[pl.ds(start, quarter), :]))
    copies = [
        pltpu.make_async_copy(source, target, sems.at[index])
        for index, (source, target) in enumerate(copies)
    ]
    for copy in copies:
        copy.start()
    for copy in copies:
        copy.wait()
    return jnp.dot(rows[:, columns], weight[...], preferred_element_type=jnp.float32)


def near_kernel(groups, half, where_ref, *refs):
    x_refs, w_refs = refs[:groups], refs[groups : groups + 2]
    out_ref, *scratch = refs[groups + 2 :]
    out_ref[...] = pair_product(groups, half, 0, where_ref, x_refs, w_refs, *scratch)


def partner_kernel(groups, half, where_ref, near_ref, *refs):
    x_refs, w_refs = refs[:groups], refs[groups : groups + 2]
    out_ref, *scratch = refs[groups + 2 :]
    sums = pair_product(groups, half, 1, where_ref, x_refs, w_refs, *scratch)
    out_ref[...] = (near_ref[...] + sums).astype(jnp.bfloat16)


def row_scale(rows):
    return lax.rsqrt(jnp.mean(rows * rows, axis=1, keepdims=True) + norm_eps)


def rows_kernel(hidden_ref, gain_ref, leaving_ref, rows_ref, normed, sem):
    p, f = lax.axis_index("pool"), lax.axis_index("fsdp")
    side = f // (lax.axis_size("fsdp") // 2)
    quarter, width = rows_ref.shape
    half_width = width // 2
    start = pl.multiple_of(p * quarter, quarter)
    copy = pltpu.make_async_copy(hidden_ref.at[pl.ds(start, quarter), :], rows_ref, sem)
    copy.start()
    copy.wait()
    rows = rows_ref[...].astype(jnp.float32)
    normed[...] = rows * row_scale(rows) * gain_ref[...].reshape(1, width)
    away = pl.multiple_of((1 - side) * half_width, 128)
    leaving_ref[...] = normed[:, pl.ds(away, half_width)].astype(jnp.bfloat16)


def join_kernel(q_ref, k_ref, v_ref, weight_ref):
    at = 0
    for ref in (q_ref, k_ref, v_ref):
        weight_ref[:, at : at + ref.shape[1]] = ref[...]
        at += ref.shape[1]


def pages_kernel(
    requests, page_len, where_ref, holder_ref, slot_ref, pool_ref, *refs
):
    f = where_ref[1]
    out_ref, valid_ref, listed, entries, counts = refs
    max_blocks = holder_ref.shape[1]
    shards = out_ref.shape[0]
    per = max_blocks // shards
    page_rows = pool_ref.shape[1]
    length, mine = jnp.int32(0), jnp.int32(0)
    for r in range(requests):
        at = where_ref[3 + r] == f
        length = length + jnp.where(at, where_ref[3 + requests + r], 0)
        mine = mine + jnp.where(at, r, 0)
    for r in range(requests):
        slot = where_ref[3 + r]

        def note(j, count):
            listed[count] = slot_ref[r, j]
            return count + jnp.where(holder_ref[r, j] == f, 1, 0)

        lax.fori_loop(0, max_blocks, note, jnp.int32(0), unroll=8)
        for k in range(per):
            out_ref[slot, k * page_rows : (k + 1) * page_rows, :] = pool_ref[listed[k]]
    for h in range(shards):
        counts[h] = 0

    def enter(j, carry):
        h = holder_ref[mine, j]
        count = counts[h]
        entries[h * per + count] = j
        counts[h] = count + 1
        return carry

    lax.fori_loop(0, max_blocks, enter, 0, unroll=4)
    row = lax.broadcasted_iota(jnp.int32, valid_ref.shape, 0)
    lane = lax.broadcasted_iota(jnp.int32, valid_ref.shape, 1)
    place_in = row * per + lane // page_len
    entry = jnp.zeros(valid_ref.shape, jnp.int32)
    for at in range(max_blocks):
        entry = jnp.where(place_in == at, entries[at], entry)
    position = entry * page_len + lane % page_len
    valid_ref[...] = jnp.where(position < length, 1.0, 0.0)


def part_pages(pages, keys, values):
    kv_local, _, head_dim = keys.shape
    span = pages.shape[1]
    per = span // kv_local
    row = lax.broadcasted_iota(jnp.int32, (span, span), 0)
    column = lax.broadcasted_iota(jnp.int32, (span, span), 1)
    part = (column == (row % per) * kv_local + row // per).astype(jnp.bfloat16)
    for holder in range(pages.shape[0]):
        parted = jnp.dot(part, pages[holder], preferred_element_type=jnp.float32)
        parted = parted.astype(jnp.bfloat16)
        at = holder * per
        for g in range(kv_local):
            lines = parted[g * per : (g + 1) * per]
            keys[g, at : at + per, :] = lines[:, :head_dim]
            values[g, at : at + per, :] = lines[:, head_dim:]


def own_kernel(requests, half, where_ref, hidden_ref, gain_ref, freq_ref, pages, *refs):
    f = where_ref[1]
    own_ref, cos_ref, sin_ref, keys, values, hidden, normed, weight, sems = refs[half:]
    rows_copy = pltpu.make_async_copy(hidden_ref, hidden, sems.at[half])
    rows_copy.start()
    copies = weight_copies(refs[:half], weight, f, half, sems)
    rows_copy.wait()
    new_len, width = hidden_ref.shape
    half_width = width // 2
    length = jnp.int32(0)
    for r in range(requests):
        length = length + jnp.where(where_ref[3 + r] == f, where_ref[3 + requests + r], 0)
    start = pl.multiple_of(where_ref[2] * half_width, 128)
    gain = gain_ref[:, pl.ds(start, half_width)]
    step = 32

    def norm(index, carry):
        at = pl.multiple_of(index * step, step)
        rows = hidden[pl.ds(at, step), :].astype(jnp.float32)
        scale = row_scale(rows)
        part = hidden[pl.ds(at, step), pl.ds(start, half_width)].astype(jnp.float32)
        normed[pl.ds(at, step), :] = (part * scale * gain).astype(jnp.bfloat16)
        return carry

    lax.fori_loop(0, new_len // step, norm, 0)
    part_pages(pages, keys, values)
    position = lax.broadcasted_iota(jnp.int32, cos_ref.shape, 0) + length
    angle = position.astype(jnp.float32) * freq_ref[...]
    lane = lax.broadcasted_iota(jnp.int32, cos_ref.shape, 1)
    cos_ref[...] = jnp.cos(angle)
    sine = jnp.sin(angle)
    sin_ref[...] = jnp.where(lane < cos_ref.shape[1] // 2, -sine, sine)
    for copy in copies:
        copy.wait()
    for at in range(0, own_ref.shape[1], 512):
        own_ref[:, at : at + 512] = jnp.dot(
            normed[...], weight[:, at : at + 512], preferred_element_type=jnp.float32
        )


def capped(scores):
    return jnp.exp2(jnp.tanh(scores * (1.0 / softcap)) * (softcap * math.log2(math.e)))


def attend_kernel(
    groups,
    kv_local,
    head_dim,
    where_ref,
    own,
    other_ref,
    cos_ref,
    sin_ref,
    valid_ref,
    keys,
    values,
    *refs,
):
    p = where_ref[0]
    out_refs = refs[:groups]
    result, other, sem = refs[groups:]
    copy = pltpu.make_async_copy(other_ref, other, sem)
    copy.start()
    new_len, q_cols = result.shape
    group = q_cols // (kv_local * head_dim)

    def sums(at):
        return own[:, at : at + head_dim] + other[:, at : at + head_dim].astype(jnp.float32)

    cosine, sine = cos_ref[...], sin_ref[...]

    def rope(vectors):
        return vectors * cosine + pltpu.roll(vectors, head_dim // 2, 1) * sine

    copy.wait()
    per = valid_ref.shape[1]
    place_at = keys.shape[1]
    span_keys = 2 * per
    t = lax.broadcasted_iota(jnp.int32, (group * new_len, new_len), 0) % new_len
    s = lax.broadcasted_iota(jnp.int32, (group * new_len, new_len), 1)
    causal = s <= t
    for g in range(kv_local):
        heads = [
            (rope(sums((g * group + j) * head_dim)) * query_scale).astype(jnp.bfloat16)
            for j in range(group)
        ]
        queries = jnp.concatenate(heads, axis=0)
        at = q_cols + g * head_dim
        new_key = rope(sums(at)).astype(jnp.bfloat16)
        new_value = sums(at + kv_local * head_dim).astype(jnp.bfloat16)

        def scores_of(key):
            return lax.dot_general(
                queries, key, (((1,), (1,)), ((), ())), preferred_element_type=jnp.float32
            )

        weights = jnp.where(causal, capped(scores_of(new_key)), 0.0)
        denom = jnp.sum(weights, axis=1, keepdims=True)
        numer = jnp.dot(
            weights.astype(jnp.bfloat16), new_value, preferred_element_type=jnp.float32
        )
        for start in range(0, place_at, span_keys):
            at = start // per
            valid = jnp.concatenate([valid_ref[at : at + 1], valid_ref[at + 1 : at + 2]], axis=1)
            valid = valid > 0.0
            weights = jnp.where(
                valid, capped(scores_of(keys[g, start : start + span_keys, :])), 0.0
            )
            denom = denom + jnp.sum(weights, axis=1, keepdims=True)
            numer = numer + jnp.dot(
                weights.astype(jnp.bfloat16),
                values[g, start : start + span_keys, :],
                preferred_element_type=jnp.float32,
            )
        attended = (numer / denom).astype(jnp.bfloat16)
        for j in range(group):
            to = (g * group + j) * head_dim
            result[:, to : to + head_dim] = attended[j * new_len : (j + 1) * new_len]
    quarter = new_len // groups
    for distance, ref in enumerate(out_refs):
        start = pl.multiple_of((p ^ distance) * quarter, quarter)
        ref[...] = result[pl.ds(start, quarter), :]


def project(groups, where_ref, token_refs, weight_ref, tokens, weight, sems):
    p = where_ref[0]
    copies = [(weight_ref.at[p ^ distance], weight.at[distance]) for distance in range(groups)]
    copies += [(ref, tokens.at[e]) for e, ref in enumerate(token_refs)]
    copies = [
        pltpu.make_async_copy(source, target, sems.at[index])
        for index, (source, target) in enumerate(copies)
    ]
    for copy in copies[groups:] + copies[:groups]:
        copy.start()
    for copy in copies[groups:]:
        copy.wait()
    projected = None
    for distance in range(groups):
        rows = jnp.concatenate([tokens[e, distance] for e in range(len(token_refs))], axis=0)
        copies[distance].wait()
        term = lax.dot_general(
            rows,
            weight[distance],
            (((1,), (1,)), ((), ())),
            preferred_element_type=jnp.float32,
        )
        projected = term if projected is None else projected + term
    return projected


def first_output_kernel(groups, count, where_ref, *refs):
    out_ref, *scratch = refs[count + 1 :]
    out_ref[...] = project(groups, where_ref, refs[:count], refs[count], *scratch)


def output_kernel(groups, count, where_ref, first_ref, *refs):
    f = where_ref[1]
    shards = 2 * count
    out_refs = refs[count + 1 : count + 1 + shards]
    total, *scratch = refs[count + 1 + shards :]
    quarter = refs[0].shape[1]
    sub = quarter // shards
    total[...] = project(groups, where_ref, refs[:count], refs[count], *scratch)
    for e in range(shards):
        source = first_ref if e < count else total
        for distance, ref in enumerate(out_refs):
            start = pl.multiple_of(e % count * quarter + (f ^ distance) * sub, sub)
            ref[f ^ e] = source[pl.ds(start, sub), :].astype(jnp.bfloat16)


def finish_kernel(shards, where_ref, gain_ref, residual_ref, *refs):
    f = where_ref[1]
    piece_refs = refs[:shards]
    out_ref, projected = refs[shards:]
    for distance, ref in enumerate(piece_refs):
        projected[f ^ distance] = ref[...].astype(jnp.float32)
    gain = gain_ref[...]
    for request in range(out_ref.shape[0]):
        slot = where_ref[3 + request]
        line = jnp.concatenate([projected[k, slot] for k in range(shards)], axis=1)
        mean_square = jnp.mean(line * line, axis=1, keepdims=True)
        line = line * lax.rsqrt(mean_square + norm_eps) * gain
        out_ref[request] = (residual_ref[slot].astype(jnp.float32) + line).astype(jnp.bfloat16)


def pool_pieces(block, groups):
    return [block] + [swap(block, "pool", distance) for distance in range(1, groups)]


def local_small(
    hidden,
    slot_of_request,
    prefix_len,
    block_holder,
    block_slot,
    kv_pool,
    norm_gain,
    q_weight,
    k_weight,
    v_weight,
    o_weight,
    post_gain,
):
    shards = lax.axis_size("fsdp")
    groups = lax.axis_size("pool")
    f = lax.axis_index("fsdp")
    p = lax.axis_index("pool")
    half = shards // 2
    side = f // half
    new_len, width = hidden.shape[1:]
    requests = slot_of_request.shape[0]
    page_len = kv_pool.shape[1]
    kv_local = kv_pool.shape[2]
    head_dim = kv_pool.shape[3] // 2
    q_cols = q_weight.shape[1]
    kv_cols = k_weight.shape[1]
    max_blocks = block_holder.shape[1]
    per_holder = max_blocks // shards
    quarter = new_len // groups
    sub = quarter // shards
    features = o_weight.shape[0]
    bf16, f32 = jnp.bfloat16, jnp.float32
    where = jnp.concatenate(
        [jnp.stack([p, f, side]).astype(jnp.int32), slot_of_request, prefix_len]
    )
    shape = jax.ShapeDtypeStruct
    gain = norm_gain.reshape(1, width)
    rows = hidden[0]

    leaving, my_quarter = call(
        rows_kernel,
        [shape((quarter, width // 2), bf16), shape((quarter, width), bf16)],
        [pltpu.VMEM((quarter, width), f32), pltpu.SemaphoreType.DMA],
        quarter * width * 8,
        4 * quarter * width,
        rows,
        norm_gain,
        specs=[HBM, VMEM],
    )
    partner_piece = swap(leaving, "fsdp", half)
    joined = call(
        join_kernel,
        shape((features, q_cols + 2 * kv_cols), bf16),
        [],
        0,
        8 * features * q_cols,
        q_weight,
        k_weight,
        v_weight,
        specs=[VMEM, VMEM, VMEM],
    )

    flat_pool = kv_pool.reshape(kv_pool.shape[0], page_len * kv_local, 2 * head_dim)
    page_rows = per_holder * page_len * kv_local
    outgoing, valid = call(
        functools.partial(pages_kernel, requests, page_len),
        [
            shape((shards, page_rows, 2 * head_dim), bf16),
            shape((shards, per_holder * page_len), f32),
        ],
        [
            pltpu.SMEM((2 * per_holder,), jnp.int32),
            pltpu.SMEM((max_blocks + per_holder,), jnp.int32),
            pltpu.SMEM((shards,), jnp.int32),
        ],
        1 << 20,
        1 << 21,
        where,
        block_holder,
        block_slot,
        flat_pool,
        specs=[SMEM, SMEM, SMEM, VMEM],
    )
    near = swap(joined, "fsdp", 1)
    far = swap(after(joined, valid), "fsdp", 2)
    partner_pieces = pool_pieces(partner_piece, groups)
    arrived = lax.all_to_all(outgoing, "fsdp", split_axis=0, concat_axis=0, tiled=True)
    near_sums = call(
        functools.partial(near_kernel, groups, half),
        shape((new_len, q_cols + 2 * kv_cols), f32),
        [
            pltpu.VMEM((new_len, width // 2), bf16),
            pltpu.VMEM((2 * features, q_cols + 2 * kv_cols), bf16),
            pltpu.SemaphoreType.DMA((groups + 2,)),
        ],
        new_len * width * q_cols,
        width * (new_len + 2 * q_cols),
        where,
        *partner_pieces,
        joined,
        near,
        specs=[SMEM] + [HBM] * (groups + 2),
    )
    near_sums, far, arrived = lax.optimization_barrier((near_sums, far, arrived))
    weights = [joined, near, far, swap(far, "fsdp", 1)]
    out_weight = lax.all_gather(after(o_weight, *partner_pieces), "pool", axis=0, tiled=False)

    partial = call(
        functools.partial(partner_kernel, groups, half),
        shape((new_len, q_cols + 2 * kv_cols), bf16),
        [
            pltpu.VMEM((new_len, width // 2), bf16),
            pltpu.VMEM((2 * features, q_cols + 2 * kv_cols), bf16),
            pltpu.SemaphoreType.DMA((groups + 2,)),
        ],
        new_len * width * q_cols,
        width * (new_len + 2 * q_cols),
        where,
        near_sums,
        *partner_pieces,
        *weights[2:],
        specs=[SMEM, VMEM] + [HBM] * (groups + 2),
    )
    other = swap(partial, "fsdp", half)
    freqs = np.exp(np.arange(head_dim // 2) * (-2.0 * math.log(10000.0) / head_dim))
    freqs = np.concatenate([freqs, freqs]).astype(np.float32).reshape(1, head_dim)
    own, cosine, sine, keys, values = call(
        functools.partial(own_kernel, requests, half),
        [
            shape((new_len, q_cols + 2 * kv_cols), f32),
            shape((new_len, head_dim), f32),
            shape((new_len, head_dim), f32),
            shape((kv_local, max_blocks * page_len, head_dim), bf16),
            shape((kv_local, max_blocks * page_len, head_dim), bf16),
        ],
        [
            pltpu.VMEM((new_len, width), bf16),
            pltpu.VMEM((new_len, width // 2), bf16),
            pltpu.VMEM((width // 2, q_cols + 2 * kv_cols), bf16),
            pltpu.SemaphoreType.DMA((half + 1,)),
        ],
        new_len * width * (q_cols + 2 * kv_cols),
        width * (2 * new_len + q_cols + 2 * kv_cols),
        where,
        after(rows, partial),
        gain,
        freqs,
        arrived,
        *weights,
        specs=[SMEM, HBM, VMEM, VMEM, VMEM] + [HBM] * half,
    )

    residual = lax.all_to_all(
        after(my_quarter, own).reshape(shards, sub, width),
        "fsdp",
        split_axis=0,
        concat_axis=0,
        tiled=True,
    )

    keys_total = max_blocks * page_len
    quarters = call(
        functools.partial(attend_kernel, groups, kv_local, head_dim),
        [shape((quarter, q_cols), bf16)] * groups,
        [
            pltpu.VMEM((new_len, q_cols), bf16),
            pltpu.VMEM(other.shape, bf16),
            pltpu.SemaphoreType.DMA,
        ],
        4 * new_len * q_cols * (keys_total + new_len),
        1 << 22,
        where,
        own,
        other,
        cosine,
        sine,
        valid,
        keys,
        values,
        specs=[SMEM, VMEM, HBM, VMEM, VMEM, VMEM, VMEM, VMEM],
    )

    quarters = [
        swap(piece, "pool", distance) if distance else piece
        for distance, piece in enumerate(quarters)
    ]
    quarters = jnp.stack(quarters)
    tokens = {0: quarters}
    for distance in range(2, shards, 2):
        tokens[distance] = swap(quarters, "fsdp", distance)
    for distance in range(0, shards, 2):
        tokens[distance ^ 1] = swap(tokens[distance], "fsdp", 1)
    scratch = [
        pltpu.VMEM((half, groups, quarter, q_cols), bf16),
        pltpu.VMEM((groups, features, q_cols), bf16),
        pltpu.SemaphoreType.DMA((groups + half,)),
    ]
    first = call(
        functools.partial(first_output_kernel, groups, half),
        shape((half * quarter, features), f32),
        scratch,
        2 * half * quarter * features * groups * q_cols,
        1 << 22,
        where,
        *[tokens[distance] for distance in range(half)],
        out_weight,
        specs=[SMEM] + [HBM] * (half + 1),
    )
    projected = call(
        functools.partial(output_kernel, groups, half),
        [shape((shards, sub, features), bf16)] * shards,
        [pltpu.VMEM((half * quarter, features), f32)] + scratch,
        2 * half * quarter * features * groups * q_cols,
        1 << 22,
        where,
        first,
        *[tokens[distance] for distance in range(half, shards)],
        out_weight,
        specs=[SMEM, VMEM] + [HBM] * (half + 1),
    )
    finished = {0: projected[0]}
    for distance in range(half, shards):
        finished[distance] = swap(projected[distance], "fsdp", distance)
    for distance in range(1, half):
        piece = after(projected[distance], finished[half])
        finished[distance] = swap(piece, "fsdp", distance)
    finished = [finished[distance] for distance in range(shards)]
    return call(
        functools.partial(finish_kernel, shards),
        shape((requests, sub, width), bf16),
        [pltpu.VMEM((shards, shards, sub, features), f32)],
        1 << 20,
        1 << 20,
        where,
        post_gain.reshape(1, width),
        residual,
        *finished,
    )


def local(*arguments):
    return local_small(*arguments) if lax.axis_size("fsdp") == 8 else local_general(*arguments)


def solution(mesh):
    in_specs = (
        P("fsdp", None, None),
        P(),
        P(),
        P(),
        P(),
        P("fsdp", None, "pool", None),
        P(),
        P("fsdp", "pool"),
        P("fsdp", "pool"),
        P("fsdp", "pool"),
        P("fsdp", "pool"),
        P(),
    )
    out_specs = P(None, ("pool", "fsdp"), None)
    return jax.shard_map(local, mesh=mesh, in_specs=in_specs, out_specs=out_specs, check_vma=False)
```

```python
import functools
import math

import jax
import jax.numpy as jnp
import numpy as np
from jax import lax
from jax.experimental import pallas as pl
from jax.experimental.pallas import tpu as pltpu
from jax.sharding import PartitionSpec as P

softcap = 50.0
query_scale = 144.0 ** (-0.5)
norm_eps = 1e-06


def rms_scale(rows, gain):
    mean_square = jnp.mean(rows * rows, axis=-1, keepdims=True)
    return rows * lax.rsqrt(mean_square + norm_eps) * gain


def rotate(vectors, cosine, sine):
    half = vectors.shape[-1] // 2
    first = vectors[..., :half]
    second = vectors[..., half:]
    return jnp.concatenate(
        [first * cosine - second * sine, second * cosine + first * sine], axis=-1
    )


def capped_weights(scores, valid):
    return jnp.where(valid, jnp.exp(softcap * jnp.tanh(scores / softcap)), 0.0)


def swap(array, axis, distance):
    size = lax.axis_size(axis)
    return lax.ppermute(array, axis, [(i, i ^ distance) for i in range(size)])


def place(pieces, index):
    first = pieces[0]
    stacked = jnp.zeros((len(pieces),) + first.shape, first.dtype)
    for distance, piece in pieces.items():
        stacked = lax.dynamic_update_index_in_dim(stacked, piece, index ^ distance, 0)
    return stacked


def exchange(chunks, axis):
    size = lax.axis_size(axis)
    index = lax.axis_index(axis)
    if size > 8:
        return lax.all_to_all(chunks, axis, split_axis=0, concat_axis=0, tiled=True)
    pieces = {}
    for distance in range(size):
        chunk = lax.dynamic_index_in_dim(chunks, index ^ distance, 0, keepdims=False)
        pieces[distance] = swap(chunk, axis, distance) if distance else chunk
    return place(pieces, index)


def doubled(block, axis, span):
    pieces = {0: block}
    bit = span // 2
    while bit:
        for distance in list(pieces):
            pieces[distance ^ bit] = swap(pieces[distance], axis, bit)
        bit //= 2
    return pieces


def attend(queries, keys_new, values_new, cached, cached_valid):
    new_len, kv_local, group, head_dim = queries.shape

    def part(keys, values, valid):
        scores = jnp.einsum("tgjd,kgd->gjtk", queries, keys, preferred_element_type=jnp.float32)
        weights = capped_weights(scores, valid)
        numer = jnp.einsum(
            "gjtk,kgd->gjtd",
            weights.astype(jnp.bfloat16),
            values,
            preferred_element_type=jnp.float32,
        )
        return numer, jnp.sum(weights, axis=-1)

    query_index = jnp.arange(new_len, dtype=jnp.int32)
    causal = query_index[None, :] <= query_index[:, None]
    numer, denom = part(
        cached[..., :head_dim], cached[..., head_dim:], cached_valid[None, None, None, :]
    )
    more, added = part(keys_new, values_new, causal[None, None])
    attended = ((numer + more) / (denom + added)[..., None]).transpose(2, 0, 1, 3)
    return attended.reshape(new_len, kv_local * group * head_dim).astype(jnp.bfloat16)


def local_general(
    hidden,
    slot_of_request,
    prefix_len,
    block_holder,
    block_slot,
    kv_pool,
    norm_gain,
    q_weight,
    k_weight,
    v_weight,
    o_weight,
    post_gain,
):
    shards = lax.axis_size("fsdp")
    groups = lax.axis_size("pool")
    f = lax.axis_index("fsdp")
    p = lax.axis_index("pool")
    half = shards // 2
    side = f // half
    new_len, width = hidden.shape[1:]
    requests = slot_of_request.shape[0]
    page_len = kv_pool.shape[1]
    kv_local = kv_pool.shape[2]
    head_dim = kv_pool.shape[3] // 2
    q_cols = q_weight.shape[1]
    kv_cols = k_weight.shape[1]
    group = q_cols // kv_cols
    max_blocks = block_holder.shape[1]
    per_holder = max_blocks // shards
    quarter = new_len // groups
    sub = quarter // shards
    features = o_weight.shape[0]

    kv_pieces = doubled(jnp.concatenate([k_weight, v_weight], axis=1), "fsdp", half)
    q_pieces = doubled(q_weight, "fsdp", half)
    out_weight = lax.all_gather(o_weight, "pool", axis=0, tiled=False)

    rows = hidden[0]
    normed = rms_scale(rows.astype(jnp.float32), norm_gain).astype(jnp.bfloat16)
    own_rows = lax.dynamic_slice(normed, (0, side * (width // 2)), (new_len, width // 2))
    leaving = lax.dynamic_slice(
        normed, (p * quarter, (1 - side) * (width // 2)), (quarter, width // 2)
    )
    partner_piece = swap(leaving, "fsdp", half)
    partner_pieces = {0: partner_piece}
    for distance in range(1, groups):
        partner_pieces[distance] = swap(partner_piece, "pool", distance)
    partner_rows = place(partner_pieces, p).reshape(new_len, width // 2)

    request_ids = jnp.arange(requests, dtype=jnp.int32)
    request_at_slot = jnp.sum(
        jnp.where(slot_of_request[None, :] == request_ids[:, None], request_ids[None, :], 0), axis=1
    )
    holder_by_slot = jnp.take(block_holder, request_at_slot, axis=0)
    page_by_slot = jnp.take(block_slot, request_at_slot, axis=0)
    held_here = holder_by_slot == f
    held_rank = jnp.cumsum(held_here.astype(jnp.int32), axis=1) - 1
    rank_ids = jnp.arange(per_holder, dtype=jnp.int32)
    picked = held_here[:, :, None] & (held_rank[:, :, None] == rank_ids[None, None, :])
    local_pages = jnp.sum(jnp.where(picked, page_by_slot[:, :, None], 0), axis=1)
    flat_pool = kv_pool.reshape(kv_pool.shape[0], page_len * kv_local, 2 * head_dim)
    outgoing = jnp.take(flat_pool, local_pages, axis=0)
    outgoing = outgoing.reshape(shards, per_holder * page_len * kv_local, 2 * head_dim)
    arrived = exchange(outgoing, "fsdp")
    cached = arrived.reshape(max_blocks * page_len, kv_local, 2 * head_dim)

    my_request = lax.dynamic_index_in_dim(request_at_slot, f, keepdims=False)
    my_length = prefix_len[my_request]
    my_holders = block_holder[my_request]
    entry_ids = jnp.arange(max_blocks, dtype=jnp.int32)
    mine = my_holders[None, :] == jnp.arange(shards, dtype=jnp.int32)[:, None]
    my_rank = jnp.cumsum(mine.astype(jnp.int32), axis=1) - 1
    chosen = mine[:, None, :] & (my_rank[:, None, :] == rank_ids[None, :, None])
    entry = jnp.sum(jnp.where(chosen, entry_ids[None, None, :], 0), axis=2)
    cached_position = entry.reshape(-1, 1) * page_len + jnp.arange(page_len, dtype=jnp.int32)
    cached_valid = (cached_position < my_length).reshape(-1)

    residual_out = lax.dynamic_slice_in_dim(rows, p * quarter, quarter, 0).reshape(
        shards, sub, width
    )
    residual = exchange(residual_out, "fsdp")

    positions = (my_length + jnp.arange(new_len, dtype=jnp.int32)).astype(jnp.float32)
    freqs = jnp.exp(
        jnp.arange(head_dim // 2, dtype=jnp.float32) * (-2.0 * math.log(10000.0) / head_dim)
    )
    angles = positions[:, None] * freqs
    cosine = jnp.cos(angles)[:, None, :]
    sine = jnp.sin(angles)[:, None, :]

    def project(pieces):
        weight = place(pieces, f % half).reshape(width // 2, -1)
        partial = jnp.dot(partner_rows, weight, preferred_element_type=jnp.float32)
        other = swap(partial.astype(jnp.bfloat16), "fsdp", half)
        own = jnp.dot(own_rows, weight, preferred_element_type=jnp.float32)
        return own + other.astype(jnp.float32)

    kv_sum = project(kv_pieces)
    q_sum = project(q_pieces)
    queries = rotate(q_sum.reshape(new_len, kv_local * group, head_dim), cosine, sine)
    queries = (queries * query_scale).astype(jnp.bfloat16)
    queries = queries.reshape(new_len, kv_local, group, head_dim)
    keys_new = kv_sum[:, :kv_cols].reshape(new_len, kv_local, head_dim)
    keys_new = rotate(keys_new, cosine, sine).astype(jnp.bfloat16)
    values_new = kv_sum[:, kv_cols:].astype(jnp.bfloat16).reshape(new_len, kv_local, head_dim)
    attended = attend(queries, keys_new, values_new, cached, cached_valid)

    quarters = exchange(attended.reshape(groups, quarter, q_cols), "pool")
    token_pieces = {0: quarters}
    for distance in range(2, shards, 2):
        token_pieces[distance] = swap(quarters, "fsdp", distance)
    for distance in range(0, shards, 2):
        token_pieces[distance ^ 1] = swap(token_pieces[distance], "fsdp", 1)
    tokens = place(token_pieces, f)
    projected = jnp.einsum(
        "sptc,pfc->stf", tokens, out_weight, preferred_element_type=jnp.float32
    ).astype(jnp.bfloat16)
    projected = projected.reshape(shards, shards, sub, features).transpose(1, 0, 2, 3)
    finished = exchange(projected, "fsdp").transpose(1, 2, 0, 3).reshape(shards, sub, width)
    finished = residual.astype(jnp.float32) + rms_scale(finished.astype(jnp.float32), post_gain)
    return jnp.take(finished.astype(jnp.bfloat16), slot_of_request, axis=0)


VMEM = pl.BlockSpec(memory_space=pltpu.VMEM)
SMEM = pl.BlockSpec(memory_space=pltpu.SMEM)
HBM = pl.BlockSpec(memory_space=pltpu.HBM)


def call(kernel, outs, scratch, flops, nbytes, *operands, specs=None, out_specs=None):
    return pl.pallas_call(
        kernel,
        out_shape=outs,
        in_specs=specs or [SMEM] + [VMEM] * (len(operands) - 1),
        out_specs=out_specs or jax.tree.map(lambda _: VMEM, outs),
        scratch_shapes=scratch,
        compiler_params=pltpu.CompilerParams(vmem_limit_bytes=60 << 20),
        cost_estimate=pl.CostEstimate(flops=flops, bytes_accessed=nbytes, transcendentals=0),
    )(*operands)


def after(array, *earlier):
    return lax.optimization_barrier((array,) + earlier)[0]


def weight_copies(weight_refs, weight, f, half, sems):
    copies = []
    for distance, ref in enumerate(weight_refs):
        count = ref.shape[0]
        start = pl.multiple_of(((f ^ distance) & (half - 1)) * count, 64)
        copies.append(
            pltpu.make_async_copy(ref, weight.at[pl.ds(start, count), :], sems.at[distance])
        )
        copies[-1].start()
    return copies


def pair_product(groups, half, pair, where_ref, x_refs, w_refs, rows, weight, sems):
    p, f = where_ref[0], where_ref[1]
    copies = []
    for distance, ref in enumerate(w_refs):
        count = ref.shape[0]
        start = pl.multiple_of(((f ^ distance) & 1) * count, 64)
        copies.append((ref, weight.at[pl.ds(start, count), :]))
    span = weight.shape[0]
    columns = pl.ds(pl.multiple_of((((f & (half - 1)) >> 1) ^ pair) * span, 128), span)
    quarter = x_refs[0].shape[0]
    for distance, ref in enumerate(x_refs):
        start = pl.multiple_of((p ^ distance) * quarter, quarter)
        copies.append((ref, rows.at[pl.ds(start, quarter), :]))
    copies = [
        pltpu.make_async_copy(source, target, sems.at[index])
        for index, (source, target) in enumerate(copies)
    ]
    for copy in copies:
        copy.start()
    for copy in copies:
        copy.wait()
    return jnp.dot(rows[:, columns], weight[...], preferred_element_type=jnp.float32)


def near_kernel(groups, half, where_ref, *refs):
    x_refs, w_refs = refs[:groups], refs[groups : groups + 2]
    out_ref, *scratch = refs[groups + 2 :]
    out_ref[...] = pair_product(groups, half, 0, where_ref, x_refs, w_refs, *scratch)


def partner_kernel(groups, half, where_ref, near_ref, *refs):
    x_refs, w_refs = refs[:groups], refs[groups : groups + 2]
    out_ref, *scratch = refs[groups + 2 :]
    sums = pair_product(groups, half, 1, where_ref, x_refs, w_refs, *scratch)
    out_ref[...] = (near_ref[...] + sums).astype(jnp.bfloat16)


def row_scale(rows):
    return lax.rsqrt(jnp.mean(rows * rows, axis=1, keepdims=True) + norm_eps)


def prologue_kernel(
    hidden_ref, gain_ref, q_ref, k_ref, v_ref, leaving_ref, rows_ref, weight_ref, normed, sem
):
    p, f = lax.axis_index("pool"), lax.axis_index("fsdp")
    side = f // (lax.axis_size("fsdp") // 2)
    quarter, width = rows_ref.shape
    half_width = width // 2
    start = pl.multiple_of(p * quarter, quarter)
    rows_copy = pltpu.make_async_copy(hidden_ref.at[pl.ds(start, quarter), :], rows_ref, sem)
    rows_copy.start()
    at = 0
    for ref in (q_ref, k_ref, v_ref):
        weight_ref[:, at : at + ref.shape[1]] = ref[...]
        at += ref.shape[1]
    rows_copy.wait()
    rows = rows_ref[...].astype(jnp.float32)
    normed[...] = rows * row_scale(rows) * gain_ref[...].reshape(1, width)
    away = pl.multiple_of((1 - side) * half_width, 128)
    leaving_ref[...] = normed[:, pl.ds(away, half_width)].astype(jnp.bfloat16)


def pages_kernel(
    requests, page_len, where_ref, holder_ref, slot_ref, pool_ref, *refs
):
    f = where_ref[1]
    out_ref, valid_ref, listed, entries, counts = refs
    max_blocks = holder_ref.shape[1]
    shards = out_ref.shape[0]
    per = max_blocks // shards
    page_rows = pool_ref.shape[1]
    length, mine = jnp.int32(0), jnp.int32(0)
    for r in range(requests):
        at = where_ref[3 + r] == f
        length = length + jnp.where(at, where_ref[3 + requests + r], 0)
        mine = mine + jnp.where(at, r, 0)
    for r in range(requests):
        slot = where_ref[3 + r]

        def note(j, count):
            listed[count] = slot_ref[r, j]
            return count + jnp.where(holder_ref[r, j] == f, 1, 0)

        lax.fori_loop(0, max_blocks, note, jnp.int32(0), unroll=8)
        for k in range(per):
            out_ref[slot, k * page_rows : (k + 1) * page_rows, :] = pool_ref[listed[k]]
    for h in range(shards):
        counts[h] = 0

    def enter(j, carry):
        h = holder_ref[mine, j]
        count = counts[h]
        entries[h * per + count] = j
        counts[h] = count + 1
        return carry

    lax.fori_loop(0, max_blocks, enter, 0, unroll=4)
    row = lax.broadcasted_iota(jnp.int32, valid_ref.shape, 0)
    lane = lax.broadcasted_iota(jnp.int32, valid_ref.shape, 1)
    place_in = row * per + lane // page_len
    entry = jnp.zeros(valid_ref.shape, jnp.int32)
    for at in range(max_blocks):
        entry = jnp.where(place_in == at, entries[at], entry)
    position = entry * page_len + lane % page_len
    valid_ref[...] = jnp.where(position < length, 1.0, 0.0)


def part_pages(pages, keys, values):
    kv_local, _, head_dim = keys.shape
    span = pages.shape[1]
    per = span // kv_local
    row = lax.broadcasted_iota(jnp.int32, (span, span), 0)
    column = lax.broadcasted_iota(jnp.int32, (span, span), 1)
    part = (column == (row % per) * kv_local + row // per).astype(jnp.bfloat16)
    for holder in range(pages.shape[0]):
        parted = jnp.dot(part, pages[holder], preferred_element_type=jnp.float32)
        parted = parted.astype(jnp.bfloat16)
        at = holder * per
        for g in range(kv_local):
            lines = parted[g * per : (g + 1) * per]
            keys[g, at : at + per, :] = lines[:, :head_dim]
            values[g, at : at + per, :] = lines[:, head_dim:]


def own_kernel(requests, half, where_ref, hidden_ref, gain_ref, freq_ref, pages, *refs):
    f = where_ref[1]
    own_ref, cos_ref, sin_ref, keys, values, hidden, normed, weight, sems = refs[half:]
    rows_copy = pltpu.make_async_copy(hidden_ref, hidden, sems.at[half])
    rows_copy.start()
    copies = weight_copies(refs[:half], weight, f, half, sems)
    rows_copy.wait()
    new_len, width = hidden_ref.shape
    half_width = width // 2
    length = jnp.int32(0)
    for r in range(requests):
        length = length + jnp.where(where_ref[3 + r] == f, where_ref[3 + requests + r], 0)
    start = pl.multiple_of(where_ref[2] * half_width, 128)
    gain = gain_ref[:, pl.ds(start, half_width)]
    step = 32

    def norm(index, carry):
        at = pl.multiple_of(index * step, step)
        rows = hidden[pl.ds(at, step), :].astype(jnp.float32)
        scale = row_scale(rows)
        part = hidden[pl.ds(at, step), pl.ds(start, half_width)].astype(jnp.float32)
        normed[pl.ds(at, step), :] = (part * scale * gain).astype(jnp.bfloat16)
        return carry

    lax.fori_loop(0, new_len // step, norm, 0)
    part_pages(pages, keys, values)
    position = lax.broadcasted_iota(jnp.int32, cos_ref.shape, 0) + length
    angle = position.astype(jnp.float32) * freq_ref[...]
    lane = lax.broadcasted_iota(jnp.int32, cos_ref.shape, 1)
    cos_ref[...] = jnp.cos(angle)
    sine = jnp.sin(angle)
    sin_ref[...] = jnp.where(lane < cos_ref.shape[1] // 2, -sine, sine)
    for copy in copies:
        copy.wait()
    for at in range(0, own_ref.shape[1], 512):
        own_ref[:, at : at + 512] = jnp.dot(
            normed[...], weight[:, at : at + 512], preferred_element_type=jnp.float32
        )


def capped(scores):
    return jnp.exp2(jnp.tanh(scores * (1.0 / softcap)) * (softcap * math.log2(math.e)))


def attend_kernel(
    groups,
    kv_local,
    head_dim,
    where_ref,
    own,
    other_ref,
    cos_ref,
    sin_ref,
    valid_ref,
    keys,
    values,
    *refs,
):
    p = where_ref[0]
    out_refs = refs[:groups]
    result, other, sem = refs[groups:]
    copy = pltpu.make_async_copy(other_ref, other, sem)
    copy.start()
    new_len, q_cols = result.shape
    group = q_cols // (kv_local * head_dim)

    def sums(at):
        return own[:, at : at + head_dim] + other[:, at : at + head_dim].astype(jnp.float32)

    cosine, sine = cos_ref[...], sin_ref[...]

    def rope(vectors):
        return vectors * cosine + pltpu.roll(vectors, head_dim // 2, 1) * sine

    copy.wait()
    per = valid_ref.shape[1]
    place_at = keys.shape[1]
    span_keys = 2 * per
    t = lax.broadcasted_iota(jnp.int32, (group * new_len, new_len), 0) % new_len
    s = lax.broadcasted_iota(jnp.int32, (group * new_len, new_len), 1)
    causal = s <= t
    for g in range(kv_local):
        heads = [
            (rope(sums((g * group + j) * head_dim)) * query_scale).astype(jnp.bfloat16)
            for j in range(group)
        ]
        queries = jnp.concatenate(heads, axis=0)
        at = q_cols + g * head_dim
        new_key = rope(sums(at)).astype(jnp.bfloat16)
        new_value = sums(at + kv_local * head_dim).astype(jnp.bfloat16)

        def scores_of(key):
            return lax.dot_general(
                queries, key, (((1,), (1,)), ((), ())), preferred_element_type=jnp.float32
            )

        weights = jnp.where(causal, capped(scores_of(new_key)), 0.0)
        denom = jnp.sum(weights, axis=1, keepdims=True)
        numer = jnp.dot(
            weights.astype(jnp.bfloat16), new_value, preferred_element_type=jnp.float32
        )
        for start in range(0, place_at, span_keys):
            at = start // per
            valid = jnp.concatenate([valid_ref[at : at + 1], valid_ref[at + 1 : at + 2]], axis=1)
            valid = valid > 0.0
            weights = jnp.where(
                valid, capped(scores_of(keys[g, start : start + span_keys, :])), 0.0
            )
            denom = denom + jnp.sum(weights, axis=1, keepdims=True)
            numer = numer + jnp.dot(
                weights.astype(jnp.bfloat16),
                values[g, start : start + span_keys, :],
                preferred_element_type=jnp.float32,
            )
        attended = (numer / denom).astype(jnp.bfloat16)
        for j in range(group):
            to = (g * group + j) * head_dim
            result[:, to : to + head_dim] = attended[j * new_len : (j + 1) * new_len]
    quarter = new_len // groups
    for distance, ref in enumerate(out_refs):
        start = pl.multiple_of((p ^ distance) * quarter, quarter)
        ref[...] = result[pl.ds(start, quarter), :]


def output_kernel(groups, shards, where_ref, *refs):
    p, f = where_ref[0], where_ref[1]
    token_refs = refs[:shards]
    weight_ref = refs[shards]
    out_refs = refs[shards + 1 : 2 * shards + 1]
    total, tokens, weight, sems, token_sems = refs[2 * shards + 1 :]
    token_copies = [
        pltpu.make_async_copy(ref, tokens.at[e], token_sems.at[e])
        for e, ref in enumerate(token_refs)
    ]
    copies = [
        pltpu.make_async_copy(weight_ref.at[p ^ distance], weight.at[distance], sems.at[distance])
        for distance in range(groups)
    ]
    for copy in token_copies + copies:
        copy.start()
    for copy in token_copies:
        copy.wait()
    quarter = token_refs[0].shape[1]
    sub = quarter // shards
    projected = None
    for distance in range(groups):
        rows = jnp.concatenate([tokens[e, distance] for e in range(shards)], axis=0)
        copies[distance].wait()
        term = lax.dot_general(
            rows,
            weight[distance],
            (((1,), (1,)), ((), ())),
            preferred_element_type=jnp.float32,
        )
        projected = term if projected is None else projected + term
    total[...] = projected
    for e in range(shards):
        for distance, ref in enumerate(out_refs):
            start = pl.multiple_of(e * quarter + (f ^ distance) * sub, sub)
            ref[f ^ e] = total[pl.ds(start, sub), :].astype(jnp.bfloat16)


def finish_kernel(shards, where_ref, gain_ref, residual_ref, *refs):
    f = where_ref[1]
    piece_refs = refs[:shards]
    out_ref, projected = refs[shards:]
    for distance, ref in enumerate(piece_refs):
        projected[f ^ distance] = ref[...].astype(jnp.float32)
    gain = gain_ref[...]
    for request in range(out_ref.shape[0]):
        slot = where_ref[3 + request]
        line = jnp.concatenate([projected[k, slot] for k in range(shards)], axis=1)
        mean_square = jnp.mean(line * line, axis=1, keepdims=True)
        line = line * lax.rsqrt(mean_square + norm_eps) * gain
        out_ref[request] = (residual_ref[slot].astype(jnp.float32) + line).astype(jnp.bfloat16)


def pool_pieces(block, groups):
    return [block] + [swap(block, "pool", distance) for distance in range(1, groups)]


def local_small(
    hidden,
    slot_of_request,
    prefix_len,
    block_holder,
    block_slot,
    kv_pool,
    norm_gain,
    q_weight,
    k_weight,
    v_weight,
    o_weight,
    post_gain,
):
    shards = lax.axis_size("fsdp")
    groups = lax.axis_size("pool")
    f = lax.axis_index("fsdp")
    p = lax.axis_index("pool")
    half = shards // 2
    side = f // half
    new_len, width = hidden.shape[1:]
    requests = slot_of_request.shape[0]
    page_len = kv_pool.shape[1]
    kv_local = kv_pool.shape[2]
    head_dim = kv_pool.shape[3] // 2
    q_cols = q_weight.shape[1]
    kv_cols = k_weight.shape[1]
    max_blocks = block_holder.shape[1]
    per_holder = max_blocks // shards
    quarter = new_len // groups
    sub = quarter // shards
    features = o_weight.shape[0]
    bf16, f32 = jnp.bfloat16, jnp.float32
    where = jnp.concatenate(
        [jnp.stack([p, f, side]).astype(jnp.int32), slot_of_request, prefix_len]
    )
    shape = jax.ShapeDtypeStruct
    gain = norm_gain.reshape(1, width)
    rows = hidden[0]

    leaving, my_quarter, joined = call(
        prologue_kernel,
        [
            shape((quarter, width // 2), bf16),
            shape((quarter, width), bf16),
            shape((features, q_cols + 2 * kv_cols), bf16),
        ],
        [pltpu.VMEM((quarter, width), f32), pltpu.SemaphoreType.DMA],
        quarter * width * 8,
        4 * features * kv_cols,
        rows,
        norm_gain,
        q_weight,
        k_weight,
        v_weight,
        specs=[HBM, VMEM, VMEM, VMEM, VMEM],
    )
    partner_piece = swap(leaving, "fsdp", half)

    flat_pool = kv_pool.reshape(kv_pool.shape[0], page_len * kv_local, 2 * head_dim)
    page_rows = per_holder * page_len * kv_local
    outgoing, valid = call(
        functools.partial(pages_kernel, requests, page_len),
        [
            shape((shards, page_rows, 2 * head_dim), bf16),
            shape((shards, per_holder * page_len), f32),
        ],
        [
            pltpu.SMEM((2 * per_holder,), jnp.int32),
            pltpu.SMEM((max_blocks + per_holder,), jnp.int32),
            pltpu.SMEM((shards,), jnp.int32),
        ],
        1 << 20,
        1 << 21,
        where,
        block_holder,
        block_slot,
        flat_pool,
        specs=[SMEM, SMEM, SMEM, VMEM],
    )
    near = swap(joined, "fsdp", 1)
    far = swap(after(joined, valid), "fsdp", 2)
    partner_piece, near, outgoing = lax.optimization_barrier((partner_piece, near, outgoing))
    partner_pieces = pool_pieces(partner_piece, groups)
    arrived = lax.all_to_all(outgoing, "fsdp", split_axis=0, concat_axis=0, tiled=True)
    near_sums = call(
        functools.partial(near_kernel, groups, half),
        shape((new_len, q_cols + 2 * kv_cols), f32),
        [
            pltpu.VMEM((new_len, width // 2), bf16),
            pltpu.VMEM((2 * features, q_cols + 2 * kv_cols), bf16),
            pltpu.SemaphoreType.DMA((groups + 2,)),
        ],
        new_len * width * q_cols,
        width * (new_len + 2 * q_cols),
        where,
        *partner_pieces,
        joined,
        near,
        specs=[SMEM] + [HBM] * (groups + 2),
    )
    near_sums, far, arrived = lax.optimization_barrier((near_sums, far, arrived))
    weights = [joined, near, far, swap(far, "fsdp", 1)]
    out_weight = lax.all_gather(after(o_weight, *partner_pieces), "pool", axis=0, tiled=False)

    partial = call(
        functools.partial(partner_kernel, groups, half),
        shape((new_len, q_cols + 2 * kv_cols), bf16),
        [
            pltpu.VMEM((new_len, width // 2), bf16),
            pltpu.VMEM((2 * features, q_cols + 2 * kv_cols), bf16),
            pltpu.SemaphoreType.DMA((groups + 2,)),
        ],
        new_len * width * q_cols,
        width * (new_len + 2 * q_cols),
        where,
        near_sums,
        *partner_pieces,
        *weights[2:],
        specs=[SMEM, VMEM] + [HBM] * (groups + 2),
    )
    other = swap(partial, "fsdp", half)
    freqs = np.exp(np.arange(head_dim // 2) * (-2.0 * math.log(10000.0) / head_dim))
    freqs = np.concatenate([freqs, freqs]).astype(np.float32).reshape(1, head_dim)
    own, cosine, sine, keys, values = call(
        functools.partial(own_kernel, requests, half),
        [
            shape((new_len, q_cols + 2 * kv_cols), f32),
            shape((new_len, head_dim), f32),
            shape((new_len, head_dim), f32),
            shape((kv_local, max_blocks * page_len, head_dim), bf16),
            shape((kv_local, max_blocks * page_len, head_dim), bf16),
        ],
        [
            pltpu.VMEM((new_len, width), bf16),
            pltpu.VMEM((new_len, width // 2), bf16),
            pltpu.VMEM((width // 2, q_cols + 2 * kv_cols), bf16),
            pltpu.SemaphoreType.DMA((half + 1,)),
        ],
        new_len * width * (q_cols + 2 * kv_cols),
        width * (2 * new_len + q_cols + 2 * kv_cols),
        where,
        after(rows, partial),
        gain,
        freqs,
        arrived,
        *weights,
        specs=[SMEM, HBM, VMEM, VMEM, VMEM] + [HBM] * half,
    )

    residual = lax.all_to_all(
        after(my_quarter, own).reshape(shards, sub, width),
        "fsdp",
        split_axis=0,
        concat_axis=0,
        tiled=True,
    )

    keys_total = max_blocks * page_len
    quarters = call(
        functools.partial(attend_kernel, groups, kv_local, head_dim),
        [shape((quarter, q_cols), bf16)] * groups,
        [
            pltpu.VMEM((new_len, q_cols), bf16),
            pltpu.VMEM(other.shape, bf16),
            pltpu.SemaphoreType.DMA,
        ],
        4 * new_len * q_cols * (keys_total + new_len),
        1 << 22,
        where,
        own,
        other,
        cosine,
        sine,
        valid,
        keys,
        values,
        specs=[SMEM, VMEM, HBM, VMEM, VMEM, VMEM, VMEM, VMEM],
    )

    quarters = [
        swap(piece, "pool", distance) if distance else piece
        for distance, piece in enumerate(quarters)
    ]
    quarters = jnp.stack(quarters)
    tokens = {0: quarters}
    for distance in range(2, shards, 2):
        tokens[distance] = swap(quarters, "fsdp", distance)
    for distance in range(0, shards, 2):
        tokens[distance ^ 1] = swap(tokens[distance], "fsdp", 1)
    projected = call(
        functools.partial(output_kernel, groups, shards),
        [shape((shards, sub, features), bf16)] * shards,
        [
            pltpu.VMEM((shards * quarter, features), f32),
            pltpu.VMEM((shards, groups, quarter, q_cols), bf16),
            pltpu.VMEM((groups, features, q_cols), bf16),
            pltpu.SemaphoreType.DMA((groups,)),
            pltpu.SemaphoreType.DMA((shards,)),
        ],
        2 * shards * quarter * features * groups * q_cols,
        1 << 22,
        where,
        *[tokens[distance] for distance in range(shards)],
        out_weight,
        specs=[SMEM] + [HBM] * (shards + 1),
    )
    finished = [
        swap(piece, "fsdp", distance) if distance else piece
        for distance, piece in enumerate(projected)
    ]
    return call(
        functools.partial(finish_kernel, shards),
        shape((requests, sub, width), bf16),
        [pltpu.VMEM((shards, shards, sub, features), f32)],
        1 << 20,
        1 << 20,
        where,
        post_gain.reshape(1, width),
        residual,
        *finished,
    )


def local(*arguments):
    return local_small(*arguments) if lax.axis_size("fsdp") == 8 else local_general(*arguments)


def solution(mesh):
    in_specs = (
        P("fsdp", None, None),
        P(),
        P(),
        P(),
        P(),
        P("fsdp", None, "pool", None),
        P(),
        P("fsdp", "pool"),
        P("fsdp", "pool"),
        P("fsdp", "pool"),
        P("fsdp", "pool"),
        P(),
    )
    out_specs = P(None, ("pool", "fsdp"), None)
    return jax.shard_map(local, mesh=mesh, in_specs=in_specs, out_specs=out_specs, check_vma=False)
```

```python
import functools
import math

import jax
import jax.numpy as jnp
import numpy as np
from jax import lax
from jax.experimental import pallas as pl
from jax.experimental.pallas import tpu as pltpu
from jax.sharding import PartitionSpec as P

softcap = 50.0
query_scale = 144.0 ** (-0.5)
norm_eps = 1e-06


def rms_scale(rows, gain):
    mean_square = jnp.mean(rows * rows, axis=-1, keepdims=True)
    return rows * lax.rsqrt(mean_square + norm_eps) * gain


def rotate(vectors, cosine, sine):
    half = vectors.shape[-1] // 2
    first = vectors[..., :half]
    second = vectors[..., half:]
    return jnp.concatenate(
        [first * cosine - second * sine, second * cosine + first * sine], axis=-1
    )


def capped_weights(scores, valid):
    return jnp.where(valid, jnp.exp(softcap * jnp.tanh(scores / softcap)), 0.0)


def swap(array, axis, distance):
    size = lax.axis_size(axis)
    return lax.ppermute(array, axis, [(i, i ^ distance) for i in range(size)])


def place(pieces, index):
    first = pieces[0]
    stacked = jnp.zeros((len(pieces),) + first.shape, first.dtype)
    for distance, piece in pieces.items():
        stacked = lax.dynamic_update_index_in_dim(stacked, piece, index ^ distance, 0)
    return stacked


def exchange(chunks, axis):
    size = lax.axis_size(axis)
    index = lax.axis_index(axis)
    if size > 8:
        return lax.all_to_all(chunks, axis, split_axis=0, concat_axis=0, tiled=True)
    pieces = {}
    for distance in range(size):
        chunk = lax.dynamic_index_in_dim(chunks, index ^ distance, 0, keepdims=False)
        pieces[distance] = swap(chunk, axis, distance) if distance else chunk
    return place(pieces, index)


def doubled(block, axis, span):
    pieces = {0: block}
    bit = span // 2
    while bit:
        for distance in list(pieces):
            pieces[distance ^ bit] = swap(pieces[distance], axis, bit)
        bit //= 2
    return pieces


def attend(queries, keys_new, values_new, cached, cached_valid):
    new_len, kv_local, group, head_dim = queries.shape

    def part(keys, values, valid):
        scores = jnp.einsum("tgjd,kgd->gjtk", queries, keys, preferred_element_type=jnp.float32)
        weights = capped_weights(scores, valid)
        numer = jnp.einsum(
            "gjtk,kgd->gjtd",
            weights.astype(jnp.bfloat16),
            values,
            preferred_element_type=jnp.float32,
        )
        return numer, jnp.sum(weights, axis=-1)

    query_index = jnp.arange(new_len, dtype=jnp.int32)
    causal = query_index[None, :] <= query_index[:, None]
    numer, denom = part(
        cached[..., :head_dim], cached[..., head_dim:], cached_valid[None, None, None, :]
    )
    more, added = part(keys_new, values_new, causal[None, None])
    attended = ((numer + more) / (denom + added)[..., None]).transpose(2, 0, 1, 3)
    return attended.reshape(new_len, kv_local * group * head_dim).astype(jnp.bfloat16)


def local_general(
    hidden,
    slot_of_request,
    prefix_len,
    block_holder,
    block_slot,
    kv_pool,
    norm_gain,
    q_weight,
    k_weight,
    v_weight,
    o_weight,
    post_gain,
):
    shards = lax.axis_size("fsdp")
    groups = lax.axis_size("pool")
    f = lax.axis_index("fsdp")
    p = lax.axis_index("pool")
    half = shards // 2
    side = f // half
    new_len, width = hidden.shape[1:]
    requests = slot_of_request.shape[0]
    page_len = kv_pool.shape[1]
    kv_local = kv_pool.shape[2]
    head_dim = kv_pool.shape[3] // 2
    q_cols = q_weight.shape[1]
    kv_cols = k_weight.shape[1]
    group = q_cols // kv_cols
    max_blocks = block_holder.shape[1]
    per_holder = max_blocks // shards
    quarter = new_len // groups
    sub = quarter // shards
    features = o_weight.shape[0]

    kv_pieces = doubled(jnp.concatenate([k_weight, v_weight], axis=1), "fsdp", half)
    q_pieces = doubled(q_weight, "fsdp", half)
    out_weight = lax.all_gather(o_weight, "pool", axis=0, tiled=False)

    rows = hidden[0]
    normed = rms_scale(rows.astype(jnp.float32), norm_gain).astype(jnp.bfloat16)
    own_rows = lax.dynamic_slice(normed, (0, side * (width // 2)), (new_len, width // 2))
    leaving = lax.dynamic_slice(
        normed, (p * quarter, (1 - side) * (width // 2)), (quarter, width // 2)
    )
    partner_piece = swap(leaving, "fsdp", half)
    partner_pieces = {0: partner_piece}
    for distance in range(1, groups):
        partner_pieces[distance] = swap(partner_piece, "pool", distance)
    partner_rows = place(partner_pieces, p).reshape(new_len, width // 2)

    request_ids = jnp.arange(requests, dtype=jnp.int32)
    request_at_slot = jnp.sum(
        jnp.where(slot_of_request[None, :] == request_ids[:, None], request_ids[None, :], 0), axis=1
    )
    holder_by_slot = jnp.take(block_holder, request_at_slot, axis=0)
    page_by_slot = jnp.take(block_slot, request_at_slot, axis=0)
    held_here = holder_by_slot == f
    held_rank = jnp.cumsum(held_here.astype(jnp.int32), axis=1) - 1
    rank_ids = jnp.arange(per_holder, dtype=jnp.int32)
    picked = held_here[:, :, None] & (held_rank[:, :, None] == rank_ids[None, None, :])
    local_pages = jnp.sum(jnp.where(picked, page_by_slot[:, :, None], 0), axis=1)
    flat_pool = kv_pool.reshape(kv_pool.shape[0], page_len * kv_local, 2 * head_dim)
    outgoing = jnp.take(flat_pool, local_pages, axis=0)
    outgoing = outgoing.reshape(shards, per_holder * page_len * kv_local, 2 * head_dim)
    arrived = exchange(outgoing, "fsdp")
    cached = arrived.reshape(max_blocks * page_len, kv_local, 2 * head_dim)

    my_request = lax.dynamic_index_in_dim(request_at_slot, f, keepdims=False)
    my_length = prefix_len[my_request]
    my_holders = block_holder[my_request]
    entry_ids = jnp.arange(max_blocks, dtype=jnp.int32)
    mine = my_holders[None, :] == jnp.arange(shards, dtype=jnp.int32)[:, None]
    my_rank = jnp.cumsum(mine.astype(jnp.int32), axis=1) - 1
    chosen = mine[:, None, :] & (my_rank[:, None, :] == rank_ids[None, :, None])
    entry = jnp.sum(jnp.where(chosen, entry_ids[None, None, :], 0), axis=2)
    cached_position = entry.reshape(-1, 1) * page_len + jnp.arange(page_len, dtype=jnp.int32)
    cached_valid = (cached_position < my_length).reshape(-1)

    residual_out = lax.dynamic_slice_in_dim(rows, p * quarter, quarter, 0).reshape(
        shards, sub, width
    )
    residual = exchange(residual_out, "fsdp")

    positions = (my_length + jnp.arange(new_len, dtype=jnp.int32)).astype(jnp.float32)
    freqs = jnp.exp(
        jnp.arange(head_dim // 2, dtype=jnp.float32) * (-2.0 * math.log(10000.0) / head_dim)
    )
    angles = positions[:, None] * freqs
    cosine = jnp.cos(angles)[:, None, :]
    sine = jnp.sin(angles)[:, None, :]

    def project(pieces):
        weight = place(pieces, f % half).reshape(width // 2, -1)
        partial = jnp.dot(partner_rows, weight, preferred_element_type=jnp.float32)
        other = swap(partial.astype(jnp.bfloat16), "fsdp", half)
        own = jnp.dot(own_rows, weight, preferred_element_type=jnp.float32)
        return own + other.astype(jnp.float32)

    kv_sum = project(kv_pieces)
    q_sum = project(q_pieces)
    queries = rotate(q_sum.reshape(new_len, kv_local * group, head_dim), cosine, sine)
    queries = (queries * query_scale).astype(jnp.bfloat16)
    queries = queries.reshape(new_len, kv_local, group, head_dim)
    keys_new = kv_sum[:, :kv_cols].reshape(new_len, kv_local, head_dim)
    keys_new = rotate(keys_new, cosine, sine).astype(jnp.bfloat16)
    values_new = kv_sum[:, kv_cols:].astype(jnp.bfloat16).reshape(new_len, kv_local, head_dim)
    attended = attend(queries, keys_new, values_new, cached, cached_valid)

    quarters = exchange(attended.reshape(groups, quarter, q_cols), "pool")
    token_pieces = {0: quarters}
    for distance in range(2, shards, 2):
        token_pieces[distance] = swap(quarters, "fsdp", distance)
    for distance in range(0, shards, 2):
        token_pieces[distance ^ 1] = swap(token_pieces[distance], "fsdp", 1)
    tokens = place(token_pieces, f)
    projected = jnp.einsum(
        "sptc,pfc->stf", tokens, out_weight, preferred_element_type=jnp.float32
    ).astype(jnp.bfloat16)
    projected = projected.reshape(shards, shards, sub, features).transpose(1, 0, 2, 3)
    finished = exchange(projected, "fsdp").transpose(1, 2, 0, 3).reshape(shards, sub, width)
    finished = residual.astype(jnp.float32) + rms_scale(finished.astype(jnp.float32), post_gain)
    return jnp.take(finished.astype(jnp.bfloat16), slot_of_request, axis=0)


VMEM = pl.BlockSpec(memory_space=pltpu.VMEM)
SMEM = pl.BlockSpec(memory_space=pltpu.SMEM)
HBM = pl.BlockSpec(memory_space=pltpu.HBM)


def call(kernel, outs, scratch, flops, nbytes, *operands, specs=None, out_specs=None):
    return pl.pallas_call(
        kernel,
        out_shape=outs,
        in_specs=specs or [SMEM] + [VMEM] * (len(operands) - 1),
        out_specs=out_specs or jax.tree.map(lambda _: VMEM, outs),
        scratch_shapes=scratch,
        compiler_params=pltpu.CompilerParams(vmem_limit_bytes=60 << 20),
        cost_estimate=pl.CostEstimate(flops=flops, bytes_accessed=nbytes, transcendentals=0),
    )(*operands)


def after(array, *earlier):
    return lax.optimization_barrier((array,) + earlier)[0]


def weight_copies(weight_refs, weight, f, half, sems):
    copies = []
    for distance, ref in enumerate(weight_refs):
        count = ref.shape[0]
        start = pl.multiple_of(((f ^ distance) & (half - 1)) * count, 64)
        copies.append(
            pltpu.make_async_copy(ref, weight.at[pl.ds(start, count), :], sems.at[distance])
        )
        copies[-1].start()
    return copies


def pair_product(groups, half, pair, where_ref, x_refs, w_refs, rows, weight, sems):
    p, f = where_ref[0], where_ref[1]
    copies = []
    for distance, ref in enumerate(w_refs):
        count = ref.shape[0]
        start = pl.multiple_of(((f ^ distance) & 1) * count, 64)
        copies.append((ref, weight.at[pl.ds(start, count), :]))
    span = weight.shape[0]
    columns = pl.ds(pl.multiple_of((((f & (half - 1)) >> 1) ^ pair) * span, 128), span)
    quarter = x_refs[0].shape[0]
    for distance, ref in enumerate(x_refs):
        start = pl.multiple_of((p ^ distance) * quarter, quarter)
        copies.append((ref, rows.at[pl.ds(start, quarter), :]))
    copies = [
        pltpu.make_async_copy(source, target, sems.at[index])
        for index, (source, target) in enumerate(copies)
    ]
    for copy in copies:
        copy.start()
    for copy in copies:
        copy.wait()
    return jnp.dot(rows[:, columns], weight[...], preferred_element_type=jnp.float32)


def near_kernel(groups, half, where_ref, *refs):
    x_refs, w_refs = refs[:groups], refs[groups : groups + 2]
    out_ref, *scratch = refs[groups + 2 :]
    out_ref[...] = pair_product(groups, half, 0, where_ref, x_refs, w_refs, *scratch)


def partner_kernel(groups, half, where_ref, near_ref, *refs):
    x_refs, w_refs = refs[:groups], refs[groups : groups + 2]
    out_ref, *scratch = refs[groups + 2 :]
    sums = pair_product(groups, half, 1, where_ref, x_refs, w_refs, *scratch)
    out_ref[...] = (near_ref[...] + sums).astype(jnp.bfloat16)


def row_scale(rows):
    return lax.rsqrt(jnp.mean(rows * rows, axis=1, keepdims=True) + norm_eps)


def prologue_kernel(
    hidden_ref, gain_ref, q_ref, k_ref, v_ref, leaving_ref, rows_ref, weight_ref, normed, sem
):
    p, f = lax.axis_index("pool"), lax.axis_index("fsdp")
    side = f // (lax.axis_size("fsdp") // 2)
    quarter, width = rows_ref.shape
    half_width = width // 2
    start = pl.multiple_of(p * quarter, quarter)
    rows_copy = pltpu.make_async_copy(hidden_ref.at[pl.ds(start, quarter), :], rows_ref, sem)
    rows_copy.start()
    at = 0
    for ref in (q_ref, k_ref, v_ref):
        weight_ref[:, at : at + ref.shape[1]] = ref[...]
        at += ref.shape[1]
    rows_copy.wait()
    rows = rows_ref[...].astype(jnp.float32)
    normed[...] = rows * row_scale(rows) * gain_ref[...].reshape(1, width)
    away = pl.multiple_of((1 - side) * half_width, 128)
    leaving_ref[...] = normed[:, pl.ds(away, half_width)].astype(jnp.bfloat16)


def pages_kernel(
    requests, page_len, where_ref, holder_ref, slot_ref, pool_ref, *refs
):
    f = where_ref[1]
    out_ref, valid_ref, listed, entries, counts = refs
    max_blocks = holder_ref.shape[1]
    shards = out_ref.shape[0]
    per = max_blocks // shards
    page_rows = pool_ref.shape[1]
    length, mine = jnp.int32(0), jnp.int32(0)
    for r in range(requests):
        at = where_ref[3 + r] == f
        length = length + jnp.where(at, where_ref[3 + requests + r], 0)
        mine = mine + jnp.where(at, r, 0)
    for r in range(requests):
        slot = where_ref[3 + r]

        def note(j, count):
            listed[count] = slot_ref[r, j]
            return count + jnp.where(holder_ref[r, j] == f, 1, 0)

        lax.fori_loop(0, max_blocks, note, jnp.int32(0), unroll=8)
        for k in range(per):
            out_ref[slot, k * page_rows : (k + 1) * page_rows, :] = pool_ref[listed[k]]
    for h in range(shards):
        counts[h] = 0

    def enter(j, carry):
        h = holder_ref[mine, j]
        count = counts[h]
        entries[h * per + count] = j
        counts[h] = count + 1
        return carry

    lax.fori_loop(0, max_blocks, enter, 0, unroll=4)
    row = lax.broadcasted_iota(jnp.int32, valid_ref.shape, 0)
    lane = lax.broadcasted_iota(jnp.int32, valid_ref.shape, 1)
    place_in = row * per + lane // page_len
    entry = jnp.zeros(valid_ref.shape, jnp.int32)
    for at in range(max_blocks):
        entry = jnp.where(place_in == at, entries[at], entry)
    position = entry * page_len + lane % page_len
    valid_ref[...] = jnp.where(position < length, 1.0, 0.0)


def part_pages(pages, keys, values):
    kv_local, _, head_dim = keys.shape
    span = pages.shape[1]
    per = span // kv_local
    row = lax.broadcasted_iota(jnp.int32, (span, span), 0)
    column = lax.broadcasted_iota(jnp.int32, (span, span), 1)
    part = (column == (row % per) * kv_local + row // per).astype(jnp.bfloat16)
    for holder in range(pages.shape[0]):
        parted = jnp.dot(part, pages[holder], preferred_element_type=jnp.float32)
        parted = parted.astype(jnp.bfloat16)
        at = holder * per
        for g in range(kv_local):
            lines = parted[g * per : (g + 1) * per]
            keys[g, at : at + per, :] = lines[:, :head_dim]
            values[g, at : at + per, :] = lines[:, head_dim:]


def own_kernel(requests, half, where_ref, hidden_ref, gain_ref, freq_ref, pages, *refs):
    f = where_ref[1]
    own_ref, cos_ref, sin_ref, keys, values, hidden, normed, weight, sems = refs[half:]
    rows_copy = pltpu.make_async_copy(hidden_ref, hidden, sems.at[half])
    rows_copy.start()
    copies = weight_copies(refs[:half], weight, f, half, sems)
    rows_copy.wait()
    new_len, width = hidden_ref.shape
    half_width = width // 2
    length = jnp.int32(0)
    for r in range(requests):
        length = length + jnp.where(where_ref[3 + r] == f, where_ref[3 + requests + r], 0)
    start = pl.multiple_of(where_ref[2] * half_width, 128)
    gain = gain_ref[:, pl.ds(start, half_width)]
    step = 32

    def norm(index, carry):
        at = pl.multiple_of(index * step, step)
        rows = hidden[pl.ds(at, step), :].astype(jnp.float32)
        scale = row_scale(rows)
        part = hidden[pl.ds(at, step), pl.ds(start, half_width)].astype(jnp.float32)
        normed[pl.ds(at, step), :] = (part * scale * gain).astype(jnp.bfloat16)
        return carry

    lax.fori_loop(0, new_len // step, norm, 0)
    part_pages(pages, keys, values)
    position = lax.broadcasted_iota(jnp.int32, cos_ref.shape, 0) + length
    angle = position.astype(jnp.float32) * freq_ref[...]
    lane = lax.broadcasted_iota(jnp.int32, cos_ref.shape, 1)
    cos_ref[...] = jnp.cos(angle)
    sine = jnp.sin(angle)
    sin_ref[...] = jnp.where(lane < cos_ref.shape[1] // 2, -sine, sine)
    for copy in copies:
        copy.wait()
    for at in range(0, own_ref.shape[1], 512):
        own_ref[:, at : at + 512] = jnp.dot(
            normed[...], weight[:, at : at + 512], preferred_element_type=jnp.float32
        )


def capped(scores):
    return jnp.exp2(jnp.tanh(scores * (1.0 / softcap)) * (softcap * math.log2(math.e)))


def attend_kernel(
    groups,
    kv_local,
    head_dim,
    where_ref,
    own,
    other_ref,
    cos_ref,
    sin_ref,
    valid_ref,
    keys,
    values,
    *refs,
):
    p = where_ref[0]
    out_refs = refs[:groups]
    result, other, sem = refs[groups:]
    copy = pltpu.make_async_copy(other_ref, other, sem)
    copy.start()
    new_len, q_cols = result.shape
    group = q_cols // (kv_local * head_dim)

    def sums(at):
        return own[:, at : at + head_dim] + other[:, at : at + head_dim].astype(jnp.float32)

    cosine, sine = cos_ref[...], sin_ref[...]

    def rope(vectors):
        return vectors * cosine + pltpu.roll(vectors, head_dim // 2, 1) * sine

    copy.wait()
    per = valid_ref.shape[1]
    place_at = keys.shape[1]
    span_keys = 2 * per
    t = lax.broadcasted_iota(jnp.int32, (group * new_len, new_len), 0) % new_len
    s = lax.broadcasted_iota(jnp.int32, (group * new_len, new_len), 1)
    causal = s <= t
    for g in range(kv_local):
        heads = [
            (rope(sums((g * group + j) * head_dim)) * query_scale).astype(jnp.bfloat16)
            for j in range(group)
        ]
        queries = jnp.concatenate(heads, axis=0)
        at = q_cols + g * head_dim
        new_key = rope(sums(at)).astype(jnp.bfloat16)
        new_value = sums(at + kv_local * head_dim).astype(jnp.bfloat16)

        def scores_of(key):
            return lax.dot_general(
                queries, key, (((1,), (1,)), ((), ())), preferred_element_type=jnp.float32
            )

        weights = jnp.where(causal, capped(scores_of(new_key)), 0.0)
        denom = jnp.sum(weights, axis=1, keepdims=True)
        numer = jnp.dot(
            weights.astype(jnp.bfloat16), new_value, preferred_element_type=jnp.float32
        )
        for start in range(0, place_at, span_keys):
            at = start // per
            valid = jnp.concatenate([valid_ref[at : at + 1], valid_ref[at + 1 : at + 2]], axis=1)
            valid = valid > 0.0
            weights = jnp.where(
                valid, capped(scores_of(keys[g, start : start + span_keys, :])), 0.0
            )
            denom = denom + jnp.sum(weights, axis=1, keepdims=True)
            numer = numer + jnp.dot(
                weights.astype(jnp.bfloat16),
                values[g, start : start + span_keys, :],
                preferred_element_type=jnp.float32,
            )
        attended = (numer / denom).astype(jnp.bfloat16)
        for j in range(group):
            to = (g * group + j) * head_dim
            result[:, to : to + head_dim] = attended[j * new_len : (j + 1) * new_len]
    quarter = new_len // groups
    for distance, ref in enumerate(out_refs):
        start = pl.multiple_of((p ^ distance) * quarter, quarter)
        ref[...] = result[pl.ds(start, quarter), :]


def output_kernel(groups, shards, where_ref, *refs):
    p, f = where_ref[0], where_ref[1]
    token_refs = refs[:shards]
    weight_ref = refs[shards]
    out_refs = refs[shards + 1 : 2 * shards + 1]
    total, tokens, weight, sems, token_sems = refs[2 * shards + 1 :]
    token_copies = [
        pltpu.make_async_copy(ref, tokens.at[e], token_sems.at[e])
        for e, ref in enumerate(token_refs)
    ]
    copies = [
        pltpu.make_async_copy(weight_ref.at[p ^ distance], weight.at[distance], sems.at[distance])
        for distance in range(groups)
    ]
    for copy in token_copies + copies:
        copy.start()
    for copy in token_copies:
        copy.wait()
    quarter = token_refs[0].shape[1]
    sub = quarter // shards
    projected = None
    for distance in range(groups):
        rows = jnp.concatenate([tokens[e, distance] for e in range(shards)], axis=0)
        copies[distance].wait()
        term = lax.dot_general(
            rows,
            weight[distance],
            (((1,), (1,)), ((), ())),
            preferred_element_type=jnp.float32,
        )
        projected = term if projected is None else projected + term
    total[...] = projected
    for e in range(shards):
        for distance, ref in enumerate(out_refs):
            start = pl.multiple_of(e * quarter + (f ^ distance) * sub, sub)
            ref[f ^ e] = total[pl.ds(start, sub), :].astype(jnp.bfloat16)


def finish_kernel(shards, where_ref, gain_ref, residual_ref, *refs):
    f = where_ref[1]
    piece_refs = refs[:shards]
    out_ref, projected = refs[shards:]
    for distance, ref in enumerate(piece_refs):
        projected[f ^ distance] = ref[...].astype(jnp.float32)
    gain = gain_ref[...]
    for request in range(out_ref.shape[0]):
        slot = where_ref[3 + request]
        line = jnp.concatenate([projected[k, slot] for k in range(shards)], axis=1)
        mean_square = jnp.mean(line * line, axis=1, keepdims=True)
        line = line * lax.rsqrt(mean_square + norm_eps) * gain
        out_ref[request] = (residual_ref[slot].astype(jnp.float32) + line).astype(jnp.bfloat16)


def pool_pieces(block, groups):
    return [block] + [swap(block, "pool", distance) for distance in range(1, groups)]


def local_small(
    hidden,
    slot_of_request,
    prefix_len,
    block_holder,
    block_slot,
    kv_pool,
    norm_gain,
    q_weight,
    k_weight,
    v_weight,
    o_weight,
    post_gain,
):
    shards = lax.axis_size("fsdp")
    groups = lax.axis_size("pool")
    f = lax.axis_index("fsdp")
    p = lax.axis_index("pool")
    half = shards // 2
    side = f // half
    new_len, width = hidden.shape[1:]
    requests = slot_of_request.shape[0]
    page_len = kv_pool.shape[1]
    kv_local = kv_pool.shape[2]
    head_dim = kv_pool.shape[3] // 2
    q_cols = q_weight.shape[1]
    kv_cols = k_weight.shape[1]
    max_blocks = block_holder.shape[1]
    per_holder = max_blocks // shards
    quarter = new_len // groups
    sub = quarter // shards
    features = o_weight.shape[0]
    bf16, f32 = jnp.bfloat16, jnp.float32
    where = jnp.concatenate(
        [jnp.stack([p, f, side]).astype(jnp.int32), slot_of_request, prefix_len]
    )
    shape = jax.ShapeDtypeStruct
    gain = norm_gain.reshape(1, width)
    rows = hidden[0]

    leaving, my_quarter, joined = call(
        prologue_kernel,
        [
            shape((quarter, width // 2), bf16),
            shape((quarter, width), bf16),
            shape((features, q_cols + 2 * kv_cols), bf16),
        ],
        [pltpu.VMEM((quarter, width), f32), pltpu.SemaphoreType.DMA],
        quarter * width * 8,
        4 * features * kv_cols,
        rows,
        norm_gain,
        q_weight,
        k_weight,
        v_weight,
        specs=[HBM, VMEM, VMEM, VMEM, VMEM],
    )
    partner_piece = swap(leaving, "fsdp", half)

    flat_pool = kv_pool.reshape(kv_pool.shape[0], page_len * kv_local, 2 * head_dim)
    page_rows = per_holder * page_len * kv_local
    outgoing, valid = call(
        functools.partial(pages_kernel, requests, page_len),
        [
            shape((shards, page_rows, 2 * head_dim), bf16),
            shape((shards, per_holder * page_len), f32),
        ],
        [
            pltpu.SMEM((2 * per_holder,), jnp.int32),
            pltpu.SMEM((max_blocks + per_holder,), jnp.int32),
            pltpu.SMEM((shards,), jnp.int32),
        ],
        1 << 20,
        1 << 21,
        where,
        block_holder,
        block_slot,
        flat_pool,
        specs=[SMEM, SMEM, SMEM, VMEM],
    )
    near = swap(joined, "fsdp", 1)
    partner_piece, near, outgoing = lax.optimization_barrier((partner_piece, near, outgoing))
    far = swap(after(joined, partner_piece), "fsdp", 2)
    partner_pieces = pool_pieces(partner_piece, groups)
    arrived = lax.all_to_all(outgoing, "fsdp", split_axis=0, concat_axis=0, tiled=True)
    near_sums = call(
        functools.partial(near_kernel, groups, half),
        shape((new_len, q_cols + 2 * kv_cols), f32),
        [
            pltpu.VMEM((new_len, width // 2), bf16),
            pltpu.VMEM((2 * features, q_cols + 2 * kv_cols), bf16),
            pltpu.SemaphoreType.DMA((groups + 2,)),
        ],
        new_len * width * q_cols,
        width * (new_len + 2 * q_cols),
        where,
        *partner_pieces,
        joined,
        near,
        specs=[SMEM] + [HBM] * (groups + 2),
    )
    near_sums, far = lax.optimization_barrier((near_sums, far))
    weights = [joined, near, far, swap(far, "fsdp", 1)]
    out_weight = lax.all_gather(after(o_weight, *partner_pieces), "pool", axis=0, tiled=False)

    partial = call(
        functools.partial(partner_kernel, groups, half),
        shape((new_len, q_cols + 2 * kv_cols), bf16),
        [
            pltpu.VMEM((new_len, width // 2), bf16),
            pltpu.VMEM((2 * features, q_cols + 2 * kv_cols), bf16),
            pltpu.SemaphoreType.DMA((groups + 2,)),
        ],
        new_len * width * q_cols,
        width * (new_len + 2 * q_cols),
        where,
        near_sums,
        *partner_pieces,
        *weights[2:],
        specs=[SMEM, VMEM] + [HBM] * (groups + 2),
    )
    other = swap(partial, "fsdp", half)
    freqs = np.exp(np.arange(head_dim // 2) * (-2.0 * math.log(10000.0) / head_dim))
    freqs = np.concatenate([freqs, freqs]).astype(np.float32).reshape(1, head_dim)
    own, cosine, sine, keys, values = call(
        functools.partial(own_kernel, requests, half),
        [
            shape((new_len, q_cols + 2 * kv_cols), f32),
            shape((new_len, head_dim), f32),
            shape((new_len, head_dim), f32),
            shape((kv_local, max_blocks * page_len, head_dim), bf16),
            shape((kv_local, max_blocks * page_len, head_dim), bf16),
        ],
        [
            pltpu.VMEM((new_len, width), bf16),
            pltpu.VMEM((new_len, width // 2), bf16),
            pltpu.VMEM((width // 2, q_cols + 2 * kv_cols), bf16),
            pltpu.SemaphoreType.DMA((half + 1,)),
        ],
        new_len * width * (q_cols + 2 * kv_cols),
        width * (2 * new_len + q_cols + 2 * kv_cols),
        where,
        after(rows, partial),
        gain,
        freqs,
        arrived,
        *weights,
        specs=[SMEM, HBM, VMEM, VMEM, VMEM] + [HBM] * half,
    )

    residual = lax.all_to_all(
        after(my_quarter, own).reshape(shards, sub, width),
        "fsdp",
        split_axis=0,
        concat_axis=0,
        tiled=True,
    )

    keys_total = max_blocks * page_len
    quarters = call(
        functools.partial(attend_kernel, groups, kv_local, head_dim),
        [shape((quarter, q_cols), bf16)] * groups,
        [
            pltpu.VMEM((new_len, q_cols), bf16),
            pltpu.VMEM(other.shape, bf16),
            pltpu.SemaphoreType.DMA,
        ],
        4 * new_len * q_cols * (keys_total + new_len),
        1 << 22,
        where,
        own,
        other,
        cosine,
        sine,
        valid,
        keys,
        values,
        specs=[SMEM, VMEM, HBM, VMEM, VMEM, VMEM, VMEM, VMEM],
    )

    quarters = [
        swap(piece, "pool", distance) if distance else piece
        for distance, piece in enumerate(quarters)
    ]
    quarters = jnp.stack(quarters)
    tokens = {0: quarters}
    for distance in range(2, shards, 2):
        tokens[distance] = swap(quarters, "fsdp", distance)
    for distance in range(0, shards, 2):
        tokens[distance ^ 1] = swap(tokens[distance], "fsdp", 1)
    projected = call(
        functools.partial(output_kernel, groups, shards),
        [shape((shards, sub, features), bf16)] * shards,
        [
            pltpu.VMEM((shards * quarter, features), f32),
            pltpu.VMEM((shards, groups, quarter, q_cols), bf16),
            pltpu.VMEM((groups, features, q_cols), bf16),
            pltpu.SemaphoreType.DMA((groups,)),
            pltpu.SemaphoreType.DMA((shards,)),
        ],
        2 * shards * quarter * features * groups * q_cols,
        1 << 22,
        where,
        *[tokens[distance] for distance in range(shards)],
        out_weight,
        specs=[SMEM] + [HBM] * (shards + 1),
    )
    finished = [
        swap(piece, "fsdp", distance) if distance else piece
        for distance, piece in enumerate(projected)
    ]
    return call(
        functools.partial(finish_kernel, shards),
        shape((requests, sub, width), bf16),
        [pltpu.VMEM((shards, shards, sub, features), f32)],
        1 << 20,
        1 << 20,
        where,
        post_gain.reshape(1, width),
        residual,
        *finished,
    )


def local(*arguments):
    return local_small(*arguments) if lax.axis_size("fsdp") == 8 else local_general(*arguments)


def solution(mesh):
    in_specs = (
        P("fsdp", None, None),
        P(),
        P(),
        P(),
        P(),
        P("fsdp", None, "pool", None),
        P(),
        P("fsdp", "pool"),
        P("fsdp", "pool"),
        P("fsdp", "pool"),
        P("fsdp", "pool"),
        P(),
    )
    out_specs = P(None, ("pool", "fsdp"), None)
    return jax.shard_map(local, mesh=mesh, in_specs=in_specs, out_specs=out_specs, check_vma=False)
```

```python
import functools
import math

import jax
import jax.numpy as jnp
import numpy as np
from jax import lax
from jax.experimental import pallas as pl
from jax.experimental.pallas import tpu as pltpu
from jax.sharding import PartitionSpec as P

softcap = 50.0
query_scale = 144.0 ** (-0.5)
norm_eps = 1e-06


def rms_scale(rows, gain):
    mean_square = jnp.mean(rows * rows, axis=-1, keepdims=True)
    return rows * lax.rsqrt(mean_square + norm_eps) * gain


def rotate(vectors, cosine, sine):
    half = vectors.shape[-1] // 2
    first = vectors[..., :half]
    second = vectors[..., half:]
    return jnp.concatenate(
        [first * cosine - second * sine, second * cosine + first * sine], axis=-1
    )


def capped_weights(scores, valid):
    return jnp.where(valid, jnp.exp(softcap * jnp.tanh(scores / softcap)), 0.0)


def swap(array, axis, distance):
    size = lax.axis_size(axis)
    return lax.ppermute(array, axis, [(i, i ^ distance) for i in range(size)])


def place(pieces, index):
    first = pieces[0]
    stacked = jnp.zeros((len(pieces),) + first.shape, first.dtype)
    for distance, piece in pieces.items():
        stacked = lax.dynamic_update_index_in_dim(stacked, piece, index ^ distance, 0)
    return stacked


def exchange(chunks, axis):
    size = lax.axis_size(axis)
    index = lax.axis_index(axis)
    if size > 8:
        return lax.all_to_all(chunks, axis, split_axis=0, concat_axis=0, tiled=True)
    pieces = {}
    for distance in range(size):
        chunk = lax.dynamic_index_in_dim(chunks, index ^ distance, 0, keepdims=False)
        pieces[distance] = swap(chunk, axis, distance) if distance else chunk
    return place(pieces, index)


def doubled(block, axis, span):
    pieces = {0: block}
    bit = span // 2
    while bit:
        for distance in list(pieces):
            pieces[distance ^ bit] = swap(pieces[distance], axis, bit)
        bit //= 2
    return pieces


def attend(queries, keys_new, values_new, cached, cached_valid):
    new_len, kv_local, group, head_dim = queries.shape

    def part(keys, values, valid):
        scores = jnp.einsum("tgjd,kgd->gjtk", queries, keys, preferred_element_type=jnp.float32)
        weights = capped_weights(scores, valid)
        numer = jnp.einsum(
            "gjtk,kgd->gjtd",
            weights.astype(jnp.bfloat16),
            values,
            preferred_element_type=jnp.float32,
        )
        return numer, jnp.sum(weights, axis=-1)

    query_index = jnp.arange(new_len, dtype=jnp.int32)
    causal = query_index[None, :] <= query_index[:, None]
    numer, denom = part(
        cached[..., :head_dim], cached[..., head_dim:], cached_valid[None, None, None, :]
    )
    more, added = part(keys_new, values_new, causal[None, None])
    attended = ((numer + more) / (denom + added)[..., None]).transpose(2, 0, 1, 3)
    return attended.reshape(new_len, kv_local * group * head_dim).astype(jnp.bfloat16)


def local_general(
    hidden,
    slot_of_request,
    prefix_len,
    block_holder,
    block_slot,
    kv_pool,
    norm_gain,
    q_weight,
    k_weight,
    v_weight,
    o_weight,
    post_gain,
):
    shards = lax.axis_size("fsdp")
    groups = lax.axis_size("pool")
    f = lax.axis_index("fsdp")
    p = lax.axis_index("pool")
    half = shards // 2
    side = f // half
    new_len, width = hidden.shape[1:]
    requests = slot_of_request.shape[0]
    page_len = kv_pool.shape[1]
    kv_local = kv_pool.shape[2]
    head_dim = kv_pool.shape[3] // 2
    q_cols = q_weight.shape[1]
    kv_cols = k_weight.shape[1]
    group = q_cols // kv_cols
    max_blocks = block_holder.shape[1]
    per_holder = max_blocks // shards
    quarter = new_len // groups
    sub = quarter // shards
    features = o_weight.shape[0]

    kv_pieces = doubled(jnp.concatenate([k_weight, v_weight], axis=1), "fsdp", half)
    q_pieces = doubled(q_weight, "fsdp", half)
    out_weight = lax.all_gather(o_weight, "pool", axis=0, tiled=False)

    rows = hidden[0]
    normed = rms_scale(rows.astype(jnp.float32), norm_gain).astype(jnp.bfloat16)
    own_rows = lax.dynamic_slice(normed, (0, side * (width // 2)), (new_len, width // 2))
    leaving = lax.dynamic_slice(
        normed, (p * quarter, (1 - side) * (width // 2)), (quarter, width // 2)
    )
    partner_piece = swap(leaving, "fsdp", half)
    partner_pieces = {0: partner_piece}
    for distance in range(1, groups):
        partner_pieces[distance] = swap(partner_piece, "pool", distance)
    partner_rows = place(partner_pieces, p).reshape(new_len, width // 2)

    request_ids = jnp.arange(requests, dtype=jnp.int32)
    request_at_slot = jnp.sum(
        jnp.where(slot_of_request[None, :] == request_ids[:, None], request_ids[None, :], 0), axis=1
    )
    holder_by_slot = jnp.take(block_holder, request_at_slot, axis=0)
    page_by_slot = jnp.take(block_slot, request_at_slot, axis=0)
    held_here = holder_by_slot == f
    held_rank = jnp.cumsum(held_here.astype(jnp.int32), axis=1) - 1
    rank_ids = jnp.arange(per_holder, dtype=jnp.int32)
    picked = held_here[:, :, None] & (held_rank[:, :, None] == rank_ids[None, None, :])
    local_pages = jnp.sum(jnp.where(picked, page_by_slot[:, :, None], 0), axis=1)
    flat_pool = kv_pool.reshape(kv_pool.shape[0], page_len * kv_local, 2 * head_dim)
    outgoing = jnp.take(flat_pool, local_pages, axis=0)
    outgoing = outgoing.reshape(shards, per_holder * page_len * kv_local, 2 * head_dim)
    arrived = exchange(outgoing, "fsdp")
    cached = arrived.reshape(max_blocks * page_len, kv_local, 2 * head_dim)

    my_request = lax.dynamic_index_in_dim(request_at_slot, f, keepdims=False)
    my_length = prefix_len[my_request]
    my_holders = block_holder[my_request]
    entry_ids = jnp.arange(max_blocks, dtype=jnp.int32)
    mine = my_holders[None, :] == jnp.arange(shards, dtype=jnp.int32)[:, None]
    my_rank = jnp.cumsum(mine.astype(jnp.int32), axis=1) - 1
    chosen = mine[:, None, :] & (my_rank[:, None, :] == rank_ids[None, :, None])
    entry = jnp.sum(jnp.where(chosen, entry_ids[None, None, :], 0), axis=2)
    cached_position = entry.reshape(-1, 1) * page_len + jnp.arange(page_len, dtype=jnp.int32)
    cached_valid = (cached_position < my_length).reshape(-1)

    residual_out = lax.dynamic_slice_in_dim(rows, p * quarter, quarter, 0).reshape(
        shards, sub, width
    )
    residual = exchange(residual_out, "fsdp")

    positions = (my_length + jnp.arange(new_len, dtype=jnp.int32)).astype(jnp.float32)
    freqs = jnp.exp(
        jnp.arange(head_dim // 2, dtype=jnp.float32) * (-2.0 * math.log(10000.0) / head_dim)
    )
    angles = positions[:, None] * freqs
    cosine = jnp.cos(angles)[:, None, :]
    sine = jnp.sin(angles)[:, None, :]

    def project(pieces):
        weight = place(pieces, f % half).reshape(width // 2, -1)
        partial = jnp.dot(partner_rows, weight, preferred_element_type=jnp.float32)
        other = swap(partial.astype(jnp.bfloat16), "fsdp", half)
        own = jnp.dot(own_rows, weight, preferred_element_type=jnp.float32)
        return own + other.astype(jnp.float32)

    kv_sum = project(kv_pieces)
    q_sum = project(q_pieces)
    queries = rotate(q_sum.reshape(new_len, kv_local * group, head_dim), cosine, sine)
    queries = (queries * query_scale).astype(jnp.bfloat16)
    queries = queries.reshape(new_len, kv_local, group, head_dim)
    keys_new = kv_sum[:, :kv_cols].reshape(new_len, kv_local, head_dim)
    keys_new = rotate(keys_new, cosine, sine).astype(jnp.bfloat16)
    values_new = kv_sum[:, kv_cols:].astype(jnp.bfloat16).reshape(new_len, kv_local, head_dim)
    attended = attend(queries, keys_new, values_new, cached, cached_valid)

    quarters = exchange(attended.reshape(groups, quarter, q_cols), "pool")
    token_pieces = {0: quarters}
    for distance in range(2, shards, 2):
        token_pieces[distance] = swap(quarters, "fsdp", distance)
    for distance in range(0, shards, 2):
        token_pieces[distance ^ 1] = swap(token_pieces[distance], "fsdp", 1)
    tokens = place(token_pieces, f)
    projected = jnp.einsum(
        "sptc,pfc->stf", tokens, out_weight, preferred_element_type=jnp.float32
    ).astype(jnp.bfloat16)
    projected = projected.reshape(shards, shards, sub, features).transpose(1, 0, 2, 3)
    finished = exchange(projected, "fsdp").transpose(1, 2, 0, 3).reshape(shards, sub, width)
    finished = residual.astype(jnp.float32) + rms_scale(finished.astype(jnp.float32), post_gain)
    return jnp.take(finished.astype(jnp.bfloat16), slot_of_request, axis=0)


VMEM = pl.BlockSpec(memory_space=pltpu.VMEM)
SMEM = pl.BlockSpec(memory_space=pltpu.SMEM)
HBM = pl.BlockSpec(memory_space=pltpu.HBM)


def call(kernel, outs, scratch, flops, nbytes, *operands, specs=None, out_specs=None):
    return pl.pallas_call(
        kernel,
        out_shape=outs,
        in_specs=specs or [SMEM] + [VMEM] * (len(operands) - 1),
        out_specs=out_specs or jax.tree.map(lambda _: VMEM, outs),
        scratch_shapes=scratch,
        compiler_params=pltpu.CompilerParams(vmem_limit_bytes=60 << 20),
        cost_estimate=pl.CostEstimate(flops=flops, bytes_accessed=nbytes, transcendentals=0),
    )(*operands)


def after(array, *earlier):
    return lax.optimization_barrier((array,) + earlier)[0]


def weight_copies(weight_refs, weight, f, half, sems):
    copies = []
    for distance, ref in enumerate(weight_refs):
        count = ref.shape[0]
        start = pl.multiple_of(((f ^ distance) & (half - 1)) * count, 64)
        copies.append(
            pltpu.make_async_copy(ref, weight.at[pl.ds(start, count), :], sems.at[distance])
        )
        copies[-1].start()
    return copies


def pair_product(groups, half, pair, where_ref, x_refs, chunks, rows, sems):
    p, f = where_ref[0], where_ref[1]
    copies = []
    quarter = x_refs[0].shape[0]
    for distance, ref in enumerate(x_refs):
        start = pl.multiple_of((p ^ distance) * quarter, quarter)
        copies.append((ref, rows.at[pl.ds(start, quarter), :]))
    for w_refs, weight in chunks:
        for distance, ref in enumerate(w_refs):
            count = ref.shape[0]
            start = pl.multiple_of(((f ^ distance) & 1) * count, 64)
            copies.append((ref, weight.at[pl.ds(start, count), :]))
    copies = [
        pltpu.make_async_copy(source, target, sems.at[index])
        for index, (source, target) in enumerate(copies)
    ]
    for copy in copies:
        copy.start()
    for copy in copies:
        copy.wait()
    span = chunks[0][1].shape[0]
    columns = pl.ds(pl.multiple_of((((f & (half - 1)) >> 1) ^ pair) * span, 128), span)
    return [
        jnp.dot(rows[:, columns], weight[...], preferred_element_type=jnp.float32)
        for _, weight in chunks
    ]


def near_kernel(groups, half, where_ref, *refs):
    x_refs, q_refs, kv_refs = refs[:groups], refs[groups : groups + 2], refs[groups + 2 : groups + 4]
    q_out, kv_out, rows, q_weight, kv_weight, sems = refs[groups + 4 :]
    chunks = [(q_refs, q_weight), (kv_refs, kv_weight)]
    q_out[...], kv_out[...] = pair_product(
        groups, half, 0, where_ref, x_refs, chunks, rows, sems
    )


def partner_kernel(groups, half, where_ref, near_ref, *refs):
    x_refs, w_refs = refs[:groups], refs[groups : groups + 2]
    out_ref, rows, weight, sems = refs[groups + 2 :]
    (sums,) = pair_product(groups, half, 1, where_ref, x_refs, [(w_refs, weight)], rows, sems)
    out_ref[...] = (near_ref[...] + sums).astype(jnp.bfloat16)


def row_scale(rows):
    return lax.rsqrt(jnp.mean(rows * rows, axis=1, keepdims=True) + norm_eps)


def prologue_kernel(
    hidden_ref, gain_ref, k_ref, v_ref, leaving_ref, rows_ref, weight_ref, normed, sem
):
    p, f = lax.axis_index("pool"), lax.axis_index("fsdp")
    side = f // (lax.axis_size("fsdp") // 2)
    quarter, width = rows_ref.shape
    half_width = width // 2
    start = pl.multiple_of(p * quarter, quarter)
    rows_copy = pltpu.make_async_copy(hidden_ref.at[pl.ds(start, quarter), :], rows_ref, sem)
    rows_copy.start()
    at = 0
    for ref in (k_ref, v_ref):
        weight_ref[:, at : at + ref.shape[1]] = ref[...]
        at += ref.shape[1]
    rows_copy.wait()
    rows = rows_ref[...].astype(jnp.float32)
    normed[...] = rows * row_scale(rows) * gain_ref[...].reshape(1, width)
    away = pl.multiple_of((1 - side) * half_width, 128)
    leaving_ref[...] = normed[:, pl.ds(away, half_width)].astype(jnp.bfloat16)


def pages_kernel(
    requests, page_len, where_ref, holder_ref, slot_ref, pool_ref, *refs
):
    f = where_ref[1]
    out_ref, valid_ref, listed, entries, counts = refs
    max_blocks = holder_ref.shape[1]
    shards = out_ref.shape[0]
    per = max_blocks // shards
    page_rows = pool_ref.shape[1]
    length, mine = jnp.int32(0), jnp.int32(0)
    for r in range(requests):
        at = where_ref[3 + r] == f
        length = length + jnp.where(at, where_ref[3 + requests + r], 0)
        mine = mine + jnp.where(at, r, 0)
    for r in range(requests):
        slot = where_ref[3 + r]

        def note(j, count):
            listed[count] = slot_ref[r, j]
            return count + jnp.where(holder_ref[r, j] == f, 1, 0)

        lax.fori_loop(0, max_blocks, note, jnp.int32(0), unroll=8)
        for k in range(per):
            out_ref[slot, k * page_rows : (k + 1) * page_rows, :] = pool_ref[listed[k]]
    for h in range(shards):
        counts[h] = 0

    def enter(j, carry):
        h = holder_ref[mine, j]
        count = counts[h]
        entries[h * per + count] = j
        counts[h] = count + 1
        return carry

    lax.fori_loop(0, max_blocks, enter, 0, unroll=4)
    row = lax.broadcasted_iota(jnp.int32, valid_ref.shape, 0)
    lane = lax.broadcasted_iota(jnp.int32, valid_ref.shape, 1)
    place_in = row * per + lane // page_len
    entry = jnp.zeros(valid_ref.shape, jnp.int32)
    for at in range(max_blocks):
        entry = jnp.where(place_in == at, entries[at], entry)
    position = entry * page_len + lane % page_len
    valid_ref[...] = jnp.where(position < length, 1.0, 0.0)


def part_pages(pages, keys, values):
    kv_local, _, head_dim = keys.shape
    span = pages.shape[1]
    per = span // kv_local
    row = lax.broadcasted_iota(jnp.int32, (span, span), 0)
    column = lax.broadcasted_iota(jnp.int32, (span, span), 1)
    part = (column == (row % per) * kv_local + row // per).astype(jnp.bfloat16)
    for holder in range(pages.shape[0]):
        parted = jnp.dot(part, pages[holder], preferred_element_type=jnp.float32)
        parted = parted.astype(jnp.bfloat16)
        at = holder * per
        for g in range(kv_local):
            lines = parted[g * per : (g + 1) * per]
            keys[g, at : at + per, :] = lines[:, :head_dim]
            values[g, at : at + per, :] = lines[:, head_dim:]


def own_kernel(requests, half, where_ref, hidden_ref, gain_ref, freq_ref, pages, *refs):
    f = where_ref[1]
    own_ref, cos_ref, sin_ref, keys, values, hidden, normed, q_weight, kv_weight, sems = refs[
        2 * half :
    ]
    rows_copy = pltpu.make_async_copy(hidden_ref, hidden, sems.at[2 * half])
    rows_copy.start()
    copies = weight_copies(refs[:half], q_weight, f, half, sems.at[:half])
    copies += weight_copies(refs[half : 2 * half], kv_weight, f, half, sems.at[half : 2 * half])
    rows_copy.wait()
    new_len, width = hidden_ref.shape
    half_width = width // 2
    length = jnp.int32(0)
    for r in range(requests):
        length = length + jnp.where(where_ref[3 + r] == f, where_ref[3 + requests + r], 0)
    start = pl.multiple_of(where_ref[2] * half_width, 128)
    gain = gain_ref[:, pl.ds(start, half_width)]
    step = 32

    def norm(index, carry):
        at = pl.multiple_of(index * step, step)
        rows = hidden[pl.ds(at, step), :].astype(jnp.float32)
        scale = row_scale(rows)
        part = hidden[pl.ds(at, step), pl.ds(start, half_width)].astype(jnp.float32)
        normed[pl.ds(at, step), :] = (part * scale * gain).astype(jnp.bfloat16)
        return carry

    lax.fori_loop(0, new_len // step, norm, 0)
    part_pages(pages, keys, values)
    position = lax.broadcasted_iota(jnp.int32, cos_ref.shape, 0) + length
    angle = position.astype(jnp.float32) * freq_ref[...]
    lane = lax.broadcasted_iota(jnp.int32, cos_ref.shape, 1)
    cos_ref[...] = jnp.cos(angle)
    sine = jnp.sin(angle)
    sin_ref[...] = jnp.where(lane < cos_ref.shape[1] // 2, -sine, sine)
    for copy in copies:
        copy.wait()
    at = 0
    for weight in (q_weight, kv_weight):
        to = at + weight.shape[1]
        own_ref[:, at:to] = jnp.dot(
            normed[...], weight[...], preferred_element_type=jnp.float32
        )
        at = to


def capped(scores):
    return jnp.exp2(jnp.tanh(scores * (1.0 / softcap)) * (softcap * math.log2(math.e)))


def attend_kernel(
    groups,
    kv_local,
    head_dim,
    where_ref,
    own,
    q_other,
    kv_other,
    cos_ref,
    sin_ref,
    valid_ref,
    keys,
    values,
    *refs,
):
    p = where_ref[0]
    out_refs = refs[:groups]
    (result,) = refs[groups:]
    new_len, q_cols = result.shape
    group = q_cols // (kv_local * head_dim)

    def sums(at):
        ref, start = (q_other, at) if at < q_cols else (kv_other, at - q_cols)
        other = ref[:, start : start + head_dim]
        return own[:, at : at + head_dim] + other.astype(jnp.float32)

    cosine, sine = cos_ref[...], sin_ref[...]

    def rope(vectors):
        return vectors * cosine + pltpu.roll(vectors, head_dim // 2, 1) * sine

    per = valid_ref.shape[1]
    place_at = keys.shape[1]
    span_keys = 2 * per
    t = lax.broadcasted_iota(jnp.int32, (group * new_len, new_len), 0) % new_len
    s = lax.broadcasted_iota(jnp.int32, (group * new_len, new_len), 1)
    causal = s <= t
    for g in range(kv_local):
        heads = [
            (rope(sums((g * group + j) * head_dim)) * query_scale).astype(jnp.bfloat16)
            for j in range(group)
        ]
        queries = jnp.concatenate(heads, axis=0)
        at = q_cols + g * head_dim
        new_key = rope(sums(at)).astype(jnp.bfloat16)
        new_value = sums(at + kv_local * head_dim).astype(jnp.bfloat16)

        def scores_of(key):
            return lax.dot_general(
                queries, key, (((1,), (1,)), ((), ())), preferred_element_type=jnp.float32
            )

        weights = jnp.where(causal, capped(scores_of(new_key)), 0.0)
        denom = jnp.sum(weights, axis=1, keepdims=True)
        numer = jnp.dot(
            weights.astype(jnp.bfloat16), new_value, preferred_element_type=jnp.float32
        )
        for start in range(0, place_at, span_keys):
            at = start // per
            valid = jnp.concatenate([valid_ref[at : at + 1], valid_ref[at + 1 : at + 2]], axis=1)
            valid = valid > 0.0
            weights = jnp.where(
                valid, capped(scores_of(keys[g, start : start + span_keys, :])), 0.0
            )
            denom = denom + jnp.sum(weights, axis=1, keepdims=True)
            numer = numer + jnp.dot(
                weights.astype(jnp.bfloat16),
                values[g, start : start + span_keys, :],
                preferred_element_type=jnp.float32,
            )
        attended = (numer / denom).astype(jnp.bfloat16)
        for j in range(group):
            to = (g * group + j) * head_dim
            result[:, to : to + head_dim] = attended[j * new_len : (j + 1) * new_len]
    quarter = new_len // groups
    for distance, ref in enumerate(out_refs):
        start = pl.multiple_of((p ^ distance) * quarter, quarter)
        ref[...] = result[pl.ds(start, quarter), :]


def output_kernel(groups, shards, where_ref, *refs):
    p, f = where_ref[0], where_ref[1]
    token_refs = refs[:shards]
    weight_ref = refs[shards]
    out_refs = refs[shards + 1 : 2 * shards + 1]
    total, tokens, weight, sems, token_sems = refs[2 * shards + 1 :]
    token_copies = [
        pltpu.make_async_copy(ref, tokens.at[e], token_sems.at[e])
        for e, ref in enumerate(token_refs)
    ]
    copies = [
        pltpu.make_async_copy(weight_ref.at[p ^ distance], weight.at[distance], sems.at[distance])
        for distance in range(groups)
    ]
    for copy in token_copies + copies:
        copy.start()
    for copy in token_copies:
        copy.wait()
    quarter = token_refs[0].shape[1]
    sub = quarter // shards
    projected = None
    for distance in range(groups):
        rows = jnp.concatenate([tokens[e, distance] for e in range(shards)], axis=0)
        copies[distance].wait()
        term = lax.dot_general(
            rows,
            weight[distance],
            (((1,), (1,)), ((), ())),
            preferred_element_type=jnp.float32,
        )
        projected = term if projected is None else projected + term
    total[...] = projected
    for e in range(shards):
        for distance, ref in enumerate(out_refs):
            start = pl.multiple_of(e * quarter + (f ^ distance) * sub, sub)
            ref[f ^ e] = total[pl.ds(start, sub), :].astype(jnp.bfloat16)


def finish_kernel(shards, where_ref, gain_ref, residual_ref, *refs):
    f = where_ref[1]
    piece_refs = refs[:shards]
    out_ref, projected = refs[shards:]
    for distance, ref in enumerate(piece_refs):
        projected[f ^ distance] = ref[...].astype(jnp.float32)
    gain = gain_ref[...]
    for request in range(out_ref.shape[0]):
        slot = where_ref[3 + request]
        line = jnp.concatenate([projected[k, slot] for k in range(shards)], axis=1)
        mean_square = jnp.mean(line * line, axis=1, keepdims=True)
        line = line * lax.rsqrt(mean_square + norm_eps) * gain
        out_ref[request] = (residual_ref[slot].astype(jnp.float32) + line).astype(jnp.bfloat16)


def pool_pieces(block, groups):
    return [block] + [swap(block, "pool", distance) for distance in range(1, groups)]


def local_small(
    hidden,
    slot_of_request,
    prefix_len,
    block_holder,
    block_slot,
    kv_pool,
    norm_gain,
    q_weight,
    k_weight,
    v_weight,
    o_weight,
    post_gain,
):
    shards = lax.axis_size("fsdp")
    groups = lax.axis_size("pool")
    f = lax.axis_index("fsdp")
    p = lax.axis_index("pool")
    half = shards // 2
    side = f // half
    new_len, width = hidden.shape[1:]
    requests = slot_of_request.shape[0]
    page_len = kv_pool.shape[1]
    kv_local = kv_pool.shape[2]
    head_dim = kv_pool.shape[3] // 2
    q_cols = q_weight.shape[1]
    kv_cols = k_weight.shape[1]
    max_blocks = block_holder.shape[1]
    per_holder = max_blocks // shards
    quarter = new_len // groups
    sub = quarter // shards
    features = o_weight.shape[0]
    bf16, f32 = jnp.bfloat16, jnp.float32
    where = jnp.concatenate(
        [jnp.stack([p, f, side]).astype(jnp.int32), slot_of_request, prefix_len]
    )
    shape = jax.ShapeDtypeStruct
    gain = norm_gain.reshape(1, width)
    rows = hidden[0]

    leaving, my_quarter, kv_weight = call(
        prologue_kernel,
        [
            shape((quarter, width // 2), bf16),
            shape((quarter, width), bf16),
            shape((features, 2 * kv_cols), bf16),
        ],
        [pltpu.VMEM((quarter, width), f32), pltpu.SemaphoreType.DMA],
        quarter * width * 8,
        4 * features * kv_cols,
        rows,
        norm_gain,
        k_weight,
        v_weight,
        specs=[HBM, VMEM, VMEM, VMEM],
    )
    partner_piece = swap(leaving, "fsdp", half)

    flat_pool = kv_pool.reshape(kv_pool.shape[0], page_len * kv_local, 2 * head_dim)
    page_rows = per_holder * page_len * kv_local
    outgoing, valid = call(
        functools.partial(pages_kernel, requests, page_len),
        [
            shape((shards, page_rows, 2 * head_dim), bf16),
            shape((shards, per_holder * page_len), f32),
        ],
        [
            pltpu.SMEM((2 * per_holder,), jnp.int32),
            pltpu.SMEM((max_blocks + per_holder,), jnp.int32),
            pltpu.SMEM((shards,), jnp.int32),
        ],
        1 << 20,
        1 << 21,
        where,
        block_holder,
        block_slot,
        flat_pool,
        specs=[SMEM, SMEM, SMEM, VMEM],
    )
    q_near, kv_near = swap(q_weight, "fsdp", 1), swap(kv_weight, "fsdp", 1)
    partner_piece, q_near, kv_near, outgoing = lax.optimization_barrier(
        (partner_piece, q_near, kv_near, outgoing)
    )
    q_far = swap(after(q_weight, partner_piece), "fsdp", 2)
    kv_far = swap(after(kv_weight, partner_piece), "fsdp", 2)
    partner_pieces = pool_pieces(partner_piece, groups)
    arrived = lax.all_to_all(outgoing, "fsdp", split_axis=0, concat_axis=0, tiled=True)
    q_near_sums, kv_near_sums = call(
        functools.partial(near_kernel, groups, half),
        [shape((new_len, q_cols), f32), shape((new_len, 2 * kv_cols), f32)],
        [
            pltpu.VMEM((new_len, width // 2), bf16),
            pltpu.VMEM((2 * features, q_cols), bf16),
            pltpu.VMEM((2 * features, 2 * kv_cols), bf16),
            pltpu.SemaphoreType.DMA((groups + 4,)),
        ],
        new_len * width * q_cols,
        width * (new_len + 2 * q_cols),
        where,
        *partner_pieces,
        q_weight,
        q_near,
        kv_weight,
        kv_near,
        specs=[SMEM] + [HBM] * (groups + 4),
    )
    q_near_sums, kv_near_sums, q_far = lax.optimization_barrier((q_near_sums, kv_near_sums, q_far))

    def partner_sums(near_sums, far, far_core):
        cols = far.shape[1]
        return call(
            functools.partial(partner_kernel, groups, half),
            shape((new_len, cols), bf16),
            [
                pltpu.VMEM((new_len, width // 2), bf16),
                pltpu.VMEM((2 * features, cols), bf16),
                pltpu.SemaphoreType.DMA((groups + 2,)),
            ],
            new_len * width * cols // 2,
            width * (new_len + cols),
            where,
            near_sums,
            *partner_pieces,
            far,
            far_core,
            specs=[SMEM, VMEM] + [HBM] * (groups + 2),
        )

    q_weights = [q_weight, q_near, q_far, swap(q_far, "fsdp", 1)]
    q_partial = partner_sums(q_near_sums, *q_weights[2:])
    q_other = swap(q_partial, "fsdp", half)
    kv_far = after(kv_far, q_partial)
    kv_weights = [kv_weight, kv_near, kv_far, swap(kv_far, "fsdp", 1)]
    kv_partial = partner_sums(kv_near_sums, *kv_weights[2:])
    kv_other = swap(kv_partial, "fsdp", half)
    out_weight = lax.all_gather(after(o_weight, *partner_pieces), "pool", axis=0, tiled=False)

    freqs = np.exp(np.arange(head_dim // 2) * (-2.0 * math.log(10000.0) / head_dim))
    freqs = np.concatenate([freqs, freqs]).astype(np.float32).reshape(1, head_dim)
    own, cosine, sine, keys, values = call(
        functools.partial(own_kernel, requests, half),
        [
            shape((new_len, q_cols + 2 * kv_cols), f32),
            shape((new_len, head_dim), f32),
            shape((new_len, head_dim), f32),
            shape((kv_local, max_blocks * page_len, head_dim), bf16),
            shape((kv_local, max_blocks * page_len, head_dim), bf16),
        ],
        [
            pltpu.VMEM((new_len, width), bf16),
            pltpu.VMEM((new_len, width // 2), bf16),
            pltpu.VMEM((width // 2, q_cols), bf16),
            pltpu.VMEM((width // 2, 2 * kv_cols), bf16),
            pltpu.SemaphoreType.DMA((2 * half + 1,)),
        ],
        new_len * width * (q_cols + 2 * kv_cols),
        width * (2 * new_len + q_cols + 2 * kv_cols),
        where,
        after(rows, kv_partial),
        gain,
        freqs,
        arrived,
        *q_weights,
        *kv_weights,
        specs=[SMEM, HBM, VMEM, VMEM, VMEM] + [HBM] * (2 * half),
    )

    residual = lax.all_to_all(
        after(my_quarter, own).reshape(shards, sub, width),
        "fsdp",
        split_axis=0,
        concat_axis=0,
        tiled=True,
    )

    keys_total = max_blocks * page_len
    quarters = call(
        functools.partial(attend_kernel, groups, kv_local, head_dim),
        [shape((quarter, q_cols), bf16)] * groups,
        [
            pltpu.VMEM((new_len, q_cols), bf16),
        ],
        4 * new_len * q_cols * (keys_total + new_len),
        1 << 22,
        where,
        own,
        q_other,
        kv_other,
        cosine,
        sine,
        valid,
        keys,
        values,
        specs=[SMEM] + [VMEM] * 8,
    )

    quarters = [
        swap(piece, "pool", distance) if distance else piece
        for distance, piece in enumerate(quarters)
    ]
    quarters = jnp.stack(quarters)
    tokens = {0: quarters}
    for distance in range(2, shards, 2):
        tokens[distance] = swap(quarters, "fsdp", distance)
    for distance in range(0, shards, 2):
        tokens[distance ^ 1] = swap(tokens[distance], "fsdp", 1)
    projected = call(
        functools.partial(output_kernel, groups, shards),
        [shape((shards, sub, features), bf16)] * shards,
        [
            pltpu.VMEM((shards * quarter, features), f32),
            pltpu.VMEM((shards, groups, quarter, q_cols), bf16),
            pltpu.VMEM((groups, features, q_cols), bf16),
            pltpu.SemaphoreType.DMA((groups,)),
            pltpu.SemaphoreType.DMA((shards,)),
        ],
        2 * shards * quarter * features * groups * q_cols,
        1 << 22,
        where,
        *[tokens[distance] for distance in range(shards)],
        out_weight,
        specs=[SMEM] + [HBM] * (shards + 1),
    )
    finished = [
        swap(piece, "fsdp", distance) if distance else piece
        for distance, piece in enumerate(projected)
    ]
    return call(
        functools.partial(finish_kernel, shards),
        shape((requests, sub, width), bf16),
        [pltpu.VMEM((shards, shards, sub, features), f32)],
        1 << 20,
        1 << 20,
        where,
        post_gain.reshape(1, width),
        residual,
        *finished,
    )


def local(*arguments):
    return local_small(*arguments) if lax.axis_size("fsdp") == 8 else local_general(*arguments)


def solution(mesh):
    in_specs = (
        P("fsdp", None, None),
        P(),
        P(),
        P(),
        P(),
        P("fsdp", None, "pool", None),
        P(),
        P("fsdp", "pool"),
        P("fsdp", "pool"),
        P("fsdp", "pool"),
        P("fsdp", "pool"),
        P(),
    )
    out_specs = P(None, ("pool", "fsdp"), None)
    return jax.shard_map(local, mesh=mesh, in_specs=in_specs, out_specs=out_specs, check_vma=False)
```

```python
import functools
import math

import jax
import jax.numpy as jnp
import numpy as np
from jax import lax
from jax.experimental import pallas as pl
from jax.experimental.pallas import tpu as pltpu
from jax.sharding import PartitionSpec as P

softcap = 50.0
query_scale = 144.0 ** (-0.5)
norm_eps = 1e-06


def rms_scale(rows, gain):
    mean_square = jnp.mean(rows * rows, axis=-1, keepdims=True)
    return rows * lax.rsqrt(mean_square + norm_eps) * gain


def rotate(vectors, cosine, sine):
    half = vectors.shape[-1] // 2
    first = vectors[..., :half]
    second = vectors[..., half:]
    return jnp.concatenate(
        [first * cosine - second * sine, second * cosine + first * sine], axis=-1
    )


def capped_weights(scores, valid):
    return jnp.where(valid, jnp.exp(softcap * jnp.tanh(scores / softcap)), 0.0)


def swap(array, axis, distance):
    size = lax.axis_size(axis)
    return lax.ppermute(array, axis, [(i, i ^ distance) for i in range(size)])


def place(pieces, index):
    first = pieces[0]
    stacked = jnp.zeros((len(pieces),) + first.shape, first.dtype)
    for distance, piece in pieces.items():
        stacked = lax.dynamic_update_index_in_dim(stacked, piece, index ^ distance, 0)
    return stacked


def exchange(chunks, axis):
    size = lax.axis_size(axis)
    index = lax.axis_index(axis)
    if size > 8:
        return lax.all_to_all(chunks, axis, split_axis=0, concat_axis=0, tiled=True)
    pieces = {}
    for distance in range(size):
        chunk = lax.dynamic_index_in_dim(chunks, index ^ distance, 0, keepdims=False)
        pieces[distance] = swap(chunk, axis, distance) if distance else chunk
    return place(pieces, index)


def doubled(block, axis, span):
    pieces = {0: block}
    bit = span // 2
    while bit:
        for distance in list(pieces):
            pieces[distance ^ bit] = swap(pieces[distance], axis, bit)
        bit //= 2
    return pieces


def attend(queries, keys_new, values_new, cached, cached_valid):
    new_len, kv_local, group, head_dim = queries.shape

    def part(keys, values, valid):
        scores = jnp.einsum("tgjd,kgd->gjtk", queries, keys, preferred_element_type=jnp.float32)
        weights = capped_weights(scores, valid)
        numer = jnp.einsum(
            "gjtk,kgd->gjtd",
            weights.astype(jnp.bfloat16),
            values,
            preferred_element_type=jnp.float32,
        )
        return numer, jnp.sum(weights, axis=-1)

    query_index = jnp.arange(new_len, dtype=jnp.int32)
    causal = query_index[None, :] <= query_index[:, None]
    numer, denom = part(
        cached[..., :head_dim], cached[..., head_dim:], cached_valid[None, None, None, :]
    )
    more, added = part(keys_new, values_new, causal[None, None])
    attended = ((numer + more) / (denom + added)[..., None]).transpose(2, 0, 1, 3)
    return attended.reshape(new_len, kv_local * group * head_dim).astype(jnp.bfloat16)


def local_general(
    hidden,
    slot_of_request,
    prefix_len,
    block_holder,
    block_slot,
    kv_pool,
    norm_gain,
    q_weight,
    k_weight,
    v_weight,
    o_weight,
    post_gain,
):
    shards = lax.axis_size("fsdp")
    groups = lax.axis_size("pool")
    f = lax.axis_index("fsdp")
    p = lax.axis_index("pool")
    half = shards // 2
    side = f // half
    new_len, width = hidden.shape[1:]
    requests = slot_of_request.shape[0]
    page_len = kv_pool.shape[1]
    kv_local = kv_pool.shape[2]
    head_dim = kv_pool.shape[3] // 2
    q_cols = q_weight.shape[1]
    kv_cols = k_weight.shape[1]
    group = q_cols // kv_cols
    max_blocks = block_holder.shape[1]
    per_holder = max_blocks // shards
    quarter = new_len // groups
    sub = quarter // shards
    features = o_weight.shape[0]

    kv_pieces = doubled(jnp.concatenate([k_weight, v_weight], axis=1), "fsdp", half)
    q_pieces = doubled(q_weight, "fsdp", half)
    out_weight = lax.all_gather(o_weight, "pool", axis=0, tiled=False)

    rows = hidden[0]
    normed = rms_scale(rows.astype(jnp.float32), norm_gain).astype(jnp.bfloat16)
    own_rows = lax.dynamic_slice(normed, (0, side * (width // 2)), (new_len, width // 2))
    leaving = lax.dynamic_slice(
        normed, (p * quarter, (1 - side) * (width // 2)), (quarter, width // 2)
    )
    partner_piece = swap(leaving, "fsdp", half)
    partner_pieces = {0: partner_piece}
    for distance in range(1, groups):
        partner_pieces[distance] = swap(partner_piece, "pool", distance)
    partner_rows = place(partner_pieces, p).reshape(new_len, width // 2)

    request_ids = jnp.arange(requests, dtype=jnp.int32)
    request_at_slot = jnp.sum(
        jnp.where(slot_of_request[None, :] == request_ids[:, None], request_ids[None, :], 0), axis=1
    )
    holder_by_slot = jnp.take(block_holder, request_at_slot, axis=0)
    page_by_slot = jnp.take(block_slot, request_at_slot, axis=0)
    held_here = holder_by_slot == f
    held_rank = jnp.cumsum(held_here.astype(jnp.int32), axis=1) - 1
    rank_ids = jnp.arange(per_holder, dtype=jnp.int32)
    picked = held_here[:, :, None] & (held_rank[:, :, None] == rank_ids[None, None, :])
    local_pages = jnp.sum(jnp.where(picked, page_by_slot[:, :, None], 0), axis=1)
    flat_pool = kv_pool.reshape(kv_pool.shape[0], page_len * kv_local, 2 * head_dim)
    outgoing = jnp.take(flat_pool, local_pages, axis=0)
    outgoing = outgoing.reshape(shards, per_holder * page_len * kv_local, 2 * head_dim)
    arrived = exchange(outgoing, "fsdp")
    cached = arrived.reshape(max_blocks * page_len, kv_local, 2 * head_dim)

    my_request = lax.dynamic_index_in_dim(request_at_slot, f, keepdims=False)
    my_length = prefix_len[my_request]
    my_holders = block_holder[my_request]
    entry_ids = jnp.arange(max_blocks, dtype=jnp.int32)
    mine = my_holders[None, :] == jnp.arange(shards, dtype=jnp.int32)[:, None]
    my_rank = jnp.cumsum(mine.astype(jnp.int32), axis=1) - 1
    chosen = mine[:, None, :] & (my_rank[:, None, :] == rank_ids[None, :, None])
    entry = jnp.sum(jnp.where(chosen, entry_ids[None, None, :], 0), axis=2)
    cached_position = entry.reshape(-1, 1) * page_len + jnp.arange(page_len, dtype=jnp.int32)
    cached_valid = (cached_position < my_length).reshape(-1)

    residual_out = lax.dynamic_slice_in_dim(rows, p * quarter, quarter, 0).reshape(
        shards, sub, width
    )
    residual = exchange(residual_out, "fsdp")

    positions = (my_length + jnp.arange(new_len, dtype=jnp.int32)).astype(jnp.float32)
    freqs = jnp.exp(
        jnp.arange(head_dim // 2, dtype=jnp.float32) * (-2.0 * math.log(10000.0) / head_dim)
    )
    angles = positions[:, None] * freqs
    cosine = jnp.cos(angles)[:, None, :]
    sine = jnp.sin(angles)[:, None, :]

    def project(pieces):
        weight = place(pieces, f % half).reshape(width // 2, -1)
        partial = jnp.dot(partner_rows, weight, preferred_element_type=jnp.float32)
        other = swap(partial.astype(jnp.bfloat16), "fsdp", half)
        own = jnp.dot(own_rows, weight, preferred_element_type=jnp.float32)
        return own + other.astype(jnp.float32)

    kv_sum = project(kv_pieces)
    q_sum = project(q_pieces)
    queries = rotate(q_sum.reshape(new_len, kv_local * group, head_dim), cosine, sine)
    queries = (queries * query_scale).astype(jnp.bfloat16)
    queries = queries.reshape(new_len, kv_local, group, head_dim)
    keys_new = kv_sum[:, :kv_cols].reshape(new_len, kv_local, head_dim)
    keys_new = rotate(keys_new, cosine, sine).astype(jnp.bfloat16)
    values_new = kv_sum[:, kv_cols:].astype(jnp.bfloat16).reshape(new_len, kv_local, head_dim)
    attended = attend(queries, keys_new, values_new, cached, cached_valid)

    quarters = exchange(attended.reshape(groups, quarter, q_cols), "pool")
    token_pieces = {0: quarters}
    for distance in range(2, shards, 2):
        token_pieces[distance] = swap(quarters, "fsdp", distance)
    for distance in range(0, shards, 2):
        token_pieces[distance ^ 1] = swap(token_pieces[distance], "fsdp", 1)
    tokens = place(token_pieces, f)
    projected = jnp.einsum(
        "sptc,pfc->stf", tokens, out_weight, preferred_element_type=jnp.float32
    ).astype(jnp.bfloat16)
    projected = projected.reshape(shards, shards, sub, features).transpose(1, 0, 2, 3)
    finished = exchange(projected, "fsdp").transpose(1, 2, 0, 3).reshape(shards, sub, width)
    finished = residual.astype(jnp.float32) + rms_scale(finished.astype(jnp.float32), post_gain)
    return jnp.take(finished.astype(jnp.bfloat16), slot_of_request, axis=0)


VMEM = pl.BlockSpec(memory_space=pltpu.VMEM)
SMEM = pl.BlockSpec(memory_space=pltpu.SMEM)
ANY = pl.BlockSpec(memory_space=pl.ANY)


def call(kernel, outs, scratch, flops, nbytes, *operands, specs=None, out_specs=None):
    return pl.pallas_call(
        kernel,
        out_shape=outs,
        in_specs=specs or [SMEM] + [VMEM] * (len(operands) - 1),
        out_specs=out_specs or jax.tree.map(lambda _: VMEM, outs),
        scratch_shapes=scratch,
        compiler_params=pltpu.CompilerParams(vmem_limit_bytes=24 << 20),
        cost_estimate=pl.CostEstimate(flops=flops, bytes_accessed=nbytes, transcendentals=0),
    )(*operands)


def after(array, *earlier):
    return lax.optimization_barrier((array,) + earlier)[0]


def weight_copies(weight_refs, weight, f, half, sems):
    copies = []
    for distance, ref in enumerate(weight_refs):
        count = ref.shape[0]
        start = pl.multiple_of(((f ^ distance) & (half - 1)) * count, 64)
        copies.append(
            pltpu.make_async_copy(ref, weight.at[pl.ds(start, count), :], sems.at[distance])
        )
        copies[-1].start()
    return copies


def pair_product(groups, half, pair, where_ref, x_refs, chunks, rows, sems):
    p, f = where_ref[0], where_ref[1]
    copies = []
    quarter = x_refs[0].shape[0]
    for distance, ref in enumerate(x_refs):
        start = pl.multiple_of((p ^ distance) * quarter, quarter)
        copies.append((ref, rows.at[pl.ds(start, quarter), :]))
    for w_refs, weight in chunks:
        for distance, ref in enumerate(w_refs):
            count = ref.shape[0]
            start = pl.multiple_of(((f ^ distance) & 1) * count, 64)
            copies.append((ref, weight.at[pl.ds(start, count), :]))
    copies = [
        pltpu.make_async_copy(source, target, sems.at[index])
        for index, (source, target) in enumerate(copies)
    ]
    for copy in copies:
        copy.start()
    for copy in copies:
        copy.wait()
    span = chunks[0][1].shape[0]
    columns = pl.ds(pl.multiple_of((((f & (half - 1)) >> 1) ^ pair) * span, 128), span)
    return [
        jnp.dot(rows[:, columns], weight[...], preferred_element_type=jnp.float32)
        for _, weight in chunks
    ]


def near_kernel(groups, half, where_ref, *refs):
    x_refs, q_refs, kv_refs = refs[:groups], refs[groups : groups + 2], refs[groups + 2 : groups + 4]
    q_out, kv_out, rows, q_weight, kv_weight, sems = refs[groups + 4 :]
    chunks = [(q_refs, q_weight), (kv_refs, kv_weight)]
    q_out[...], kv_out[...] = pair_product(
        groups, half, 0, where_ref, x_refs, chunks, rows, sems
    )


def partner_kernel(groups, half, where_ref, near_ref, *refs):
    x_refs, w_refs = refs[:groups], refs[groups : groups + 2]
    out_ref, rows, weight, sems = refs[groups + 2 :]
    (sums,) = pair_product(groups, half, 1, where_ref, x_refs, [(w_refs, weight)], rows, sems)
    out_ref[...] = (near_ref[...] + sums).astype(jnp.bfloat16)


def row_scale(rows):
    return lax.rsqrt(jnp.mean(rows * rows, axis=1, keepdims=True) + norm_eps)


def prologue_kernel(
    hidden_ref, gain_ref, k_ref, v_ref, leaving_ref, rows_ref, weight_ref, normed, sem
):
    p, f = lax.axis_index("pool"), lax.axis_index("fsdp")
    side = f // (lax.axis_size("fsdp") // 2)
    quarter, width = rows_ref.shape
    half_width = width // 2
    start = pl.multiple_of(p * quarter, quarter)
    rows_copy = pltpu.make_async_copy(hidden_ref.at[pl.ds(start, quarter), :], rows_ref, sem)
    rows_copy.start()
    at = 0
    for ref in (k_ref, v_ref):
        weight_ref[:, at : at + ref.shape[1]] = ref[...]
        at += ref.shape[1]
    rows_copy.wait()
    rows = rows_ref[...].astype(jnp.float32)
    normed[...] = rows * row_scale(rows) * gain_ref[...].reshape(1, width)
    away = pl.multiple_of((1 - side) * half_width, 128)
    leaving_ref[...] = normed[:, pl.ds(away, half_width)].astype(jnp.bfloat16)


def pages_kernel(
    requests, page_len, where_ref, holder_ref, slot_ref, pool_ref, *refs
):
    f = where_ref[1]
    out_ref, valid_ref, listed, entries, counts = refs
    max_blocks = holder_ref.shape[1]
    shards = out_ref.shape[0]
    per = max_blocks // shards
    page_rows = pool_ref.shape[1]
    length, mine = jnp.int32(0), jnp.int32(0)
    for r in range(requests):
        at = where_ref[3 + r] == f
        length = length + jnp.where(at, where_ref[3 + requests + r], 0)
        mine = mine + jnp.where(at, r, 0)
    for r in range(requests):
        slot = where_ref[3 + r]

        def note(j, count):
            listed[count] = slot_ref[r, j]
            return count + jnp.where(holder_ref[r, j] == f, 1, 0)

        lax.fori_loop(0, max_blocks, note, jnp.int32(0), unroll=8)
        for k in range(per):
            out_ref[slot, k * page_rows : (k + 1) * page_rows, :] = pool_ref[listed[k]]
    for h in range(shards):
        counts[h] = 0

    def enter(j, carry):
        h = holder_ref[mine, j]
        count = counts[h]
        entries[h * per + count] = j
        counts[h] = count + 1
        return carry

    lax.fori_loop(0, max_blocks, enter, 0, unroll=4)
    row = lax.broadcasted_iota(jnp.int32, valid_ref.shape, 0)
    lane = lax.broadcasted_iota(jnp.int32, valid_ref.shape, 1)
    place_in = row * per + lane // page_len
    entry = jnp.zeros(valid_ref.shape, jnp.int32)
    for at in range(max_blocks):
        entry = jnp.where(place_in == at, entries[at], entry)
    position = entry * page_len + lane % page_len
    valid_ref[...] = jnp.where(position < length, 1.0, 0.0)


def part_pages(pages, keys, values):
    kv_local, _, head_dim = keys.shape
    span = pages.shape[1]
    per = span // kv_local
    row = lax.broadcasted_iota(jnp.int32, (span, span), 0)
    column = lax.broadcasted_iota(jnp.int32, (span, span), 1)
    part = (column == (row % per) * kv_local + row // per).astype(jnp.bfloat16)
    for holder in range(pages.shape[0]):
        parted = jnp.dot(part, pages[holder], preferred_element_type=jnp.float32)
        parted = parted.astype(jnp.bfloat16)
        at = holder * per
        for g in range(kv_local):
            lines = parted[g * per : (g + 1) * per]
            keys[g, at : at + per, :] = lines[:, :head_dim]
            values[g, at : at + per, :] = lines[:, head_dim:]


def own_kernel(requests, half, where_ref, hidden_ref, gain_ref, freq_ref, pages, *refs):
    f = where_ref[1]
    own_ref, cos_ref, sin_ref, keys, values, hidden, normed, q_weight, kv_weight, sems = refs[
        2 * half :
    ]
    rows_copy = pltpu.make_async_copy(hidden_ref, hidden, sems.at[2 * half])
    rows_copy.start()
    copies = weight_copies(refs[:half], q_weight, f, half, sems.at[:half])
    copies += weight_copies(refs[half : 2 * half], kv_weight, f, half, sems.at[half : 2 * half])
    rows_copy.wait()
    new_len, width = hidden_ref.shape
    half_width = width // 2
    length = jnp.int32(0)
    for r in range(requests):
        length = length + jnp.where(where_ref[3 + r] == f, where_ref[3 + requests + r], 0)
    start = pl.multiple_of(where_ref[2] * half_width, 128)
    gain = gain_ref[:, pl.ds(start, half_width)]
    step = 32

    def norm(index, carry):
        at = pl.multiple_of(index * step, step)
        rows = hidden[pl.ds(at, step), :].astype(jnp.float32)
        scale = row_scale(rows)
        part = hidden[pl.ds(at, step), pl.ds(start, half_width)].astype(jnp.float32)
        normed[pl.ds(at, step), :] = (part * scale * gain).astype(jnp.bfloat16)
        return carry

    lax.fori_loop(0, new_len // step, norm, 0)
    part_pages(pages, keys, values)
    position = lax.broadcasted_iota(jnp.int32, cos_ref.shape, 0) + length
    angle = position.astype(jnp.float32) * freq_ref[...]
    lane = lax.broadcasted_iota(jnp.int32, cos_ref.shape, 1)
    cos_ref[...] = jnp.cos(angle)
    sine = jnp.sin(angle)
    sin_ref[...] = jnp.where(lane < cos_ref.shape[1] // 2, -sine, sine)
    for copy in copies:
        copy.wait()
    at = 0
    for weight in (q_weight, kv_weight):
        to = at + weight.shape[1]
        own_ref[:, at:to] = jnp.dot(
            normed[...], weight[...], preferred_element_type=jnp.float32
        )
        at = to


def capped(scores):
    return jnp.exp2(jnp.tanh(scores * (1.0 / softcap)) * (softcap * math.log2(math.e)))


def attend_kernel(
    groups,
    kv_local,
    head_dim,
    where_ref,
    own,
    q_other,
    kv_other,
    cos_ref,
    sin_ref,
    valid_ref,
    keys,
    values,
    *refs,
):
    p = where_ref[0]
    out_refs = refs[:groups]
    (result,) = refs[groups:]
    new_len, q_cols = result.shape
    group = q_cols // (kv_local * head_dim)

    def sums(at):
        ref, start = (q_other, at) if at < q_cols else (kv_other, at - q_cols)
        other = ref[:, start : start + head_dim]
        return own[:, at : at + head_dim] + other.astype(jnp.float32)

    cosine, sine = cos_ref[...], sin_ref[...]

    def rope(vectors):
        return vectors * cosine + pltpu.roll(vectors, head_dim // 2, 1) * sine

    per = valid_ref.shape[1]
    place_at = keys.shape[1]
    span_keys = 2 * per
    t = lax.broadcasted_iota(jnp.int32, (group * new_len, new_len), 0) % new_len
    s = lax.broadcasted_iota(jnp.int32, (group * new_len, new_len), 1)
    causal = s <= t
    for g in range(kv_local):
        heads = [
            (rope(sums((g * group + j) * head_dim)) * query_scale).astype(jnp.bfloat16)
            for j in range(group)
        ]
        queries = jnp.concatenate(heads, axis=0)
        at = q_cols + g * head_dim
        new_key = rope(sums(at)).astype(jnp.bfloat16)
        new_value = sums(at + kv_local * head_dim).astype(jnp.bfloat16)

        def scores_of(key):
            return lax.dot_general(
                queries, key, (((1,), (1,)), ((), ())), preferred_element_type=jnp.float32
            )

        weights = jnp.where(causal, capped(scores_of(new_key)), 0.0)
        denom = jnp.sum(weights, axis=1, keepdims=True)
        numer = jnp.dot(
            weights.astype(jnp.bfloat16), new_value, preferred_element_type=jnp.float32
        )
        for start in range(0, place_at, span_keys):
            at = start // per
            valid = jnp.concatenate([valid_ref[at : at + 1], valid_ref[at + 1 : at + 2]], axis=1)
            valid = valid > 0.0
            weights = jnp.where(
                valid, capped(scores_of(keys[g, start : start + span_keys, :])), 0.0
            )
            denom = denom + jnp.sum(weights, axis=1, keepdims=True)
            numer = numer + jnp.dot(
                weights.astype(jnp.bfloat16),
                values[g, start : start + span_keys, :],
                preferred_element_type=jnp.float32,
            )
        attended = (numer / denom).astype(jnp.bfloat16)
        for j in range(group):
            to = (g * group + j) * head_dim
            result[:, to : to + head_dim] = attended[j * new_len : (j + 1) * new_len]
    quarter = new_len // groups
    for distance, ref in enumerate(out_refs):
        start = pl.multiple_of((p ^ distance) * quarter, quarter)
        ref[...] = result[pl.ds(start, quarter), :]


def output_kernel(groups, shards, where_ref, *refs):
    p, f = where_ref[0], where_ref[1]
    token_refs = refs[:shards]
    weight_ref = refs[shards]
    out_refs = refs[shards + 1 : 2 * shards + 1]
    total, weight, sems = refs[2 * shards + 1 :]
    copies = [
        pltpu.make_async_copy(weight_ref.at[p ^ distance], weight.at[distance], sems.at[distance])
        for distance in range(groups)
    ]
    for copy in copies:
        copy.start()
    quarter = token_refs[0].shape[1]
    sub = quarter // shards
    projected = None
    for distance in range(groups):
        rows = jnp.concatenate([ref[distance] for ref in token_refs], axis=0)
        copies[distance].wait()
        term = lax.dot_general(
            rows,
            weight[distance],
            (((1,), (1,)), ((), ())),
            preferred_element_type=jnp.float32,
        )
        projected = term if projected is None else projected + term
    total[...] = projected
    for e in range(shards):
        for distance, ref in enumerate(out_refs):
            start = pl.multiple_of(e * quarter + (f ^ distance) * sub, sub)
            ref[f ^ e] = total[pl.ds(start, sub), :].astype(jnp.bfloat16)


def finish_kernel(shards, where_ref, gain_ref, residual_ref, *refs):
    f = where_ref[1]
    piece_refs = refs[:shards]
    out_ref, projected = refs[shards:]
    for distance, ref in enumerate(piece_refs):
        projected[f ^ distance] = ref[...].astype(jnp.float32)
    gain = gain_ref[...]
    for request in range(out_ref.shape[0]):
        slot = where_ref[3 + request]
        line = jnp.concatenate([projected[k, slot] for k in range(shards)], axis=1)
        mean_square = jnp.mean(line * line, axis=1, keepdims=True)
        line = line * lax.rsqrt(mean_square + norm_eps) * gain
        out_ref[request] = (residual_ref[slot].astype(jnp.float32) + line).astype(jnp.bfloat16)


def pool_pieces(block, groups):
    return [block] + [swap(block, "pool", distance) for distance in range(1, groups)]


def local_small(
    hidden,
    slot_of_request,
    prefix_len,
    block_holder,
    block_slot,
    kv_pool,
    norm_gain,
    q_weight,
    k_weight,
    v_weight,
    o_weight,
    post_gain,
):
    shards = lax.axis_size("fsdp")
    groups = lax.axis_size("pool")
    f = lax.axis_index("fsdp")
    p = lax.axis_index("pool")
    half = shards // 2
    side = f // half
    new_len, width = hidden.shape[1:]
    requests = slot_of_request.shape[0]
    page_len = kv_pool.shape[1]
    kv_local = kv_pool.shape[2]
    head_dim = kv_pool.shape[3] // 2
    q_cols = q_weight.shape[1]
    kv_cols = k_weight.shape[1]
    max_blocks = block_holder.shape[1]
    per_holder = max_blocks // shards
    quarter = new_len // groups
    sub = quarter // shards
    features = o_weight.shape[0]
    bf16, f32 = jnp.bfloat16, jnp.float32
    where = jnp.concatenate(
        [jnp.stack([p, f, side]).astype(jnp.int32), slot_of_request, prefix_len]
    )
    shape = jax.ShapeDtypeStruct
    gain = norm_gain.reshape(1, width)
    rows = hidden[0]

    leaving, my_quarter, kv_weight = call(
        prologue_kernel,
        [
            shape((quarter, width // 2), bf16),
            shape((quarter, width), bf16),
            shape((features, 2 * kv_cols), bf16),
        ],
        [pltpu.VMEM((quarter, width), f32), pltpu.SemaphoreType.DMA],
        quarter * width * 8,
        4 * features * kv_cols,
        rows,
        norm_gain,
        k_weight,
        v_weight,
        specs=[ANY, VMEM, VMEM, VMEM],
    )
    partner_piece = swap(leaving, "fsdp", half)

    flat_pool = kv_pool.reshape(kv_pool.shape[0], page_len * kv_local, 2 * head_dim)
    page_rows = per_holder * page_len * kv_local
    outgoing, valid = call(
        functools.partial(pages_kernel, requests, page_len),
        [
            shape((shards, page_rows, 2 * head_dim), bf16),
            shape((shards, per_holder * page_len), f32),
        ],
        [
            pltpu.SMEM((2 * per_holder,), jnp.int32),
            pltpu.SMEM((max_blocks + per_holder,), jnp.int32),
            pltpu.SMEM((shards,), jnp.int32),
        ],
        1 << 20,
        1 << 21,
        where,
        block_holder,
        block_slot,
        flat_pool,
        specs=[SMEM, SMEM, SMEM, VMEM],
    )
    q_near, kv_near = swap(q_weight, "fsdp", 1), swap(kv_weight, "fsdp", 1)
    partner_piece, q_near, kv_near, outgoing = lax.optimization_barrier(
        (partner_piece, q_near, kv_near, outgoing)
    )
    q_far = swap(after(q_weight, partner_piece), "fsdp", 2)
    kv_far = swap(after(kv_weight, partner_piece), "fsdp", 2)
    partner_pieces = pool_pieces(partner_piece, groups)
    arrived = lax.all_to_all(outgoing, "fsdp", split_axis=0, concat_axis=0, tiled=True)
    partner_pieces, q_far = lax.optimization_barrier((partner_pieces, q_far))
    q_near_sums, kv_near_sums = call(
        functools.partial(near_kernel, groups, half),
        [shape((new_len, q_cols), f32), shape((new_len, 2 * kv_cols), f32)],
        [
            pltpu.VMEM((new_len, width // 2), bf16),
            pltpu.VMEM((2 * features, q_cols), bf16),
            pltpu.VMEM((2 * features, 2 * kv_cols), bf16),
            pltpu.SemaphoreType.DMA((groups + 4,)),
        ],
        new_len * width * q_cols,
        width * (new_len + 2 * q_cols),
        where,
        *partner_pieces,
        q_weight,
        q_near,
        kv_weight,
        kv_near,
        specs=[SMEM] + [ANY] * (groups + 4),
    )
    def partner_sums(near_sums, far, far_core):
        cols = far.shape[1]
        return call(
            functools.partial(partner_kernel, groups, half),
            shape((new_len, cols), bf16),
            [
                pltpu.VMEM((new_len, width // 2), bf16),
                pltpu.VMEM((2 * features, cols), bf16),
                pltpu.SemaphoreType.DMA((groups + 2,)),
            ],
            new_len * width * cols // 2,
            width * (new_len + cols),
            where,
            near_sums,
            *partner_pieces,
            far,
            far_core,
            specs=[SMEM, VMEM] + [ANY] * (groups + 2),
        )

    q_weights = [q_weight, q_near, q_far, swap(q_far, "fsdp", 1)]
    q_partial = partner_sums(q_near_sums, *q_weights[2:])
    q_other = swap(q_partial, "fsdp", half)
    kv_far = after(kv_far, q_partial)
    kv_weights = [kv_weight, kv_near, kv_far, swap(kv_far, "fsdp", 1)]
    kv_partial = partner_sums(kv_near_sums, *kv_weights[2:])
    kv_other = swap(kv_partial, "fsdp", half)
    out_weight = lax.all_gather(after(o_weight, *partner_pieces), "pool", axis=0, tiled=False)

    freqs = np.exp(np.arange(head_dim // 2) * (-2.0 * math.log(10000.0) / head_dim))
    freqs = np.concatenate([freqs, freqs]).astype(np.float32).reshape(1, head_dim)
    own, cosine, sine, keys, values = call(
        functools.partial(own_kernel, requests, half),
        [
            shape((new_len, q_cols + 2 * kv_cols), f32),
            shape((new_len, head_dim), f32),
            shape((new_len, head_dim), f32),
            shape((kv_local, max_blocks * page_len, head_dim), bf16),
            shape((kv_local, max_blocks * page_len, head_dim), bf16),
        ],
        [
            pltpu.VMEM((new_len, width), bf16),
            pltpu.VMEM((new_len, width // 2), bf16),
            pltpu.VMEM((width // 2, q_cols), bf16),
            pltpu.VMEM((width // 2, 2 * kv_cols), bf16),
            pltpu.SemaphoreType.DMA((2 * half + 1,)),
        ],
        new_len * width * (q_cols + 2 * kv_cols),
        width * (2 * new_len + q_cols + 2 * kv_cols),
        where,
        after(rows, kv_partial),
        gain,
        freqs,
        arrived,
        *q_weights,
        *kv_weights,
        specs=[SMEM, ANY, VMEM, VMEM, VMEM] + [ANY] * (2 * half),
    )

    residual = lax.all_to_all(
        after(my_quarter, own).reshape(shards, sub, width),
        "fsdp",
        split_axis=0,
        concat_axis=0,
        tiled=True,
    )

    keys_total = max_blocks * page_len
    quarters = call(
        functools.partial(attend_kernel, groups, kv_local, head_dim),
        [shape((quarter, q_cols), bf16)] * groups,
        [
            pltpu.VMEM((new_len, q_cols), bf16),
        ],
        4 * new_len * q_cols * (keys_total + new_len),
        1 << 22,
        where,
        own,
        q_other,
        kv_other,
        cosine,
        sine,
        valid,
        keys,
        values,
        specs=[SMEM] + [VMEM] * 8,
    )

    quarters = [
        swap(piece, "pool", distance) if distance else piece
        for distance, piece in enumerate(quarters)
    ]
    quarters = jnp.stack(quarters)
    tokens = {0: quarters}
    for distance in range(2, shards, 2):
        tokens[distance] = swap(quarters, "fsdp", distance)
    for distance in range(0, shards, 2):
        tokens[distance ^ 1] = swap(tokens[distance], "fsdp", 1)
    projected = call(
        functools.partial(output_kernel, groups, shards),
        [shape((shards, sub, features), bf16)] * shards,
        [
            pltpu.VMEM((shards * quarter, features), f32),
            pltpu.VMEM((groups, features, q_cols), bf16),
            pltpu.SemaphoreType.DMA((groups,)),
        ],
        2 * shards * quarter * features * groups * q_cols,
        1 << 22,
        where,
        *[tokens[distance] for distance in range(shards)],
        out_weight,
        specs=[SMEM] + [VMEM] * shards + [ANY],
    )
    finished = [
        swap(piece, "fsdp", distance) if distance else piece
        for distance, piece in enumerate(projected)
    ]
    return call(
        functools.partial(finish_kernel, shards),
        shape((requests, sub, width), bf16),
        [pltpu.VMEM((shards, shards, sub, features), f32)],
        1 << 20,
        1 << 20,
        where,
        post_gain.reshape(1, width),
        residual,
        *finished,
    )


def local(*arguments):
    return local_small(*arguments) if lax.axis_size("fsdp") == 8 else local_general(*arguments)


def solution(mesh):
    in_specs = (
        P("fsdp", None, None),
        P(),
        P(),
        P(),
        P(),
        P("fsdp", None, "pool", None),
        P(),
        P("fsdp", "pool"),
        P("fsdp", "pool"),
        P("fsdp", "pool"),
        P("fsdp", "pool"),
        P(),
    )
    out_specs = P(None, ("pool", "fsdp"), None)
    return jax.shard_map(local, mesh=mesh, in_specs=in_specs, out_specs=out_specs, check_vma=False)
```

```python
import functools
import math

import jax
import jax.numpy as jnp
import numpy as np
from jax import lax
from jax.experimental import pallas as pl
from jax.experimental.pallas import tpu as pltpu
from jax.sharding import PartitionSpec as P

softcap = 50.0
query_scale = 144.0 ** (-0.5)
norm_eps = 1e-06


def rms_scale(rows, gain):
    mean_square = jnp.mean(rows * rows, axis=-1, keepdims=True)
    return rows * lax.rsqrt(mean_square + norm_eps) * gain


def rotate(vectors, cosine, sine):
    half = vectors.shape[-1] // 2
    first = vectors[..., :half]
    second = vectors[..., half:]
    return jnp.concatenate(
        [first * cosine - second * sine, second * cosine + first * sine], axis=-1
    )


def capped_weights(scores, valid):
    return jnp.where(valid, jnp.exp(softcap * jnp.tanh(scores / softcap)), 0.0)


def swap(array, axis, distance):
    size = lax.axis_size(axis)
    return lax.ppermute(array, axis, [(i, i ^ distance) for i in range(size)])


def place(pieces, index):
    first = pieces[0]
    stacked = jnp.zeros((len(pieces),) + first.shape, first.dtype)
    for distance, piece in pieces.items():
        stacked = lax.dynamic_update_index_in_dim(stacked, piece, index ^ distance, 0)
    return stacked


def exchange(chunks, axis):
    size = lax.axis_size(axis)
    index = lax.axis_index(axis)
    if size > 8:
        return lax.all_to_all(chunks, axis, split_axis=0, concat_axis=0, tiled=True)
    pieces = {}
    for distance in range(size):
        chunk = lax.dynamic_index_in_dim(chunks, index ^ distance, 0, keepdims=False)
        pieces[distance] = swap(chunk, axis, distance) if distance else chunk
    return place(pieces, index)


def doubled(block, axis, span):
    pieces = {0: block}
    bit = span // 2
    while bit:
        for distance in list(pieces):
            pieces[distance ^ bit] = swap(pieces[distance], axis, bit)
        bit //= 2
    return pieces


def attend(queries, keys_new, values_new, cached, cached_valid):
    new_len, kv_local, group, head_dim = queries.shape

    def part(keys, values, valid):
        scores = jnp.einsum("tgjd,kgd->gjtk", queries, keys, preferred_element_type=jnp.float32)
        weights = capped_weights(scores, valid)
        numer = jnp.einsum(
            "gjtk,kgd->gjtd",
            weights.astype(jnp.bfloat16),
            values,
            preferred_element_type=jnp.float32,
        )
        return numer, jnp.sum(weights, axis=-1)

    query_index = jnp.arange(new_len, dtype=jnp.int32)
    causal = query_index[None, :] <= query_index[:, None]
    numer, denom = part(
        cached[..., :head_dim], cached[..., head_dim:], cached_valid[None, None, None, :]
    )
    more, added = part(keys_new, values_new, causal[None, None])
    attended = ((numer + more) / (denom + added)[..., None]).transpose(2, 0, 1, 3)
    return attended.reshape(new_len, kv_local * group * head_dim).astype(jnp.bfloat16)


def local_general(
    hidden,
    slot_of_request,
    prefix_len,
    block_holder,
    block_slot,
    kv_pool,
    norm_gain,
    q_weight,
    k_weight,
    v_weight,
    o_weight,
    post_gain,
):
    shards = lax.axis_size("fsdp")
    groups = lax.axis_size("pool")
    f = lax.axis_index("fsdp")
    p = lax.axis_index("pool")
    half = shards // 2
    side = f // half
    new_len, width = hidden.shape[1:]
    requests = slot_of_request.shape[0]
    page_len = kv_pool.shape[1]
    kv_local = kv_pool.shape[2]
    head_dim = kv_pool.shape[3] // 2
    q_cols = q_weight.shape[1]
    kv_cols = k_weight.shape[1]
    group = q_cols // kv_cols
    max_blocks = block_holder.shape[1]
    per_holder = max_blocks // shards
    quarter = new_len // groups
    sub = quarter // shards
    features = o_weight.shape[0]

    kv_pieces = doubled(jnp.concatenate([k_weight, v_weight], axis=1), "fsdp", half)
    q_pieces = doubled(q_weight, "fsdp", half)
    out_weight = lax.all_gather(o_weight, "pool", axis=0, tiled=False)

    rows = hidden[0]
    normed = rms_scale(rows.astype(jnp.float32), norm_gain).astype(jnp.bfloat16)
    own_rows = lax.dynamic_slice(normed, (0, side * (width // 2)), (new_len, width // 2))
    leaving = lax.dynamic_slice(
        normed, (p * quarter, (1 - side) * (width // 2)), (quarter, width // 2)
    )
    partner_piece = swap(leaving, "fsdp", half)
    partner_pieces = {0: partner_piece}
    for distance in range(1, groups):
        partner_pieces[distance] = swap(partner_piece, "pool", distance)
    partner_rows = place(partner_pieces, p).reshape(new_len, width // 2)

    request_ids = jnp.arange(requests, dtype=jnp.int32)
    request_at_slot = jnp.sum(
        jnp.where(slot_of_request[None, :] == request_ids[:, None], request_ids[None, :], 0), axis=1
    )
    holder_by_slot = jnp.take(block_holder, request_at_slot, axis=0)
    page_by_slot = jnp.take(block_slot, request_at_slot, axis=0)
    held_here = holder_by_slot == f
    held_rank = jnp.cumsum(held_here.astype(jnp.int32), axis=1) - 1
    rank_ids = jnp.arange(per_holder, dtype=jnp.int32)
    picked = held_here[:, :, None] & (held_rank[:, :, None] == rank_ids[None, None, :])
    local_pages = jnp.sum(jnp.where(picked, page_by_slot[:, :, None], 0), axis=1)
    flat_pool = kv_pool.reshape(kv_pool.shape[0], page_len * kv_local, 2 * head_dim)
    outgoing = jnp.take(flat_pool, local_pages, axis=0)
    outgoing = outgoing.reshape(shards, per_holder * page_len * kv_local, 2 * head_dim)
    arrived = exchange(outgoing, "fsdp")
    cached = arrived.reshape(max_blocks * page_len, kv_local, 2 * head_dim)

    my_request = lax.dynamic_index_in_dim(request_at_slot, f, keepdims=False)
    my_length = prefix_len[my_request]
    my_holders = block_holder[my_request]
    entry_ids = jnp.arange(max_blocks, dtype=jnp.int32)
    mine = my_holders[None, :] == jnp.arange(shards, dtype=jnp.int32)[:, None]
    my_rank = jnp.cumsum(mine.astype(jnp.int32), axis=1) - 1
    chosen = mine[:, None, :] & (my_rank[:, None, :] == rank_ids[None, :, None])
    entry = jnp.sum(jnp.where(chosen, entry_ids[None, None, :], 0), axis=2)
    cached_position = entry.reshape(-1, 1) * page_len + jnp.arange(page_len, dtype=jnp.int32)
    cached_valid = (cached_position < my_length).reshape(-1)

    residual_out = lax.dynamic_slice_in_dim(rows, p * quarter, quarter, 0).reshape(
        shards, sub, width
    )
    residual = exchange(residual_out, "fsdp")

    positions = (my_length + jnp.arange(new_len, dtype=jnp.int32)).astype(jnp.float32)
    freqs = jnp.exp(
        jnp.arange(head_dim // 2, dtype=jnp.float32) * (-2.0 * math.log(10000.0) / head_dim)
    )
    angles = positions[:, None] * freqs
    cosine = jnp.cos(angles)[:, None, :]
    sine = jnp.sin(angles)[:, None, :]

    def project(pieces):
        weight = place(pieces, f % half).reshape(width // 2, -1)
        partial = jnp.dot(partner_rows, weight, preferred_element_type=jnp.float32)
        other = swap(partial.astype(jnp.bfloat16), "fsdp", half)
        own = jnp.dot(own_rows, weight, preferred_element_type=jnp.float32)
        return own + other.astype(jnp.float32)

    kv_sum = project(kv_pieces)
    q_sum = project(q_pieces)
    queries = rotate(q_sum.reshape(new_len, kv_local * group, head_dim), cosine, sine)
    queries = (queries * query_scale).astype(jnp.bfloat16)
    queries = queries.reshape(new_len, kv_local, group, head_dim)
    keys_new = kv_sum[:, :kv_cols].reshape(new_len, kv_local, head_dim)
    keys_new = rotate(keys_new, cosine, sine).astype(jnp.bfloat16)
    values_new = kv_sum[:, kv_cols:].astype(jnp.bfloat16).reshape(new_len, kv_local, head_dim)
    attended = attend(queries, keys_new, values_new, cached, cached_valid)

    quarters = exchange(attended.reshape(groups, quarter, q_cols), "pool")
    token_pieces = {0: quarters}
    for distance in range(2, shards, 2):
        token_pieces[distance] = swap(quarters, "fsdp", distance)
    for distance in range(0, shards, 2):
        token_pieces[distance ^ 1] = swap(token_pieces[distance], "fsdp", 1)
    tokens = place(token_pieces, f)
    projected = jnp.einsum(
        "sptc,pfc->stf", tokens, out_weight, preferred_element_type=jnp.float32
    ).astype(jnp.bfloat16)
    projected = projected.reshape(shards, shards, sub, features).transpose(1, 0, 2, 3)
    finished = exchange(projected, "fsdp").transpose(1, 2, 0, 3).reshape(shards, sub, width)
    finished = residual.astype(jnp.float32) + rms_scale(finished.astype(jnp.float32), post_gain)
    return jnp.take(finished.astype(jnp.bfloat16), slot_of_request, axis=0)


VMEM = pl.BlockSpec(memory_space=pltpu.VMEM)
SMEM = pl.BlockSpec(memory_space=pltpu.SMEM)
HBM = pl.BlockSpec(memory_space=pltpu.HBM)


def call(kernel, outs, scratch, flops, nbytes, *operands, specs=None, out_specs=None):
    return pl.pallas_call(
        kernel,
        out_shape=outs,
        in_specs=specs or [SMEM] + [VMEM] * (len(operands) - 1),
        out_specs=out_specs or jax.tree.map(lambda _: VMEM, outs),
        scratch_shapes=scratch,
        compiler_params=pltpu.CompilerParams(vmem_limit_bytes=60 << 20),
        cost_estimate=pl.CostEstimate(flops=flops, bytes_accessed=nbytes, transcendentals=0),
    )(*operands)


def after(array, *earlier):
    return lax.optimization_barrier((array,) + earlier)[0]


def weight_copies(weight_refs, weight, f, half, sems):
    copies = []
    for distance, ref in enumerate(weight_refs):
        count = ref.shape[0]
        start = pl.multiple_of(((f ^ distance) & (half - 1)) * count, 64)
        copies.append(
            pltpu.make_async_copy(ref, weight.at[pl.ds(start, count), :], sems.at[distance])
        )
        copies[-1].start()
    return copies


def pair_product(groups, half, pair, where_ref, x_refs, w_refs, rows, weight, sems):
    p, f = where_ref[0], where_ref[1]
    copies = []
    for distance, ref in enumerate(w_refs):
        count = ref.shape[0]
        start = pl.multiple_of(((f ^ distance) & 1) * count, 64)
        copies.append((ref, weight.at[pl.ds(start, count), :]))
    span = weight.shape[0]
    columns = pl.ds(pl.multiple_of((((f & (half - 1)) >> 1) ^ pair) * span, 128), span)
    quarter = x_refs[0].shape[0]
    for distance, ref in enumerate(x_refs):
        start = pl.multiple_of((p ^ distance) * quarter, quarter)
        copies.append((ref, rows.at[pl.ds(start, quarter), :]))
    copies = [
        pltpu.make_async_copy(source, target, sems.at[index])
        for index, (source, target) in enumerate(copies)
    ]
    for copy in copies:
        copy.start()
    for copy in copies:
        copy.wait()
    return jnp.dot(rows[:, columns], weight[...], preferred_element_type=jnp.float32)


def near_kernel(groups, half, where_ref, *refs):
    x_refs, w_refs = refs[:groups], refs[groups : groups + 2]
    out_ref, *scratch = refs[groups + 2 :]
    out_ref[...] = pair_product(groups, half, 0, where_ref, x_refs, w_refs, *scratch)


def partner_kernel(groups, half, where_ref, near_ref, *refs):
    x_refs, w_refs = refs[:groups], refs[groups : groups + 2]
    out_ref, *scratch = refs[groups + 2 :]
    sums = pair_product(groups, half, 1, where_ref, x_refs, w_refs, *scratch)
    out_ref[...] = (near_ref[...] + sums).astype(jnp.bfloat16)


def row_scale(rows):
    return lax.rsqrt(jnp.mean(rows * rows, axis=1, keepdims=True) + norm_eps)


def prologue_kernel(
    hidden_ref, gain_ref, q_ref, k_ref, v_ref, leaving_ref, rows_ref, weight_ref, normed, sem
):
    p, f = lax.axis_index("pool"), lax.axis_index("fsdp")
    side = f // (lax.axis_size("fsdp") // 2)
    quarter, width = rows_ref.shape
    half_width = width // 2
    start = pl.multiple_of(p * quarter, quarter)
    rows_copy = pltpu.make_async_copy(hidden_ref.at[pl.ds(start, quarter), :], rows_ref, sem)
    rows_copy.start()
    at = 0
    for ref in (q_ref, k_ref, v_ref):
        weight_ref[:, at : at + ref.shape[1]] = ref[...]
        at += ref.shape[1]
    rows_copy.wait()
    rows = rows_ref[...].astype(jnp.float32)
    normed[...] = rows * row_scale(rows) * gain_ref[...].reshape(1, width)
    away = pl.multiple_of((1 - side) * half_width, 128)
    leaving_ref[...] = normed[:, pl.ds(away, half_width)].astype(jnp.bfloat16)


def pages_kernel(
    requests, page_len, where_ref, holder_ref, slot_ref, pool_ref, *refs
):
    f = where_ref[1]
    out_ref, valid_ref, listed, entries, counts = refs
    max_blocks = holder_ref.shape[1]
    shards = out_ref.shape[0]
    per = max_blocks // shards
    page_rows = pool_ref.shape[1]
    length, mine = jnp.int32(0), jnp.int32(0)
    for r in range(requests):
        at = where_ref[3 + r] == f
        length = length + jnp.where(at, where_ref[3 + requests + r], 0)
        mine = mine + jnp.where(at, r, 0)
    for r in range(requests):
        slot = where_ref[3 + r]

        def note(j, count):
            listed[count] = slot_ref[r, j]
            return count + jnp.where(holder_ref[r, j] == f, 1, 0)

        lax.fori_loop(0, max_blocks, note, jnp.int32(0), unroll=8)
        for k in range(per):
            out_ref[slot, k * page_rows : (k + 1) * page_rows, :] = pool_ref[listed[k]]
    for h in range(shards):
        counts[h] = 0

    def enter(j, carry):
        h = holder_ref[mine, j]
        count = counts[h]
        entries[h * per + count] = j
        counts[h] = count + 1
        return carry

    lax.fori_loop(0, max_blocks, enter, 0, unroll=4)
    row = lax.broadcasted_iota(jnp.int32, valid_ref.shape, 0)
    lane = lax.broadcasted_iota(jnp.int32, valid_ref.shape, 1)
    place_in = row * per + lane // page_len
    entry = jnp.zeros(valid_ref.shape, jnp.int32)
    for at in range(max_blocks):
        entry = jnp.where(place_in == at, entries[at], entry)
    position = entry * page_len + lane % page_len
    valid_ref[...] = jnp.where(position < length, 1.0, 0.0)


def part_pages(pages, keys, values):
    kv_local, _, head_dim = keys.shape
    span = pages.shape[1]
    per = span // kv_local
    row = lax.broadcasted_iota(jnp.int32, (span, span), 0)
    column = lax.broadcasted_iota(jnp.int32, (span, span), 1)
    part = (column == (row % per) * kv_local + row // per).astype(jnp.bfloat16)
    for holder in range(pages.shape[0]):
        parted = jnp.dot(part, pages[holder], preferred_element_type=jnp.float32)
        parted = parted.astype(jnp.bfloat16)
        at = holder * per
        for g in range(kv_local):
            lines = parted[g * per : (g + 1) * per]
            keys[g, at : at + per, :] = lines[:, :head_dim]
            values[g, at : at + per, :] = lines[:, head_dim:]


def own_kernel(requests, half, where_ref, hidden_ref, gain_ref, freq_ref, pages, *refs):
    f = where_ref[1]
    own_ref, cos_ref, sin_ref, keys, values, hidden, normed, weight, sems = refs[half:]
    rows_copy = pltpu.make_async_copy(hidden_ref, hidden, sems.at[half])
    rows_copy.start()
    copies = weight_copies(refs[:half], weight, f, half, sems)
    rows_copy.wait()
    new_len, width = hidden_ref.shape
    half_width = width // 2
    length = jnp.int32(0)
    for r in range(requests):
        length = length + jnp.where(where_ref[3 + r] == f, where_ref[3 + requests + r], 0)
    start = pl.multiple_of(where_ref[2] * half_width, 128)
    gain = gain_ref[:, pl.ds(start, half_width)]
    step = 32

    def norm(index, carry):
        at = pl.multiple_of(index * step, step)
        rows = hidden[pl.ds(at, step), :].astype(jnp.float32)
        scale = row_scale(rows)
        part = hidden[pl.ds(at, step), pl.ds(start, half_width)].astype(jnp.float32)
        normed[pl.ds(at, step), :] = (part * scale * gain).astype(jnp.bfloat16)
        return carry

    lax.fori_loop(0, new_len // step, norm, 0)
    part_pages(pages, keys, values)
    position = lax.broadcasted_iota(jnp.int32, cos_ref.shape, 0) + length
    angle = position.astype(jnp.float32) * freq_ref[...]
    lane = lax.broadcasted_iota(jnp.int32, cos_ref.shape, 1)
    cos_ref[...] = jnp.cos(angle)
    sine = jnp.sin(angle)
    sin_ref[...] = jnp.where(lane < cos_ref.shape[1] // 2, -sine, sine)
    for copy in copies:
        copy.wait()
    for at in range(0, own_ref.shape[1], 512):
        own_ref[:, at : at + 512] = jnp.dot(
            normed[...], weight[:, at : at + 512], preferred_element_type=jnp.float32
        )


def capped(scores):
    return jnp.exp2(jnp.tanh(scores * (1.0 / softcap)) * (softcap * math.log2(math.e)))


def attend_kernel(
    groups,
    kv_local,
    head_dim,
    where_ref,
    own,
    other_ref,
    cos_ref,
    sin_ref,
    valid_ref,
    keys,
    values,
    *refs,
):
    p = where_ref[0]
    out_refs = refs[:groups]
    result, other, sem = refs[groups:]
    copy = pltpu.make_async_copy(other_ref, other, sem)
    copy.start()
    new_len, q_cols = result.shape
    group = q_cols // (kv_local * head_dim)

    def sums(at):
        return own[:, at : at + head_dim] + other[:, at : at + head_dim].astype(jnp.float32)

    cosine, sine = cos_ref[...], sin_ref[...]

    def rope(vectors):
        return vectors * cosine + pltpu.roll(vectors, head_dim // 2, 1) * sine

    copy.wait()
    per = valid_ref.shape[1]
    place_at = keys.shape[1]
    span_keys = 2 * per
    t = lax.broadcasted_iota(jnp.int32, (group * new_len, new_len), 0) % new_len
    s = lax.broadcasted_iota(jnp.int32, (group * new_len, new_len), 1)
    causal = s <= t
    for g in range(kv_local):
        heads = [
            (rope(sums((g * group + j) * head_dim)) * query_scale).astype(jnp.bfloat16)
            for j in range(group)
        ]
        queries = jnp.concatenate(heads, axis=0)
        at = q_cols + g * head_dim
        new_key = rope(sums(at)).astype(jnp.bfloat16)
        new_value = sums(at + kv_local * head_dim).astype(jnp.bfloat16)

        def scores_of(key):
            return lax.dot_general(
                queries, key, (((1,), (1,)), ((), ())), preferred_element_type=jnp.float32
            )

        weights = jnp.where(causal, capped(scores_of(new_key)), 0.0)
        denom = jnp.sum(weights, axis=1, keepdims=True)
        numer = jnp.dot(
            weights.astype(jnp.bfloat16), new_value, preferred_element_type=jnp.float32
        )
        for start in range(0, place_at, span_keys):
            at = start // per
            valid = jnp.concatenate([valid_ref[at : at + 1], valid_ref[at + 1 : at + 2]], axis=1)
            valid = valid > 0.0
            weights = jnp.where(
                valid, capped(scores_of(keys[g, start : start + span_keys, :])), 0.0
            )
            denom = denom + jnp.sum(weights, axis=1, keepdims=True)
            numer = numer + jnp.dot(
                weights.astype(jnp.bfloat16),
                values[g, start : start + span_keys, :],
                preferred_element_type=jnp.float32,
            )
        attended = (numer / denom).astype(jnp.bfloat16)
        for j in range(group):
            to = (g * group + j) * head_dim
            result[:, to : to + head_dim] = attended[j * new_len : (j + 1) * new_len]
    quarter = new_len // groups
    for distance, ref in enumerate(out_refs):
        start = pl.multiple_of((p ^ distance) * quarter, quarter)
        ref[...] = result[pl.ds(start, quarter), :]


def output_kernel(groups, shards, where_ref, *refs):
    p, f = where_ref[0], where_ref[1]
    token_refs = refs[:shards]
    weight_ref = refs[shards]
    out_refs = refs[shards + 1 : 2 * shards + 1]
    total, tokens, weight, sems, token_sems = refs[2 * shards + 1 :]
    token_copies = [
        pltpu.make_async_copy(ref, tokens.at[e], token_sems.at[e])
        for e, ref in enumerate(token_refs)
    ]
    copies = [
        pltpu.make_async_copy(weight_ref.at[p ^ distance], weight.at[distance], sems.at[distance])
        for distance in range(groups)
    ]
    for copy in token_copies + copies:
        copy.start()
    for copy in token_copies:
        copy.wait()
    quarter = token_refs[0].shape[1]
    sub = quarter // shards
    projected = None
    for distance in range(groups):
        rows = jnp.concatenate([tokens[e, distance] for e in range(shards)], axis=0)
        copies[distance].wait()
        term = lax.dot_general(
            rows,
            weight[distance],
            (((1,), (1,)), ((), ())),
            preferred_element_type=jnp.float32,
        )
        projected = term if projected is None else projected + term
    total[...] = projected
    for e in range(shards):
        for distance, ref in enumerate(out_refs):
            start = pl.multiple_of(e * quarter + (f ^ distance) * sub, sub)
            ref[f ^ e] = total[pl.ds(start, sub), :].astype(jnp.bfloat16)


def finish_kernel(shards, where_ref, gain_ref, residual_ref, *refs):
    f = where_ref[1]
    piece_refs = refs[:shards]
    out_ref, projected = refs[shards:]
    for distance, ref in enumerate(piece_refs):
        projected[f ^ distance] = ref[...].astype(jnp.float32)
    gain = gain_ref[...]
    for request in range(out_ref.shape[0]):
        slot = where_ref[3 + request]
        line = jnp.concatenate([projected[k, slot] for k in range(shards)], axis=1)
        mean_square = jnp.mean(line * line, axis=1, keepdims=True)
        line = line * lax.rsqrt(mean_square + norm_eps) * gain
        out_ref[request] = (residual_ref[slot].astype(jnp.float32) + line).astype(jnp.bfloat16)


def pool_pieces(block, groups):
    return [block] + [swap(block, "pool", distance) for distance in range(1, groups)]


def local_small(
    hidden,
    slot_of_request,
    prefix_len,
    block_holder,
    block_slot,
    kv_pool,
    norm_gain,
    q_weight,
    k_weight,
    v_weight,
    o_weight,
    post_gain,
):
    shards = lax.axis_size("fsdp")
    groups = lax.axis_size("pool")
    f = lax.axis_index("fsdp")
    p = lax.axis_index("pool")
    half = shards // 2
    side = f // half
    new_len, width = hidden.shape[1:]
    requests = slot_of_request.shape[0]
    page_len = kv_pool.shape[1]
    kv_local = kv_pool.shape[2]
    head_dim = kv_pool.shape[3] // 2
    q_cols = q_weight.shape[1]
    kv_cols = k_weight.shape[1]
    max_blocks = block_holder.shape[1]
    per_holder = max_blocks // shards
    quarter = new_len // groups
    sub = quarter // shards
    features = o_weight.shape[0]
    bf16, f32 = jnp.bfloat16, jnp.float32
    where = jnp.concatenate(
        [jnp.stack([p, f, side]).astype(jnp.int32), slot_of_request, prefix_len]
    )
    shape = jax.ShapeDtypeStruct
    gain = norm_gain.reshape(1, width)
    rows = hidden[0]

    leaving, my_quarter, joined = call(
        prologue_kernel,
        [
            shape((quarter, width // 2), bf16),
            shape((quarter, width), bf16),
            shape((features, q_cols + 2 * kv_cols), bf16),
        ],
        [pltpu.VMEM((quarter, width), f32), pltpu.SemaphoreType.DMA],
        quarter * width * 8,
        4 * features * kv_cols,
        rows,
        norm_gain,
        q_weight,
        k_weight,
        v_weight,
        specs=[HBM, VMEM, VMEM, VMEM, VMEM],
    )
    partner_piece = swap(leaving, "fsdp", half)

    flat_pool = kv_pool.reshape(kv_pool.shape[0], page_len * kv_local, 2 * head_dim)
    page_rows = per_holder * page_len * kv_local
    outgoing, valid = call(
        functools.partial(pages_kernel, requests, page_len),
        [
            shape((shards, page_rows, 2 * head_dim), bf16),
            shape((shards, per_holder * page_len), f32),
        ],
        [
            pltpu.SMEM((2 * per_holder,), jnp.int32),
            pltpu.SMEM((max_blocks + per_holder,), jnp.int32),
            pltpu.SMEM((shards,), jnp.int32),
        ],
        1 << 20,
        1 << 21,
        after(where, leaving),
        block_holder,
        block_slot,
        flat_pool,
        specs=[SMEM, SMEM, SMEM, VMEM],
    )
    near = swap(joined, "fsdp", 1)
    arrived = lax.all_to_all(outgoing, "fsdp", split_axis=0, concat_axis=0, tiled=True)
    partner_piece, near, valid = lax.optimization_barrier((partner_piece, near, valid))
    far = swap(after(joined, partner_piece), "fsdp", 2)
    partner_pieces = pool_pieces(partner_piece, groups)
    partner_pieces, arrived = lax.optimization_barrier((partner_pieces, arrived))
    near_sums = call(
        functools.partial(near_kernel, groups, half),
        shape((new_len, q_cols + 2 * kv_cols), f32),
        [
            pltpu.VMEM((new_len, width // 2), bf16),
            pltpu.VMEM((2 * features, q_cols + 2 * kv_cols), bf16),
            pltpu.SemaphoreType.DMA((groups + 2,)),
        ],
        new_len * width * q_cols,
        width * (new_len + 2 * q_cols),
        where,
        *partner_pieces,
        joined,
        near,
        specs=[SMEM] + [HBM] * (groups + 2),
    )
    near_sums, far = lax.optimization_barrier((near_sums, far))
    weights = [joined, near, far, swap(far, "fsdp", 1)]
    out_weight = lax.all_gather(after(o_weight, *partner_pieces), "pool", axis=0, tiled=False)

    partial = call(
        functools.partial(partner_kernel, groups, half),
        shape((new_len, q_cols + 2 * kv_cols), bf16),
        [
            pltpu.VMEM((new_len, width // 2), bf16),
            pltpu.VMEM((2 * features, q_cols + 2 * kv_cols), bf16),
            pltpu.SemaphoreType.DMA((groups + 2,)),
        ],
        new_len * width * q_cols,
        width * (new_len + 2 * q_cols),
        where,
        near_sums,
        *partner_pieces,
        *weights[2:],
        specs=[SMEM, VMEM] + [HBM] * (groups + 2),
    )
    other = swap(partial, "fsdp", half)
    freqs = np.exp(np.arange(head_dim // 2) * (-2.0 * math.log(10000.0) / head_dim))
    freqs = np.concatenate([freqs, freqs]).astype(np.float32).reshape(1, head_dim)
    own, cosine, sine, keys, values = call(
        functools.partial(own_kernel, requests, half),
        [
            shape((new_len, q_cols + 2 * kv_cols), f32),
            shape((new_len, head_dim), f32),
            shape((new_len, head_dim), f32),
            shape((kv_local, max_blocks * page_len, head_dim), bf16),
            shape((kv_local, max_blocks * page_len, head_dim), bf16),
        ],
        [
            pltpu.VMEM((new_len, width), bf16),
            pltpu.VMEM((new_len, width // 2), bf16),
            pltpu.VMEM((width // 2, q_cols + 2 * kv_cols), bf16),
            pltpu.SemaphoreType.DMA((half + 1,)),
        ],
        new_len * width * (q_cols + 2 * kv_cols),
        width * (2 * new_len + q_cols + 2 * kv_cols),
        where,
        after(rows, partial),
        gain,
        freqs,
        arrived,
        *weights,
        specs=[SMEM, HBM, VMEM, VMEM, VMEM] + [HBM] * half,
    )

    residual = lax.all_to_all(
        after(my_quarter, own).reshape(shards, sub, width),
        "fsdp",
        split_axis=0,
        concat_axis=0,
        tiled=True,
    )

    keys_total = max_blocks * page_len
    quarters = call(
        functools.partial(attend_kernel, groups, kv_local, head_dim),
        [shape((quarter, q_cols), bf16)] * groups,
        [
            pltpu.VMEM((new_len, q_cols), bf16),
            pltpu.VMEM(other.shape, bf16),
            pltpu.SemaphoreType.DMA,
        ],
        4 * new_len * q_cols * (keys_total + new_len),
        1 << 22,
        where,
        own,
        other,
        cosine,
        sine,
        valid,
        keys,
        values,
        specs=[SMEM, VMEM, HBM, VMEM, VMEM, VMEM, VMEM, VMEM],
    )

    quarters = [
        swap(piece, "pool", distance) if distance else piece
        for distance, piece in enumerate(quarters)
    ]
    quarters = jnp.stack(quarters)
    tokens = {0: quarters}
    for distance in range(2, shards, 2):
        tokens[distance] = swap(quarters, "fsdp", distance)
    for distance in range(0, shards, 2):
        tokens[distance ^ 1] = swap(tokens[distance], "fsdp", 1)
    projected = call(
        functools.partial(output_kernel, groups, shards),
        [shape((shards, sub, features), bf16)] * shards,
        [
            pltpu.VMEM((shards * quarter, features), f32),
            pltpu.VMEM((shards, groups, quarter, q_cols), bf16),
            pltpu.VMEM((groups, features, q_cols), bf16),
            pltpu.SemaphoreType.DMA((groups,)),
            pltpu.SemaphoreType.DMA((shards,)),
        ],
        2 * shards * quarter * features * groups * q_cols,
        1 << 22,
        where,
        *[tokens[distance] for distance in range(shards)],
        out_weight,
        specs=[SMEM] + [HBM] * (shards + 1),
    )
    finished = [
        swap(piece, "fsdp", distance) if distance else piece
        for distance, piece in enumerate(projected)
    ]
    return call(
        functools.partial(finish_kernel, shards),
        shape((requests, sub, width), bf16),
        [pltpu.VMEM((shards, shards, sub, features), f32)],
        1 << 20,
        1 << 20,
        where,
        post_gain.reshape(1, width),
        residual,
        *finished,
    )


def local(*arguments):
    return local_small(*arguments) if lax.axis_size("fsdp") == 8 else local_general(*arguments)


def solution(mesh):
    in_specs = (
        P("fsdp", None, None),
        P(),
        P(),
        P(),
        P(),
        P("fsdp", None, "pool", None),
        P(),
        P("fsdp", "pool"),
        P("fsdp", "pool"),
        P("fsdp", "pool"),
        P("fsdp", "pool"),
        P(),
    )
    out_specs = P(None, ("pool", "fsdp"), None)
    return jax.shard_map(local, mesh=mesh, in_specs=in_specs, out_specs=out_specs, check_vma=False)
```

```python
import functools
import math

import jax
import jax.numpy as jnp
import numpy as np
from jax import lax
from jax.experimental import pallas as pl
from jax.experimental.pallas import tpu as pltpu
from jax.sharding import PartitionSpec as P

softcap = 50.0
query_scale = 144.0 ** (-0.5)
norm_eps = 1e-06


def rms_scale(rows, gain):
    mean_square = jnp.mean(rows * rows, axis=-1, keepdims=True)
    return rows * lax.rsqrt(mean_square + norm_eps) * gain


def rotate(vectors, cosine, sine):
    half = vectors.shape[-1] // 2
    first = vectors[..., :half]
    second = vectors[..., half:]
    return jnp.concatenate(
        [first * cosine - second * sine, second * cosine + first * sine], axis=-1
    )


def capped_weights(scores, valid):
    return jnp.where(valid, jnp.exp(softcap * jnp.tanh(scores / softcap)), 0.0)


def swap(array, axis, distance):
    size = lax.axis_size(axis)
    return lax.ppermute(array, axis, [(i, i ^ distance) for i in range(size)])


def place(pieces, index):
    first = pieces[0]
    stacked = jnp.zeros((len(pieces),) + first.shape, first.dtype)
    for distance, piece in pieces.items():
        stacked = lax.dynamic_update_index_in_dim(stacked, piece, index ^ distance, 0)
    return stacked


def exchange(chunks, axis):
    size = lax.axis_size(axis)
    index = lax.axis_index(axis)
    if size > 8:
        return lax.all_to_all(chunks, axis, split_axis=0, concat_axis=0, tiled=True)
    pieces = {}
    for distance in range(size):
        chunk = lax.dynamic_index_in_dim(chunks, index ^ distance, 0, keepdims=False)
        pieces[distance] = swap(chunk, axis, distance) if distance else chunk
    return place(pieces, index)


def doubled(block, axis, span):
    pieces = {0: block}
    bit = span // 2
    while bit:
        for distance in list(pieces):
            pieces[distance ^ bit] = swap(pieces[distance], axis, bit)
        bit //= 2
    return pieces


def attend(queries, keys_new, values_new, cached, cached_valid):
    new_len, kv_local, group, head_dim = queries.shape

    def part(keys, values, valid):
        scores = jnp.einsum("tgjd,kgd->gjtk", queries, keys, preferred_element_type=jnp.float32)
        weights = capped_weights(scores, valid)
        numer = jnp.einsum(
            "gjtk,kgd->gjtd",
            weights.astype(jnp.bfloat16),
            values,
            preferred_element_type=jnp.float32,
        )
        return numer, jnp.sum(weights, axis=-1)

    query_index = jnp.arange(new_len, dtype=jnp.int32)
    causal = query_index[None, :] <= query_index[:, None]
    numer, denom = part(
        cached[..., :head_dim], cached[..., head_dim:], cached_valid[None, None, None, :]
    )
    more, added = part(keys_new, values_new, causal[None, None])
    attended = ((numer + more) / (denom + added)[..., None]).transpose(2, 0, 1, 3)
    return attended.reshape(new_len, kv_local * group * head_dim).astype(jnp.bfloat16)


def local_general(
    hidden,
    slot_of_request,
    prefix_len,
    block_holder,
    block_slot,
    kv_pool,
    norm_gain,
    q_weight,
    k_weight,
    v_weight,
    o_weight,
    post_gain,
):
    shards = lax.axis_size("fsdp")
    groups = lax.axis_size("pool")
    f = lax.axis_index("fsdp")
    p = lax.axis_index("pool")
    half = shards // 2
    side = f // half
    new_len, width = hidden.shape[1:]
    requests = slot_of_request.shape[0]
    page_len = kv_pool.shape[1]
    kv_local = kv_pool.shape[2]
    head_dim = kv_pool.shape[3] // 2
    q_cols = q_weight.shape[1]
    kv_cols = k_weight.shape[1]
    group = q_cols // kv_cols
    max_blocks = block_holder.shape[1]
    per_holder = max_blocks // shards
    quarter = new_len // groups
    sub = quarter // shards
    features = o_weight.shape[0]

    kv_pieces = doubled(jnp.concatenate([k_weight, v_weight], axis=1), "fsdp", half)
    q_pieces = doubled(q_weight, "fsdp", half)
    out_weight = lax.all_gather(o_weight, "pool", axis=0, tiled=False)

    rows = hidden[0]
    normed = rms_scale(rows.astype(jnp.float32), norm_gain).astype(jnp.bfloat16)
    own_rows = lax.dynamic_slice(normed, (0, side * (width // 2)), (new_len, width // 2))
    leaving = lax.dynamic_slice(
        normed, (p * quarter, (1 - side) * (width // 2)), (quarter, width // 2)
    )
    partner_piece = swap(leaving, "fsdp", half)
    partner_pieces = {0: partner_piece}
    for distance in range(1, groups):
        partner_pieces[distance] = swap(partner_piece, "pool", distance)
    partner_rows = place(partner_pieces, p).reshape(new_len, width // 2)

    request_ids = jnp.arange(requests, dtype=jnp.int32)
    request_at_slot = jnp.sum(
        jnp.where(slot_of_request[None, :] == request_ids[:, None], request_ids[None, :], 0), axis=1
    )
    holder_by_slot = jnp.take(block_holder, request_at_slot, axis=0)
    page_by_slot = jnp.take(block_slot, request_at_slot, axis=0)
    held_here = holder_by_slot == f
    held_rank = jnp.cumsum(held_here.astype(jnp.int32), axis=1) - 1
    rank_ids = jnp.arange(per_holder, dtype=jnp.int32)
    picked = held_here[:, :, None] & (held_rank[:, :, None] == rank_ids[None, None, :])
    local_pages = jnp.sum(jnp.where(picked, page_by_slot[:, :, None], 0), axis=1)
    flat_pool = kv_pool.reshape(kv_pool.shape[0], page_len * kv_local, 2 * head_dim)
    outgoing = jnp.take(flat_pool, local_pages, axis=0)
    outgoing = outgoing.reshape(shards, per_holder * page_len * kv_local, 2 * head_dim)
    arrived = exchange(outgoing, "fsdp")
    cached = arrived.reshape(max_blocks * page_len, kv_local, 2 * head_dim)

    my_request = lax.dynamic_index_in_dim(request_at_slot, f, keepdims=False)
    my_length = prefix_len[my_request]
    my_holders = block_holder[my_request]
    entry_ids = jnp.arange(max_blocks, dtype=jnp.int32)
    mine = my_holders[None, :] == jnp.arange(shards, dtype=jnp.int32)[:, None]
    my_rank = jnp.cumsum(mine.astype(jnp.int32), axis=1) - 1
    chosen = mine[:, None, :] & (my_rank[:, None, :] == rank_ids[None, :, None])
    entry = jnp.sum(jnp.where(chosen, entry_ids[None, None, :], 0), axis=2)
    cached_position = entry.reshape(-1, 1) * page_len + jnp.arange(page_len, dtype=jnp.int32)
    cached_valid = (cached_position < my_length).reshape(-1)

    residual_out = lax.dynamic_slice_in_dim(rows, p * quarter, quarter, 0).reshape(
        shards, sub, width
    )
    residual = exchange(residual_out, "fsdp")

    positions = (my_length + jnp.arange(new_len, dtype=jnp.int32)).astype(jnp.float32)
    freqs = jnp.exp(
        jnp.arange(head_dim // 2, dtype=jnp.float32) * (-2.0 * math.log(10000.0) / head_dim)
    )
    angles = positions[:, None] * freqs
    cosine = jnp.cos(angles)[:, None, :]
    sine = jnp.sin(angles)[:, None, :]

    def project(pieces):
        weight = place(pieces, f % half).reshape(width // 2, -1)
        partial = jnp.dot(partner_rows, weight, preferred_element_type=jnp.float32)
        other = swap(partial.astype(jnp.bfloat16), "fsdp", half)
        own = jnp.dot(own_rows, weight, preferred_element_type=jnp.float32)
        return own + other.astype(jnp.float32)

    kv_sum = project(kv_pieces)
    q_sum = project(q_pieces)
    queries = rotate(q_sum.reshape(new_len, kv_local * group, head_dim), cosine, sine)
    queries = (queries * query_scale).astype(jnp.bfloat16)
    queries = queries.reshape(new_len, kv_local, group, head_dim)
    keys_new = kv_sum[:, :kv_cols].reshape(new_len, kv_local, head_dim)
    keys_new = rotate(keys_new, cosine, sine).astype(jnp.bfloat16)
    values_new = kv_sum[:, kv_cols:].astype(jnp.bfloat16).reshape(new_len, kv_local, head_dim)
    attended = attend(queries, keys_new, values_new, cached, cached_valid)

    quarters = exchange(attended.reshape(groups, quarter, q_cols), "pool")
    token_pieces = {0: quarters}
    for distance in range(2, shards, 2):
        token_pieces[distance] = swap(quarters, "fsdp", distance)
    for distance in range(0, shards, 2):
        token_pieces[distance ^ 1] = swap(token_pieces[distance], "fsdp", 1)
    tokens = place(token_pieces, f)
    projected = jnp.einsum(
        "sptc,pfc->stf", tokens, out_weight, preferred_element_type=jnp.float32
    ).astype(jnp.bfloat16)
    projected = projected.reshape(shards, shards, sub, features).transpose(1, 0, 2, 3)
    finished = exchange(projected, "fsdp").transpose(1, 2, 0, 3).reshape(shards, sub, width)
    finished = residual.astype(jnp.float32) + rms_scale(finished.astype(jnp.float32), post_gain)
    return jnp.take(finished.astype(jnp.bfloat16), slot_of_request, axis=0)


VMEM = pl.BlockSpec(memory_space=pltpu.VMEM)
SMEM = pl.BlockSpec(memory_space=pltpu.SMEM)
HBM = pl.BlockSpec(memory_space=pltpu.HBM)


def call(kernel, outs, scratch, flops, nbytes, *operands, specs=None, out_specs=None, mib=60):
    return pl.pallas_call(
        kernel,
        out_shape=outs,
        in_specs=specs or [SMEM] + [VMEM] * (len(operands) - 1),
        out_specs=out_specs or jax.tree.map(lambda _: VMEM, outs),
        scratch_shapes=scratch,
        compiler_params=pltpu.CompilerParams(vmem_limit_bytes=mib << 20),
        cost_estimate=pl.CostEstimate(flops=flops, bytes_accessed=nbytes, transcendentals=0),
    )(*operands)


def after(array, *earlier):
    return lax.optimization_barrier((array,) + earlier)[0]


def weight_copies(weight_refs, weight, f, half, sems):
    copies = []
    for distance, ref in enumerate(weight_refs):
        count = ref.shape[0]
        start = pl.multiple_of(((f ^ distance) & (half - 1)) * count, 64)
        copies.append(
            pltpu.make_async_copy(ref, weight.at[pl.ds(start, count), :], sems.at[distance])
        )
        copies[-1].start()
    return copies


def pair_product(groups, half, pair, where_ref, x_refs, w_refs, rows, weight, sems):
    p, f = where_ref[0], where_ref[1]
    copies = []
    for distance, ref in enumerate(w_refs):
        count = ref.shape[0]
        start = pl.multiple_of(((f ^ distance) & 1) * count, 64)
        copies.append((ref, weight.at[pl.ds(start, count), :]))
    span = weight.shape[0]
    columns = pl.ds(pl.multiple_of((((f & (half - 1)) >> 1) ^ pair) * span, 128), span)
    quarter = x_refs[0].shape[0]
    for distance, ref in enumerate(x_refs):
        start = pl.multiple_of((p ^ distance) * quarter, quarter)
        copies.append((ref, rows.at[pl.ds(start, quarter), :]))
    copies = [
        pltpu.make_async_copy(source, target, sems.at[index])
        for index, (source, target) in enumerate(copies)
    ]
    for copy in copies:
        copy.start()
    for copy in copies:
        copy.wait()
    return jnp.dot(rows[:, columns], weight[...], preferred_element_type=jnp.float32)


def near_kernel(groups, half, where_ref, *refs):
    x_refs, w_refs = refs[:groups], refs[groups : groups + 2]
    out_ref, *scratch = refs[groups + 2 :]
    out_ref[...] = pair_product(groups, half, 0, where_ref, x_refs, w_refs, *scratch)


def partner_kernel(groups, half, where_ref, near_ref, *refs):
    x_refs, w_refs = refs[:groups], refs[groups : groups + 2]
    out_ref, *scratch = refs[groups + 2 :]
    sums = pair_product(groups, half, 1, where_ref, x_refs, w_refs, *scratch)
    out_ref[...] = (near_ref[...] + sums).astype(jnp.bfloat16)


def row_scale(rows):
    return lax.rsqrt(jnp.mean(rows * rows, axis=1, keepdims=True) + norm_eps)


def prologue_kernel(
    hidden_ref, gain_ref, q_ref, k_ref, v_ref, leaving_ref, rows_ref, weight_ref, normed, sem
):
    p, f = lax.axis_index("pool"), lax.axis_index("fsdp")
    side = f // (lax.axis_size("fsdp") // 2)
    quarter, width = rows_ref.shape
    half_width = width // 2
    start = pl.multiple_of(p * quarter, quarter)
    rows_copy = pltpu.make_async_copy(hidden_ref.at[pl.ds(start, quarter), :], rows_ref, sem)
    rows_copy.start()
    at = 0
    for ref in (q_ref, k_ref, v_ref):
        weight_ref[:, at : at + ref.shape[1]] = ref[...]
        at += ref.shape[1]
    rows_copy.wait()
    rows = rows_ref[...].astype(jnp.float32)
    normed[...] = rows * row_scale(rows) * gain_ref[...].reshape(1, width)
    away = pl.multiple_of((1 - side) * half_width, 128)
    leaving_ref[...] = normed[:, pl.ds(away, half_width)].astype(jnp.bfloat16)


def pages_kernel(
    requests, page_len, where_ref, holder_ref, slot_ref, pool_ref, *refs
):
    f = where_ref[1]
    out_ref, valid_ref, listed, entries, counts = refs
    max_blocks = holder_ref.shape[1]
    shards = out_ref.shape[0]
    per = max_blocks // shards
    page_rows = pool_ref.shape[1]
    length, mine = jnp.int32(0), jnp.int32(0)
    for r in range(requests):
        at = where_ref[3 + r] == f
        length = length + jnp.where(at, where_ref[3 + requests + r], 0)
        mine = mine + jnp.where(at, r, 0)
    for r in range(requests):
        slot = where_ref[3 + r]

        def note(j, count):
            listed[count] = slot_ref[r, j]
            return count + jnp.where(holder_ref[r, j] == f, 1, 0)

        lax.fori_loop(0, max_blocks, note, jnp.int32(0), unroll=8)
        for k in range(per):
            out_ref[slot, k * page_rows : (k + 1) * page_rows, :] = pool_ref[listed[k]]
    for h in range(shards):
        counts[h] = 0

    def enter(j, carry):
        h = holder_ref[mine, j]
        count = counts[h]
        entries[h * per + count] = j
        counts[h] = count + 1
        return carry

    lax.fori_loop(0, max_blocks, enter, 0, unroll=4)
    row = lax.broadcasted_iota(jnp.int32, valid_ref.shape, 0)
    lane = lax.broadcasted_iota(jnp.int32, valid_ref.shape, 1)
    place_in = row * per + lane // page_len
    entry = jnp.zeros(valid_ref.shape, jnp.int32)
    for at in range(max_blocks):
        entry = jnp.where(place_in == at, entries[at], entry)
    position = entry * page_len + lane % page_len
    valid_ref[...] = jnp.where(position < length, 1.0, 0.0)


def part_pages(pages, keys, values):
    kv_local, _, head_dim = keys.shape
    span = pages.shape[1]
    per = span // kv_local
    row = lax.broadcasted_iota(jnp.int32, (span, span), 0)
    column = lax.broadcasted_iota(jnp.int32, (span, span), 1)
    part = (column == (row % per) * kv_local + row // per).astype(jnp.bfloat16)
    for holder in range(pages.shape[0]):
        parted = jnp.dot(part, pages[holder], preferred_element_type=jnp.float32)
        parted = parted.astype(jnp.bfloat16)
        at = holder * per
        for g in range(kv_local):
            lines = parted[g * per : (g + 1) * per]
            keys[g, at : at + per, :] = lines[:, :head_dim]
            values[g, at : at + per, :] = lines[:, head_dim:]


def own_kernel(requests, half, where_ref, hidden_ref, gain_ref, freq_ref, pages, *refs):
    f = where_ref[1]
    own_ref, cos_ref, sin_ref, keys, values, hidden, normed, weight, sems = refs[half:]
    rows_copy = pltpu.make_async_copy(hidden_ref, hidden, sems.at[half])
    rows_copy.start()
    copies = weight_copies(refs[:half], weight, f, half, sems)
    rows_copy.wait()
    new_len, width = hidden_ref.shape
    half_width = width // 2
    length = jnp.int32(0)
    for r in range(requests):
        length = length + jnp.where(where_ref[3 + r] == f, where_ref[3 + requests + r], 0)
    start = pl.multiple_of(where_ref[2] * half_width, 128)
    gain = gain_ref[:, pl.ds(start, half_width)]
    step = 32

    def norm(index, carry):
        at = pl.multiple_of(index * step, step)
        rows = hidden[pl.ds(at, step), :].astype(jnp.float32)
        scale = row_scale(rows)
        part = hidden[pl.ds(at, step), pl.ds(start, half_width)].astype(jnp.float32)
        normed[pl.ds(at, step), :] = (part * scale * gain).astype(jnp.bfloat16)
        return carry

    lax.fori_loop(0, new_len // step, norm, 0)
    part_pages(pages, keys, values)
    position = lax.broadcasted_iota(jnp.int32, cos_ref.shape, 0) + length
    angle = position.astype(jnp.float32) * freq_ref[...]
    lane = lax.broadcasted_iota(jnp.int32, cos_ref.shape, 1)
    cos_ref[...] = jnp.cos(angle)
    sine = jnp.sin(angle)
    sin_ref[...] = jnp.where(lane < cos_ref.shape[1] // 2, -sine, sine)
    for copy in copies:
        copy.wait()
    for at in range(0, own_ref.shape[1], 512):
        own_ref[:, at : at + 512] = jnp.dot(
            normed[...], weight[:, at : at + 512], preferred_element_type=jnp.float32
        )


def capped(scores):
    return jnp.exp2(jnp.tanh(scores * (1.0 / softcap)) * (softcap * math.log2(math.e)))


def attend_kernel(
    groups,
    kv_local,
    head_dim,
    where_ref,
    own,
    other_ref,
    cos_ref,
    sin_ref,
    valid_ref,
    keys,
    values,
    *refs,
):
    p = where_ref[0]
    out_refs = refs[:groups]
    result, other, sem = refs[groups:]
    copy = pltpu.make_async_copy(other_ref, other, sem)
    copy.start()
    new_len, q_cols = result.shape
    group = q_cols // (kv_local * head_dim)

    def sums(at):
        return own[:, at : at + head_dim] + other[:, at : at + head_dim].astype(jnp.float32)

    cosine, sine = cos_ref[...], sin_ref[...]

    def rope(vectors):
        return vectors * cosine + pltpu.roll(vectors, head_dim // 2, 1) * sine

    copy.wait()
    per = valid_ref.shape[1]
    place_at = keys.shape[1]
    span_keys = 2 * per
    t = lax.broadcasted_iota(jnp.int32, (group * new_len, new_len), 0) % new_len
    s = lax.broadcasted_iota(jnp.int32, (group * new_len, new_len), 1)
    causal = s <= t
    for g in range(kv_local):
        heads = [
            (rope(sums((g * group + j) * head_dim)) * query_scale).astype(jnp.bfloat16)
            for j in range(group)
        ]
        queries = jnp.concatenate(heads, axis=0)
        at = q_cols + g * head_dim
        new_key = rope(sums(at)).astype(jnp.bfloat16)
        new_value = sums(at + kv_local * head_dim).astype(jnp.bfloat16)

        def scores_of(key):
            return lax.dot_general(
                queries, key, (((1,), (1,)), ((), ())), preferred_element_type=jnp.float32
            )

        weights = jnp.where(causal, capped(scores_of(new_key)), 0.0)
        denom = jnp.sum(weights, axis=1, keepdims=True)
        numer = jnp.dot(
            weights.astype(jnp.bfloat16), new_value, preferred_element_type=jnp.float32
        )
        for start in range(0, place_at, span_keys):
            at = start // per
            valid = jnp.concatenate([valid_ref[at : at + 1], valid_ref[at + 1 : at + 2]], axis=1)
            valid = valid > 0.0
            weights = jnp.where(
                valid, capped(scores_of(keys[g, start : start + span_keys, :])), 0.0
            )
            denom = denom + jnp.sum(weights, axis=1, keepdims=True)
            numer = numer + jnp.dot(
                weights.astype(jnp.bfloat16),
                values[g, start : start + span_keys, :],
                preferred_element_type=jnp.float32,
            )
        attended = (numer / denom).astype(jnp.bfloat16)
        for j in range(group):
            to = (g * group + j) * head_dim
            result[:, to : to + head_dim] = attended[j * new_len : (j + 1) * new_len]
    quarter = new_len // groups
    for distance, ref in enumerate(out_refs):
        start = pl.multiple_of((p ^ distance) * quarter, quarter)
        ref[...] = result[pl.ds(start, quarter), :]


def output_kernel(groups, shards, where_ref, *refs):
    p, f = where_ref[0], where_ref[1]
    token_refs = refs[:shards]
    weight_ref = refs[shards]
    out_refs = refs[shards + 1 : 2 * shards + 1]
    total, weight, sems = refs[2 * shards + 1 :]
    copies = [
        pltpu.make_async_copy(weight_ref.at[p ^ distance], weight.at[distance], sems.at[distance])
        for distance in range(groups)
    ]
    for copy in copies:
        copy.start()
    quarter = token_refs[0].shape[1]
    sub = quarter // shards
    projected = None
    for distance in range(groups):
        rows = jnp.concatenate([ref[distance] for ref in token_refs], axis=0)
        copies[distance].wait()
        term = lax.dot_general(
            rows,
            weight[distance],
            (((1,), (1,)), ((), ())),
            preferred_element_type=jnp.float32,
        )
        projected = term if projected is None else projected + term
    total[...] = projected
    for e in range(shards):
        for distance, ref in enumerate(out_refs):
            start = pl.multiple_of(e * quarter + (f ^ distance) * sub, sub)
            ref[f ^ e] = total[pl.ds(start, sub), :].astype(jnp.bfloat16)


def finish_kernel(shards, where_ref, gain_ref, residual_ref, *refs):
    f = where_ref[1]
    piece_refs = refs[:shards]
    out_ref, projected = refs[shards:]
    for distance, ref in enumerate(piece_refs):
        projected[f ^ distance] = ref[...].astype(jnp.float32)
    gain = gain_ref[...]
    for request in range(out_ref.shape[0]):
        slot = where_ref[3 + request]
        line = jnp.concatenate([projected[k, slot] for k in range(shards)], axis=1)
        mean_square = jnp.mean(line * line, axis=1, keepdims=True)
        line = line * lax.rsqrt(mean_square + norm_eps) * gain
        out_ref[request] = (residual_ref[slot].astype(jnp.float32) + line).astype(jnp.bfloat16)


def pool_pieces(block, groups):
    return [block] + [swap(block, "pool", distance) for distance in range(1, groups)]


def local_small(
    hidden,
    slot_of_request,
    prefix_len,
    block_holder,
    block_slot,
    kv_pool,
    norm_gain,
    q_weight,
    k_weight,
    v_weight,
    o_weight,
    post_gain,
):
    shards = lax.axis_size("fsdp")
    groups = lax.axis_size("pool")
    f = lax.axis_index("fsdp")
    p = lax.axis_index("pool")
    half = shards // 2
    side = f // half
    new_len, width = hidden.shape[1:]
    requests = slot_of_request.shape[0]
    page_len = kv_pool.shape[1]
    kv_local = kv_pool.shape[2]
    head_dim = kv_pool.shape[3] // 2
    q_cols = q_weight.shape[1]
    kv_cols = k_weight.shape[1]
    max_blocks = block_holder.shape[1]
    per_holder = max_blocks // shards
    quarter = new_len // groups
    sub = quarter // shards
    features = o_weight.shape[0]
    bf16, f32 = jnp.bfloat16, jnp.float32
    where = jnp.concatenate(
        [jnp.stack([p, f, side]).astype(jnp.int32), slot_of_request, prefix_len]
    )
    shape = jax.ShapeDtypeStruct
    gain = norm_gain.reshape(1, width)
    rows = hidden[0]

    leaving, my_quarter, joined = call(
        prologue_kernel,
        [
            shape((quarter, width // 2), bf16),
            shape((quarter, width), bf16),
            shape((features, q_cols + 2 * kv_cols), bf16),
        ],
        [pltpu.VMEM((quarter, width), f32), pltpu.SemaphoreType.DMA],
        quarter * width * 8,
        4 * features * kv_cols,
        rows,
        norm_gain,
        q_weight,
        k_weight,
        v_weight,
        specs=[HBM, VMEM, VMEM, VMEM, VMEM],
    )
    partner_piece = swap(leaving, "fsdp", half)

    flat_pool = kv_pool.reshape(kv_pool.shape[0], page_len * kv_local, 2 * head_dim)
    page_rows = per_holder * page_len * kv_local
    outgoing, valid = call(
        functools.partial(pages_kernel, requests, page_len),
        [
            shape((shards, page_rows, 2 * head_dim), bf16),
            shape((shards, per_holder * page_len), f32),
        ],
        [
            pltpu.SMEM((2 * per_holder,), jnp.int32),
            pltpu.SMEM((max_blocks + per_holder,), jnp.int32),
            pltpu.SMEM((shards,), jnp.int32),
        ],
        1 << 20,
        1 << 21,
        where,
        block_holder,
        block_slot,
        flat_pool,
        specs=[SMEM, SMEM, SMEM, VMEM],
    )
    near = swap(joined, "fsdp", 1)
    partner_piece, near, outgoing = lax.optimization_barrier((partner_piece, near, outgoing))
    far = swap(after(joined, partner_piece), "fsdp", 2)
    partner_pieces = pool_pieces(partner_piece, groups)
    arrived = lax.all_to_all(outgoing, "fsdp", split_axis=0, concat_axis=0, tiled=True)
    near_sums = call(
        functools.partial(near_kernel, groups, half),
        shape((new_len, q_cols + 2 * kv_cols), f32),
        [
            pltpu.VMEM((new_len, width // 2), bf16),
            pltpu.VMEM((2 * features, q_cols + 2 * kv_cols), bf16),
            pltpu.SemaphoreType.DMA((groups + 2,)),
        ],
        new_len * width * q_cols,
        width * (new_len + 2 * q_cols),
        where,
        *partner_pieces,
        joined,
        near,
        specs=[SMEM] + [HBM] * (groups + 2),
    )
    near_sums, far = lax.optimization_barrier((near_sums, far))
    weights = [joined, near, far, swap(far, "fsdp", 1)]
    out_weight = lax.all_gather(after(o_weight, *partner_pieces), "pool", axis=0, tiled=False)

    partial = call(
        functools.partial(partner_kernel, groups, half),
        shape((new_len, q_cols + 2 * kv_cols), bf16),
        [
            pltpu.VMEM((new_len, width // 2), bf16),
            pltpu.VMEM((2 * features, q_cols + 2 * kv_cols), bf16),
            pltpu.SemaphoreType.DMA((groups + 2,)),
        ],
        new_len * width * q_cols,
        width * (new_len + 2 * q_cols),
        where,
        near_sums,
        *partner_pieces,
        *weights[2:],
        specs=[SMEM, VMEM] + [HBM] * (groups + 2),
    )
    other = swap(partial, "fsdp", half)
    freqs = np.exp(np.arange(head_dim // 2) * (-2.0 * math.log(10000.0) / head_dim))
    freqs = np.concatenate([freqs, freqs]).astype(np.float32).reshape(1, head_dim)
    own, cosine, sine, keys, values = call(
        functools.partial(own_kernel, requests, half),
        [
            shape((new_len, q_cols + 2 * kv_cols), f32),
            shape((new_len, head_dim), f32),
            shape((new_len, head_dim), f32),
            shape((kv_local, max_blocks * page_len, head_dim), bf16),
            shape((kv_local, max_blocks * page_len, head_dim), bf16),
        ],
        [
            pltpu.VMEM((new_len, width), bf16),
            pltpu.VMEM((new_len, width // 2), bf16),
            pltpu.VMEM((width // 2, q_cols + 2 * kv_cols), bf16),
            pltpu.SemaphoreType.DMA((half + 1,)),
        ],
        new_len * width * (q_cols + 2 * kv_cols),
        width * (2 * new_len + q_cols + 2 * kv_cols),
        where,
        after(rows, partial),
        gain,
        freqs,
        arrived,
        *weights,
        specs=[SMEM, HBM, VMEM, VMEM, VMEM] + [HBM] * half,
    )

    residual = lax.all_to_all(
        after(my_quarter, own, other).reshape(shards, sub, width),
        "fsdp",
        split_axis=0,
        concat_axis=0,
        tiled=True,
    )

    keys_total = max_blocks * page_len
    quarters = call(
        functools.partial(attend_kernel, groups, kv_local, head_dim),
        [shape((quarter, q_cols), bf16)] * groups,
        [
            pltpu.VMEM((new_len, q_cols), bf16),
            pltpu.VMEM(other.shape, bf16),
            pltpu.SemaphoreType.DMA,
        ],
        4 * new_len * q_cols * (keys_total + new_len),
        1 << 22,
        where,
        own,
        other,
        cosine,
        sine,
        valid,
        keys,
        values,
        specs=[SMEM, VMEM, HBM, VMEM, VMEM, VMEM, VMEM, VMEM],
    )

    quarters = [
        swap(piece, "pool", distance) if distance else piece
        for distance, piece in enumerate(quarters)
    ]
    quarters = jnp.stack(quarters)
    tokens = {0: quarters}
    for distance in range(2, shards, 2):
        tokens[distance] = swap(quarters, "fsdp", distance)
    for distance in range(0, shards, 2):
        tokens[distance ^ 1] = swap(tokens[distance], "fsdp", 1)
    projected = call(
        functools.partial(output_kernel, groups, shards),
        [shape((shards, sub, features), bf16)] * shards,
        [
            pltpu.VMEM((shards * quarter, features), f32),
            pltpu.VMEM((groups, features, q_cols), bf16),
            pltpu.SemaphoreType.DMA((groups,)),
        ],
        2 * shards * quarter * features * groups * q_cols,
        1 << 22,
        where,
        *[tokens[distance] for distance in range(shards)],
        out_weight,
        specs=[SMEM] + [VMEM] * shards + [HBM],
        mib=24,
    )
    finished = [
        swap(piece, "fsdp", distance) if distance else piece
        for distance, piece in enumerate(projected)
    ]
    return call(
        functools.partial(finish_kernel, shards),
        shape((requests, sub, width), bf16),
        [pltpu.VMEM((shards, shards, sub, features), f32)],
        1 << 20,
        1 << 20,
        where,
        post_gain.reshape(1, width),
        residual,
        *finished,
        mib=24,
    )


def local(*arguments):
    return local_small(*arguments) if lax.axis_size("fsdp") == 8 else local_general(*arguments)


def solution(mesh):
    in_specs = (
        P("fsdp", None, None),
        P(),
        P(),
        P(),
        P(),
        P("fsdp", None, "pool", None),
        P(),
        P("fsdp", "pool"),
        P("fsdp", "pool"),
        P("fsdp", "pool"),
        P("fsdp", "pool"),
        P(),
    )
    out_specs = P(None, ("pool", "fsdp"), None)
    return jax.shard_map(local, mesh=mesh, in_specs=in_specs, out_specs=out_specs, check_vma=False)
```

```python
import functools
import math

import jax
import jax.numpy as jnp
import numpy as np
from jax import lax
from jax.experimental import pallas as pl
from jax.experimental.pallas import tpu as pltpu
from jax.sharding import PartitionSpec as P

softcap = 50.0
query_scale = 144.0 ** (-0.5)
norm_eps = 1e-06


def rms_scale(rows, gain):
    mean_square = jnp.mean(rows * rows, axis=-1, keepdims=True)
    return rows * lax.rsqrt(mean_square + norm_eps) * gain


def rotate(vectors, cosine, sine):
    half = vectors.shape[-1] // 2
    first = vectors[..., :half]
    second = vectors[..., half:]
    return jnp.concatenate(
        [first * cosine - second * sine, second * cosine + first * sine], axis=-1
    )


def capped_weights(scores, valid):
    return jnp.where(valid, jnp.exp(softcap * jnp.tanh(scores / softcap)), 0.0)


def swap(array, axis, distance):
    size = lax.axis_size(axis)
    return lax.ppermute(array, axis, [(i, i ^ distance) for i in range(size)])


def place(pieces, index):
    first = pieces[0]
    stacked = jnp.zeros((len(pieces),) + first.shape, first.dtype)
    for distance, piece in pieces.items():
        stacked = lax.dynamic_update_index_in_dim(stacked, piece, index ^ distance, 0)
    return stacked


def exchange(chunks, axis):
    size = lax.axis_size(axis)
    index = lax.axis_index(axis)
    if size > 8:
        return lax.all_to_all(chunks, axis, split_axis=0, concat_axis=0, tiled=True)
    pieces = {}
    for distance in range(size):
        chunk = lax.dynamic_index_in_dim(chunks, index ^ distance, 0, keepdims=False)
        pieces[distance] = swap(chunk, axis, distance) if distance else chunk
    return place(pieces, index)


def doubled(block, axis, span):
    pieces = {0: block}
    bit = span // 2
    while bit:
        for distance in list(pieces):
            pieces[distance ^ bit] = swap(pieces[distance], axis, bit)
        bit //= 2
    return pieces


def attend(queries, keys_new, values_new, cached, cached_valid):
    new_len, kv_local, group, head_dim = queries.shape

    def part(keys, values, valid):
        scores = jnp.einsum("tgjd,kgd->gjtk", queries, keys, preferred_element_type=jnp.float32)
        weights = capped_weights(scores, valid)
        numer = jnp.einsum(
            "gjtk,kgd->gjtd",
            weights.astype(jnp.bfloat16),
            values,
            preferred_element_type=jnp.float32,
        )
        return numer, jnp.sum(weights, axis=-1)

    query_index = jnp.arange(new_len, dtype=jnp.int32)
    causal = query_index[None, :] <= query_index[:, None]
    numer, denom = part(
        cached[..., :head_dim], cached[..., head_dim:], cached_valid[None, None, None, :]
    )
    more, added = part(keys_new, values_new, causal[None, None])
    attended = ((numer + more) / (denom + added)[..., None]).transpose(2, 0, 1, 3)
    return attended.reshape(new_len, kv_local * group * head_dim).astype(jnp.bfloat16)


def local_general(
    hidden,
    slot_of_request,
    prefix_len,
    block_holder,
    block_slot,
    kv_pool,
    norm_gain,
    q_weight,
    k_weight,
    v_weight,
    o_weight,
    post_gain,
):
    shards = lax.axis_size("fsdp")
    groups = lax.axis_size("pool")
    f = lax.axis_index("fsdp")
    p = lax.axis_index("pool")
    half = shards // 2
    side = f // half
    new_len, width = hidden.shape[1:]
    requests = slot_of_request.shape[0]
    page_len = kv_pool.shape[1]
    kv_local = kv_pool.shape[2]
    head_dim = kv_pool.shape[3] // 2
    q_cols = q_weight.shape[1]
    kv_cols = k_weight.shape[1]
    group = q_cols // kv_cols
    max_blocks = block_holder.shape[1]
    per_holder = max_blocks // shards
    quarter = new_len // groups
    sub = quarter // shards
    features = o_weight.shape[0]

    kv_pieces = doubled(jnp.concatenate([k_weight, v_weight], axis=1), "fsdp", half)
    q_pieces = doubled(q_weight, "fsdp", half)
    out_weight = lax.all_gather(o_weight, "pool", axis=0, tiled=False)

    rows = hidden[0]
    normed = rms_scale(rows.astype(jnp.float32), norm_gain).astype(jnp.bfloat16)
    own_rows = lax.dynamic_slice(normed, (0, side * (width // 2)), (new_len, width // 2))
    leaving = lax.dynamic_slice(
        normed, (p * quarter, (1 - side) * (width // 2)), (quarter, width // 2)
    )
    partner_piece = swap(leaving, "fsdp", half)
    partner_pieces = {0: partner_piece}
    for distance in range(1, groups):
        partner_pieces[distance] = swap(partner_piece, "pool", distance)
    partner_rows = place(partner_pieces, p).reshape(new_len, width // 2)

    request_ids = jnp.arange(requests, dtype=jnp.int32)
    request_at_slot = jnp.sum(
        jnp.where(slot_of_request[None, :] == request_ids[:, None], request_ids[None, :], 0), axis=1
    )
    holder_by_slot = jnp.take(block_holder, request_at_slot, axis=0)
    page_by_slot = jnp.take(block_slot, request_at_slot, axis=0)
    held_here = holder_by_slot == f
    held_rank = jnp.cumsum(held_here.astype(jnp.int32), axis=1) - 1
    rank_ids = jnp.arange(per_holder, dtype=jnp.int32)
    picked = held_here[:, :, None] & (held_rank[:, :, None] == rank_ids[None, None, :])
    local_pages = jnp.sum(jnp.where(picked, page_by_slot[:, :, None], 0), axis=1)
    flat_pool = kv_pool.reshape(kv_pool.shape[0], page_len * kv_local, 2 * head_dim)
    outgoing = jnp.take(flat_pool, local_pages, axis=0)
    outgoing = outgoing.reshape(shards, per_holder * page_len * kv_local, 2 * head_dim)
    arrived = exchange(outgoing, "fsdp")
    cached = arrived.reshape(max_blocks * page_len, kv_local, 2 * head_dim)

    my_request = lax.dynamic_index_in_dim(request_at_slot, f, keepdims=False)
    my_length = prefix_len[my_request]
    my_holders = block_holder[my_request]
    entry_ids = jnp.arange(max_blocks, dtype=jnp.int32)
    mine = my_holders[None, :] == jnp.arange(shards, dtype=jnp.int32)[:, None]
    my_rank = jnp.cumsum(mine.astype(jnp.int32), axis=1) - 1
    chosen = mine[:, None, :] & (my_rank[:, None, :] == rank_ids[None, :, None])
    entry = jnp.sum(jnp.where(chosen, entry_ids[None, None, :], 0), axis=2)
    cached_position = entry.reshape(-1, 1) * page_len + jnp.arange(page_len, dtype=jnp.int32)
    cached_valid = (cached_position < my_length).reshape(-1)

    residual_out = lax.dynamic_slice_in_dim(rows, p * quarter, quarter, 0).reshape(
        shards, sub, width
    )
    residual = exchange(residual_out, "fsdp")

    positions = (my_length + jnp.arange(new_len, dtype=jnp.int32)).astype(jnp.float32)
    freqs = jnp.exp(
        jnp.arange(head_dim // 2, dtype=jnp.float32) * (-2.0 * math.log(10000.0) / head_dim)
    )
    angles = positions[:, None] * freqs
    cosine = jnp.cos(angles)[:, None, :]
    sine = jnp.sin(angles)[:, None, :]

    def project(pieces):
        weight = place(pieces, f % half).reshape(width // 2, -1)
        partial = jnp.dot(partner_rows, weight, preferred_element_type=jnp.float32)
        other = swap(partial.astype(jnp.bfloat16), "fsdp", half)
        own = jnp.dot(own_rows, weight, preferred_element_type=jnp.float32)
        return own + other.astype(jnp.float32)

    kv_sum = project(kv_pieces)
    q_sum = project(q_pieces)
    queries = rotate(q_sum.reshape(new_len, kv_local * group, head_dim), cosine, sine)
    queries = (queries * query_scale).astype(jnp.bfloat16)
    queries = queries.reshape(new_len, kv_local, group, head_dim)
    keys_new = kv_sum[:, :kv_cols].reshape(new_len, kv_local, head_dim)
    keys_new = rotate(keys_new, cosine, sine).astype(jnp.bfloat16)
    values_new = kv_sum[:, kv_cols:].astype(jnp.bfloat16).reshape(new_len, kv_local, head_dim)
    attended = attend(queries, keys_new, values_new, cached, cached_valid)

    quarters = exchange(attended.reshape(groups, quarter, q_cols), "pool")
    token_pieces = {0: quarters}
    for distance in range(2, shards, 2):
        token_pieces[distance] = swap(quarters, "fsdp", distance)
    for distance in range(0, shards, 2):
        token_pieces[distance ^ 1] = swap(token_pieces[distance], "fsdp", 1)
    tokens = place(token_pieces, f)
    projected = jnp.einsum(
        "sptc,pfc->stf", tokens, out_weight, preferred_element_type=jnp.float32
    ).astype(jnp.bfloat16)
    projected = projected.reshape(shards, shards, sub, features).transpose(1, 0, 2, 3)
    finished = exchange(projected, "fsdp").transpose(1, 2, 0, 3).reshape(shards, sub, width)
    finished = residual.astype(jnp.float32) + rms_scale(finished.astype(jnp.float32), post_gain)
    return jnp.take(finished.astype(jnp.bfloat16), slot_of_request, axis=0)


VMEM = pl.BlockSpec(memory_space=pltpu.VMEM)
SMEM = pl.BlockSpec(memory_space=pltpu.SMEM)
HBM = pl.BlockSpec(memory_space=pltpu.HBM)


def call(kernel, outs, scratch, flops, nbytes, *operands, specs=None, out_specs=None, mib=60):
    return pl.pallas_call(
        kernel,
        out_shape=outs,
        in_specs=specs or [SMEM] + [VMEM] * (len(operands) - 1),
        out_specs=out_specs or jax.tree.map(lambda _: VMEM, outs),
        scratch_shapes=scratch,
        compiler_params=pltpu.CompilerParams(vmem_limit_bytes=mib << 20),
        cost_estimate=pl.CostEstimate(flops=flops, bytes_accessed=nbytes, transcendentals=0),
    )(*operands)


def after(array, *earlier):
    return lax.optimization_barrier((array,) + earlier)[0]


def weight_copies(weight_refs, weight, f, half, sems):
    copies = []
    for distance, ref in enumerate(weight_refs):
        count = ref.shape[0]
        start = pl.multiple_of(((f ^ distance) & (half - 1)) * count, 64)
        copies.append(
            pltpu.make_async_copy(ref, weight.at[pl.ds(start, count), :], sems.at[distance])
        )
        copies[-1].start()
    return copies


def pair_product(half, pair, where_ref, x_ref, w_refs, rows, weight, sems):
    f = where_ref[1]
    span = weight.shape[0]
    columns = pl.ds(pl.multiple_of((((f & (half - 1)) >> 1) ^ pair) * span, 128), span)
    copies = [(x_ref.at[:, columns], rows)]
    for distance, ref in enumerate(w_refs):
        count = ref.shape[0]
        start = pl.multiple_of(((f ^ distance) & 1) * count, 64)
        copies.append((ref, weight.at[pl.ds(start, count), :]))
    copies = [
        pltpu.make_async_copy(source, target, sems.at[index])
        for index, (source, target) in enumerate(copies)
    ]
    for copy in copies:
        copy.start()
    for copy in copies:
        copy.wait()
    return jnp.dot(rows[...], weight[...], preferred_element_type=jnp.float32)


def near_kernel(half, where_ref, x_ref, own_ref, core_ref, out_ref, *scratch):
    out_ref[...] = pair_product(half, 0, where_ref, x_ref, (own_ref, core_ref), *scratch)


def partner_kernel(half, where_ref, near_ref, x_ref, far_ref, core_ref, out_ref, *scratch):
    sums = pair_product(half, 1, where_ref, x_ref, (far_ref, core_ref), *scratch)
    out_ref[...] = (near_ref[...] + sums).astype(jnp.bfloat16)


def row_scale(rows):
    return lax.rsqrt(jnp.mean(rows * rows, axis=1, keepdims=True) + norm_eps)


def prologue_kernel(
    hidden_ref, gain_ref, q_ref, k_ref, v_ref, leaving_ref, rows_ref, weight_ref, normed, sem
):
    p, f = lax.axis_index("pool"), lax.axis_index("fsdp")
    side = f // (lax.axis_size("fsdp") // 2)
    quarter, width = rows_ref.shape
    half_width = width // 2
    start = pl.multiple_of(p * quarter, quarter)
    rows_copy = pltpu.make_async_copy(hidden_ref.at[pl.ds(start, quarter), :], rows_ref, sem)
    rows_copy.start()
    at = 0
    for ref in (q_ref, k_ref, v_ref):
        weight_ref[:, at : at + ref.shape[1]] = ref[...]
        at += ref.shape[1]
    rows_copy.wait()
    rows = rows_ref[...].astype(jnp.float32)
    normed[...] = rows * row_scale(rows) * gain_ref[...].reshape(1, width)
    away = pl.multiple_of((1 - side) * half_width, 128)
    leaving_ref[...] = normed[:, pl.ds(away, half_width)].astype(jnp.bfloat16)


def pages_kernel(
    requests, page_len, where_ref, holder_ref, slot_ref, pool_ref, *refs
):
    f = where_ref[1]
    out_ref, valid_ref, listed, entries, counts = refs
    max_blocks = holder_ref.shape[1]
    shards = out_ref.shape[0]
    per = max_blocks // shards
    page_rows = pool_ref.shape[1]
    length, mine = jnp.int32(0), jnp.int32(0)
    for r in range(requests):
        at = where_ref[3 + r] == f
        length = length + jnp.where(at, where_ref[3 + requests + r], 0)
        mine = mine + jnp.where(at, r, 0)
    for r in range(requests):
        slot = where_ref[3 + r]

        def note(j, count):
            listed[count] = slot_ref[r, j]
            return count + jnp.where(holder_ref[r, j] == f, 1, 0)

        lax.fori_loop(0, max_blocks, note, jnp.int32(0), unroll=8)
        for k in range(per):
            out_ref[slot, k * page_rows : (k + 1) * page_rows, :] = pool_ref[listed[k]]
    for h in range(shards):
        counts[h] = 0

    def enter(j, carry):
        h = holder_ref[mine, j]
        count = counts[h]
        entries[h * per + count] = j
        counts[h] = count + 1
        return carry

    lax.fori_loop(0, max_blocks, enter, 0, unroll=4)
    row = lax.broadcasted_iota(jnp.int32, valid_ref.shape, 0)
    lane = lax.broadcasted_iota(jnp.int32, valid_ref.shape, 1)
    place_in = row * per + lane // page_len
    entry = jnp.zeros(valid_ref.shape, jnp.int32)
    for at in range(max_blocks):
        entry = jnp.where(place_in == at, entries[at], entry)
    position = entry * page_len + lane % page_len
    valid_ref[...] = jnp.where(position < length, 1.0, 0.0)


def part_pages(pages, keys, values):
    kv_local, _, head_dim = keys.shape
    span = pages.shape[1]
    per = span // kv_local
    row = lax.broadcasted_iota(jnp.int32, (span, span), 0)
    column = lax.broadcasted_iota(jnp.int32, (span, span), 1)
    part = (column == (row % per) * kv_local + row // per).astype(jnp.bfloat16)
    for holder in range(pages.shape[0]):
        parted = jnp.dot(part, pages[holder], preferred_element_type=jnp.float32)
        parted = parted.astype(jnp.bfloat16)
        at = holder * per
        for g in range(kv_local):
            lines = parted[g * per : (g + 1) * per]
            keys[g, at : at + per, :] = lines[:, :head_dim]
            values[g, at : at + per, :] = lines[:, head_dim:]


def own_kernel(requests, half, where_ref, hidden_ref, gain_ref, freq_ref, pages, *refs):
    f = where_ref[1]
    own_ref, cos_ref, sin_ref, keys, values, hidden, normed, weight, sems = refs[half:]
    rows_copy = pltpu.make_async_copy(hidden_ref, hidden, sems.at[half])
    rows_copy.start()
    copies = weight_copies(refs[:half], weight, f, half, sems)
    rows_copy.wait()
    new_len, width = hidden_ref.shape
    half_width = width // 2
    length = jnp.int32(0)
    for r in range(requests):
        length = length + jnp.where(where_ref[3 + r] == f, where_ref[3 + requests + r], 0)
    start = pl.multiple_of(where_ref[2] * half_width, 128)
    gain = gain_ref[:, pl.ds(start, half_width)]
    step = 32

    def norm(index, carry):
        at = pl.multiple_of(index * step, step)
        rows = hidden[pl.ds(at, step), :].astype(jnp.float32)
        scale = row_scale(rows)
        part = hidden[pl.ds(at, step), pl.ds(start, half_width)].astype(jnp.float32)
        normed[pl.ds(at, step), :] = (part * scale * gain).astype(jnp.bfloat16)
        return carry

    lax.fori_loop(0, new_len // step, norm, 0)
    part_pages(pages, keys, values)
    position = lax.broadcasted_iota(jnp.int32, cos_ref.shape, 0) + length
    angle = position.astype(jnp.float32) * freq_ref[...]
    lane = lax.broadcasted_iota(jnp.int32, cos_ref.shape, 1)
    cos_ref[...] = jnp.cos(angle)
    sine = jnp.sin(angle)
    sin_ref[...] = jnp.where(lane < cos_ref.shape[1] // 2, -sine, sine)
    for copy in copies:
        copy.wait()
    for at in range(0, own_ref.shape[1], 512):
        own_ref[:, at : at + 512] = jnp.dot(
            normed[...], weight[:, at : at + 512], preferred_element_type=jnp.float32
        )


def capped(scores):
    return jnp.exp2(jnp.tanh(scores * (1.0 / softcap)) * (softcap * math.log2(math.e)))


def attend_kernel(
    groups,
    kv_local,
    head_dim,
    where_ref,
    own,
    other_ref,
    cos_ref,
    sin_ref,
    valid_ref,
    keys,
    values,
    *refs,
):
    p = where_ref[0]
    out_refs = refs[:groups]
    result, other, sem = refs[groups:]
    copy = pltpu.make_async_copy(other_ref, other, sem)
    copy.start()
    new_len, q_cols = result.shape
    group = q_cols // (kv_local * head_dim)

    def sums(at):
        return own[:, at : at + head_dim] + other[:, at : at + head_dim].astype(jnp.float32)

    cosine, sine = cos_ref[...], sin_ref[...]

    def rope(vectors):
        return vectors * cosine + pltpu.roll(vectors, head_dim // 2, 1) * sine

    copy.wait()
    per = valid_ref.shape[1]
    place_at = keys.shape[1]
    span_keys = 2 * per
    t = lax.broadcasted_iota(jnp.int32, (group * new_len, new_len), 0) % new_len
    s = lax.broadcasted_iota(jnp.int32, (group * new_len, new_len), 1)
    causal = s <= t
    for g in range(kv_local):
        heads = [
            (rope(sums((g * group + j) * head_dim)) * query_scale).astype(jnp.bfloat16)
            for j in range(group)
        ]
        queries = jnp.concatenate(heads, axis=0)
        at = q_cols + g * head_dim
        new_key = rope(sums(at)).astype(jnp.bfloat16)
        new_value = sums(at + kv_local * head_dim).astype(jnp.bfloat16)

        def scores_of(key):
            return lax.dot_general(
                queries, key, (((1,), (1,)), ((), ())), preferred_element_type=jnp.float32
            )

        weights = jnp.where(causal, capped(scores_of(new_key)), 0.0)
        denom = jnp.sum(weights, axis=1, keepdims=True)
        numer = jnp.dot(
            weights.astype(jnp.bfloat16), new_value, preferred_element_type=jnp.float32
        )
        for start in range(0, place_at, span_keys):
            at = start // per
            valid = jnp.concatenate([valid_ref[at : at + 1], valid_ref[at + 1 : at + 2]], axis=1)
            valid = valid > 0.0
            weights = jnp.where(
                valid, capped(scores_of(keys[g, start : start + span_keys, :])), 0.0
            )
            denom = denom + jnp.sum(weights, axis=1, keepdims=True)
            numer = numer + jnp.dot(
                weights.astype(jnp.bfloat16),
                values[g, start : start + span_keys, :],
                preferred_element_type=jnp.float32,
            )
        attended = (numer / denom).astype(jnp.bfloat16)
        for j in range(group):
            to = (g * group + j) * head_dim
            result[:, to : to + head_dim] = attended[j * new_len : (j + 1) * new_len]
    quarter = new_len // groups
    for distance, ref in enumerate(out_refs):
        start = pl.multiple_of((p ^ distance) * quarter, quarter)
        ref[...] = result[pl.ds(start, quarter), :]


def output_kernel(groups, shards, where_ref, *refs):
    p, f = where_ref[0], where_ref[1]
    token_refs = refs[:shards]
    weight_ref = refs[shards]
    out_refs = refs[shards + 1 : 2 * shards + 1]
    (total,) = refs[2 * shards + 1 :]
    quarter = token_refs[0].shape[1]
    sub = quarter // shards
    projected = None
    for distance in range(groups):
        rows = jnp.concatenate([ref[distance] for ref in token_refs], axis=0)
        term = lax.dot_general(
            rows,
            weight_ref[p ^ distance],
            (((1,), (1,)), ((), ())),
            preferred_element_type=jnp.float32,
        )
        projected = term if projected is None else projected + term
    total[...] = projected
    for e in range(shards):
        for distance, ref in enumerate(out_refs):
            start = pl.multiple_of(e * quarter + (f ^ distance) * sub, sub)
            ref[f ^ e] = total[pl.ds(start, sub), :].astype(jnp.bfloat16)


def finish_kernel(shards, where_ref, gain_ref, residual_ref, *refs):
    f = where_ref[1]
    piece_refs = refs[:shards]
    out_ref, projected = refs[shards:]
    for distance, ref in enumerate(piece_refs):
        projected[f ^ distance] = ref[...].astype(jnp.float32)
    gain = gain_ref[...]
    for request in range(out_ref.shape[0]):
        slot = where_ref[3 + request]
        line = jnp.concatenate([projected[k, slot] for k in range(shards)], axis=1)
        mean_square = jnp.mean(line * line, axis=1, keepdims=True)
        line = line * lax.rsqrt(mean_square + norm_eps) * gain
        out_ref[request] = (residual_ref[slot].astype(jnp.float32) + line).astype(jnp.bfloat16)


def local_small(
    hidden,
    slot_of_request,
    prefix_len,
    block_holder,
    block_slot,
    kv_pool,
    norm_gain,
    q_weight,
    k_weight,
    v_weight,
    o_weight,
    post_gain,
):
    shards = lax.axis_size("fsdp")
    groups = lax.axis_size("pool")
    f = lax.axis_index("fsdp")
    p = lax.axis_index("pool")
    half = shards // 2
    side = f // half
    new_len, width = hidden.shape[1:]
    requests = slot_of_request.shape[0]
    page_len = kv_pool.shape[1]
    kv_local = kv_pool.shape[2]
    head_dim = kv_pool.shape[3] // 2
    q_cols = q_weight.shape[1]
    kv_cols = k_weight.shape[1]
    max_blocks = block_holder.shape[1]
    per_holder = max_blocks // shards
    quarter = new_len // groups
    sub = quarter // shards
    features = o_weight.shape[0]
    bf16, f32 = jnp.bfloat16, jnp.float32
    where = jnp.concatenate(
        [jnp.stack([p, f, side]).astype(jnp.int32), slot_of_request, prefix_len]
    )
    shape = jax.ShapeDtypeStruct
    gain = norm_gain.reshape(1, width)
    rows = hidden[0]

    leaving, my_quarter, joined = call(
        prologue_kernel,
        [
            shape((quarter, width // 2), bf16),
            shape((quarter, width), bf16),
            shape((features, q_cols + 2 * kv_cols), bf16),
        ],
        [pltpu.VMEM((quarter, width), f32), pltpu.SemaphoreType.DMA],
        quarter * width * 8,
        4 * features * kv_cols,
        rows,
        norm_gain,
        q_weight,
        k_weight,
        v_weight,
        specs=[HBM, VMEM, VMEM, VMEM, VMEM],
    )
    partner_piece = swap(leaving, "fsdp", half)

    flat_pool = kv_pool.reshape(kv_pool.shape[0], page_len * kv_local, 2 * head_dim)
    page_rows = per_holder * page_len * kv_local
    outgoing, valid = call(
        functools.partial(pages_kernel, requests, page_len),
        [
            shape((shards, page_rows, 2 * head_dim), bf16),
            shape((shards, per_holder * page_len), f32),
        ],
        [
            pltpu.SMEM((2 * per_holder,), jnp.int32),
            pltpu.SMEM((max_blocks + per_holder,), jnp.int32),
            pltpu.SMEM((shards,), jnp.int32),
        ],
        1 << 20,
        1 << 21,
        where,
        block_holder,
        block_slot,
        flat_pool,
        specs=[SMEM, SMEM, SMEM, VMEM],
    )
    near = swap(joined, "fsdp", 1)
    partner_piece, near, outgoing = lax.optimization_barrier((partner_piece, near, outgoing))
    far = swap(after(joined, partner_piece), "fsdp", 2)
    partner_rows = lax.all_gather(partner_piece, "pool", axis=0, tiled=True)
    arrived = lax.all_to_all(outgoing, "fsdp", split_axis=0, concat_axis=0, tiled=True)
    near_sums = call(
        functools.partial(near_kernel, half),
        shape((new_len, q_cols + 2 * kv_cols), f32),
        [
            pltpu.VMEM((new_len, 2 * features), bf16),
            pltpu.VMEM((2 * features, q_cols + 2 * kv_cols), bf16),
            pltpu.SemaphoreType.DMA((3,)),
        ],
        new_len * width * q_cols,
        width * (new_len + 2 * q_cols),
        where,
        partner_rows,
        joined,
        near,
        specs=[SMEM] + [HBM] * 3,
    )
    near_sums, far = lax.optimization_barrier((near_sums, far))
    weights = [joined, near, far, swap(far, "fsdp", 1)]
    out_weight = lax.all_gather(after(o_weight, partner_rows), "pool", axis=0, tiled=False)

    partial = call(
        functools.partial(partner_kernel, half),
        shape((new_len, q_cols + 2 * kv_cols), bf16),
        [
            pltpu.VMEM((new_len, 2 * features), bf16),
            pltpu.VMEM((2 * features, q_cols + 2 * kv_cols), bf16),
            pltpu.SemaphoreType.DMA((3,)),
        ],
        new_len * width * q_cols,
        width * (new_len + 2 * q_cols),
        where,
        near_sums,
        partner_rows,
        *weights[2:],
        specs=[SMEM, VMEM] + [HBM] * 3,
    )
    other = swap(partial, "fsdp", half)
    freqs = np.exp(np.arange(head_dim // 2) * (-2.0 * math.log(10000.0) / head_dim))
    freqs = np.concatenate([freqs, freqs]).astype(np.float32).reshape(1, head_dim)
    own, cosine, sine, keys, values = call(
        functools.partial(own_kernel, requests, half),
        [
            shape((new_len, q_cols + 2 * kv_cols), f32),
            shape((new_len, head_dim), f32),
            shape((new_len, head_dim), f32),
            shape((kv_local, max_blocks * page_len, head_dim), bf16),
            shape((kv_local, max_blocks * page_len, head_dim), bf16),
        ],
        [
            pltpu.VMEM((new_len, width), bf16),
            pltpu.VMEM((new_len, width // 2), bf16),
            pltpu.VMEM((width // 2, q_cols + 2 * kv_cols), bf16),
            pltpu.SemaphoreType.DMA((half + 1,)),
        ],
        new_len * width * (q_cols + 2 * kv_cols),
        width * (2 * new_len + q_cols + 2 * kv_cols),
        where,
        after(rows, partial),
        gain,
        freqs,
        arrived,
        *weights,
        specs=[SMEM, HBM, VMEM, VMEM, VMEM] + [HBM] * half,
    )

    residual = lax.all_to_all(
        after(my_quarter, own, other).reshape(shards, sub, width),
        "fsdp",
        split_axis=0,
        concat_axis=0,
        tiled=True,
    )

    keys_total = max_blocks * page_len
    quarters = call(
        functools.partial(attend_kernel, groups, kv_local, head_dim),
        [shape((quarter, q_cols), bf16)] * groups,
        [
            pltpu.VMEM((new_len, q_cols), bf16),
            pltpu.VMEM(other.shape, bf16),
            pltpu.SemaphoreType.DMA,
        ],
        4 * new_len * q_cols * (keys_total + new_len),
        1 << 22,
        where,
        own,
        other,
        cosine,
        sine,
        valid,
        keys,
        values,
        specs=[SMEM, VMEM, HBM, VMEM, VMEM, VMEM, VMEM, VMEM],
    )

    quarters = [
        swap(piece, "pool", distance) if distance else piece
        for distance, piece in enumerate(quarters)
    ]
    quarters = jnp.stack(quarters)
    tokens = {0: quarters}
    for distance in range(2, shards, 2):
        tokens[distance] = swap(quarters, "fsdp", distance)
    for distance in range(0, shards, 2):
        tokens[distance ^ 1] = swap(tokens[distance], "fsdp", 1)
    projected = call(
        functools.partial(output_kernel, groups, shards),
        [shape((shards, sub, features), bf16)] * shards,
        [
            pltpu.VMEM((shards * quarter, features), f32),
        ],
        2 * shards * quarter * features * groups * q_cols,
        1 << 22,
        where,
        *[tokens[distance] for distance in range(shards)],
        out_weight,
        mib=24,
    )
    finished = [
        swap(piece, "fsdp", distance) if distance else piece
        for distance, piece in enumerate(projected)
    ]
    return call(
        functools.partial(finish_kernel, shards),
        shape((requests, sub, width), bf16),
        [pltpu.VMEM((shards, shards, sub, features), f32)],
        1 << 20,
        1 << 20,
        where,
        post_gain.reshape(1, width),
        residual,
        *finished,
        mib=24,
    )


def local(*arguments):
    return local_small(*arguments) if lax.axis_size("fsdp") == 8 else local_general(*arguments)


def solution(mesh):
    in_specs = (
        P("fsdp", None, None),
        P(),
        P(),
        P(),
        P(),
        P("fsdp", None, "pool", None),
        P(),
        P("fsdp", "pool"),
        P("fsdp", "pool"),
        P("fsdp", "pool"),
        P("fsdp", "pool"),
        P(),
    )
    out_specs = P(None, ("pool", "fsdp"), None)
    return jax.shard_map(local, mesh=mesh, in_specs=in_specs, out_specs=out_specs, check_vma=False)
```

```python
import functools
import math

import jax
import jax.numpy as jnp
import numpy as np
from jax import lax
from jax.experimental import pallas as pl
from jax.experimental.pallas import tpu as pltpu
from jax.sharding import PartitionSpec as P

softcap = 50.0
query_scale = 144.0 ** (-0.5)
norm_eps = 1e-06


def rms_scale(rows, gain):
    mean_square = jnp.mean(rows * rows, axis=-1, keepdims=True)
    return rows * lax.rsqrt(mean_square + norm_eps) * gain


def rotate(vectors, cosine, sine):
    half = vectors.shape[-1] // 2
    first = vectors[..., :half]
    second = vectors[..., half:]
    return jnp.concatenate(
        [first * cosine - second * sine, second * cosine + first * sine], axis=-1
    )


def capped_weights(scores, valid):
    return jnp.where(valid, jnp.exp(softcap * jnp.tanh(scores / softcap)), 0.0)


def swap(array, axis, distance):
    size = lax.axis_size(axis)
    return lax.ppermute(array, axis, [(i, i ^ distance) for i in range(size)])


def place(pieces, index):
    first = pieces[0]
    stacked = jnp.zeros((len(pieces),) + first.shape, first.dtype)
    for distance, piece in pieces.items():
        stacked = lax.dynamic_update_index_in_dim(stacked, piece, index ^ distance, 0)
    return stacked


def exchange(chunks, axis):
    size = lax.axis_size(axis)
    index = lax.axis_index(axis)
    if size > 8:
        return lax.all_to_all(chunks, axis, split_axis=0, concat_axis=0, tiled=True)
    pieces = {}
    for distance in range(size):
        chunk = lax.dynamic_index_in_dim(chunks, index ^ distance, 0, keepdims=False)
        pieces[distance] = swap(chunk, axis, distance) if distance else chunk
    return place(pieces, index)


def doubled(block, axis, span):
    pieces = {0: block}
    bit = span // 2
    while bit:
        for distance in list(pieces):
            pieces[distance ^ bit] = swap(pieces[distance], axis, bit)
        bit //= 2
    return pieces


def attend(queries, keys_new, values_new, cached, cached_valid):
    new_len, kv_local, group, head_dim = queries.shape

    def part(keys, values, valid):
        scores = jnp.einsum("tgjd,kgd->gjtk", queries, keys, preferred_element_type=jnp.float32)
        weights = capped_weights(scores, valid)
        numer = jnp.einsum(
            "gjtk,kgd->gjtd",
            weights.astype(jnp.bfloat16),
            values,
            preferred_element_type=jnp.float32,
        )
        return numer, jnp.sum(weights, axis=-1)

    query_index = jnp.arange(new_len, dtype=jnp.int32)
    causal = query_index[None, :] <= query_index[:, None]
    numer, denom = part(
        cached[..., :head_dim], cached[..., head_dim:], cached_valid[None, None, None, :]
    )
    more, added = part(keys_new, values_new, causal[None, None])
    attended = ((numer + more) / (denom + added)[..., None]).transpose(2, 0, 1, 3)
    return attended.reshape(new_len, kv_local * group * head_dim).astype(jnp.bfloat16)


def local_general(
    hidden,
    slot_of_request,
    prefix_len,
    block_holder,
    block_slot,
    kv_pool,
    norm_gain,
    q_weight,
    k_weight,
    v_weight,
    o_weight,
    post_gain,
):
    shards = lax.axis_size("fsdp")
    groups = lax.axis_size("pool")
    f = lax.axis_index("fsdp")
    p = lax.axis_index("pool")
    half = shards // 2
    side = f // half
    new_len, width = hidden.shape[1:]
    requests = slot_of_request.shape[0]
    page_len = kv_pool.shape[1]
    kv_local = kv_pool.shape[2]
    head_dim = kv_pool.shape[3] // 2
    q_cols = q_weight.shape[1]
    kv_cols = k_weight.shape[1]
    group = q_cols // kv_cols
    max_blocks = block_holder.shape[1]
    per_holder = max_blocks // shards
    quarter = new_len // groups
    sub = quarter // shards
    features = o_weight.shape[0]

    kv_pieces = doubled(jnp.concatenate([k_weight, v_weight], axis=1), "fsdp", half)
    q_pieces = doubled(q_weight, "fsdp", half)
    out_weight = lax.all_gather(o_weight, "pool", axis=0, tiled=False)

    rows = hidden[0]
    normed = rms_scale(rows.astype(jnp.float32), norm_gain).astype(jnp.bfloat16)
    own_rows = lax.dynamic_slice(normed, (0, side * (width // 2)), (new_len, width // 2))
    leaving = lax.dynamic_slice(
        normed, (p * quarter, (1 - side) * (width // 2)), (quarter, width // 2)
    )
    partner_piece = swap(leaving, "fsdp", half)
    partner_pieces = {0: partner_piece}
    for distance in range(1, groups):
        partner_pieces[distance] = swap(partner_piece, "pool", distance)
    partner_rows = place(partner_pieces, p).reshape(new_len, width // 2)

    request_ids = jnp.arange(requests, dtype=jnp.int32)
    request_at_slot = jnp.sum(
        jnp.where(slot_of_request[None, :] == request_ids[:, None], request_ids[None, :], 0), axis=1
    )
    holder_by_slot = jnp.take(block_holder, request_at_slot, axis=0)
    page_by_slot = jnp.take(block_slot, request_at_slot, axis=0)
    held_here = holder_by_slot == f
    held_rank = jnp.cumsum(held_here.astype(jnp.int32), axis=1) - 1
    rank_ids = jnp.arange(per_holder, dtype=jnp.int32)
    picked = held_here[:, :, None] & (held_rank[:, :, None] == rank_ids[None, None, :])
    local_pages = jnp.sum(jnp.where(picked, page_by_slot[:, :, None], 0), axis=1)
    flat_pool = kv_pool.reshape(kv_pool.shape[0], page_len * kv_local, 2 * head_dim)
    outgoing = jnp.take(flat_pool, local_pages, axis=0)
    outgoing = outgoing.reshape(shards, per_holder * page_len * kv_local, 2 * head_dim)
    arrived = exchange(outgoing, "fsdp")
    cached = arrived.reshape(max_blocks * page_len, kv_local, 2 * head_dim)

    my_request = lax.dynamic_index_in_dim(request_at_slot, f, keepdims=False)
    my_length = prefix_len[my_request]
    my_holders = block_holder[my_request]
    entry_ids = jnp.arange(max_blocks, dtype=jnp.int32)
    mine = my_holders[None, :] == jnp.arange(shards, dtype=jnp.int32)[:, None]
    my_rank = jnp.cumsum(mine.astype(jnp.int32), axis=1) - 1
    chosen = mine[:, None, :] & (my_rank[:, None, :] == rank_ids[None, :, None])
    entry = jnp.sum(jnp.where(chosen, entry_ids[None, None, :], 0), axis=2)
    cached_position = entry.reshape(-1, 1) * page_len + jnp.arange(page_len, dtype=jnp.int32)
    cached_valid = (cached_position < my_length).reshape(-1)

    residual_out = lax.dynamic_slice_in_dim(rows, p * quarter, quarter, 0).reshape(
        shards, sub, width
    )
    residual = exchange(residual_out, "fsdp")

    positions = (my_length + jnp.arange(new_len, dtype=jnp.int32)).astype(jnp.float32)
    freqs = jnp.exp(
        jnp.arange(head_dim // 2, dtype=jnp.float32) * (-2.0 * math.log(10000.0) / head_dim)
    )
    angles = positions[:, None] * freqs
    cosine = jnp.cos(angles)[:, None, :]
    sine = jnp.sin(angles)[:, None, :]

    def project(pieces):
        weight = place(pieces, f % half).reshape(width // 2, -1)
        partial = jnp.dot(partner_rows, weight, preferred_element_type=jnp.float32)
        other = swap(partial.astype(jnp.bfloat16), "fsdp", half)
        own = jnp.dot(own_rows, weight, preferred_element_type=jnp.float32)
        return own + other.astype(jnp.float32)

    kv_sum = project(kv_pieces)
    q_sum = project(q_pieces)
    queries = rotate(q_sum.reshape(new_len, kv_local * group, head_dim), cosine, sine)
    queries = (queries * query_scale).astype(jnp.bfloat16)
    queries = queries.reshape(new_len, kv_local, group, head_dim)
    keys_new = kv_sum[:, :kv_cols].reshape(new_len, kv_local, head_dim)
    keys_new = rotate(keys_new, cosine, sine).astype(jnp.bfloat16)
    values_new = kv_sum[:, kv_cols:].astype(jnp.bfloat16).reshape(new_len, kv_local, head_dim)
    attended = attend(queries, keys_new, values_new, cached, cached_valid)

    quarters = exchange(attended.reshape(groups, quarter, q_cols), "pool")
    token_pieces = {0: quarters}
    for distance in range(2, shards, 2):
        token_pieces[distance] = swap(quarters, "fsdp", distance)
    for distance in range(0, shards, 2):
        token_pieces[distance ^ 1] = swap(token_pieces[distance], "fsdp", 1)
    tokens = place(token_pieces, f)
    projected = jnp.einsum(
        "sptc,pfc->stf", tokens, out_weight, preferred_element_type=jnp.float32
    ).astype(jnp.bfloat16)
    projected = projected.reshape(shards, shards, sub, features).transpose(1, 0, 2, 3)
    finished = exchange(projected, "fsdp").transpose(1, 2, 0, 3).reshape(shards, sub, width)
    finished = residual.astype(jnp.float32) + rms_scale(finished.astype(jnp.float32), post_gain)
    return jnp.take(finished.astype(jnp.bfloat16), slot_of_request, axis=0)


VMEM = pl.BlockSpec(memory_space=pltpu.VMEM)
SMEM = pl.BlockSpec(memory_space=pltpu.SMEM)
HBM = pl.BlockSpec(memory_space=pltpu.HBM)


def call(kernel, outs, scratch, flops, nbytes, *operands, specs=None, out_specs=None, mib=60):
    return pl.pallas_call(
        kernel,
        out_shape=outs,
        in_specs=specs or [SMEM] + [VMEM] * (len(operands) - 1),
        out_specs=out_specs or jax.tree.map(lambda _: VMEM, outs),
        scratch_shapes=scratch,
        compiler_params=pltpu.CompilerParams(vmem_limit_bytes=mib << 20),
        cost_estimate=pl.CostEstimate(flops=flops, bytes_accessed=nbytes, transcendentals=0),
    )(*operands)


def after(array, *earlier):
    return lax.optimization_barrier((array,) + earlier)[0]


def weight_copies(weight_refs, weight, f, half, sems):
    copies = []
    for distance, ref in enumerate(weight_refs):
        count = ref.shape[0]
        start = pl.multiple_of(((f ^ distance) & (half - 1)) * count, 64)
        copies.append(
            pltpu.make_async_copy(ref, weight.at[pl.ds(start, count), :], sems.at[distance])
        )
        copies[-1].start()
    return copies


def partner_kernel(groups, half, where_ref, *refs):
    p, f = where_ref[0], where_ref[1]
    x_refs, w_refs = refs[:groups], refs[groups : groups + half]
    out_ref, rows, weight, x_sems, w_sems = refs[groups + half :]
    quarter = x_refs[0].shape[0]
    copies = weight_copies(w_refs, weight, f, half, w_sems)
    for distance, ref in enumerate(x_refs):
        start = pl.multiple_of((p ^ distance) * quarter, quarter)
        copies.append(
            pltpu.make_async_copy(ref, rows.at[pl.ds(start, quarter), :], x_sems.at[distance])
        )
        copies[-1].start()
    for copy in copies:
        copy.wait()
    for at in range(0, out_ref.shape[1], 512):
        out_ref[:, at : at + 512] = jnp.dot(
            rows[...], weight[:, at : at + 512], preferred_element_type=jnp.float32
        ).astype(jnp.bfloat16)


def row_scale(rows):
    return lax.rsqrt(jnp.mean(rows * rows, axis=1, keepdims=True) + norm_eps)


def prologue_kernel(
    hidden_ref, gain_ref, q_ref, k_ref, v_ref, leaving_ref, rows_ref, weight_ref, normed, sem
):
    p, f = lax.axis_index("pool"), lax.axis_index("fsdp")
    side = f // (lax.axis_size("fsdp") // 2)
    quarter, width = rows_ref.shape
    half_width = width // 2
    start = pl.multiple_of(p * quarter, quarter)
    rows_copy = pltpu.make_async_copy(hidden_ref.at[pl.ds(start, quarter), :], rows_ref, sem)
    rows_copy.start()
    at = 0
    for ref in (q_ref, k_ref, v_ref):
        weight_ref[:, at : at + ref.shape[1]] = ref[...]
        at += ref.shape[1]
    rows_copy.wait()
    rows = rows_ref[...].astype(jnp.float32)
    normed[...] = rows * row_scale(rows) * gain_ref[...].reshape(1, width)
    away = pl.multiple_of((1 - side) * half_width, 128)
    leaving_ref[...] = normed[:, pl.ds(away, half_width)].astype(jnp.bfloat16)


def pages_kernel(
    requests, page_len, where_ref, holder_ref, slot_ref, pool_ref, *refs
):
    f = where_ref[1]
    *out_refs, valid_ref, listed, entries, counts = refs
    max_blocks = holder_ref.shape[1]
    shards = out_refs[0].shape[0]
    per = max_blocks // shards
    each = per // len(out_refs)
    page_rows = pool_ref.shape[1]
    length, mine = jnp.int32(0), jnp.int32(0)
    for r in range(requests):
        at = where_ref[3 + r] == f
        length = length + jnp.where(at, where_ref[3 + requests + r], 0)
        mine = mine + jnp.where(at, r, 0)
    for r in range(requests):
        slot = where_ref[3 + r]

        def note(j, count):
            listed[count] = slot_ref[r, j]
            return count + jnp.where(holder_ref[r, j] == f, 1, 0)

        lax.fori_loop(0, max_blocks, note, jnp.int32(0), unroll=8)
        for k in range(per):
            at = k % each * page_rows
            out_refs[k // each][slot, at : at + page_rows, :] = pool_ref[listed[k]]
    for h in range(shards):
        counts[h] = 0

    def enter(j, carry):
        h = holder_ref[mine, j]
        count = counts[h]
        entries[h * per + count] = j
        counts[h] = count + 1
        return carry

    lax.fori_loop(0, max_blocks, enter, 0, unroll=4)
    row = lax.broadcasted_iota(jnp.int32, valid_ref.shape, 0)
    lane = lax.broadcasted_iota(jnp.int32, valid_ref.shape, 1)
    place_in = row * per + lane // page_len
    entry = jnp.zeros(valid_ref.shape, jnp.int32)
    for at in range(max_blocks):
        entry = jnp.where(place_in == at, entries[at], entry)
    position = entry * page_len + lane % page_len
    valid_ref[...] = jnp.where(position < length, 1.0, 0.0)


def own_kernel(requests, half, where_ref, hidden_ref, gain_ref, freq_ref, *refs):
    f = where_ref[1]
    own_ref, cos_ref, sin_ref, hidden, normed, weight, sems = refs[half:]
    rows_copy = pltpu.make_async_copy(hidden_ref, hidden, sems.at[half])
    rows_copy.start()
    copies = weight_copies(refs[:half], weight, f, half, sems)
    rows_copy.wait()
    new_len, width = hidden_ref.shape
    half_width = width // 2
    length = jnp.int32(0)
    for r in range(requests):
        length = length + jnp.where(where_ref[3 + r] == f, where_ref[3 + requests + r], 0)
    start = pl.multiple_of(where_ref[2] * half_width, 128)
    gain = gain_ref[:, pl.ds(start, half_width)]
    step = 32

    def norm(index, carry):
        at = pl.multiple_of(index * step, step)
        rows = hidden[pl.ds(at, step), :].astype(jnp.float32)
        scale = row_scale(rows)
        part = hidden[pl.ds(at, step), pl.ds(start, half_width)].astype(jnp.float32)
        normed[pl.ds(at, step), :] = (part * scale * gain).astype(jnp.bfloat16)
        return carry

    lax.fori_loop(0, new_len // step, norm, 0)
    position = lax.broadcasted_iota(jnp.int32, cos_ref.shape, 0) + length
    angle = position.astype(jnp.float32) * freq_ref[...]
    lane = lax.broadcasted_iota(jnp.int32, cos_ref.shape, 1)
    cos_ref[...] = jnp.cos(angle)
    sine = jnp.sin(angle)
    sin_ref[...] = jnp.where(lane < cos_ref.shape[1] // 2, -sine, sine)
    for copy in copies:
        copy.wait()
    for at in range(0, own_ref.shape[1], 512):
        own_ref[:, at : at + 512] = jnp.dot(
            normed[...], weight[:, at : at + 512], preferred_element_type=jnp.float32
        )


def capped(scores):
    return jnp.exp2(jnp.tanh(scores * (1.0 / softcap)) * (softcap * math.log2(math.e)))


def attend_kernel(
    groups,
    kv_local,
    head_dim,
    where_ref,
    own,
    other_ref,
    cos_ref,
    sin_ref,
    valid_ref,
    *refs,
):
    p = where_ref[0]
    page_refs, out_refs = refs[:2], refs[2 : 2 + groups]
    keys, values, result, other, pages, sems = refs[2 + groups :]
    copies = [pltpu.make_async_copy(other_ref, other, sems.at[0])]
    for index, ref in enumerate(page_refs):
        lines = pl.ds(index * ref.shape[1], ref.shape[1])
        copies.append(
            pltpu.make_async_copy(ref, pages.at[:, lines, :], sems.at[1 + index])
        )
    for copy in copies:
        copy.start()
    new_len, q_cols = result.shape
    group = q_cols // (kv_local * head_dim)

    def sums(at):
        return own[:, at : at + head_dim] + other[:, at : at + head_dim].astype(jnp.float32)

    cosine, sine = cos_ref[...], sin_ref[...]

    def rope(vectors):
        return vectors * cosine + pltpu.roll(vectors, head_dim // 2, 1) * sine

    span = pages.shape[1]
    per = span // kv_local
    row = lax.broadcasted_iota(jnp.int32, (span, span), 0)
    column = lax.broadcasted_iota(jnp.int32, (span, span), 1)
    part = (column == (row % per) * kv_local + row // per).astype(jnp.bfloat16)
    place_at = 0
    for copy in copies[1:]:
        copy.wait()
    for holder in range(pages.shape[0]):
        parted = jnp.dot(part, pages[holder], preferred_element_type=jnp.float32)
        parted = parted.astype(jnp.bfloat16)
        for g in range(kv_local):
            lines = parted[g * per : (g + 1) * per]
            keys[g, place_at : place_at + per, :] = lines[:, :head_dim]
            values[g, place_at : place_at + per, :] = lines[:, head_dim:]
        place_at += per

    copies[0].wait()
    span_keys = 2 * per
    t = lax.broadcasted_iota(jnp.int32, (group * new_len, new_len), 0) % new_len
    s = lax.broadcasted_iota(jnp.int32, (group * new_len, new_len), 1)
    causal = s <= t
    for g in range(kv_local):
        heads = [
            (rope(sums((g * group + j) * head_dim)) * query_scale).astype(jnp.bfloat16)
            for j in range(group)
        ]
        queries = jnp.concatenate(heads, axis=0)
        at = q_cols + g * head_dim
        new_key = rope(sums(at)).astype(jnp.bfloat16)
        new_value = sums(at + kv_local * head_dim).astype(jnp.bfloat16)

        def scores_of(key):
            return lax.dot_general(
                queries, key, (((1,), (1,)), ((), ())), preferred_element_type=jnp.float32
            )

        weights = jnp.where(causal, capped(scores_of(new_key)), 0.0)
        denom = jnp.sum(weights, axis=1, keepdims=True)
        numer = jnp.dot(
            weights.astype(jnp.bfloat16), new_value, preferred_element_type=jnp.float32
        )
        for start in range(0, place_at, span_keys):
            at = start // per
            valid = jnp.concatenate([valid_ref[at : at + 1], valid_ref[at + 1 : at + 2]], axis=1)
            valid = valid > 0.0
            weights = jnp.where(
                valid, capped(scores_of(keys[g, start : start + span_keys, :])), 0.0
            )
            denom = denom + jnp.sum(weights, axis=1, keepdims=True)
            numer = numer + jnp.dot(
                weights.astype(jnp.bfloat16),
                values[g, start : start + span_keys, :],
                preferred_element_type=jnp.float32,
            )
        attended = (numer / denom).astype(jnp.bfloat16)
        for j in range(group):
            to = (g * group + j) * head_dim
            result[:, to : to + head_dim] = attended[j * new_len : (j + 1) * new_len]
    quarter = new_len // groups
    for distance, ref in enumerate(out_refs):
        start = pl.multiple_of((p ^ distance) * quarter, quarter)
        ref[...] = result[pl.ds(start, quarter), :]


def output_kernel(groups, shards, where_ref, *refs):
    p, f = where_ref[0], where_ref[1]
    token_refs = refs[:shards]
    weight_ref = refs[shards]
    out_refs = refs[shards + 1 : 2 * shards + 1]
    (total,) = refs[2 * shards + 1 :]
    quarter = token_refs[0].shape[1]
    sub = quarter // shards
    projected = None
    for distance in range(groups):
        rows = jnp.concatenate([ref[distance] for ref in token_refs], axis=0)
        term = lax.dot_general(
            rows,
            weight_ref[p ^ distance],
            (((1,), (1,)), ((), ())),
            preferred_element_type=jnp.float32,
        )
        projected = term if projected is None else projected + term
    total[...] = projected
    for e in range(shards):
        for distance, ref in enumerate(out_refs):
            start = pl.multiple_of(e * quarter + (f ^ distance) * sub, sub)
            ref[f ^ e] = total[pl.ds(start, sub), :].astype(jnp.bfloat16)


def finish_kernel(shards, where_ref, gain_ref, residual_ref, *refs):
    f = where_ref[1]
    piece_refs = refs[:shards]
    out_ref, projected = refs[shards:]
    for distance, ref in enumerate(piece_refs):
        projected[f ^ distance] = ref[...].astype(jnp.float32)
    gain = gain_ref[...]
    for request in range(out_ref.shape[0]):
        slot = where_ref[3 + request]
        line = jnp.concatenate([projected[k, slot] for k in range(shards)], axis=1)
        mean_square = jnp.mean(line * line, axis=1, keepdims=True)
        line = line * lax.rsqrt(mean_square + norm_eps) * gain
        out_ref[request] = (residual_ref[slot].astype(jnp.float32) + line).astype(jnp.bfloat16)


def pool_pieces(block, groups):
    return [block] + [swap(block, "pool", distance) for distance in range(1, groups)]


def local_small(
    hidden,
    slot_of_request,
    prefix_len,
    block_holder,
    block_slot,
    kv_pool,
    norm_gain,
    q_weight,
    k_weight,
    v_weight,
    o_weight,
    post_gain,
):
    shards = lax.axis_size("fsdp")
    groups = lax.axis_size("pool")
    f = lax.axis_index("fsdp")
    p = lax.axis_index("pool")
    half = shards // 2
    side = f // half
    new_len, width = hidden.shape[1:]
    requests = slot_of_request.shape[0]
    page_len = kv_pool.shape[1]
    kv_local = kv_pool.shape[2]
    head_dim = kv_pool.shape[3] // 2
    q_cols = q_weight.shape[1]
    kv_cols = k_weight.shape[1]
    max_blocks = block_holder.shape[1]
    per_holder = max_blocks // shards
    quarter = new_len // groups
    sub = quarter // shards
    features = o_weight.shape[0]
    bf16, f32 = jnp.bfloat16, jnp.float32
    where = jnp.concatenate(
        [jnp.stack([p, f, side]).astype(jnp.int32), slot_of_request, prefix_len]
    )
    shape = jax.ShapeDtypeStruct
    gain = norm_gain.reshape(1, width)
    rows = hidden[0]

    leaving, my_quarter, joined = call(
        prologue_kernel,
        [
            shape((quarter, width // 2), bf16),
            shape((quarter, width), bf16),
            shape((features, q_cols + 2 * kv_cols), bf16),
        ],
        [pltpu.VMEM((quarter, width), f32), pltpu.SemaphoreType.DMA],
        quarter * width * 8,
        4 * features * kv_cols,
        rows,
        norm_gain,
        q_weight,
        k_weight,
        v_weight,
        specs=[HBM, VMEM, VMEM, VMEM, VMEM],
    )
    partner_piece = swap(leaving, "fsdp", half)

    flat_pool = kv_pool.reshape(kv_pool.shape[0], page_len * kv_local, 2 * head_dim)
    page_rows = per_holder * page_len * kv_local
    first_pages, second_pages, valid = call(
        functools.partial(pages_kernel, requests, page_len),
        [
            shape((shards, page_rows // 2, 2 * head_dim), bf16),
            shape((shards, page_rows // 2, 2 * head_dim), bf16),
            shape((shards, per_holder * page_len), f32),
        ],
        [
            pltpu.SMEM((2 * per_holder,), jnp.int32),
            pltpu.SMEM((max_blocks + per_holder,), jnp.int32),
            pltpu.SMEM((shards,), jnp.int32),
        ],
        1 << 20,
        1 << 21,
        where,
        block_holder,
        block_slot,
        flat_pool,
        specs=[SMEM, SMEM, SMEM, VMEM],
    )
    near = swap(joined, "fsdp", 1)
    partner_piece, near, first_pages, second_pages, valid = lax.optimization_barrier(
        (partner_piece, near, first_pages, second_pages, valid)
    )
    far = swap(after(joined, partner_piece), "fsdp", 2)
    partner_pieces = pool_pieces(partner_piece, groups)
    arrived = lax.all_to_all(first_pages, "fsdp", split_axis=0, concat_axis=0, tiled=True)
    partner_pieces, far, arrived = lax.optimization_barrier((partner_pieces, far, arrived))
    arrived = [arrived]
    weights = [joined, near, far, swap(far, "fsdp", 1)]
    arrived.append(
        lax.all_to_all(
            after(second_pages, far), "fsdp", split_axis=0, concat_axis=0, tiled=True
        )
    )
    out_weight = lax.all_gather(after(o_weight, *partner_pieces), "pool", axis=0, tiled=False)

    partial = call(
        functools.partial(partner_kernel, groups, half),
        shape((new_len, q_cols + 2 * kv_cols), bf16),
        [
            pltpu.VMEM((new_len, width // 2), bf16),
            pltpu.VMEM((width // 2, q_cols + 2 * kv_cols), bf16),
            pltpu.SemaphoreType.DMA((groups,)),
            pltpu.SemaphoreType.DMA((half,)),
        ],
        new_len * width * (q_cols + 2 * kv_cols),
        width * (new_len + q_cols + 2 * kv_cols),
        where,
        *partner_pieces,
        *weights,
        specs=[SMEM] + [HBM] * (groups + half),
    )
    other = swap(partial, "fsdp", half)
    freqs = np.exp(np.arange(head_dim // 2) * (-2.0 * math.log(10000.0) / head_dim))
    freqs = np.concatenate([freqs, freqs]).astype(np.float32).reshape(1, head_dim)
    own, cosine, sine = call(
        functools.partial(own_kernel, requests, half),
        [
            shape((new_len, q_cols + 2 * kv_cols), f32),
            shape((new_len, head_dim), f32),
            shape((new_len, head_dim), f32),
        ],
        [
            pltpu.VMEM((new_len, width), bf16),
            pltpu.VMEM((new_len, width // 2), bf16),
            pltpu.VMEM((width // 2, q_cols + 2 * kv_cols), bf16),
            pltpu.SemaphoreType.DMA((half + 1,)),
        ],
        new_len * width * (q_cols + 2 * kv_cols),
        width * (2 * new_len + q_cols + 2 * kv_cols),
        where,
        after(rows, partial),
        gain,
        freqs,
        *weights,
        specs=[SMEM, HBM, VMEM, VMEM] + [HBM] * half,
    )

    residual = lax.all_to_all(
        after(my_quarter, own, other, *arrived).reshape(shards, sub, width),
        "fsdp",
        split_axis=0,
        concat_axis=0,
        tiled=True,
    )

    keys_total = max_blocks * page_len
    quarters = call(
        functools.partial(attend_kernel, groups, kv_local, head_dim),
        [shape((quarter, q_cols), bf16)] * groups,
        [
            pltpu.VMEM((kv_local, keys_total, head_dim), bf16),
            pltpu.VMEM((kv_local, keys_total, head_dim), bf16),
            pltpu.VMEM((new_len, q_cols), bf16),
            pltpu.VMEM(other.shape, bf16),
            pltpu.VMEM((shards, page_rows, 2 * head_dim), bf16),
            pltpu.SemaphoreType.DMA((3,)),
        ],
        4 * new_len * q_cols * (keys_total + new_len),
        1 << 22,
        where,
        own,
        other,
        cosine,
        sine,
        valid,
        *arrived,
        specs=[SMEM, VMEM, HBM, VMEM, VMEM, VMEM, HBM, HBM],
    )

    quarters = [
        swap(piece, "pool", distance) if distance else piece
        for distance, piece in enumerate(quarters)
    ]
    quarters = jnp.stack(quarters)
    tokens = {0: quarters}
    for distance in range(2, shards, 2):
        tokens[distance] = swap(quarters, "fsdp", distance)
    for distance in range(0, shards, 2):
        tokens[distance ^ 1] = swap(tokens[distance], "fsdp", 1)
    projected = call(
        functools.partial(output_kernel, groups, shards),
        [shape((shards, sub, features), bf16)] * shards,
        [
            pltpu.VMEM((shards * quarter, features), f32),
        ],
        2 * shards * quarter * features * groups * q_cols,
        1 << 22,
        where,
        *[tokens[distance] for distance in range(shards)],
        out_weight,
        mib=24,
    )
    finished = [
        swap(piece, "fsdp", distance) if distance else piece
        for distance, piece in enumerate(projected)
    ]
    return call(
        functools.partial(finish_kernel, shards),
        shape((requests, sub, width), bf16),
        [pltpu.VMEM((shards, shards, sub, features), f32)],
        1 << 20,
        1 << 20,
        where,
        post_gain.reshape(1, width),
        residual,
        *finished,
        mib=24,
    )


def local(*arguments):
    return local_small(*arguments) if lax.axis_size("fsdp") == 8 else local_general(*arguments)


def solution(mesh):
    in_specs = (
        P("fsdp", None, None),
        P(),
        P(),
        P(),
        P(),
        P("fsdp", None, "pool", None),
        P(),
        P("fsdp", "pool"),
        P("fsdp", "pool"),
        P("fsdp", "pool"),
        P("fsdp", "pool"),
        P(),
    )
    out_specs = P(None, ("pool", "fsdp"), None)
    return jax.shard_map(local, mesh=mesh, in_specs=in_specs, out_specs=out_specs, check_vma=False)
```

```python
import functools
import math

import jax
import jax.numpy as jnp
import numpy as np
from jax import lax
from jax.experimental import pallas as pl
from jax.experimental.pallas import tpu as pltpu
from jax.sharding import PartitionSpec as P

softcap = 50.0
query_scale = 144.0 ** (-0.5)
norm_eps = 1e-06


def rms_scale(rows, gain):
    mean_square = jnp.mean(rows * rows, axis=-1, keepdims=True)
    return rows * lax.rsqrt(mean_square + norm_eps) * gain


def rotate(vectors, cosine, sine):
    half = vectors.shape[-1] // 2
    first = vectors[..., :half]
    second = vectors[..., half:]
    return jnp.concatenate(
        [first * cosine - second * sine, second * cosine + first * sine], axis=-1
    )


def capped_weights(scores, valid):
    return jnp.where(valid, jnp.exp(softcap * jnp.tanh(scores / softcap)), 0.0)


def swap(array, axis, distance):
    size = lax.axis_size(axis)
    return lax.ppermute(array, axis, [(i, i ^ distance) for i in range(size)])


def place(pieces, index):
    first = pieces[0]
    stacked = jnp.zeros((len(pieces),) + first.shape, first.dtype)
    for distance, piece in pieces.items():
        stacked = lax.dynamic_update_index_in_dim(stacked, piece, index ^ distance, 0)
    return stacked


def exchange(chunks, axis):
    size = lax.axis_size(axis)
    index = lax.axis_index(axis)
    if size > 8:
        return lax.all_to_all(chunks, axis, split_axis=0, concat_axis=0, tiled=True)
    pieces = {}
    for distance in range(size):
        chunk = lax.dynamic_index_in_dim(chunks, index ^ distance, 0, keepdims=False)
        pieces[distance] = swap(chunk, axis, distance) if distance else chunk
    return place(pieces, index)


def doubled(block, axis, span):
    pieces = {0: block}
    bit = span // 2
    while bit:
        for distance in list(pieces):
            pieces[distance ^ bit] = swap(pieces[distance], axis, bit)
        bit //= 2
    return pieces


def attend(queries, keys_new, values_new, cached, cached_valid):
    new_len, kv_local, group, head_dim = queries.shape

    def part(keys, values, valid):
        scores = jnp.einsum("tgjd,kgd->gjtk", queries, keys, preferred_element_type=jnp.float32)
        weights = capped_weights(scores, valid)
        numer = jnp.einsum(
            "gjtk,kgd->gjtd",
            weights.astype(jnp.bfloat16),
            values,
            preferred_element_type=jnp.float32,
        )
        return numer, jnp.sum(weights, axis=-1)

    query_index = jnp.arange(new_len, dtype=jnp.int32)
    causal = query_index[None, :] <= query_index[:, None]
    numer, denom = part(
        cached[..., :head_dim], cached[..., head_dim:], cached_valid[None, None, None, :]
    )
    more, added = part(keys_new, values_new, causal[None, None])
    attended = ((numer + more) / (denom + added)[..., None]).transpose(2, 0, 1, 3)
    return attended.reshape(new_len, kv_local * group * head_dim).astype(jnp.bfloat16)


def local_general(
    hidden,
    slot_of_request,
    prefix_len,
    block_holder,
    block_slot,
    kv_pool,
    norm_gain,
    q_weight,
    k_weight,
    v_weight,
    o_weight,
    post_gain,
):
    shards = lax.axis_size("fsdp")
    groups = lax.axis_size("pool")
    f = lax.axis_index("fsdp")
    p = lax.axis_index("pool")
    half = shards // 2
    side = f // half
    new_len, width = hidden.shape[1:]
    requests = slot_of_request.shape[0]
    page_len = kv_pool.shape[1]
    kv_local = kv_pool.shape[2]
    head_dim = kv_pool.shape[3] // 2
    q_cols = q_weight.shape[1]
    kv_cols = k_weight.shape[1]
    group = q_cols // kv_cols
    max_blocks = block_holder.shape[1]
    per_holder = max_blocks // shards
    quarter = new_len // groups
    sub = quarter // shards
    features = o_weight.shape[0]

    kv_pieces = doubled(jnp.concatenate([k_weight, v_weight], axis=1), "fsdp", half)
    q_pieces = doubled(q_weight, "fsdp", half)
    out_weight = lax.all_gather(o_weight, "pool", axis=0, tiled=False)

    rows = hidden[0]
    normed = rms_scale(rows.astype(jnp.float32), norm_gain).astype(jnp.bfloat16)
    own_rows = lax.dynamic_slice(normed, (0, side * (width // 2)), (new_len, width // 2))
    leaving = lax.dynamic_slice(
        normed, (p * quarter, (1 - side) * (width // 2)), (quarter, width // 2)
    )
    partner_piece = swap(leaving, "fsdp", half)
    partner_pieces = {0: partner_piece}
    for distance in range(1, groups):
        partner_pieces[distance] = swap(partner_piece, "pool", distance)
    partner_rows = place(partner_pieces, p).reshape(new_len, width // 2)

    request_ids = jnp.arange(requests, dtype=jnp.int32)
    request_at_slot = jnp.sum(
        jnp.where(slot_of_request[None, :] == request_ids[:, None], request_ids[None, :], 0), axis=1
    )
    holder_by_slot = jnp.take(block_holder, request_at_slot, axis=0)
    page_by_slot = jnp.take(block_slot, request_at_slot, axis=0)
    held_here = holder_by_slot == f
    held_rank = jnp.cumsum(held_here.astype(jnp.int32), axis=1) - 1
    rank_ids = jnp.arange(per_holder, dtype=jnp.int32)
    picked = held_here[:, :, None] & (held_rank[:, :, None] == rank_ids[None, None, :])
    local_pages = jnp.sum(jnp.where(picked, page_by_slot[:, :, None], 0), axis=1)
    flat_pool = kv_pool.reshape(kv_pool.shape[0], page_len * kv_local, 2 * head_dim)
    outgoing = jnp.take(flat_pool, local_pages, axis=0)
    outgoing = outgoing.reshape(shards, per_holder * page_len * kv_local, 2 * head_dim)
    arrived = exchange(outgoing, "fsdp")
    cached = arrived.reshape(max_blocks * page_len, kv_local, 2 * head_dim)

    my_request = lax.dynamic_index_in_dim(request_at_slot, f, keepdims=False)
    my_length = prefix_len[my_request]
    my_holders = block_holder[my_request]
    entry_ids = jnp.arange(max_blocks, dtype=jnp.int32)
    mine = my_holders[None, :] == jnp.arange(shards, dtype=jnp.int32)[:, None]
    my_rank = jnp.cumsum(mine.astype(jnp.int32), axis=1) - 1
    chosen = mine[:, None, :] & (my_rank[:, None, :] == rank_ids[None, :, None])
    entry = jnp.sum(jnp.where(chosen, entry_ids[None, None, :], 0), axis=2)
    cached_position = entry.reshape(-1, 1) * page_len + jnp.arange(page_len, dtype=jnp.int32)
    cached_valid = (cached_position < my_length).reshape(-1)

    residual_out = lax.dynamic_slice_in_dim(rows, p * quarter, quarter, 0).reshape(
        shards, sub, width
    )
    residual = exchange(residual_out, "fsdp")

    positions = (my_length + jnp.arange(new_len, dtype=jnp.int32)).astype(jnp.float32)
    freqs = jnp.exp(
        jnp.arange(head_dim // 2, dtype=jnp.float32) * (-2.0 * math.log(10000.0) / head_dim)
    )
    angles = positions[:, None] * freqs
    cosine = jnp.cos(angles)[:, None, :]
    sine = jnp.sin(angles)[:, None, :]

    def project(pieces):
        weight = place(pieces, f % half).reshape(width // 2, -1)
        partial = jnp.dot(partner_rows, weight, preferred_element_type=jnp.float32)
        other = swap(partial.astype(jnp.bfloat16), "fsdp", half)
        own = jnp.dot(own_rows, weight, preferred_element_type=jnp.float32)
        return own + other.astype(jnp.float32)

    kv_sum = project(kv_pieces)
    q_sum = project(q_pieces)
    queries = rotate(q_sum.reshape(new_len, kv_local * group, head_dim), cosine, sine)
    queries = (queries * query_scale).astype(jnp.bfloat16)
    queries = queries.reshape(new_len, kv_local, group, head_dim)
    keys_new = kv_sum[:, :kv_cols].reshape(new_len, kv_local, head_dim)
    keys_new = rotate(keys_new, cosine, sine).astype(jnp.bfloat16)
    values_new = kv_sum[:, kv_cols:].astype(jnp.bfloat16).reshape(new_len, kv_local, head_dim)
    attended = attend(queries, keys_new, values_new, cached, cached_valid)

    quarters = exchange(attended.reshape(groups, quarter, q_cols), "pool")
    token_pieces = {0: quarters}
    for distance in range(2, shards, 2):
        token_pieces[distance] = swap(quarters, "fsdp", distance)
    for distance in range(0, shards, 2):
        token_pieces[distance ^ 1] = swap(token_pieces[distance], "fsdp", 1)
    tokens = place(token_pieces, f)
    projected = jnp.einsum(
        "sptc,pfc->stf", tokens, out_weight, preferred_element_type=jnp.float32
    ).astype(jnp.bfloat16)
    projected = projected.reshape(shards, shards, sub, features).transpose(1, 0, 2, 3)
    finished = exchange(projected, "fsdp").transpose(1, 2, 0, 3).reshape(shards, sub, width)
    finished = residual.astype(jnp.float32) + rms_scale(finished.astype(jnp.float32), post_gain)
    return jnp.take(finished.astype(jnp.bfloat16), slot_of_request, axis=0)


VMEM = pl.BlockSpec(memory_space=pltpu.VMEM)
SMEM = pl.BlockSpec(memory_space=pltpu.SMEM)
HBM = pl.BlockSpec(memory_space=pltpu.HBM)


def call(kernel, outs, scratch, flops, nbytes, *operands, specs=None, out_specs=None, mib=60):
    return pl.pallas_call(
        kernel,
        out_shape=outs,
        in_specs=specs or [SMEM] + [VMEM] * (len(operands) - 1),
        out_specs=out_specs or jax.tree.map(lambda _: VMEM, outs),
        scratch_shapes=scratch,
        compiler_params=pltpu.CompilerParams(vmem_limit_bytes=mib << 20),
        cost_estimate=pl.CostEstimate(flops=flops, bytes_accessed=nbytes, transcendentals=0),
    )(*operands)


def after(array, *earlier):
    return lax.optimization_barrier((array,) + earlier)[0]


def weight_copies(weight_refs, weight, f, half, sems):
    copies = []
    for distance, ref in enumerate(weight_refs):
        count = ref.shape[0]
        start = pl.multiple_of(((f ^ distance) & (half - 1)) * count, 64)
        copies.append(
            pltpu.make_async_copy(ref, weight.at[pl.ds(start, count), :], sems.at[distance])
        )
        copies[-1].start()
    return copies


def partner_kernel(groups, half, where_ref, *refs):
    p, f = where_ref[0], where_ref[1]
    x_refs, w_refs = refs[:groups], refs[groups : groups + half]
    out_ref, rows, weight, x_sems, w_sems = refs[groups + half :]
    quarter = x_refs[0].shape[0]
    copies = weight_copies(w_refs, weight, f, half, w_sems)
    for distance, ref in enumerate(x_refs):
        start = pl.multiple_of((p ^ distance) * quarter, quarter)
        copies.append(
            pltpu.make_async_copy(ref, rows.at[pl.ds(start, quarter), :], x_sems.at[distance])
        )
        copies[-1].start()
    for copy in copies:
        copy.wait()
    for at in range(0, out_ref.shape[1], 512):
        out_ref[:, at : at + 512] = jnp.dot(
            rows[...], weight[:, at : at + 512], preferred_element_type=jnp.float32
        ).astype(jnp.bfloat16)


def row_scale(rows):
    return lax.rsqrt(jnp.mean(rows * rows, axis=1, keepdims=True) + norm_eps)


def prologue_kernel(
    hidden_ref, gain_ref, q_ref, k_ref, v_ref, leaving_ref, rows_ref, weight_ref, normed, sem
):
    p, f = lax.axis_index("pool"), lax.axis_index("fsdp")
    side = f // (lax.axis_size("fsdp") // 2)
    quarter, width = rows_ref.shape
    half_width = width // 2
    start = pl.multiple_of(p * quarter, quarter)
    rows_copy = pltpu.make_async_copy(hidden_ref.at[pl.ds(start, quarter), :], rows_ref, sem)
    rows_copy.start()
    at = 0
    for ref in (q_ref, k_ref, v_ref):
        weight_ref[:, at : at + ref.shape[1]] = ref[...]
        at += ref.shape[1]
    rows_copy.wait()
    rows = rows_ref[...].astype(jnp.float32)
    normed[...] = rows * row_scale(rows) * gain_ref[...].reshape(1, width)
    away = pl.multiple_of((1 - side) * half_width, 128)
    leaving_ref[...] = normed[:, pl.ds(away, half_width)].astype(jnp.bfloat16)


def pages_kernel(
    requests, page_len, where_ref, holder_ref, slot_ref, pool_ref, *refs
):
    f = where_ref[1]
    *out_refs, valid_ref, listed, entries, counts = refs
    max_blocks = holder_ref.shape[1]
    shards = out_refs[0].shape[0]
    per = max_blocks // shards
    each = per // len(out_refs)
    page_rows = pool_ref.shape[1]
    length, mine = jnp.int32(0), jnp.int32(0)
    for r in range(requests):
        at = where_ref[3 + r] == f
        length = length + jnp.where(at, where_ref[3 + requests + r], 0)
        mine = mine + jnp.where(at, r, 0)
    for r in range(requests):
        slot = where_ref[3 + r]

        def note(j, count):
            listed[count] = slot_ref[r, j]
            return count + jnp.where(holder_ref[r, j] == f, 1, 0)

        lax.fori_loop(0, max_blocks, note, jnp.int32(0), unroll=8)
        for k in range(per):
            at = k % each * page_rows
            out_refs[k // each][slot, at : at + page_rows, :] = pool_ref[listed[k]]
    for h in range(shards):
        counts[h] = 0

    def enter(j, carry):
        h = holder_ref[mine, j]
        count = counts[h]
        entries[h * per + count] = j
        counts[h] = count + 1
        return carry

    lax.fori_loop(0, max_blocks, enter, 0, unroll=4)
    row = lax.broadcasted_iota(jnp.int32, valid_ref.shape, 0)
    lane = lax.broadcasted_iota(jnp.int32, valid_ref.shape, 1)
    place_in = row * per + lane // page_len
    entry = jnp.zeros(valid_ref.shape, jnp.int32)
    for at in range(max_blocks):
        entry = jnp.where(place_in == at, entries[at], entry)
    position = entry * page_len + lane % page_len
    valid_ref[...] = jnp.where(position < length, 1.0, 0.0)


def own_kernel(requests, half, where_ref, hidden_ref, gain_ref, freq_ref, *refs):
    f = where_ref[1]
    own_ref, cos_ref, sin_ref, hidden, normed, weight, sems = refs[half:]
    rows_copy = pltpu.make_async_copy(hidden_ref, hidden, sems.at[half])
    rows_copy.start()
    copies = weight_copies(refs[:half], weight, f, half, sems)
    rows_copy.wait()
    new_len, width = hidden_ref.shape
    half_width = width // 2
    length = jnp.int32(0)
    for r in range(requests):
        length = length + jnp.where(where_ref[3 + r] == f, where_ref[3 + requests + r], 0)
    start = pl.multiple_of(where_ref[2] * half_width, 128)
    gain = gain_ref[:, pl.ds(start, half_width)]
    step = 32

    def norm(index, carry):
        at = pl.multiple_of(index * step, step)
        rows = hidden[pl.ds(at, step), :].astype(jnp.float32)
        scale = row_scale(rows)
        part = hidden[pl.ds(at, step), pl.ds(start, half_width)].astype(jnp.float32)
        normed[pl.ds(at, step), :] = (part * scale * gain).astype(jnp.bfloat16)
        return carry

    lax.fori_loop(0, new_len // step, norm, 0)
    position = lax.broadcasted_iota(jnp.int32, cos_ref.shape, 0) + length
    angle = position.astype(jnp.float32) * freq_ref[...]
    lane = lax.broadcasted_iota(jnp.int32, cos_ref.shape, 1)
    cos_ref[...] = jnp.cos(angle)
    sine = jnp.sin(angle)
    sin_ref[...] = jnp.where(lane < cos_ref.shape[1] // 2, -sine, sine)
    for copy in copies:
        copy.wait()
    for at in range(0, own_ref.shape[1], 512):
        own_ref[:, at : at + 512] = jnp.dot(
            normed[...], weight[:, at : at + 512], preferred_element_type=jnp.float32
        )


def capped(scores):
    return jnp.exp2(jnp.tanh(scores * (1.0 / softcap)) * (softcap * math.log2(math.e)))


def attend_kernel(
    groups,
    kv_local,
    head_dim,
    where_ref,
    own,
    other_ref,
    cos_ref,
    sin_ref,
    valid_ref,
    *refs,
):
    p = where_ref[0]
    page_refs, out_refs = refs[:2], refs[2 : 2 + groups]
    keys, values, result, other, pages, sems = refs[2 + groups :]
    copies = [pltpu.make_async_copy(other_ref, other, sems.at[0])]
    for index, ref in enumerate(page_refs):
        lines = pl.ds(index * ref.shape[1], ref.shape[1])
        copies.append(
            pltpu.make_async_copy(ref, pages.at[:, lines, :], sems.at[1 + index])
        )
    for copy in copies:
        copy.start()
    new_len, q_cols = result.shape
    group = q_cols // (kv_local * head_dim)

    def sums(at):
        return own[:, at : at + head_dim] + other[:, at : at + head_dim].astype(jnp.float32)

    cosine, sine = cos_ref[...], sin_ref[...]

    def rope(vectors):
        return vectors * cosine + pltpu.roll(vectors, head_dim // 2, 1) * sine

    span = pages.shape[1]
    per = span // kv_local
    row = lax.broadcasted_iota(jnp.int32, (span, span), 0)
    column = lax.broadcasted_iota(jnp.int32, (span, span), 1)
    part = (column == (row % per) * kv_local + row // per).astype(jnp.bfloat16)
    place_at = 0
    for copy in copies[1:]:
        copy.wait()
    for holder in range(pages.shape[0]):
        parted = jnp.dot(part, pages[holder], preferred_element_type=jnp.float32)
        parted = parted.astype(jnp.bfloat16)
        for g in range(kv_local):
            lines = parted[g * per : (g + 1) * per]
            keys[g, place_at : place_at + per, :] = lines[:, :head_dim]
            values[g, place_at : place_at + per, :] = lines[:, head_dim:]
        place_at += per

    copies[0].wait()
    span_keys = 2 * per
    t = lax.broadcasted_iota(jnp.int32, (group * new_len, new_len), 0) % new_len
    s = lax.broadcasted_iota(jnp.int32, (group * new_len, new_len), 1)
    causal = s <= t
    for g in range(kv_local):
        heads = [
            (rope(sums((g * group + j) * head_dim)) * query_scale).astype(jnp.bfloat16)
            for j in range(group)
        ]
        queries = jnp.concatenate(heads, axis=0)
        at = q_cols + g * head_dim
        new_key = rope(sums(at)).astype(jnp.bfloat16)
        new_value = sums(at + kv_local * head_dim).astype(jnp.bfloat16)

        def scores_of(key):
            return lax.dot_general(
                queries, key, (((1,), (1,)), ((), ())), preferred_element_type=jnp.float32
            )

        weights = jnp.where(causal, capped(scores_of(new_key)), 0.0)
        denom = jnp.sum(weights, axis=1, keepdims=True)
        numer = jnp.dot(
            weights.astype(jnp.bfloat16), new_value, preferred_element_type=jnp.float32
        )
        for start in range(0, place_at, span_keys):
            at = start // per
            valid = jnp.concatenate([valid_ref[at : at + 1], valid_ref[at + 1 : at + 2]], axis=1)
            valid = valid > 0.0
            weights = jnp.where(
                valid, capped(scores_of(keys[g, start : start + span_keys, :])), 0.0
            )
            denom = denom + jnp.sum(weights, axis=1, keepdims=True)
            numer = numer + jnp.dot(
                weights.astype(jnp.bfloat16),
                values[g, start : start + span_keys, :],
                preferred_element_type=jnp.float32,
            )
        attended = (numer / denom).astype(jnp.bfloat16)
        for j in range(group):
            to = (g * group + j) * head_dim
            result[:, to : to + head_dim] = attended[j * new_len : (j + 1) * new_len]
    quarter = new_len // groups
    for distance, ref in enumerate(out_refs):
        start = pl.multiple_of((p ^ distance) * quarter, quarter)
        ref[...] = result[pl.ds(start, quarter), :]


def output_kernel(groups, shards, where_ref, *refs):
    p, f = where_ref[0], where_ref[1]
    token_refs = refs[:shards]
    weight_ref = refs[shards]
    out_refs = refs[shards + 1 : 2 * shards + 1]
    (total,) = refs[2 * shards + 1 :]
    quarter = token_refs[0].shape[1]
    sub = quarter // shards
    projected = None
    for distance in range(groups):
        rows = jnp.concatenate([ref[distance] for ref in token_refs], axis=0)
        term = lax.dot_general(
            rows,
            weight_ref[p ^ distance],
            (((1,), (1,)), ((), ())),
            preferred_element_type=jnp.float32,
        )
        projected = term if projected is None else projected + term
    total[...] = projected
    for e in range(shards):
        for distance, ref in enumerate(out_refs):
            start = pl.multiple_of(e * quarter + (f ^ distance) * sub, sub)
            ref[f ^ e] = total[pl.ds(start, sub), :].astype(jnp.bfloat16)


def finish_kernel(shards, where_ref, gain_ref, residual_ref, *refs):
    f = where_ref[1]
    piece_refs = refs[:shards]
    out_ref, projected = refs[shards:]
    for distance, ref in enumerate(piece_refs):
        projected[f ^ distance] = ref[...].astype(jnp.float32)
    gain = gain_ref[...]
    for request in range(out_ref.shape[0]):
        slot = where_ref[3 + request]
        line = jnp.concatenate([projected[k, slot] for k in range(shards)], axis=1)
        mean_square = jnp.mean(line * line, axis=1, keepdims=True)
        line = line * lax.rsqrt(mean_square + norm_eps) * gain
        out_ref[request] = (residual_ref[slot].astype(jnp.float32) + line).astype(jnp.bfloat16)


def pool_pieces(block, groups):
    return [block] + [swap(block, "pool", distance) for distance in range(1, groups)]


def local_small(
    hidden,
    slot_of_request,
    prefix_len,
    block_holder,
    block_slot,
    kv_pool,
    norm_gain,
    q_weight,
    k_weight,
    v_weight,
    o_weight,
    post_gain,
):
    shards = lax.axis_size("fsdp")
    groups = lax.axis_size("pool")
    f = lax.axis_index("fsdp")
    p = lax.axis_index("pool")
    half = shards // 2
    side = f // half
    new_len, width = hidden.shape[1:]
    requests = slot_of_request.shape[0]
    page_len = kv_pool.shape[1]
    kv_local = kv_pool.shape[2]
    head_dim = kv_pool.shape[3] // 2
    q_cols = q_weight.shape[1]
    kv_cols = k_weight.shape[1]
    max_blocks = block_holder.shape[1]
    per_holder = max_blocks // shards
    quarter = new_len // groups
    sub = quarter // shards
    features = o_weight.shape[0]
    bf16, f32 = jnp.bfloat16, jnp.float32
    where = jnp.concatenate(
        [jnp.stack([p, f, side]).astype(jnp.int32), slot_of_request, prefix_len]
    )
    shape = jax.ShapeDtypeStruct
    gain = norm_gain.reshape(1, width)
    rows = hidden[0]

    leaving, my_quarter, joined = call(
        prologue_kernel,
        [
            shape((quarter, width // 2), bf16),
            shape((quarter, width), bf16),
            shape((features, q_cols + 2 * kv_cols), bf16),
        ],
        [pltpu.VMEM((quarter, width), f32), pltpu.SemaphoreType.DMA],
        quarter * width * 8,
        4 * features * kv_cols,
        rows,
        norm_gain,
        q_weight,
        k_weight,
        v_weight,
        specs=[HBM, VMEM, VMEM, VMEM, VMEM],
    )
    partner_piece = swap(leaving, "fsdp", half)

    flat_pool = kv_pool.reshape(kv_pool.shape[0], page_len * kv_local, 2 * head_dim)
    page_rows = per_holder * page_len * kv_local
    first_pages, second_pages, valid = call(
        functools.partial(pages_kernel, requests, page_len),
        [
            shape((shards, page_rows // 2, 2 * head_dim), bf16),
            shape((shards, page_rows // 2, 2 * head_dim), bf16),
            shape((shards, per_holder * page_len), f32),
        ],
        [
            pltpu.SMEM((2 * per_holder,), jnp.int32),
            pltpu.SMEM((max_blocks + per_holder,), jnp.int32),
            pltpu.SMEM((shards,), jnp.int32),
        ],
        1 << 20,
        1 << 21,
        where,
        block_holder,
        block_slot,
        flat_pool,
        specs=[SMEM, SMEM, SMEM, VMEM],
    )
    near = swap(joined, "fsdp", 1)
    partner_piece, near, first_pages, second_pages, valid = lax.optimization_barrier(
        (partner_piece, near, first_pages, second_pages, valid)
    )
    far = swap(after(joined, partner_piece), "fsdp", 2)
    partner_pieces = pool_pieces(partner_piece, groups)
    arrived = lax.all_to_all(first_pages, "fsdp", split_axis=0, concat_axis=0, tiled=True)
    partner_pieces, far, arrived = lax.optimization_barrier((partner_pieces, far, arrived))
    arrived = [arrived]
    weights = [joined, near, far, swap(far, "fsdp", 1)]
    arrived.append(
        lax.all_to_all(
            after(second_pages, far), "fsdp", split_axis=0, concat_axis=0, tiled=True
        )
    )
    out_weight = lax.all_gather(after(o_weight, *partner_pieces), "pool", axis=0, tiled=False)

    partial = call(
        functools.partial(partner_kernel, groups, half),
        shape((new_len, q_cols + 2 * kv_cols), bf16),
        [
            pltpu.VMEM((new_len, width // 2), bf16),
            pltpu.VMEM((width // 2, q_cols + 2 * kv_cols), bf16),
            pltpu.SemaphoreType.DMA((groups,)),
            pltpu.SemaphoreType.DMA((half,)),
        ],
        new_len * width * (q_cols + 2 * kv_cols),
        width * (new_len + q_cols + 2 * kv_cols),
        where,
        *partner_pieces,
        *weights,
        specs=[SMEM] + [HBM] * (groups + half),
    )
    other = swap(partial, "fsdp", half)
    freqs = np.exp(np.arange(head_dim // 2) * (-2.0 * math.log(10000.0) / head_dim))
    freqs = np.concatenate([freqs, freqs]).astype(np.float32).reshape(1, head_dim)
    own, cosine, sine = call(
        functools.partial(own_kernel, requests, half),
        [
            shape((new_len, q_cols + 2 * kv_cols), f32),
            shape((new_len, head_dim), f32),
            shape((new_len, head_dim), f32),
        ],
        [
            pltpu.VMEM((new_len, width), bf16),
            pltpu.VMEM((new_len, width // 2), bf16),
            pltpu.VMEM((width // 2, q_cols + 2 * kv_cols), bf16),
            pltpu.SemaphoreType.DMA((half + 1,)),
        ],
        new_len * width * (q_cols + 2 * kv_cols),
        width * (2 * new_len + q_cols + 2 * kv_cols),
        where,
        after(rows, partial),
        gain,
        freqs,
        *weights,
        specs=[SMEM, HBM, VMEM, VMEM] + [HBM] * half,
    )

    residual = lax.all_to_all(
        after(my_quarter, own, other, *arrived).reshape(shards, sub, width),
        "fsdp",
        split_axis=0,
        concat_axis=0,
        tiled=True,
    )

    keys_total = max_blocks * page_len
    quarters = call(
        functools.partial(attend_kernel, groups, kv_local, head_dim),
        [shape((quarter, q_cols), bf16)] * groups,
        [
            pltpu.VMEM((kv_local, keys_total, head_dim), bf16),
            pltpu.VMEM((kv_local, keys_total, head_dim), bf16),
            pltpu.VMEM((new_len, q_cols), bf16),
            pltpu.VMEM(other.shape, bf16),
            pltpu.VMEM((shards, page_rows, 2 * head_dim), bf16),
            pltpu.SemaphoreType.DMA((3,)),
        ],
        4 * new_len * q_cols * (keys_total + new_len),
        1 << 22,
        where,
        own,
        other,
        cosine,
        sine,
        valid,
        *arrived,
        specs=[SMEM, VMEM, HBM, VMEM, VMEM, VMEM, HBM, HBM],
    )

    quarters = [
        swap(piece, "pool", distance) if distance else piece
        for distance, piece in enumerate(quarters)
    ]
    quarters, out_weight = lax.optimization_barrier((jnp.stack(quarters), out_weight))
    tokens = {0: quarters, 1: swap(quarters, "fsdp", 1)}
    for distance in range(half, shards, 2):
        tokens[distance] = swap(quarters, "fsdp", distance)
    tokens[2] = swap(after(quarters, tokens[1]), "fsdp", 2)
    for distance in range(2, shards, 2):
        tokens[distance ^ 1] = swap(tokens[distance], "fsdp", 1)
    projected = call(
        functools.partial(output_kernel, groups, shards),
        [shape((shards, sub, features), bf16)] * shards,
        [
            pltpu.VMEM((shards * quarter, features), f32),
        ],
        2 * shards * quarter * features * groups * q_cols,
        1 << 22,
        where,
        *[tokens[distance] for distance in range(shards)],
        out_weight,
        mib=24,
    )
    finished = [
        swap(piece, "fsdp", distance) if distance else piece
        for distance, piece in enumerate(projected)
    ]
    return call(
        functools.partial(finish_kernel, shards),
        shape((requests, sub, width), bf16),
        [pltpu.VMEM((shards, shards, sub, features), f32)],
        1 << 20,
        1 << 20,
        where,
        post_gain.reshape(1, width),
        residual,
        *finished,
        mib=24,
    )


def local(*arguments):
    return local_small(*arguments) if lax.axis_size("fsdp") == 8 else local_general(*arguments)


def solution(mesh):
    in_specs = (
        P("fsdp", None, None),
        P(),
        P(),
        P(),
        P(),
        P("fsdp", None, "pool", None),
        P(),
        P("fsdp", "pool"),
        P("fsdp", "pool"),
        P("fsdp", "pool"),
        P("fsdp", "pool"),
        P(),
    )
    out_specs = P(None, ("pool", "fsdp"), None)
    return jax.shard_map(local, mesh=mesh, in_specs=in_specs, out_specs=out_specs, check_vma=False)
```

```python
import functools
import math

import jax
import jax.numpy as jnp
import numpy as np
from jax import lax
from jax.experimental import pallas as pl
from jax.experimental.pallas import tpu as pltpu
from jax.sharding import PartitionSpec as P

softcap = 50.0
query_scale = 144.0 ** (-0.5)
norm_eps = 1e-06


def rms_scale(rows, gain):
    mean_square = jnp.mean(rows * rows, axis=-1, keepdims=True)
    return rows * lax.rsqrt(mean_square + norm_eps) * gain


def rotate(vectors, cosine, sine):
    half = vectors.shape[-1] // 2
    first = vectors[..., :half]
    second = vectors[..., half:]
    return jnp.concatenate(
        [first * cosine - second * sine, second * cosine + first * sine], axis=-1
    )


def capped_weights(scores, valid):
    return jnp.where(valid, jnp.exp(softcap * jnp.tanh(scores / softcap)), 0.0)


def swap(array, axis, distance):
    size = lax.axis_size(axis)
    return lax.ppermute(array, axis, [(i, i ^ distance) for i in range(size)])


def place(pieces, index):
    first = pieces[0]
    stacked = jnp.zeros((len(pieces),) + first.shape, first.dtype)
    for distance, piece in pieces.items():
        stacked = lax.dynamic_update_index_in_dim(stacked, piece, index ^ distance, 0)
    return stacked


def exchange(chunks, axis):
    size = lax.axis_size(axis)
    index = lax.axis_index(axis)
    if size > 8:
        return lax.all_to_all(chunks, axis, split_axis=0, concat_axis=0, tiled=True)
    pieces = {}
    for distance in range(size):
        chunk = lax.dynamic_index_in_dim(chunks, index ^ distance, 0, keepdims=False)
        pieces[distance] = swap(chunk, axis, distance) if distance else chunk
    return place(pieces, index)


def doubled(block, axis, span):
    pieces = {0: block}
    bit = span // 2
    while bit:
        for distance in list(pieces):
            pieces[distance ^ bit] = swap(pieces[distance], axis, bit)
        bit //= 2
    return pieces


def attend(queries, keys_new, values_new, cached, cached_valid):
    new_len, kv_local, group, head_dim = queries.shape

    def part(keys, values, valid):
        scores = jnp.einsum("tgjd,kgd->gjtk", queries, keys, preferred_element_type=jnp.float32)
        weights = capped_weights(scores, valid)
        numer = jnp.einsum(
            "gjtk,kgd->gjtd",
            weights.astype(jnp.bfloat16),
            values,
            preferred_element_type=jnp.float32,
        )
        return numer, jnp.sum(weights, axis=-1)

    query_index = jnp.arange(new_len, dtype=jnp.int32)
    causal = query_index[None, :] <= query_index[:, None]
    numer, denom = part(
        cached[..., :head_dim], cached[..., head_dim:], cached_valid[None, None, None, :]
    )
    more, added = part(keys_new, values_new, causal[None, None])
    attended = ((numer + more) / (denom + added)[..., None]).transpose(2, 0, 1, 3)
    return attended.reshape(new_len, kv_local * group * head_dim).astype(jnp.bfloat16)


def local_general(
    hidden,
    slot_of_request,
    prefix_len,
    block_holder,
    block_slot,
    kv_pool,
    norm_gain,
    q_weight,
    k_weight,
    v_weight,
    o_weight,
    post_gain,
):
    shards = lax.axis_size("fsdp")
    groups = lax.axis_size("pool")
    f = lax.axis_index("fsdp")
    p = lax.axis_index("pool")
    half = shards // 2
    side = f // half
    new_len, width = hidden.shape[1:]
    requests = slot_of_request.shape[0]
    page_len = kv_pool.shape[1]
    kv_local = kv_pool.shape[2]
    head_dim = kv_pool.shape[3] // 2
    q_cols = q_weight.shape[1]
    kv_cols = k_weight.shape[1]
    group = q_cols // kv_cols
    max_blocks = block_holder.shape[1]
    per_holder = max_blocks // shards
    quarter = new_len // groups
    sub = quarter // shards
    features = o_weight.shape[0]

    kv_pieces = doubled(jnp.concatenate([k_weight, v_weight], axis=1), "fsdp", half)
    q_pieces = doubled(q_weight, "fsdp", half)
    out_weight = lax.all_gather(o_weight, "pool", axis=0, tiled=False)

    rows = hidden[0]
    normed = rms_scale(rows.astype(jnp.float32), norm_gain).astype(jnp.bfloat16)
    own_rows = lax.dynamic_slice(normed, (0, side * (width // 2)), (new_len, width // 2))
    leaving = lax.dynamic_slice(
        normed, (p * quarter, (1 - side) * (width // 2)), (quarter, width // 2)
    )
    partner_piece = swap(leaving, "fsdp", half)
    partner_pieces = {0: partner_piece}
    for distance in range(1, groups):
        partner_pieces[distance] = swap(partner_piece, "pool", distance)
    partner_rows = place(partner_pieces, p).reshape(new_len, width // 2)

    request_ids = jnp.arange(requests, dtype=jnp.int32)
    request_at_slot = jnp.sum(
        jnp.where(slot_of_request[None, :] == request_ids[:, None], request_ids[None, :], 0), axis=1
    )
    holder_by_slot = jnp.take(block_holder, request_at_slot, axis=0)
    page_by_slot = jnp.take(block_slot, request_at_slot, axis=0)
    held_here = holder_by_slot == f
    held_rank = jnp.cumsum(held_here.astype(jnp.int32), axis=1) - 1
    rank_ids = jnp.arange(per_holder, dtype=jnp.int32)
    picked = held_here[:, :, None] & (held_rank[:, :, None] == rank_ids[None, None, :])
    local_pages = jnp.sum(jnp.where(picked, page_by_slot[:, :, None], 0), axis=1)
    flat_pool = kv_pool.reshape(kv_pool.shape[0], page_len * kv_local, 2 * head_dim)
    outgoing = jnp.take(flat_pool, local_pages, axis=0)
    outgoing = outgoing.reshape(shards, per_holder * page_len * kv_local, 2 * head_dim)
    arrived = exchange(outgoing, "fsdp")
    cached = arrived.reshape(max_blocks * page_len, kv_local, 2 * head_dim)

    my_request = lax.dynamic_index_in_dim(request_at_slot, f, keepdims=False)
    my_length = prefix_len[my_request]
    my_holders = block_holder[my_request]
    entry_ids = jnp.arange(max_blocks, dtype=jnp.int32)
    mine = my_holders[None, :] == jnp.arange(shards, dtype=jnp.int32)[:, None]
    my_rank = jnp.cumsum(mine.astype(jnp.int32), axis=1) - 1
    chosen = mine[:, None, :] & (my_rank[:, None, :] == rank_ids[None, :, None])
    entry = jnp.sum(jnp.where(chosen, entry_ids[None, None, :], 0), axis=2)
    cached_position = entry.reshape(-1, 1) * page_len + jnp.arange(page_len, dtype=jnp.int32)
    cached_valid = (cached_position < my_length).reshape(-1)

    residual_out = lax.dynamic_slice_in_dim(rows, p * quarter, quarter, 0).reshape(
        shards, sub, width
    )
    residual = exchange(residual_out, "fsdp")

    positions = (my_length + jnp.arange(new_len, dtype=jnp.int32)).astype(jnp.float32)
    freqs = jnp.exp(
        jnp.arange(head_dim // 2, dtype=jnp.float32) * (-2.0 * math.log(10000.0) / head_dim)
    )
    angles = positions[:, None] * freqs
    cosine = jnp.cos(angles)[:, None, :]
    sine = jnp.sin(angles)[:, None, :]

    def project(pieces):
        weight = place(pieces, f % half).reshape(width // 2, -1)
        partial = jnp.dot(partner_rows, weight, preferred_element_type=jnp.float32)
        other = swap(partial.astype(jnp.bfloat16), "fsdp", half)
        own = jnp.dot(own_rows, weight, preferred_element_type=jnp.float32)
        return own + other.astype(jnp.float32)

    kv_sum = project(kv_pieces)
    q_sum = project(q_pieces)
    queries = rotate(q_sum.reshape(new_len, kv_local * group, head_dim), cosine, sine)
    queries = (queries * query_scale).astype(jnp.bfloat16)
    queries = queries.reshape(new_len, kv_local, group, head_dim)
    keys_new = kv_sum[:, :kv_cols].reshape(new_len, kv_local, head_dim)
    keys_new = rotate(keys_new, cosine, sine).astype(jnp.bfloat16)
    values_new = kv_sum[:, kv_cols:].astype(jnp.bfloat16).reshape(new_len, kv_local, head_dim)
    attended = attend(queries, keys_new, values_new, cached, cached_valid)

    quarters = exchange(attended.reshape(groups, quarter, q_cols), "pool")
    token_pieces = {0: quarters}
    for distance in range(2, shards, 2):
        token_pieces[distance] = swap(quarters, "fsdp", distance)
    for distance in range(0, shards, 2):
        token_pieces[distance ^ 1] = swap(token_pieces[distance], "fsdp", 1)
    tokens = place(token_pieces, f)
    projected = jnp.einsum(
        "sptc,pfc->stf", tokens, out_weight, preferred_element_type=jnp.float32
    ).astype(jnp.bfloat16)
    projected = projected.reshape(shards, shards, sub, features).transpose(1, 0, 2, 3)
    finished = exchange(projected, "fsdp").transpose(1, 2, 0, 3).reshape(shards, sub, width)
    finished = residual.astype(jnp.float32) + rms_scale(finished.astype(jnp.float32), post_gain)
    return jnp.take(finished.astype(jnp.bfloat16), slot_of_request, axis=0)


VMEM = pl.BlockSpec(memory_space=pltpu.VMEM)
SMEM = pl.BlockSpec(memory_space=pltpu.SMEM)
HBM = pl.BlockSpec(memory_space=pltpu.HBM)


def call(kernel, outs, scratch, flops, nbytes, *operands, specs=None, out_specs=None, mib=60):
    return pl.pallas_call(
        kernel,
        out_shape=outs,
        in_specs=specs or [SMEM] + [VMEM] * (len(operands) - 1),
        out_specs=out_specs or jax.tree.map(lambda _: VMEM, outs),
        scratch_shapes=scratch,
        compiler_params=pltpu.CompilerParams(vmem_limit_bytes=mib << 20),
        cost_estimate=pl.CostEstimate(flops=flops, bytes_accessed=nbytes, transcendentals=0),
    )(*operands)


def after(array, *earlier):
    return lax.optimization_barrier((array,) + earlier)[0]


def weight_copies(weight_refs, weight, f, half, sems):
    copies = []
    for distance, ref in enumerate(weight_refs):
        count = ref.shape[0]
        start = pl.multiple_of(((f ^ distance) & (half - 1)) * count, 64)
        copies.append(
            pltpu.make_async_copy(ref, weight.at[pl.ds(start, count), :], sems.at[distance])
        )
        copies[-1].start()
    return copies


def partner_kernel(groups, half, where_ref, *refs):
    p, f = where_ref[0], where_ref[1]
    x_refs, refs = refs[:groups], refs[groups:]
    out_ref, rows, q_weight, kv_weight, x_sems, w_sems = refs[2 * half :]
    quarter = x_refs[0].shape[0]
    copies = weight_copies(refs[:half], q_weight, f, half, w_sems.at[:half])
    copies += weight_copies(refs[half : 2 * half], kv_weight, f, half, w_sems.at[half:])
    for distance, ref in enumerate(x_refs):
        start = pl.multiple_of((p ^ distance) * quarter, quarter)
        copies.append(
            pltpu.make_async_copy(ref, rows.at[pl.ds(start, quarter), :], x_sems.at[distance])
        )
        copies[-1].start()
    for copy in copies:
        copy.wait()
    at = 0
    for weight in (q_weight, kv_weight):
        to = at + weight.shape[1]
        out_ref[:, at:to] = jnp.dot(
            rows[...], weight[...], preferred_element_type=jnp.float32
        ).astype(jnp.bfloat16)
        at = to


def row_scale(rows):
    return lax.rsqrt(jnp.mean(rows * rows, axis=1, keepdims=True) + norm_eps)


def prologue_kernel(
    hidden_ref, gain_ref, k_ref, v_ref, leaving_ref, rows_ref, weight_ref, normed, sem
):
    p, f = lax.axis_index("pool"), lax.axis_index("fsdp")
    side = f // (lax.axis_size("fsdp") // 2)
    quarter, width = rows_ref.shape
    half_width = width // 2
    start = pl.multiple_of(p * quarter, quarter)
    rows_copy = pltpu.make_async_copy(hidden_ref.at[pl.ds(start, quarter), :], rows_ref, sem)
    rows_copy.start()
    at = 0
    for ref in (k_ref, v_ref):
        weight_ref[:, at : at + ref.shape[1]] = ref[...]
        at += ref.shape[1]
    rows_copy.wait()
    rows = rows_ref[...].astype(jnp.float32)
    normed[...] = rows * row_scale(rows) * gain_ref[...].reshape(1, width)
    away = pl.multiple_of((1 - side) * half_width, 128)
    leaving_ref[...] = normed[:, pl.ds(away, half_width)].astype(jnp.bfloat16)


def pages_kernel(
    requests, page_len, where_ref, holder_ref, slot_ref, pool_ref, *refs
):
    f = where_ref[1]
    *out_refs, valid_ref, listed, entries, counts = refs
    max_blocks = holder_ref.shape[1]
    shards = out_refs[0].shape[0]
    per = max_blocks // shards
    each = per // len(out_refs)
    page_rows = pool_ref.shape[1]
    length, mine = jnp.int32(0), jnp.int32(0)
    for r in range(requests):
        at = where_ref[3 + r] == f
        length = length + jnp.where(at, where_ref[3 + requests + r], 0)
        mine = mine + jnp.where(at, r, 0)
    for r in range(requests):
        slot = where_ref[3 + r]

        def note(j, count):
            listed[count] = slot_ref[r, j]
            return count + jnp.where(holder_ref[r, j] == f, 1, 0)

        lax.fori_loop(0, max_blocks, note, jnp.int32(0), unroll=8)
        for k in range(per):
            at = k % each * page_rows
            out_refs[k // each][slot, at : at + page_rows, :] = pool_ref[listed[k]]
    for h in range(shards):
        counts[h] = 0

    def enter(j, carry):
        h = holder_ref[mine, j]
        count = counts[h]
        entries[h * per + count] = j
        counts[h] = count + 1
        return carry

    lax.fori_loop(0, max_blocks, enter, 0, unroll=4)
    row = lax.broadcasted_iota(jnp.int32, valid_ref.shape, 0)
    lane = lax.broadcasted_iota(jnp.int32, valid_ref.shape, 1)
    place_in = row * per + lane // page_len
    entry = jnp.zeros(valid_ref.shape, jnp.int32)
    for at in range(max_blocks):
        entry = jnp.where(place_in == at, entries[at], entry)
    position = entry * page_len + lane % page_len
    valid_ref[...] = jnp.where(position < length, 1.0, 0.0)


def own_kernel(requests, half, where_ref, hidden_ref, gain_ref, freq_ref, *refs):
    f = where_ref[1]
    own_ref, cos_ref, sin_ref, hidden, normed, q_weight, kv_weight, sems = refs[2 * half :]
    rows_copy = pltpu.make_async_copy(hidden_ref, hidden, sems.at[2 * half])
    rows_copy.start()
    copies = weight_copies(refs[:half], q_weight, f, half, sems.at[:half])
    copies += weight_copies(refs[half : 2 * half], kv_weight, f, half, sems.at[half : 2 * half])
    rows_copy.wait()
    new_len, width = hidden_ref.shape
    half_width = width // 2
    length = jnp.int32(0)
    for r in range(requests):
        length = length + jnp.where(where_ref[3 + r] == f, where_ref[3 + requests + r], 0)
    start = pl.multiple_of(where_ref[2] * half_width, 128)
    gain = gain_ref[:, pl.ds(start, half_width)]
    step = 32

    def norm(index, carry):
        at = pl.multiple_of(index * step, step)
        rows = hidden[pl.ds(at, step), :].astype(jnp.float32)
        scale = row_scale(rows)
        part = hidden[pl.ds(at, step), pl.ds(start, half_width)].astype(jnp.float32)
        normed[pl.ds(at, step), :] = (part * scale * gain).astype(jnp.bfloat16)
        return carry

    lax.fori_loop(0, new_len // step, norm, 0)
    position = lax.broadcasted_iota(jnp.int32, cos_ref.shape, 0) + length
    angle = position.astype(jnp.float32) * freq_ref[...]
    lane = lax.broadcasted_iota(jnp.int32, cos_ref.shape, 1)
    cos_ref[...] = jnp.cos(angle)
    sine = jnp.sin(angle)
    sin_ref[...] = jnp.where(lane < cos_ref.shape[1] // 2, -sine, sine)
    for copy in copies:
        copy.wait()
    at = 0
    for weight in (q_weight, kv_weight):
        to = at + weight.shape[1]
        own_ref[:, at:to] = jnp.dot(
            normed[...], weight[...], preferred_element_type=jnp.float32
        )
        at = to


def capped(scores):
    return jnp.exp2(jnp.tanh(scores * (1.0 / softcap)) * (softcap * math.log2(math.e)))


def attend_kernel(
    groups,
    kv_local,
    head_dim,
    where_ref,
    own,
    other_ref,
    cos_ref,
    sin_ref,
    valid_ref,
    *refs,
):
    p = where_ref[0]
    page_refs, out_refs = refs[:2], refs[2 : 2 + groups]
    keys, values, result, other, pages, sems = refs[2 + groups :]
    copies = [pltpu.make_async_copy(other_ref, other, sems.at[0])]
    for index, ref in enumerate(page_refs):
        lines = pl.ds(index * ref.shape[1], ref.shape[1])
        copies.append(
            pltpu.make_async_copy(ref, pages.at[:, lines, :], sems.at[1 + index])
        )
    for copy in copies:
        copy.start()
    new_len, q_cols = result.shape
    group = q_cols // (kv_local * head_dim)

    def sums(at):
        return own[:, at : at + head_dim] + other[:, at : at + head_dim].astype(jnp.float32)

    cosine, sine = cos_ref[...], sin_ref[...]

    def rope(vectors):
        return vectors * cosine + pltpu.roll(vectors, head_dim // 2, 1) * sine

    span = pages.shape[1]
    per = span // kv_local
    row = lax.broadcasted_iota(jnp.int32, (span, span), 0)
    column = lax.broadcasted_iota(jnp.int32, (span, span), 1)
    part = (column == (row % per) * kv_local + row // per).astype(jnp.bfloat16)
    place_at = 0
    for copy in copies[1:]:
        copy.wait()
    for holder in range(pages.shape[0]):
        parted = jnp.dot(part, pages[holder], preferred_element_type=jnp.float32)
        parted = parted.astype(jnp.bfloat16)
        for g in range(kv_local):
            lines = parted[g * per : (g + 1) * per]
            keys[g, place_at : place_at + per, :] = lines[:, :head_dim]
            values[g, place_at : place_at + per, :] = lines[:, head_dim:]
        place_at += per

    copies[0].wait()
    span_keys = 2 * per
    t = lax.broadcasted_iota(jnp.int32, (group * new_len, new_len), 0) % new_len
    s = lax.broadcasted_iota(jnp.int32, (group * new_len, new_len), 1)
    causal = s <= t
    for g in range(kv_local):
        heads = [
            (rope(sums((g * group + j) * head_dim)) * query_scale).astype(jnp.bfloat16)
            for j in range(group)
        ]
        queries = jnp.concatenate(heads, axis=0)
        at = q_cols + g * head_dim
        new_key = rope(sums(at)).astype(jnp.bfloat16)
        new_value = sums(at + kv_local * head_dim).astype(jnp.bfloat16)

        def scores_of(key):
            return lax.dot_general(
                queries, key, (((1,), (1,)), ((), ())), preferred_element_type=jnp.float32
            )

        weights = jnp.where(causal, capped(scores_of(new_key)), 0.0)
        denom = jnp.sum(weights, axis=1, keepdims=True)
        numer = jnp.dot(
            weights.astype(jnp.bfloat16), new_value, preferred_element_type=jnp.float32
        )
        for start in range(0, place_at, span_keys):
            at = start // per
            valid = jnp.concatenate([valid_ref[at : at + 1], valid_ref[at + 1 : at + 2]], axis=1)
            valid = valid > 0.0
            weights = jnp.where(
                valid, capped(scores_of(keys[g, start : start + span_keys, :])), 0.0
            )
            denom = denom + jnp.sum(weights, axis=1, keepdims=True)
            numer = numer + jnp.dot(
                weights.astype(jnp.bfloat16),
                values[g, start : start + span_keys, :],
                preferred_element_type=jnp.float32,
            )
        attended = (numer / denom).astype(jnp.bfloat16)
        for j in range(group):
            to = (g * group + j) * head_dim
            result[:, to : to + head_dim] = attended[j * new_len : (j + 1) * new_len]
    quarter = new_len // groups
    for distance, ref in enumerate(out_refs):
        start = pl.multiple_of((p ^ distance) * quarter, quarter)
        ref[...] = result[pl.ds(start, quarter), :]


def output_kernel(groups, shards, where_ref, *refs):
    p, f = where_ref[0], where_ref[1]
    token_refs = refs[:shards]
    weight_ref = refs[shards]
    out_refs = refs[shards + 1 : 2 * shards + 1]
    (total,) = refs[2 * shards + 1 :]
    quarter = token_refs[0].shape[1]
    sub = quarter // shards
    projected = None
    for distance in range(groups):
        rows = jnp.concatenate([ref[distance] for ref in token_refs], axis=0)
        term = lax.dot_general(
            rows,
            weight_ref[p ^ distance],
            (((1,), (1,)), ((), ())),
            preferred_element_type=jnp.float32,
        )
        projected = term if projected is None else projected + term
    total[...] = projected
    for e in range(shards):
        for distance, ref in enumerate(out_refs):
            start = pl.multiple_of(e * quarter + (f ^ distance) * sub, sub)
            ref[f ^ e] = total[pl.ds(start, sub), :].astype(jnp.bfloat16)


def finish_kernel(shards, where_ref, gain_ref, residual_ref, *refs):
    f = where_ref[1]
    piece_refs = refs[:shards]
    out_ref, projected = refs[shards:]
    for distance, ref in enumerate(piece_refs):
        projected[f ^ distance] = ref[...].astype(jnp.float32)
    gain = gain_ref[...]
    for request in range(out_ref.shape[0]):
        slot = where_ref[3 + request]
        line = jnp.concatenate([projected[k, slot] for k in range(shards)], axis=1)
        mean_square = jnp.mean(line * line, axis=1, keepdims=True)
        line = line * lax.rsqrt(mean_square + norm_eps) * gain
        out_ref[request] = (residual_ref[slot].astype(jnp.float32) + line).astype(jnp.bfloat16)


def pool_pieces(block, groups):
    return [block] + [swap(block, "pool", distance) for distance in range(1, groups)]


def local_small(
    hidden,
    slot_of_request,
    prefix_len,
    block_holder,
    block_slot,
    kv_pool,
    norm_gain,
    q_weight,
    k_weight,
    v_weight,
    o_weight,
    post_gain,
):
    shards = lax.axis_size("fsdp")
    groups = lax.axis_size("pool")
    f = lax.axis_index("fsdp")
    p = lax.axis_index("pool")
    half = shards // 2
    side = f // half
    new_len, width = hidden.shape[1:]
    requests = slot_of_request.shape[0]
    page_len = kv_pool.shape[1]
    kv_local = kv_pool.shape[2]
    head_dim = kv_pool.shape[3] // 2
    q_cols = q_weight.shape[1]
    kv_cols = k_weight.shape[1]
    max_blocks = block_holder.shape[1]
    per_holder = max_blocks // shards
    quarter = new_len // groups
    sub = quarter // shards
    features = o_weight.shape[0]
    bf16, f32 = jnp.bfloat16, jnp.float32
    where = jnp.concatenate(
        [jnp.stack([p, f, side]).astype(jnp.int32), slot_of_request, prefix_len]
    )
    shape = jax.ShapeDtypeStruct
    gain = norm_gain.reshape(1, width)
    rows = hidden[0]

    leaving, my_quarter, kv_weight = call(
        prologue_kernel,
        [
            shape((quarter, width // 2), bf16),
            shape((quarter, width), bf16),
            shape((features, 2 * kv_cols), bf16),
        ],
        [pltpu.VMEM((quarter, width), f32), pltpu.SemaphoreType.DMA],
        quarter * width * 8,
        4 * features * kv_cols,
        rows,
        norm_gain,
        k_weight,
        v_weight,
        specs=[HBM, VMEM, VMEM, VMEM],
    )
    partner_piece = swap(leaving, "fsdp", half)

    flat_pool = kv_pool.reshape(kv_pool.shape[0], page_len * kv_local, 2 * head_dim)
    page_rows = per_holder * page_len * kv_local
    first_pages, second_pages, valid = call(
        functools.partial(pages_kernel, requests, page_len),
        [
            shape((shards, page_rows // 2, 2 * head_dim), bf16),
            shape((shards, page_rows // 2, 2 * head_dim), bf16),
            shape((shards, per_holder * page_len), f32),
        ],
        [
            pltpu.SMEM((2 * per_holder,), jnp.int32),
            pltpu.SMEM((max_blocks + per_holder,), jnp.int32),
            pltpu.SMEM((shards,), jnp.int32),
        ],
        1 << 20,
        1 << 21,
        where,
        block_holder,
        block_slot,
        flat_pool,
        specs=[SMEM, SMEM, SMEM, VMEM],
    )
    q_near, q_far = swap(q_weight, "fsdp", 1), swap(q_weight, "fsdp", 2)
    kv_near = swap(kv_weight, "fsdp", 1)
    partner_piece, q_near, q_far, kv_near, first_pages, second_pages, valid = (
        lax.optimization_barrier(
            (partner_piece, q_near, q_far, kv_near, first_pages, second_pages, valid)
        )
    )
    kv_far = swap(after(kv_weight, partner_piece), "fsdp", 2)
    partner_pieces = pool_pieces(partner_piece, groups)
    arrived = lax.all_to_all(first_pages, "fsdp", split_axis=0, concat_axis=0, tiled=True)
    partner_pieces, kv_far, arrived = lax.optimization_barrier((partner_pieces, kv_far, arrived))
    arrived = [arrived]
    weights = [q_weight, q_near, q_far, swap(q_far, "fsdp", 1)]
    weights += [kv_weight, kv_near, kv_far, swap(kv_far, "fsdp", 1)]
    arrived.append(
        lax.all_to_all(
            after(second_pages, kv_far), "fsdp", split_axis=0, concat_axis=0, tiled=True
        )
    )
    out_weight = lax.all_gather(after(o_weight, *partner_pieces), "pool", axis=0, tiled=False)

    partial = call(
        functools.partial(partner_kernel, groups, half),
        shape((new_len, q_cols + 2 * kv_cols), bf16),
        [
            pltpu.VMEM((new_len, width // 2), bf16),
            pltpu.VMEM((width // 2, q_cols), bf16),
            pltpu.VMEM((width // 2, 2 * kv_cols), bf16),
            pltpu.SemaphoreType.DMA((groups,)),
            pltpu.SemaphoreType.DMA((2 * half,)),
        ],
        new_len * width * (q_cols + 2 * kv_cols),
        width * (new_len + q_cols + 2 * kv_cols),
        where,
        *partner_pieces,
        *weights,
        specs=[SMEM] + [HBM] * (groups + 2 * half),
    )
    other = swap(partial, "fsdp", half)
    freqs = np.exp(np.arange(head_dim // 2) * (-2.0 * math.log(10000.0) / head_dim))
    freqs = np.concatenate([freqs, freqs]).astype(np.float32).reshape(1, head_dim)
    own, cosine, sine = call(
        functools.partial(own_kernel, requests, half),
        [
            shape((new_len, q_cols + 2 * kv_cols), f32),
            shape((new_len, head_dim), f32),
            shape((new_len, head_dim), f32),
        ],
        [
            pltpu.VMEM((new_len, width), bf16),
            pltpu.VMEM((new_len, width // 2), bf16),
            pltpu.VMEM((width // 2, q_cols), bf16),
            pltpu.VMEM((width // 2, 2 * kv_cols), bf16),
            pltpu.SemaphoreType.DMA((2 * half + 1,)),
        ],
        new_len * width * (q_cols + 2 * kv_cols),
        width * (2 * new_len + q_cols + 2 * kv_cols),
        where,
        after(rows, partial),
        gain,
        freqs,
        *weights,
        specs=[SMEM, HBM, VMEM, VMEM] + [HBM] * (2 * half),
    )

    residual = lax.all_to_all(
        after(my_quarter, own, other, *arrived).reshape(shards, sub, width),
        "fsdp",
        split_axis=0,
        concat_axis=0,
        tiled=True,
    )

    keys_total = max_blocks * page_len
    quarters = call(
        functools.partial(attend_kernel, groups, kv_local, head_dim),
        [shape((quarter, q_cols), bf16)] * groups,
        [
            pltpu.VMEM((kv_local, keys_total, head_dim), bf16),
            pltpu.VMEM((kv_local, keys_total, head_dim), bf16),
            pltpu.VMEM((new_len, q_cols), bf16),
            pltpu.VMEM(other.shape, bf16),
            pltpu.VMEM((shards, page_rows, 2 * head_dim), bf16),
            pltpu.SemaphoreType.DMA((3,)),
        ],
        4 * new_len * q_cols * (keys_total + new_len),
        1 << 22,
        where,
        own,
        other,
        cosine,
        sine,
        valid,
        *arrived,
        specs=[SMEM, VMEM, HBM, VMEM, VMEM, VMEM, HBM, HBM],
    )

    quarters = [
        swap(piece, "pool", distance) if distance else piece
        for distance, piece in enumerate(quarters)
    ]
    quarters = jnp.stack(quarters)
    tokens = {0: quarters}
    for distance in range(2, shards, 2):
        tokens[distance] = swap(quarters, "fsdp", distance)
    for distance in range(0, shards, 2):
        tokens[distance ^ 1] = swap(tokens[distance], "fsdp", 1)
    projected = call(
        functools.partial(output_kernel, groups, shards),
        [shape((shards, sub, features), bf16)] * shards,
        [
            pltpu.VMEM((shards * quarter, features), f32),
        ],
        2 * shards * quarter * features * groups * q_cols,
        1 << 22,
        where,
        *[tokens[distance] for distance in range(shards)],
        out_weight,
        mib=24,
    )
    finished = [
        swap(piece, "fsdp", distance) if distance else piece
        for distance, piece in enumerate(projected)
    ]
    return call(
        functools.partial(finish_kernel, shards),
        shape((requests, sub, width), bf16),
        [pltpu.VMEM((shards, shards, sub, features), f32)],
        1 << 20,
        1 << 20,
        where,
        post_gain.reshape(1, width),
        residual,
        *finished,
        mib=24,
    )


def local(*arguments):
    return local_small(*arguments) if lax.axis_size("fsdp") == 8 else local_general(*arguments)


def solution(mesh):
    in_specs = (
        P("fsdp", None, None),
        P(),
        P(),
        P(),
        P(),
        P("fsdp", None, "pool", None),
        P(),
        P("fsdp", "pool"),
        P("fsdp", "pool"),
        P("fsdp", "pool"),
        P("fsdp", "pool"),
        P(),
    )
    out_specs = P(None, ("pool", "fsdp"), None)
    return jax.shard_map(local, mesh=mesh, in_specs=in_specs, out_specs=out_specs, check_vma=False)
```

```python
import functools
import math

import jax
import jax.numpy as jnp
import numpy as np
from jax import lax
from jax.experimental import pallas as pl
from jax.experimental.pallas import tpu as pltpu
from jax.sharding import PartitionSpec as P

softcap = 50.0
query_scale = 144.0 ** (-0.5)
norm_eps = 1e-06


def rms_scale(rows, gain):
    mean_square = jnp.mean(rows * rows, axis=-1, keepdims=True)
    return rows * lax.rsqrt(mean_square + norm_eps) * gain


def rotate(vectors, cosine, sine):
    half = vectors.shape[-1] // 2
    first = vectors[..., :half]
    second = vectors[..., half:]
    return jnp.concatenate(
        [first * cosine - second * sine, second * cosine + first * sine], axis=-1
    )


def capped_weights(scores, valid):
    return jnp.where(valid, jnp.exp(softcap * jnp.tanh(scores / softcap)), 0.0)


def swap(array, axis, distance):
    size = lax.axis_size(axis)
    return lax.ppermute(array, axis, [(i, i ^ distance) for i in range(size)])


def place(pieces, index):
    first = pieces[0]
    stacked = jnp.zeros((len(pieces),) + first.shape, first.dtype)
    for distance, piece in pieces.items():
        stacked = lax.dynamic_update_index_in_dim(stacked, piece, index ^ distance, 0)
    return stacked


def exchange(chunks, axis):
    size = lax.axis_size(axis)
    index = lax.axis_index(axis)
    if size > 8:
        return lax.all_to_all(chunks, axis, split_axis=0, concat_axis=0, tiled=True)
    pieces = {}
    for distance in range(size):
        chunk = lax.dynamic_index_in_dim(chunks, index ^ distance, 0, keepdims=False)
        pieces[distance] = swap(chunk, axis, distance) if distance else chunk
    return place(pieces, index)


def doubled(block, axis, span):
    pieces = {0: block}
    bit = span // 2
    while bit:
        for distance in list(pieces):
            pieces[distance ^ bit] = swap(pieces[distance], axis, bit)
        bit //= 2
    return pieces


def attend(queries, keys_new, values_new, cached, cached_valid):
    new_len, kv_local, group, head_dim = queries.shape

    def part(keys, values, valid):
        scores = jnp.einsum("tgjd,kgd->gjtk", queries, keys, preferred_element_type=jnp.float32)
        weights = capped_weights(scores, valid)
        numer = jnp.einsum(
            "gjtk,kgd->gjtd",
            weights.astype(jnp.bfloat16),
            values,
            preferred_element_type=jnp.float32,
        )
        return numer, jnp.sum(weights, axis=-1)

    query_index = jnp.arange(new_len, dtype=jnp.int32)
    causal = query_index[None, :] <= query_index[:, None]
    numer, denom = part(
        cached[..., :head_dim], cached[..., head_dim:], cached_valid[None, None, None, :]
    )
    more, added = part(keys_new, values_new, causal[None, None])
    attended = ((numer + more) / (denom + added)[..., None]).transpose(2, 0, 1, 3)
    return attended.reshape(new_len, kv_local * group * head_dim).astype(jnp.bfloat16)


def local_general(
    hidden,
    slot_of_request,
    prefix_len,
    block_holder,
    block_slot,
    kv_pool,
    norm_gain,
    q_weight,
    k_weight,
    v_weight,
    o_weight,
    post_gain,
):
    shards = lax.axis_size("fsdp")
    groups = lax.axis_size("pool")
    f = lax.axis_index("fsdp")
    p = lax.axis_index("pool")
    half = shards // 2
    side = f // half
    new_len, width = hidden.shape[1:]
    requests = slot_of_request.shape[0]
    page_len = kv_pool.shape[1]
    kv_local = kv_pool.shape[2]
    head_dim = kv_pool.shape[3] // 2
    q_cols = q_weight.shape[1]
    kv_cols = k_weight.shape[1]
    group = q_cols // kv_cols
    max_blocks = block_holder.shape[1]
    per_holder = max_blocks // shards
    quarter = new_len // groups
    sub = quarter // shards
    features = o_weight.shape[0]

    kv_pieces = doubled(jnp.concatenate([k_weight, v_weight], axis=1), "fsdp", half)
    q_pieces = doubled(q_weight, "fsdp", half)
    out_weight = lax.all_gather(o_weight, "pool", axis=0, tiled=False)

    rows = hidden[0]
    normed = rms_scale(rows.astype(jnp.float32), norm_gain).astype(jnp.bfloat16)
    own_rows = lax.dynamic_slice(normed, (0, side * (width // 2)), (new_len, width // 2))
    leaving = lax.dynamic_slice(
        normed, (p * quarter, (1 - side) * (width // 2)), (quarter, width // 2)
    )
    partner_piece = swap(leaving, "fsdp", half)
    partner_pieces = {0: partner_piece}
    for distance in range(1, groups):
        partner_pieces[distance] = swap(partner_piece, "pool", distance)
    partner_rows = place(partner_pieces, p).reshape(new_len, width // 2)

    request_ids = jnp.arange(requests, dtype=jnp.int32)
    request_at_slot = jnp.sum(
        jnp.where(slot_of_request[None, :] == request_ids[:, None], request_ids[None, :], 0), axis=1
    )
    holder_by_slot = jnp.take(block_holder, request_at_slot, axis=0)
    page_by_slot = jnp.take(block_slot, request_at_slot, axis=0)
    held_here = holder_by_slot == f
    held_rank = jnp.cumsum(held_here.astype(jnp.int32), axis=1) - 1
    rank_ids = jnp.arange(per_holder, dtype=jnp.int32)
    picked = held_here[:, :, None] & (held_rank[:, :, None] == rank_ids[None, None, :])
    local_pages = jnp.sum(jnp.where(picked, page_by_slot[:, :, None], 0), axis=1)
    flat_pool = kv_pool.reshape(kv_pool.shape[0], page_len * kv_local, 2 * head_dim)
    outgoing = jnp.take(flat_pool, local_pages, axis=0)
    outgoing = outgoing.reshape(shards, per_holder * page_len * kv_local, 2 * head_dim)
    arrived = exchange(outgoing, "fsdp")
    cached = arrived.reshape(max_blocks * page_len, kv_local, 2 * head_dim)

    my_request = lax.dynamic_index_in_dim(request_at_slot, f, keepdims=False)
    my_length = prefix_len[my_request]
    my_holders = block_holder[my_request]
    entry_ids = jnp.arange(max_blocks, dtype=jnp.int32)
    mine = my_holders[None, :] == jnp.arange(shards, dtype=jnp.int32)[:, None]
    my_rank = jnp.cumsum(mine.astype(jnp.int32), axis=1) - 1
    chosen = mine[:, None, :] & (my_rank[:, None, :] == rank_ids[None, :, None])
    entry = jnp.sum(jnp.where(chosen, entry_ids[None, None, :], 0), axis=2)
    cached_position = entry.reshape(-1, 1) * page_len + jnp.arange(page_len, dtype=jnp.int32)
    cached_valid = (cached_position < my_length).reshape(-1)

    residual_out = lax.dynamic_slice_in_dim(rows, p * quarter, quarter, 0).reshape(
        shards, sub, width
    )
    residual = exchange(residual_out, "fsdp")

    positions = (my_length + jnp.arange(new_len, dtype=jnp.int32)).astype(jnp.float32)
    freqs = jnp.exp(
        jnp.arange(head_dim // 2, dtype=jnp.float32) * (-2.0 * math.log(10000.0) / head_dim)
    )
    angles = positions[:, None] * freqs
    cosine = jnp.cos(angles)[:, None, :]
    sine = jnp.sin(angles)[:, None, :]

    def project(pieces):
        weight = place(pieces, f % half).reshape(width // 2, -1)
        partial = jnp.dot(partner_rows, weight, preferred_element_type=jnp.float32)
        other = swap(partial.astype(jnp.bfloat16), "fsdp", half)
        own = jnp.dot(own_rows, weight, preferred_element_type=jnp.float32)
        return own + other.astype(jnp.float32)

    kv_sum = project(kv_pieces)
    q_sum = project(q_pieces)
    queries = rotate(q_sum.reshape(new_len, kv_local * group, head_dim), cosine, sine)
    queries = (queries * query_scale).astype(jnp.bfloat16)
    queries = queries.reshape(new_len, kv_local, group, head_dim)
    keys_new = kv_sum[:, :kv_cols].reshape(new_len, kv_local, head_dim)
    keys_new = rotate(keys_new, cosine, sine).astype(jnp.bfloat16)
    values_new = kv_sum[:, kv_cols:].astype(jnp.bfloat16).reshape(new_len, kv_local, head_dim)
    attended = attend(queries, keys_new, values_new, cached, cached_valid)

    quarters = exchange(attended.reshape(groups, quarter, q_cols), "pool")
    token_pieces = {0: quarters}
    for distance in range(2, shards, 2):
        token_pieces[distance] = swap(quarters, "fsdp", distance)
    for distance in range(0, shards, 2):
        token_pieces[distance ^ 1] = swap(token_pieces[distance], "fsdp", 1)
    tokens = place(token_pieces, f)
    projected = jnp.einsum(
        "sptc,pfc->stf", tokens, out_weight, preferred_element_type=jnp.float32
    ).astype(jnp.bfloat16)
    projected = projected.reshape(shards, shards, sub, features).transpose(1, 0, 2, 3)
    finished = exchange(projected, "fsdp").transpose(1, 2, 0, 3).reshape(shards, sub, width)
    finished = residual.astype(jnp.float32) + rms_scale(finished.astype(jnp.float32), post_gain)
    return jnp.take(finished.astype(jnp.bfloat16), slot_of_request, axis=0)


VMEM = pl.BlockSpec(memory_space=pltpu.VMEM)
SMEM = pl.BlockSpec(memory_space=pltpu.SMEM)
HBM = pl.BlockSpec(memory_space=pltpu.HBM)


def call(kernel, outs, scratch, flops, nbytes, *operands, specs=None, out_specs=None, mib=60):
    return pl.pallas_call(
        kernel,
        out_shape=outs,
        in_specs=specs or [SMEM] + [VMEM] * (len(operands) - 1),
        out_specs=out_specs or jax.tree.map(lambda _: VMEM, outs),
        scratch_shapes=scratch,
        compiler_params=pltpu.CompilerParams(vmem_limit_bytes=mib << 20),
        cost_estimate=pl.CostEstimate(flops=flops, bytes_accessed=nbytes, transcendentals=0),
    )(*operands)


def after(array, *earlier):
    return lax.optimization_barrier((array,) + earlier)[0]


def weight_copies(weight_refs, weight, f, half, sems):
    copies = []
    for distance, ref in enumerate(weight_refs):
        count = ref.shape[0]
        start = pl.multiple_of(((f ^ distance) & (half - 1)) * count, 64)
        copies.append(
            pltpu.make_async_copy(ref, weight.at[pl.ds(start, count), :], sems.at[distance])
        )
        copies[-1].start()
    return copies


def partner_kernel(groups, half, where_ref, *refs):
    p, f = where_ref[0], where_ref[1]
    x_refs, refs = refs[:groups], refs[groups:]
    out_ref, rows, q_weight, kv_weight, x_sems, w_sems = refs[2 * half :]
    quarter = x_refs[0].shape[0]
    copies = weight_copies(refs[:half], q_weight, f, half, w_sems.at[:half])
    copies += weight_copies(refs[half : 2 * half], kv_weight, f, half, w_sems.at[half:])
    for distance, ref in enumerate(x_refs):
        start = pl.multiple_of((p ^ distance) * quarter, quarter)
        copies.append(
            pltpu.make_async_copy(ref, rows.at[pl.ds(start, quarter), :], x_sems.at[distance])
        )
        copies[-1].start()
    for copy in copies:
        copy.wait()
    at = 0
    for weight in (q_weight, kv_weight):
        to = at + weight.shape[1]
        out_ref[:, at:to] = jnp.dot(
            rows[...], weight[...], preferred_element_type=jnp.float32
        ).astype(jnp.bfloat16)
        at = to


def row_scale(rows):
    return lax.rsqrt(jnp.mean(rows * rows, axis=1, keepdims=True) + norm_eps)


def prologue_kernel(
    hidden_ref, gain_ref, k_ref, v_ref, leaving_ref, rows_ref, weight_ref, normed, sem
):
    p, f = lax.axis_index("pool"), lax.axis_index("fsdp")
    side = f // (lax.axis_size("fsdp") // 2)
    quarter, width = rows_ref.shape
    half_width = width // 2
    start = pl.multiple_of(p * quarter, quarter)
    rows_copy = pltpu.make_async_copy(hidden_ref.at[pl.ds(start, quarter), :], rows_ref, sem)
    rows_copy.start()
    at = 0
    for ref in (k_ref, v_ref):
        weight_ref[:, at : at + ref.shape[1]] = ref[...]
        at += ref.shape[1]
    rows_copy.wait()
    rows = rows_ref[...].astype(jnp.float32)
    normed[...] = rows * row_scale(rows) * gain_ref[...].reshape(1, width)
    away = pl.multiple_of((1 - side) * half_width, 128)
    leaving_ref[...] = normed[:, pl.ds(away, half_width)].astype(jnp.bfloat16)


def pages_kernel(
    requests, page_len, where_ref, holder_ref, slot_ref, pool_ref, *refs
):
    f = where_ref[1]
    *out_refs, valid_ref, listed, entries, counts = refs
    max_blocks = holder_ref.shape[1]
    shards = out_refs[0].shape[0]
    per = max_blocks // shards
    each = per // len(out_refs)
    page_rows = pool_ref.shape[1]
    length, mine = jnp.int32(0), jnp.int32(0)
    for r in range(requests):
        at = where_ref[3 + r] == f
        length = length + jnp.where(at, where_ref[3 + requests + r], 0)
        mine = mine + jnp.where(at, r, 0)
    for r in range(requests):
        slot = where_ref[3 + r]

        def note(j, count):
            listed[count] = slot_ref[r, j]
            return count + jnp.where(holder_ref[r, j] == f, 1, 0)

        lax.fori_loop(0, max_blocks, note, jnp.int32(0), unroll=8)
        for k in range(per):
            at = k % each * page_rows
            out_refs[k // each][slot, at : at + page_rows, :] = pool_ref[listed[k]]
    for h in range(shards):
        counts[h] = 0

    def enter(j, carry):
        h = holder_ref[mine, j]
        count = counts[h]
        entries[h * per + count] = j
        counts[h] = count + 1
        return carry

    lax.fori_loop(0, max_blocks, enter, 0, unroll=4)
    row = lax.broadcasted_iota(jnp.int32, valid_ref.shape, 0)
    lane = lax.broadcasted_iota(jnp.int32, valid_ref.shape, 1)
    place_in = row * per + lane // page_len
    entry = jnp.zeros(valid_ref.shape, jnp.int32)
    for at in range(max_blocks):
        entry = jnp.where(place_in == at, entries[at], entry)
    position = entry * page_len + lane % page_len
    valid_ref[...] = jnp.where(position < length, 1.0, 0.0)


def own_kernel(requests, half, where_ref, hidden_ref, gain_ref, freq_ref, *refs):
    f = where_ref[1]
    own_ref, cos_ref, sin_ref, hidden, normed, q_weight, kv_weight, sems = refs[2 * half :]
    rows_copy = pltpu.make_async_copy(hidden_ref, hidden, sems.at[2 * half])
    rows_copy.start()
    copies = weight_copies(refs[:half], q_weight, f, half, sems.at[:half])
    copies += weight_copies(refs[half : 2 * half], kv_weight, f, half, sems.at[half : 2 * half])
    rows_copy.wait()
    new_len, width = hidden_ref.shape
    half_width = width // 2
    length = jnp.int32(0)
    for r in range(requests):
        length = length + jnp.where(where_ref[3 + r] == f, where_ref[3 + requests + r], 0)
    start = pl.multiple_of(where_ref[2] * half_width, 128)
    gain = gain_ref[:, pl.ds(start, half_width)]
    step = 32

    def norm(index, carry):
        at = pl.multiple_of(index * step, step)
        rows = hidden[pl.ds(at, step), :].astype(jnp.float32)
        scale = row_scale(rows)
        part = hidden[pl.ds(at, step), pl.ds(start, half_width)].astype(jnp.float32)
        normed[pl.ds(at, step), :] = (part * scale * gain).astype(jnp.bfloat16)
        return carry

    lax.fori_loop(0, new_len // step, norm, 0)
    position = lax.broadcasted_iota(jnp.int32, cos_ref.shape, 0) + length
    angle = position.astype(jnp.float32) * freq_ref[...]
    lane = lax.broadcasted_iota(jnp.int32, cos_ref.shape, 1)
    cos_ref[...] = jnp.cos(angle)
    sine = jnp.sin(angle)
    sin_ref[...] = jnp.where(lane < cos_ref.shape[1] // 2, -sine, sine)
    for copy in copies:
        copy.wait()
    at = 0
    for weight in (q_weight, kv_weight):
        to = at + weight.shape[1]
        own_ref[:, at:to] = jnp.dot(
            normed[...], weight[...], preferred_element_type=jnp.float32
        )
        at = to


def capped(scores):
    return jnp.exp2(jnp.tanh(scores * (1.0 / softcap)) * (softcap * math.log2(math.e)))


def attend_kernel(
    groups,
    kv_local,
    head_dim,
    where_ref,
    own,
    other_ref,
    cos_ref,
    sin_ref,
    valid_ref,
    *refs,
):
    p = where_ref[0]
    page_refs, out_refs = refs[:2], refs[2 : 2 + groups]
    keys, values, result, other, pages, sems = refs[2 + groups :]
    copies = [pltpu.make_async_copy(other_ref, other, sems.at[0])]
    for index, ref in enumerate(page_refs):
        lines = pl.ds(index * ref.shape[1], ref.shape[1])
        copies.append(
            pltpu.make_async_copy(ref, pages.at[:, lines, :], sems.at[1 + index])
        )
    for copy in copies:
        copy.start()
    new_len, q_cols = result.shape
    group = q_cols // (kv_local * head_dim)

    def sums(at):
        return own[:, at : at + head_dim] + other[:, at : at + head_dim].astype(jnp.float32)

    cosine, sine = cos_ref[...], sin_ref[...]

    def rope(vectors):
        return vectors * cosine + pltpu.roll(vectors, head_dim // 2, 1) * sine

    span = pages.shape[1]
    per = span // kv_local
    row = lax.broadcasted_iota(jnp.int32, (span, span), 0)
    column = lax.broadcasted_iota(jnp.int32, (span, span), 1)
    part = (column == (row % per) * kv_local + row // per).astype(jnp.bfloat16)
    place_at = 0
    for copy in copies[1:]:
        copy.wait()
    for holder in range(pages.shape[0]):
        parted = jnp.dot(part, pages[holder], preferred_element_type=jnp.float32)
        parted = parted.astype(jnp.bfloat16)
        for g in range(kv_local):
            lines = parted[g * per : (g + 1) * per]
            keys[g, place_at : place_at + per, :] = lines[:, :head_dim]
            values[g, place_at : place_at + per, :] = lines[:, head_dim:]
        place_at += per

    copies[0].wait()
    span_keys = 2 * per
    t = lax.broadcasted_iota(jnp.int32, (group * new_len, new_len), 0) % new_len
    s = lax.broadcasted_iota(jnp.int32, (group * new_len, new_len), 1)
    causal = s <= t
    for g in range(kv_local):
        heads = [
            (rope(sums((g * group + j) * head_dim)) * query_scale).astype(jnp.bfloat16)
            for j in range(group)
        ]
        queries = jnp.concatenate(heads, axis=0)
        at = q_cols + g * head_dim
        new_key = rope(sums(at)).astype(jnp.bfloat16)
        new_value = sums(at + kv_local * head_dim).astype(jnp.bfloat16)

        def scores_of(key):
            return lax.dot_general(
                queries, key, (((1,), (1,)), ((), ())), preferred_element_type=jnp.float32
            )

        weights = jnp.where(causal, capped(scores_of(new_key)), 0.0)
        denom = jnp.sum(weights, axis=1, keepdims=True)
        numer = jnp.dot(
            weights.astype(jnp.bfloat16), new_value, preferred_element_type=jnp.float32
        )
        for start in range(0, place_at, span_keys):
            at = start // per
            valid = jnp.concatenate([valid_ref[at : at + 1], valid_ref[at + 1 : at + 2]], axis=1)
            valid = valid > 0.0
            weights = jnp.where(
                valid, capped(scores_of(keys[g, start : start + span_keys, :])), 0.0
            )
            denom = denom + jnp.sum(weights, axis=1, keepdims=True)
            numer = numer + jnp.dot(
                weights.astype(jnp.bfloat16),
                values[g, start : start + span_keys, :],
                preferred_element_type=jnp.float32,
            )
        attended = (numer / denom).astype(jnp.bfloat16)
        for j in range(group):
            to = (g * group + j) * head_dim
            result[:, to : to + head_dim] = attended[j * new_len : (j + 1) * new_len]
    quarter = new_len // groups
    for distance, ref in enumerate(out_refs):
        start = pl.multiple_of((p ^ distance) * quarter, quarter)
        ref[...] = result[pl.ds(start, quarter), :]


def output_kernel(groups, shards, where_ref, *refs):
    p, f = where_ref[0], where_ref[1]
    token_refs = refs[:shards]
    weight_ref = refs[shards]
    out_refs = refs[shards + 1 : 2 * shards + 1]
    (total,) = refs[2 * shards + 1 :]
    quarter = token_refs[0].shape[1]
    sub = quarter // shards
    projected = None
    for distance in range(groups):
        rows = jnp.concatenate([ref[distance] for ref in token_refs], axis=0)
        term = lax.dot_general(
            rows,
            weight_ref[p ^ distance],
            (((1,), (1,)), ((), ())),
            preferred_element_type=jnp.float32,
        )
        projected = term if projected is None else projected + term
    total[...] = projected
    for e in range(shards):
        for distance, ref in enumerate(out_refs):
            start = pl.multiple_of(e * quarter + (f ^ distance) * sub, sub)
            ref[f ^ e] = total[pl.ds(start, sub), :].astype(jnp.bfloat16)


def finish_kernel(shards, where_ref, gain_ref, residual_ref, *refs):
    f = where_ref[1]
    piece_refs = refs[:shards]
    out_ref, projected = refs[shards:]
    for distance, ref in enumerate(piece_refs):
        projected[f ^ distance] = ref[...].astype(jnp.float32)
    gain = gain_ref[...]
    for request in range(out_ref.shape[0]):
        slot = where_ref[3 + request]
        line = jnp.concatenate([projected[k, slot] for k in range(shards)], axis=1)
        mean_square = jnp.mean(line * line, axis=1, keepdims=True)
        line = line * lax.rsqrt(mean_square + norm_eps) * gain
        out_ref[request] = (residual_ref[slot].astype(jnp.float32) + line).astype(jnp.bfloat16)


def pool_pieces(block, groups):
    return [block] + [swap(block, "pool", distance) for distance in range(1, groups)]


def local_small(
    hidden,
    slot_of_request,
    prefix_len,
    block_holder,
    block_slot,
    kv_pool,
    norm_gain,
    q_weight,
    k_weight,
    v_weight,
    o_weight,
    post_gain,
):
    shards = lax.axis_size("fsdp")
    groups = lax.axis_size("pool")
    f = lax.axis_index("fsdp")
    p = lax.axis_index("pool")
    half = shards // 2
    side = f // half
    new_len, width = hidden.shape[1:]
    requests = slot_of_request.shape[0]
    page_len = kv_pool.shape[1]
    kv_local = kv_pool.shape[2]
    head_dim = kv_pool.shape[3] // 2
    q_cols = q_weight.shape[1]
    kv_cols = k_weight.shape[1]
    max_blocks = block_holder.shape[1]
    per_holder = max_blocks // shards
    quarter = new_len // groups
    sub = quarter // shards
    features = o_weight.shape[0]
    bf16, f32 = jnp.bfloat16, jnp.float32
    where = jnp.concatenate(
        [jnp.stack([p, f, side]).astype(jnp.int32), slot_of_request, prefix_len]
    )
    shape = jax.ShapeDtypeStruct
    gain = norm_gain.reshape(1, width)
    rows = hidden[0]

    leaving, my_quarter, kv_weight = call(
        prologue_kernel,
        [
            shape((quarter, width // 2), bf16),
            shape((quarter, width), bf16),
            shape((features, 2 * kv_cols), bf16),
        ],
        [pltpu.VMEM((quarter, width), f32), pltpu.SemaphoreType.DMA],
        quarter * width * 8,
        4 * features * kv_cols,
        rows,
        norm_gain,
        k_weight,
        v_weight,
        specs=[HBM, VMEM, VMEM, VMEM],
    )
    partner_piece = swap(leaving, "fsdp", half)

    flat_pool = kv_pool.reshape(kv_pool.shape[0], page_len * kv_local, 2 * head_dim)
    page_rows = per_holder * page_len * kv_local
    first_pages, second_pages, valid = call(
        functools.partial(pages_kernel, requests, page_len),
        [
            shape((shards, page_rows // 2, 2 * head_dim), bf16),
            shape((shards, page_rows // 2, 2 * head_dim), bf16),
            shape((shards, per_holder * page_len), f32),
        ],
        [
            pltpu.SMEM((2 * per_holder,), jnp.int32),
            pltpu.SMEM((max_blocks + per_holder,), jnp.int32),
            pltpu.SMEM((shards,), jnp.int32),
        ],
        1 << 20,
        1 << 21,
        where,
        block_holder,
        block_slot,
        flat_pool,
        specs=[SMEM, SMEM, SMEM, VMEM],
    )
    q_near, q_far = swap(q_weight, "fsdp", 1), swap(q_weight, "fsdp", 2)
    kv_near = swap(kv_weight, "fsdp", 1)
    partner_piece, q_near, q_far, kv_near, first_pages, second_pages, valid = (
        lax.optimization_barrier(
            (partner_piece, q_near, q_far, kv_near, first_pages, second_pages, valid)
        )
    )
    kv_far = swap(after(kv_weight, partner_piece), "fsdp", 2)
    partner_pieces = pool_pieces(partner_piece, groups)
    arrived = lax.all_to_all(first_pages, "fsdp", split_axis=0, concat_axis=0, tiled=True)
    partner_pieces, kv_far, arrived = lax.optimization_barrier((partner_pieces, kv_far, arrived))
    arrived = [arrived]
    weights = [q_weight, q_near, q_far, swap(q_far, "fsdp", 1)]
    weights += [kv_weight, kv_near, kv_far, swap(kv_far, "fsdp", 1)]
    arrived.append(
        lax.all_to_all(
            after(second_pages, kv_far), "fsdp", split_axis=0, concat_axis=0, tiled=True
        )
    )
    out_weight = lax.all_gather(after(o_weight, *partner_pieces), "pool", axis=0, tiled=False)

    partial = call(
        functools.partial(partner_kernel, groups, half),
        shape((new_len, q_cols + 2 * kv_cols), bf16),
        [
            pltpu.VMEM((new_len, width // 2), bf16),
            pltpu.VMEM((width // 2, q_cols), bf16),
            pltpu.VMEM((width // 2, 2 * kv_cols), bf16),
            pltpu.SemaphoreType.DMA((groups,)),
            pltpu.SemaphoreType.DMA((2 * half,)),
        ],
        new_len * width * (q_cols + 2 * kv_cols),
        width * (new_len + q_cols + 2 * kv_cols),
        where,
        *partner_pieces,
        *weights,
        specs=[SMEM] + [HBM] * (groups + 2 * half),
        mib=24,
    )
    other = swap(partial, "fsdp", half)
    freqs = np.exp(np.arange(head_dim // 2) * (-2.0 * math.log(10000.0) / head_dim))
    freqs = np.concatenate([freqs, freqs]).astype(np.float32).reshape(1, head_dim)
    own, cosine, sine = call(
        functools.partial(own_kernel, requests, half),
        [
            shape((new_len, q_cols + 2 * kv_cols), f32),
            shape((new_len, head_dim), f32),
            shape((new_len, head_dim), f32),
        ],
        [
            pltpu.VMEM((new_len, width), bf16),
            pltpu.VMEM((new_len, width // 2), bf16),
            pltpu.VMEM((width // 2, q_cols), bf16),
            pltpu.VMEM((width // 2, 2 * kv_cols), bf16),
            pltpu.SemaphoreType.DMA((2 * half + 1,)),
        ],
        new_len * width * (q_cols + 2 * kv_cols),
        width * (2 * new_len + q_cols + 2 * kv_cols),
        where,
        after(rows, partial),
        gain,
        freqs,
        *weights,
        specs=[SMEM, HBM, VMEM, VMEM] + [HBM] * (2 * half),
    )

    residual = lax.all_to_all(
        after(my_quarter, own, other, *arrived).reshape(shards, sub, width),
        "fsdp",
        split_axis=0,
        concat_axis=0,
        tiled=True,
    )

    keys_total = max_blocks * page_len
    quarters = call(
        functools.partial(attend_kernel, groups, kv_local, head_dim),
        [shape((quarter, q_cols), bf16)] * groups,
        [
            pltpu.VMEM((kv_local, keys_total, head_dim), bf16),
            pltpu.VMEM((kv_local, keys_total, head_dim), bf16),
            pltpu.VMEM((new_len, q_cols), bf16),
            pltpu.VMEM(other.shape, bf16),
            pltpu.VMEM((shards, page_rows, 2 * head_dim), bf16),
            pltpu.SemaphoreType.DMA((3,)),
        ],
        4 * new_len * q_cols * (keys_total + new_len),
        1 << 22,
        where,
        own,
        other,
        cosine,
        sine,
        valid,
        *arrived,
        specs=[SMEM, VMEM, HBM, VMEM, VMEM, VMEM, HBM, HBM],
    )

    quarters = [
        swap(piece, "pool", distance) if distance else piece
        for distance, piece in enumerate(quarters)
    ]
    quarters = jnp.stack(quarters)
    tokens = {0: quarters}
    for distance in range(2, shards, 2):
        tokens[distance] = swap(quarters, "fsdp", distance)
    for distance in range(0, shards, 2):
        tokens[distance ^ 1] = swap(tokens[distance], "fsdp", 1)
    projected = call(
        functools.partial(output_kernel, groups, shards),
        [shape((shards, sub, features), bf16)] * shards,
        [
            pltpu.VMEM((shards * quarter, features), f32),
        ],
        2 * shards * quarter * features * groups * q_cols,
        1 << 22,
        where,
        *[tokens[distance] for distance in range(shards)],
        out_weight,
        mib=24,
    )
    finished = [
        swap(piece, "fsdp", distance) if distance else piece
        for distance, piece in enumerate(projected)
    ]
    return call(
        functools.partial(finish_kernel, shards),
        shape((requests, sub, width), bf16),
        [pltpu.VMEM((shards, shards, sub, features), f32)],
        1 << 20,
        1 << 20,
        where,
        post_gain.reshape(1, width),
        residual,
        *finished,
        mib=24,
    )


def local(*arguments):
    return local_small(*arguments) if lax.axis_size("fsdp") == 8 else local_general(*arguments)


def solution(mesh):
    in_specs = (
        P("fsdp", None, None),
        P(),
        P(),
        P(),
        P(),
        P("fsdp", None, "pool", None),
        P(),
        P("fsdp", "pool"),
        P("fsdp", "pool"),
        P("fsdp", "pool"),
        P("fsdp", "pool"),
        P(),
    )
    out_specs = P(None, ("pool", "fsdp"), None)
    return jax.shard_map(local, mesh=mesh, in_specs=in_specs, out_specs=out_specs, check_vma=False)
```
